32 devices in a mesh: dp: 4 (over z), context: 4 (over x, core), expert: 2 (over y).
Axes of the slice: x: 2, y: 2, z: 4, core: 2. Of those that a mesh axis runs over, the one named last changes fastest.
Arguments:
- tokens: bfloat16 [4096, 2048], P(('dp', 'context', 'expert')), may hold values from -6 to 6
- out_grad: bfloat16 [4096, 2048], P(('dp', 'context', 'expert')), may hold values from -6 to 6
- expert_ids: int32 [4096, 4], P(('dp', 'context', 'expert')), may hold values from 0 to 7, all different within a row; in each aligned block of 128 rows (0 to 127, 128 to 255, ...) at most 96 rows name the same one
- norm1_gain: bfloat16 [2048], P(('dp', 'context')), may hold values from 0.5 to 1.5
- w_query: bfloat16 [2048, 2048], P(('dp', 'context'), 'expert'), may hold values from -0.125 to 0.125
- w_key: bfloat16 [2048, 2048], P(('dp', 'context'), 'expert'), may hold values from -0.125 to 0.125
- w_value: bfloat16 [2048, 2048], P(('dp', 'context'), 'expert'), may hold values from -0.125 to 0.125
- query_bias_heads: bfloat16 [16, 128], P('expert'), may hold values from -3 to 3
- bias_key: bfloat16 [16, 128], P('expert'), may hold values from -3 to 3
- bias_value: bfloat16 [16, 128], P('expert'), may hold values from -0.119628906 to 0.119628906
- w_out: bfloat16 [2048, 2048], P('expert', ('dp', 'context')), may hold values from -3 to 3
- norm2_gain: bfloat16 [2048], P(('dp', 'context')), may hold values from 0.5 to 1.5
- w_router: bfloat16 [2048, 8], P(('dp', 'context')), may hold values from -0.0625 to 0.0625
- shared_mix: bfloat16 [2048], P(('dp', 'context')), may hold values from -0.125 to 0.125
- shared_in_gate: bfloat16 [2048, 5632], P(('dp', 'context'), 'expert'), may hold values from -0.125 to 0.125
- shared_in_up: bfloat16 [2048, 5632], P(('dp', 'context'), 'expert'), may hold values from -0.125 to 0.125
- shared_down: bfloat16 [5632, 2048], P('expert', ('dp', 'context')), may hold values from -0.21875 to 0.21875
- expert_gate: bfloat16 [8, 2048, 1408], P(('dp', 'expert')), may hold values from -0.125 to 0.125
- expert_up: bfloat16 [8, 2048, 1408], P(('dp', 'expert')), may hold values from -0.125 to 0.125
- expert_down: bfloat16 [8, 1408, 2048], P(('dp', 'expert')), may hold values from -1.25 to 1.25
Outputs:
- mixed: bfloat16 [4096, 2048], P(('dp', 'context', 'expert'))
- input_grad: bfloat16 [4096, 2048], P(('dp', 'context', 'expert'))
- norm1_gain_grad: float32 [2048], P(('dp', 'context'))
- w_query_grad: float32 [2048, 2048], P(('dp', 'context'), 'expert')
- w_key_grad: float32 [2048, 2048], P(('dp', 'context'), 'expert')
- w_value_grad: float32 [2048, 2048], P(('dp', 'context'), 'expert')
- bias_query_grad: float32 [16, 128], P('expert', ('dp', 'context'))
- bias_key_grad: float32 [16, 128], P('expert', ('dp', 'context'))
- bias_value_grad: float32 [16, 128], P('expert', ('dp', 'context'))
- w_out_grad: float32 [2048, 2048], P('expert', ('dp', 'context'))
- norm2_gain_grad: float32 [2048], P(('dp', 'context'))
- w_router_grad: float32 [2048, 8], P(('dp', 'context'))
- shared_mix_grad: float32 [2048], P(('dp', 'context'))
- shared_in_gate_grad: float32 [2048, 5632], P(('dp', 'context'), 'expert')
- shared_in_up_grad: float32 [2048, 5632], P(('dp', 'context'), 'expert')
- shared_down_grad: float32 [5632, 2048], P('expert', ('dp', 'context'))
- expert_gate_grad: float32 [8, 2048, 1408], P(('dp', 'expert'), 'context')
- expert_up_grad: float32 [8, 2048, 1408], P(('dp', 'expert'), 'context')
- expert_down_grad: float32 [8, 1408, 2048], P(('dp', 'expert'), None, 'context')
The draws below stay inside these ranges and needn't reach their ends.
Inputs may be any that keep to these rules, and one draw needn't show every extreme that they name: `expert_ids`: each row names 4 different experts. In the rows of one device no expert is named more than 96 times, and 96 is reached on some device in every draw.
All inputs are finite; a program needn't handle non-finite values.
Results may differ from the reference program's by a relative error of at most 0.023.
Values may be sent and summed in bfloat16 or wider, within the bound.
A program may use at most 320 MiB of HBM per device.

```python
import math
import jax
import jax.numpy as jnp
import numpy as np
from jax import lax

D = 2048
HEADS = 16
HEAD_DIM = 128
FF_E = 1408
FFS = 5632
TOP = 4
BLOCK = 256
TOK_DEV = 128
CAP = 96
SEQ = 1024
TOKENS = 4096
EXPERTS = 8
N_DP = 4


def with_spikes(array, stream_key, source, target, blocks, factor):
    owner, partner = [(jnp.arange(array.shape[position]) // (array.shape[position] // blocks)).reshape([-1 if axis == position else 1 for axis in range(array.ndim)]) for position in (source, target)]
    chosen = jax.random.permutation(stream_key, blocks)[partner]
    strong = (owner == chosen) | (owner == (partner + blocks // 2) % blocks)
    return jnp.where(strong, factor * array, array)


def steps_of(stream_key, shape, pieces, smallest, top_value):
    def one(dim, blocks):
        draws = jax.random.uniform(jax.random.fold_in(jax.random.fold_in(stream_key, 6), dim), (blocks,), jnp.float32, smallest / len(pieces), top_value / len(pieces))
        return jnp.repeat(jnp.exp(draws), shape[dim] // blocks).reshape((-1,) + (1,) * (len(shape) - dim - 1))

    gain = one(*pieces[0])
    for cut in pieces[1:]:
        gain = gain * one(*cut)
    return gain


def shared_out(own_key, own, number, rows, count, top, bound, slope):
    sequence = jax.random.permutation(own_key, count)
    heavy_load, common = shares(count, rows * top, bound, slope, True), shares(count, rows * top, bound, slope, False)
    places = jnp.arange(count)

    def named(lengths, turn):
        used = int((lengths > 0).sum())
        fixed = max(1, used // 4)
        moved = fixed + (places - fixed + turn * (used - fixed)) % max(1, count - fixed)
        return jnp.zeros((count,), jnp.int32).at[sequence[jnp.where(places < fixed, places, moved)]].set(jnp.asarray(lengths, jnp.int32))

    lengths = jnp.where(number % 4 == 0, named(heavy_load, number // 4), named(common, number - number // 4 - 1))
    mixed = jax.random.permutation(jax.random.fold_in(own, 3), count)
    giver, taker = mixed[0:count // 2 * 2:2], mixed[1:count // 2 * 2:2]
    slack = jnp.minimum(lengths[giver] - 1, bound - lengths[taker]) // 2
    slack = jnp.where((giver == sequence[0]) | (taker == sequence[0]) | (lengths[taker] == 0), 0, jnp.maximum(slack, 0))
    moved = jax.random.randint(jax.random.fold_in(own, 4), (count // 2,), 0, 1 << 20) % (slack + 1)
    lengths = lengths.at[giver].add(-moved).at[taker].add(moved)
    items = jnp.searchsorted(jnp.cumsum(lengths), jnp.arange(rows * top), side="right").astype(jnp.int32)
    grid = items.reshape(top, rows).T
    grid = grid[jax.random.permutation(jax.random.fold_in(own, 1), rows)]
    turn = jax.random.randint(jax.random.fold_in(own, 2), (rows, 1), 0, top)
    return jnp.take_along_axis(grid, (jnp.arange(top)[None, :] + turn) % top, axis=1)


def shares(count, total, most, skew, full):
    loads = [(1 << 20) // math.isqrt(standing ** skew) + 1 for standing in range(1, count + 1)]
    largest = most if full else min(most, max(-(-total // count), total * loads[0] // sum(loads)))
    least = 1 if total - largest >= count - 1 else 0
    counts, spare = [largest] + [least] * (count - 1), total - largest - least * (count - 1)
    while spare > 0:
        free = [i for i in range(1, count) if counts[i] < largest] or [i for i in range(1, count) if counts[i] < most]
        mass, budget = sum([loads[i] for i in free]), spare
        for i in free:
            more = min(most - counts[i], max(1, budget * loads[i] // mass), spare)
            counts[i] = counts[i] + more
            spare = spare - more
    return np.array(counts)


def scatter_about(rng, extent, deviation, limit, shards=(), kind=jnp.bfloat16):
    factor_of = steps_of(rng, extent, shards, -0.22, 0.18) if shards else 1.0
    drawn = jax.random.normal(rng, extent, jnp.float32) * deviation * factor_of
    return jnp.minimum(jnp.maximum(drawn, -limit), limit).astype(kind)


def heavy_noise(stream_key, shape, scale, most, cuts, heavy, held_as=jnp.bfloat16):
    array = scale * jax.random.normal(stream_key, shape, jnp.float32)
    if cuts:
        array = array * steps_of(stream_key, shape, cuts, -0.22, 0.18)
    return jnp.clip(with_spikes(array, jax.random.fold_in(stream_key, 3), *heavy), -most, most).astype(held_as)


def setup_inputs(seed: int = 0) -> dict:
    streams_of = jax.random.split(jax.random.key(seed), 21)
    tokens = scatter_about(streams_of[0], (TOKENS, D), 1.0, 6.0, ((0, 32),))
    out_grad = heavy_noise(streams_of[1], (TOKENS, D), 1.0, 6.0, ((0, 32),), (0, 1, 32, 2.75))
    expert_ids_keys = jax.random.split(jax.random.fold_in(streams_of[2], 1), TOKENS // TOK_DEV)
    expert_ids_turns = jax.random.permutation(jax.random.fold_in(streams_of[2], 3), TOKENS // TOK_DEV)
    expert_ids = jax.vmap(lambda own, number: shared_out(jax.random.fold_in(streams_of[2], 2), own, number, TOK_DEV, EXPERTS, TOP, CAP, 2))(expert_ids_keys, expert_ids_turns).reshape((TOKENS, TOP))
    norm1_gain = jnp.clip(1.0 + 0.1 * jax.random.normal(streams_of[3], (D,), jnp.float32), 0.5, 1.5).astype(jnp.bfloat16)
    w_query = scatter_about(streams_of[4], (D, D), D ** -0.5, 0.125, ((0, 16), (1, 2)))
    w_key = scatter_about(streams_of[5], (D, D), D ** -0.5, 0.125, ((0, 16), (1, 2)))
    w_value = scatter_about(streams_of[6], (D, D), D ** -0.5, 0.125, ((0, 16), (1, 2)))
    query_bias_heads = scatter_about(streams_of[7], (HEADS, HEAD_DIM), 0.5, 3.0, ((0, 2),))
    bias_key = scatter_about(streams_of[8], (HEADS, HEAD_DIM), 0.5, 3.0, ((0, 2),))
    bias_value = scatter_about(streams_of[9], (HEADS, HEAD_DIM), 0.02, 0.119628906, ((0, 2),))
    w_out = scatter_about(streams_of[10], (D, D), 4 ** -0.5, 3.0, ((0, 2), (1, 16)))
    norm2_gain = jnp.clip(1.0 + 0.1 * jax.random.normal(streams_of[11], (D,), jnp.float32), 0.5, 1.5).astype(jnp.bfloat16)
    w_router = scatter_about(streams_of[12], (D, EXPERTS), (4 * D) ** -0.5, 0.0625, ((0, 16),))
    shared_mix = scatter_about(streams_of[13], (D,), D ** -0.5, 0.125, ((0, 16),))
    shared_in_gate = scatter_about(streams_of[14], (D, FFS), D ** -0.5, 0.125, ((0, 16), (1, 2)))
    shared_in_up = scatter_about(streams_of[15], (D, FFS), D ** -0.5, 0.125, ((0, 16), (1, 2)))
    shared_down = scatter_about(streams_of[16], (FFS, D), (FFS // 8) ** -0.5, 0.21875, ((0, 2), (1, 16)))
    expert_gate = scatter_about(streams_of[17], (EXPERTS, D, FF_E), D ** -0.5, 0.125, ((0, 8),))
    expert_up = scatter_about(streams_of[18], (EXPERTS, D, FF_E), D ** -0.5, 0.125, ((0, 8),))
    expert_down = scatter_about(streams_of[19], (EXPERTS, FF_E, D), (FF_E // 64) ** -0.5, 1.25, ((0, 8),))
    return {"tokens": tokens, "out_grad": out_grad, "expert_ids": expert_ids, "norm1_gain": norm1_gain, "w_query": w_query, "w_key": w_key, "w_value": w_value, "query_bias_heads": query_bias_heads, "bias_key": bias_key, "bias_value": bias_value, "w_out": w_out, "norm2_gain": norm2_gain, "w_router": w_router, "shared_mix": shared_mix, "shared_in_gate": shared_in_gate, "shared_in_up": shared_in_up, "shared_down": shared_down, "expert_gate": expert_gate, "expert_up": expert_up, "expert_down": expert_down}


EPS = 1e-06
THETA = 1000000.0
HIGH = lax.Precision.HIGHEST

@jax.custom_vjp
def low(v):
    return lax.optimization_barrier(v.astype(jnp.bfloat16)).astype(jnp.float32)

@jax.custom_vjp
def low_back(v):
    return v

def low_keep(v):
    return (low(v), None)

def low_pass(kept, grad):
    return (grad,)

def back_keep(v):
    return (v, None)

def back_low(kept, grad):
    return (low(grad),)
low.defvjp(low_keep, low_pass)
low_back.defvjp(back_keep, back_low)

def matmul(left, right):
    return jnp.dot(left, right, precision=HIGH)

def rms_scale(values):
    return values * lax.rsqrt(lax.optimization_barrier(jnp.mean(values * values, axis=-1, keepdims=True)) + EPS)

def rope_tables(positions, head_dim):
    half = head_dim // 2
    freq = THETA ** (-(2.0 * jnp.arange(half, dtype=jnp.float32)) / head_dim)
    angle = positions.astype(jnp.float32)[:, None] * freq[None, :]
    return (jnp.cos(angle)[:, None, :], jnp.sin(angle)[:, None, :])

def rotate(values, cosine, sine):
    half = values.shape[-1] // 2
    first = values[..., :half]
    second = values[..., half:]
    return jnp.concatenate([first * cosine - second * sine, second * cosine + first * sine], axis=-1)

def layer(params, rows, route_ids):
    gain_one, w_query, w_key, w_value, query_bias_heads, bias_key, bias_value, w_out, gain_two, w_router, shared_mix, shared_in_gate, shared_in_up, shared_down, expert_gate, expert_up, expert_down = params
    seq_len = rows.shape[0]
    heads = query_bias_heads.shape[0]
    head_dim = query_bias_heads.shape[1]
    positions = jnp.arange(seq_len)
    cosine, sine = rope_tables(positions, head_dim)
    attn_in = low(rms_scale(rows) * gain_one)
    q_pre = low_back(matmul(attn_in, w_query) + query_bias_heads.reshape(-1))
    k_pre = low_back(matmul(attn_in, w_key) + bias_key.reshape(-1))
    v_pre = low_back(matmul(attn_in, w_value) + bias_value.reshape(-1))
    query = low(rotate(q_pre.reshape(seq_len, heads, head_dim), cosine, sine))
    keys = low(rotate(k_pre.reshape(seq_len, heads, head_dim), cosine, sine))
    values = low(v_pre.reshape(seq_len, heads, head_dim))
    blocks = positions // BLOCK
    visible = blocks[None, :] <= blocks[:, None]
    score_scale = 1.0 / math.sqrt(head_dim)

    def one_head(args):
        head_query, head_keys, head_values = args
        scores = low_back(matmul(head_query, head_keys.T) * score_scale)
        probs = jax.nn.softmax(jnp.where(visible, scores, -jnp.inf), axis=-1)
        return matmul(low(probs), head_values)
    attn = lax.map(jax.checkpoint(one_head), (query.transpose(1, 0, 2), keys.transpose(1, 0, 2), values.transpose(1, 0, 2)))
    attn = low(low_back(attn.transpose(1, 0, 2).reshape(seq_len, heads * head_dim)))
    hidden_one = rows + low_back(matmul(attn, w_out))
    moe_in = low(rms_scale(hidden_one) * gain_two)
    router_probs = jax.nn.softmax(matmul(moe_in, w_router), axis=-1)
    n_experts = w_router.shape[1]
    picked = (route_ids[:, :, None] == jnp.arange(n_experts)[None, None, :]).astype(jnp.float32)
    weights = lax.optimization_barrier(jnp.sum(picked * router_probs[:, None, :], axis=1))
    mix = jax.nn.sigmoid(matmul(moe_in, shared_mix))
    s_gate = low_back(matmul(moe_in, shared_in_gate))
    s_up = low_back(matmul(moe_in, shared_in_up))
    s_hidden = low(jax.nn.silu(s_gate) * s_up)
    shared = low_back(matmul(s_hidden, shared_down))

    def one_expert(total, args):
        gate_weight, up_weight, down_weight, weight_column = args
        expert_in = low_back(moe_in)
        e_gate = low_back(matmul(expert_in, gate_weight))
        e_up = low_back(matmul(expert_in, up_weight))
        e_hidden = low(jax.nn.silu(e_gate) * e_up)
        e_out = low(low_back(matmul(e_hidden, down_weight)))
        return (total + weight_column[:, None] * e_out, None)
    routed, unused = lax.scan(jax.checkpoint(one_expert), jnp.zeros_like(rows), (expert_gate, expert_up, expert_down, weights.T))
    return hidden_one + routed + mix[:, None] * shared

def reference(tokens, out_grad, expert_ids, norm1_gain, w_query, w_key, w_value, query_bias_heads, bias_key, bias_value, w_out, norm2_gain, w_router, shared_mix, shared_in_gate, shared_in_up, shared_down, expert_gate, expert_up, expert_down):
    params = tuple((item.astype(jnp.float32) for item in (norm1_gain, w_query, w_key, w_value, query_bias_heads, bias_key, bias_value, w_out, norm2_gain, w_router, shared_mix, shared_in_gate, shared_in_up, shared_down, expert_gate, expert_up, expert_down)))
    rows_all = tokens.astype(jnp.float32).reshape(N_DP, SEQ, D)
    cotangents = out_grad.astype(jnp.float32).reshape(N_DP, SEQ, D)
    ids_all = expert_ids.reshape(N_DP, SEQ, TOP)

    def one_sequence(totals, args):
        rows, cotangent, route_ids = args
        output, pullback = jax.vjp(lambda given, inputs: layer(given, inputs, route_ids), params, rows)
        param_grads, row_grads = pullback(cotangent)
        totals = jax.tree.map(lambda left, right: left + right, totals, param_grads)
        return (totals, (output, row_grads))
    zeros = jax.tree.map(jnp.zeros_like, params)
    totals, (outputs, row_grads) = lax.scan(one_sequence, zeros, (rows_all, cotangents, ids_all))
    return (outputs.reshape(TOKENS, D).astype(jnp.bfloat16), row_grads.reshape(TOKENS, D).astype(jnp.bfloat16), totals[0], totals[1], totals[2], totals[3], totals[4], totals[5], totals[6], totals[7], totals[8], totals[9], totals[10], totals[11], totals[12], totals[13], totals[14], totals[15], totals[16])
```

```python
import math

import jax
import jax.numpy as jnp
from jax import lax
from jax.experimental import pallas as pl
from jax.experimental.pallas import tpu as pltpu
from jax.sharding import PartitionSpec as P

DP, CONTEXT, EXPERT = "dp", "context", "expert"
BLOCK = 256
CAP = 96


EPS = 1e-06
THETA = 1000000.0
HIGH = lax.Precision.HIGHEST


def rope_tables(positions, head_dim):
    half = head_dim // 2
    freq = THETA ** (-(2.0 * jnp.arange(half, dtype=jnp.float32)) / head_dim)
    angle = positions.astype(jnp.float32)[:, None] * freq[None, :]
    return (jnp.cos(angle)[:, None, :], jnp.sin(angle)[:, None, :])


def rotate(values, cosine, sine):
    half = values.shape[-1] // 2
    first = values[..., :half]
    second = values[..., half:]
    return jnp.concatenate(
        [first * cosine - second * sine, second * cosine + first * sine], axis=-1
    )


def rotate_back(values, cosine, sine):
    half = values.shape[-1] // 2
    first = values[..., :half]
    second = values[..., half:]
    return jnp.concatenate(
        [first * cosine + second * sine, second * cosine - first * sine], axis=-1
    )


def to_groups(matrix, groups, group_size, head_dim):
    return matrix.reshape(matrix.shape[0], groups, group_size, head_dim).transpose(1, 2, 0, 3)


def from_groups(stacked):
    return stacked.transpose(2, 0, 1, 3).reshape(stacked.shape[2], -1)


def silu_slope(values):
    sigma = jax.nn.sigmoid(values)
    return sigma * (1.0 + values * (1.0 - sigma))


def left_operand(left, right):
    return jnp.dot(left.T, right, preferred_element_type=jnp.float32)


def mat_right(left, right):
    return jnp.dot(left, right.T, preferred_element_type=jnp.float32)


def weights_plan(
    tokens,
    out_grad,
    expert_ids,
    norm1_gain,
    w_query,
    w_key,
    w_value,
    query_bias_heads,
    bias_key,
    bias_value,
    w_out,
    norm2_gain,
    w_router,
    shared_mix,
    shared_in_gate,
    shared_in_up,
    shared_down,
    expert_gate,
    expert_up,
    expert_down,
):
    tok_rows = tokens.shape[0]
    width = tokens.shape[1]
    my_half = lax.axis_index(EXPERT)
    my_piece = lax.axis_index(CONTEXT)
    n_pieces = lax.axis_size(CONTEXT)
    local_heads = query_bias_heads.shape[0]
    head_dim = query_bias_heads.shape[1]
    group_size = 2
    groups = local_heads // group_size
    score_scale = 1.0 / math.sqrt(head_dim)
    (
        full_query,
        full_key,
        full_value,
        full_out,
        full_sgate,
        full_sup,
        full_sdown,
        full_router,
        full_mix,
        full_gain_one,
        full_gain_two,
    ) = (
        lax.all_gather(w_query, (DP, CONTEXT), axis=0, tiled=True),
        lax.all_gather(w_key, (DP, CONTEXT), axis=0, tiled=True),
        lax.all_gather(w_value, (DP, CONTEXT), axis=0, tiled=True),
        lax.all_gather(w_out, (DP, CONTEXT), axis=1, tiled=True),
        lax.all_gather(shared_in_gate, (DP, CONTEXT), axis=0, tiled=True),
        lax.all_gather(shared_in_up, (DP, CONTEXT), axis=0, tiled=True),
        lax.all_gather(shared_down, (DP, CONTEXT), axis=1, tiled=True),
        lax.all_gather(w_router, (DP, CONTEXT), axis=0, tiled=True),
        lax.all_gather(shared_mix, (DP, CONTEXT), axis=0, tiled=True),
        lax.all_gather(norm1_gain, (DP, CONTEXT), axis=0, tiled=True),
        lax.all_gather(norm2_gain, (DP, CONTEXT), axis=0, tiled=True),
    )
    x_piece, dy_piece = (
        lax.all_gather(tokens, EXPERT, axis=0, tiled=True),
        lax.all_gather(out_grad, EXPERT, axis=0, tiled=True),
    )
    piece_rows = x_piece.shape[0]
    seq_len = piece_rows * n_pieces
    own_start = my_half * tok_rows
    positions = my_piece * piece_rows + jnp.arange(piece_rows)
    cosine, sine = rope_tables(positions, head_dim)
    query_blocks = positions // BLOCK
    key_blocks = jnp.arange(seq_len) // BLOCK
    visible = key_blocks[None, :] <= query_blocks[:, None]
    x_float = x_piece.astype(jnp.float32)
    rstd_one = lax.rsqrt(jnp.mean(x_float * x_float, axis=1, keepdims=True) + EPS)
    normed_one = x_float * rstd_one
    gain_one = full_gain_one.astype(jnp.float32)
    attn_in = (normed_one * gain_one).astype(jnp.bfloat16)
    q_pre = jnp.dot(
        attn_in, full_query, preferred_element_type=jnp.float32
    ) + query_bias_heads.astype(jnp.float32).reshape(-1)
    k_pre = jnp.dot(attn_in, full_key, preferred_element_type=jnp.float32) + bias_key.astype(
        jnp.float32
    ).reshape(-1)
    v_pre = jnp.dot(attn_in, full_value, preferred_element_type=jnp.float32) + bias_value.astype(
        jnp.float32
    ).reshape(-1)
    q_rot = (
        rotate(q_pre.reshape(piece_rows, local_heads, head_dim), cosine, sine)
        .reshape(piece_rows, -1)
        .astype(jnp.bfloat16)
    )
    k_rot = (
        rotate(k_pre.reshape(piece_rows, local_heads, head_dim), cosine, sine)
        .reshape(piece_rows, -1)
        .astype(jnp.bfloat16)
    )
    v_low = v_pre.astype(jnp.bfloat16)
    keys_all, values_all = (
        lax.all_gather(k_rot, CONTEXT, axis=0, tiled=True),
        lax.all_gather(v_low, CONTEXT, axis=0, tiled=True),
    )
    query_grp = to_groups(q_rot, groups, group_size, head_dim)
    keys_grp = to_groups(keys_all, groups, group_size, head_dim)
    values_grp = to_groups(values_all, groups, group_size, head_dim)

    def attend_group(args):
        group_query, group_keys, group_values = args
        scores = (
            jnp.einsum("hqd,hkd->hqk", group_query, group_keys, preferred_element_type=jnp.float32)
            * score_scale
        )
        scores = jnp.where(visible[None], scores, -jnp.inf)
        row_top = jnp.max(scores, axis=2, keepdims=True)
        expo = jnp.exp(scores - row_top)
        totals = jnp.sum(expo, axis=2, keepdims=True)
        probs = (expo / totals).astype(jnp.bfloat16)
        result = jnp.einsum("hqk,hkd->hqd", probs, group_values, preferred_element_type=jnp.float32)
        return (result, row_top[..., 0] + jnp.log(totals[..., 0]))

    attn_grp, lse_grp = lax.map(attend_group, (query_grp, keys_grp, values_grp))
    attn_low = from_groups(attn_grp).astype(jnp.bfloat16)
    out_partial = jnp.dot(attn_low, full_out, preferred_element_type=jnp.float32)
    out_full = lax.psum(out_partial, EXPERT)
    hidden_one = x_float + out_full
    rstd_two = lax.rsqrt(jnp.mean(hidden_one * hidden_one, axis=1, keepdims=True) + EPS)
    normed_two = hidden_one * rstd_two
    gain_two = full_gain_two.astype(jnp.float32)
    moe_in = (normed_two * gain_two).astype(jnp.bfloat16)
    mix = jax.nn.sigmoid(jnp.dot(moe_in, full_mix, preferred_element_type=jnp.float32))
    s_gate = jnp.dot(moe_in, full_sgate, preferred_element_type=jnp.float32)
    s_up = jnp.dot(moe_in, full_sup, preferred_element_type=jnp.float32)
    s_silu = jax.nn.silu(s_gate)
    s_hidden = (s_silu * s_up).astype(jnp.bfloat16)
    shared_own = lax.psum_scatter(
        jnp.dot(s_hidden, full_sdown, preferred_element_type=jnp.float32),
        EXPERT,
        scatter_dimension=0,
        tiled=True,
    )
    moe_own = lax.dynamic_slice_in_dim(moe_in, own_start, tok_rows, 0)
    hidden_own = lax.dynamic_slice_in_dim(hidden_one, own_start, tok_rows, 0)
    mix_own = lax.dynamic_slice_in_dim(mix, own_start, tok_rows, 0)
    dy_own = out_grad.astype(jnp.float32)
    n_experts = full_router.shape[1]
    router_probs = jax.nn.softmax(
        jnp.dot(moe_own, full_router, preferred_element_type=jnp.float32), axis=1
    )
    picked = (expert_ids[:, :, None] == jnp.arange(n_experts)[None, None, :]).astype(jnp.float32)
    gates = jnp.sum(picked * router_probs[:, None, :], axis=2)
    route_hot = (
        (expert_ids[:, :, None] == jnp.arange(n_experts)[None, None, :])
        .astype(jnp.int32)
        .reshape(-1, n_experts)
    )
    earlier = jnp.cumsum(route_hot, axis=0) - route_hot
    slots = jnp.sum(earlier * route_hot, axis=1)
    places = expert_ids.reshape(-1) * CAP + slots
    route_rows = jnp.repeat(moe_own, expert_ids.shape[1], axis=0)
    route_grads = (
        gates.reshape(-1)[:, None] * jnp.repeat(dy_own, expert_ids.shape[1], axis=0)
    ).astype(jnp.bfloat16)
    send_rows = (
        jnp.zeros((n_experts * CAP, width), jnp.bfloat16)
        .at[places]
        .set(route_rows)
        .reshape(n_experts, CAP, width)
    )
    send_grads = (
        jnp.zeros((n_experts * CAP, width), jnp.bfloat16)
        .at[places]
        .set(route_grads)
        .reshape(n_experts, CAP, width)
    )
    gate_weight = expert_gate[0]
    up_weight = expert_up[0]
    down_weight = expert_down[0]
    rows_in = lax.all_to_all(send_rows, (DP, EXPERT), split_axis=0, concat_axis=0, tiled=True)
    grads_in = lax.all_to_all(send_grads, (DP, EXPERT), split_axis=0, concat_axis=0, tiled=True)
    sources = rows_in.shape[0]
    items = rows_in.shape[1]
    flat_in = rows_in.reshape(-1, width)
    flat_grad = grads_in.reshape(-1, width)
    e_gate = jnp.dot(flat_in, gate_weight, preferred_element_type=jnp.float32)
    e_up = jnp.dot(flat_in, up_weight, preferred_element_type=jnp.float32)
    e_silu = jax.nn.silu(e_gate)
    e_hidden = (e_silu * e_up).astype(jnp.bfloat16)
    e_out = jnp.dot(e_hidden, down_weight, preferred_element_type=jnp.float32).astype(jnp.bfloat16)
    d_hidden = mat_right(flat_grad, down_weight)
    d_gate = (d_hidden * e_up * silu_slope(e_gate)).astype(jnp.bfloat16)
    d_up = (d_hidden * e_silu).astype(jnp.bfloat16)
    d_in = (mat_right(d_gate, gate_weight) + mat_right(d_up, up_weight)).astype(jnp.bfloat16)
    back_out = lax.all_to_all(
        e_out.reshape(sources, items, width),
        (DP, EXPERT),
        split_axis=0,
        concat_axis=0,
        tiled=True,
    )
    back_in = lax.all_to_all(
        d_in.reshape(sources, items, width),
        (DP, EXPERT),
        split_axis=0,
        concat_axis=0,
        tiled=True,
    )
    back_out, back_in, rows_seen, grads_seen, hidden_seen, dgate_seen, duplicate_visits = (
        back_out,
        back_in,
        rows_in,
        grads_in,
        e_hidden.reshape(sources, items, -1),
        d_gate.reshape(sources, items, -1),
        d_up.reshape(sources, items, -1),
    )
    flattened_rows = rows_seen.reshape(-1, width)
    routed_gate_gradient = left_operand(
        flattened_rows, dgate_seen.reshape(flattened_rows.shape[0], -1)
    )
    routed_up_gradient = left_operand(
        flattened_rows, duplicate_visits.reshape(flattened_rows.shape[0], -1)
    )
    routed_down_gradient = left_operand(
        hidden_seen.reshape(flattened_rows.shape[0], -1), grads_seen.reshape(-1, width)
    )
    routed_gate_gradient, routed_up_gradient, routed_down_gradient = (
        lax.psum_scatter(
            routed_gate_gradient[None].astype(jnp.bfloat16),
            CONTEXT,
            scatter_dimension=1,
            tiled=True,
        ).astype(jnp.float32),
        lax.psum_scatter(
            routed_up_gradient[None].astype(jnp.bfloat16),
            CONTEXT,
            scatter_dimension=1,
            tiled=True,
        ).astype(jnp.float32),
        lax.psum_scatter(
            routed_down_gradient[None].astype(jnp.bfloat16),
            CONTEXT,
            scatter_dimension=2,
            tiled=True,
        ).astype(jnp.float32),
    )
    route_out = back_out.reshape(-1, width)[places].astype(jnp.float32).reshape(tok_rows, -1, width)
    route_din = back_in.reshape(-1, width)[places].astype(jnp.float32).reshape(tok_rows, -1, width)
    moe_sum = jnp.sum(gates[:, :, None] * route_out, axis=1)
    mixed = (hidden_own + moe_sum + mix_own[:, None] * shared_own).astype(jnp.bfloat16)
    d_gates = jnp.sum(route_out * dy_own[:, None, :], axis=2)
    d_rprobs = jnp.sum(picked * d_gates[:, :, None], axis=1)
    d_logits = router_probs * (d_rprobs - jnp.sum(router_probs * d_rprobs, axis=1, keepdims=True))
    moe_own_float = moe_own.astype(jnp.float32)
    router_part = jnp.dot(moe_own_float.T, d_logits, precision=HIGH)
    d_mixlogit = jnp.sum(shared_own * dy_own, axis=1) * mix_own * (1.0 - mix_own)
    mix_part = jnp.dot(moe_own_float.T, d_mixlogit, precision=HIGH)
    d_in_own = (
        jnp.sum(route_din, axis=1)
        + jnp.dot(d_logits, full_router.astype(jnp.float32).T, precision=HIGH)
        + d_mixlogit[:, None] * full_mix.astype(jnp.float32)[None, :]
    )
    dy_float = dy_piece.astype(jnp.float32)
    d_shared = (mix[:, None] * dy_float).astype(jnp.bfloat16)
    grad_sdown = left_operand(s_hidden, d_shared)
    d_shidden = mat_right(d_shared, full_sdown)
    d_sgate = (d_shidden * s_up * silu_slope(s_gate)).astype(jnp.bfloat16)
    d_sup = (d_shidden * s_silu).astype(jnp.bfloat16)
    grad_sgate = left_operand(moe_in, d_sgate)
    grad_sup = left_operand(moe_in, d_sup)
    d_in_part = mat_right(d_sgate, full_sgate) + mat_right(d_sup, full_sup)
    d_in_part = lax.dynamic_update_slice_in_dim(
        d_in_part,
        lax.dynamic_slice_in_dim(d_in_part, own_start, tok_rows, 0) + d_in_own,
        own_start,
        0,
    )
    d_moe_in, router_grad, mix_grad = lax.psum((d_in_part, router_part, mix_part), EXPERT)
    d_norm_two = d_moe_in * gain_two
    gain_two_grad = jnp.sum(d_moe_in * normed_two, axis=0)
    d_hidden_one = dy_float + rstd_two * (
        d_norm_two - normed_two * jnp.mean(d_norm_two * normed_two, axis=1, keepdims=True)
    )
    d_proj = d_hidden_one.astype(jnp.bfloat16)
    grad_out = left_operand(attn_low, d_proj)
    d_attn = mat_right(d_proj, full_out).astype(jnp.bfloat16)
    dattn_grp = to_groups(d_attn, groups, group_size, head_dim)

    def query_side(args):
        group_query, group_keys, group_values, group_lse, group_attention_gradient = args
        scores = (
            jnp.einsum("hqd,hkd->hqk", group_query, group_keys, preferred_element_type=jnp.float32)
            * score_scale
        )
        probs = jnp.where(
            visible[None],
            jnp.exp(jnp.where(visible[None], scores, 0.0) - group_lse[..., None]),
            0.0,
        )
        d_probs = jnp.einsum(
            "hqd,hkd->hqk",
            group_attention_gradient,
            group_values,
            preferred_element_type=jnp.float32,
        )
        delta = jnp.sum(probs * d_probs, axis=2)
        d_scores = (probs * (d_probs - delta[..., None])).astype(jnp.bfloat16)
        d_query = (
            jnp.einsum("hqk,hkd->hqd", d_scores, group_keys, preferred_element_type=jnp.float32)
            * score_scale
        )
        return (probs, d_scores, d_query, delta)

    def both_sides(args):
        probs, d_scores, d_query, delta = query_side(args)
        d_key = (
            jnp.einsum("hqk,hqd->hkd", d_scores, args[0], preferred_element_type=jnp.float32)
            * score_scale
        )
        d_value = jnp.einsum(
            "hqk,hqd->hkd", probs.astype(jnp.bfloat16), args[4], preferred_element_type=jnp.float32
        )
        return (d_query, d_key, d_value)

    dq_grp, dk_grp, dv_grp = lax.map(
        both_sides, (query_grp, keys_grp, values_grp, lse_grp, dattn_grp)
    )
    d_query = from_groups(dq_grp)
    d_key_own, d_value_own = (
        lax.psum_scatter(from_groups(dk_grp), CONTEXT, scatter_dimension=0, tiled=True),
        lax.psum_scatter(from_groups(dv_grp), CONTEXT, scatter_dimension=0, tiled=True),
    )
    d_q_pre = (
        rotate_back(d_query.reshape(piece_rows, local_heads, head_dim), cosine, sine)
        .reshape(piece_rows, -1)
        .astype(jnp.bfloat16)
    )
    d_k_pre = (
        rotate_back(d_key_own.reshape(piece_rows, local_heads, head_dim), cosine, sine)
        .reshape(piece_rows, -1)
        .astype(jnp.bfloat16)
    )
    d_v_pre = d_value_own.astype(jnp.bfloat16)
    grad_bq = jnp.sum(d_q_pre.astype(jnp.float32), axis=0).reshape(local_heads, head_dim)
    grad_bk = jnp.sum(d_k_pre.astype(jnp.float32), axis=0).reshape(local_heads, head_dim)
    grad_bv = jnp.sum(d_v_pre.astype(jnp.float32), axis=0).reshape(local_heads, head_dim)
    grad_query = left_operand(attn_in, d_q_pre)
    grad_key = left_operand(attn_in, d_k_pre)
    grad_value = left_operand(attn_in, d_v_pre)
    d_attn_in = (
        mat_right(d_q_pre, full_query)
        + mat_right(d_k_pre, full_key)
        + mat_right(d_v_pre, full_value)
    )
    d_attn_in = lax.psum(d_attn_in.astype(jnp.bfloat16), EXPERT).astype(jnp.float32)
    d_norm_one = d_attn_in * gain_one
    gain_one_grad = jnp.sum(d_attn_in * normed_one, axis=0)
    d_x = d_hidden_one + rstd_one * (
        d_norm_one - normed_one * jnp.mean(d_norm_one * normed_one, axis=1, keepdims=True)
    )
    input_grad = lax.dynamic_slice_in_dim(d_x, own_start, tok_rows, 0).astype(jnp.bfloat16)
    (
        grad_query,
        grad_key,
        grad_value,
        grad_out,
        grad_sgate,
        grad_sup,
        grad_sdown,
        router_grad,
        mix_grad,
        gain_one_grad,
        gain_two_grad,
        grad_bq,
        grad_bk,
        grad_bv,
    ) = (
        lax.psum_scatter(grad_query, (DP, CONTEXT), scatter_dimension=0, tiled=True),
        lax.psum_scatter(grad_key, (DP, CONTEXT), scatter_dimension=0, tiled=True),
        lax.psum_scatter(grad_value, (DP, CONTEXT), scatter_dimension=0, tiled=True),
        lax.psum_scatter(grad_out, (DP, CONTEXT), scatter_dimension=1, tiled=True),
        lax.psum_scatter(grad_sgate, (DP, CONTEXT), scatter_dimension=0, tiled=True),
        lax.psum_scatter(grad_sup, (DP, CONTEXT), scatter_dimension=0, tiled=True),
        lax.psum_scatter(grad_sdown, (DP, CONTEXT), scatter_dimension=1, tiled=True),
        lax.psum_scatter(router_grad, (DP, CONTEXT), scatter_dimension=0, tiled=True),
        lax.psum_scatter(mix_grad, (DP, CONTEXT), scatter_dimension=0, tiled=True),
        lax.psum_scatter(gain_one_grad, (DP, CONTEXT), scatter_dimension=0, tiled=True),
        lax.psum_scatter(gain_two_grad, (DP, CONTEXT), scatter_dimension=0, tiled=True),
        lax.psum_scatter(grad_bq, (DP, CONTEXT), scatter_dimension=1, tiled=True),
        lax.psum_scatter(grad_bk, (DP, CONTEXT), scatter_dimension=1, tiled=True),
        lax.psum_scatter(grad_bv, (DP, CONTEXT), scatter_dimension=1, tiled=True),
    )
    return (
        mixed,
        input_grad,
        gain_one_grad,
        grad_query,
        grad_key,
        grad_value,
        grad_bq,
        grad_bk,
        grad_bv,
        grad_out,
        gain_two_grad,
        router_grad,
        mix_grad,
        grad_sgate,
        grad_sup,
        grad_sdown,
        routed_gate_gradient,
        routed_up_gradient,
        routed_down_gradient,
    )


def dot_f32(left, right, left_dim, right_dim):
    return lax.dot_general(
        left, right, (((left_dim,), (right_dim,)), ((), ())), preferred_element_type=jnp.float32
    )


def whole_vmem(count):
    return [pl.BlockSpec(memory_space=pltpu.VMEM)] * count


def like(shape, dtype):
    return jax.ShapeDtypeStruct(shape, dtype)


MESH_ID = pl.DeviceIdType.MESH


class Wire:
    def __init__(self, send, recv):
        self.send = send
        self.recv = recv
        self.sent = 0
        self.received = 0
        self.own = []

    def copy(self, src, dst, device):
        out = self.copy_to(src, dst, device, self.take(1), self.take_send(1))
        self.own.append(out)
        return out

    def take(self, count):
        self.received += count
        assert self.received <= self.recv.shape[0], self.received
        return self.received - count

    def take_send(self, count):
        self.sent += count
        assert self.sent <= self.send.shape[0], self.sent
        return self.sent - count

    def copy_to(self, src, dst, device, recv_slot, send_slot):
        return pltpu.make_async_remote_copy(
            src_ref=src,
            dst_ref=dst,
            send_sem=self.send.at[send_slot],
            recv_sem=self.recv.at[recv_slot],
            device_id=device,
            device_id_type=MESH_ID,
        )

    def drain(self):
        for item in self.own:
            item.wait_send()
        self.own = []


class Local:
    def __init__(self, sems):
        self.sems = sems
        self.count = 0

    def start(self, src, dst):
        assert self.count < self.sems.shape[0], self.count
        item = pltpu.make_async_copy(src, dst, self.sems.at[self.count])
        self.count += 1
        item.start()
        return item


class Place:
    def __init__(self, n_dp):
        self.n_dp = n_dp
        self.z = lax.axis_index(DP)
        self.c = lax.axis_index(CONTEXT)
        self.y = lax.axis_index(EXPERT)
        self.cx = lax.bitwise_xor(self.c, jnp.int32(2))
        self.cs = lax.bitwise_xor(self.c, jnp.int32(1))
        self.cd = lax.bitwise_xor(self.c, jnp.int32(3))
        self.yn = lax.bitwise_xor(self.y, jnp.int32(1))
        self.core = (self.z, self.cs, self.y)
        self.over_x = (self.z, self.cx, self.y)
        self.over_y = (self.z, self.c, self.yn)
        self.up = (self.z + 1, self.c, self.y)
        self.down = (self.z - 1, self.c, self.y)

    def block(self, c, y):
        return c * 2 + y


def barrier(devices):
    sem = pltpu.get_barrier_semaphore()
    for device in devices:
        pl.semaphore_signal(sem, inc=1, device_id=device, device_id_type=MESH_ID)
    pl.semaphore_wait(sem, len(devices))


def rows_of(index, count):
    return pl.ds(pl.multiple_of(index * count, count), count)


def by_rows(total, step, body):
    def one(index, carry):
        body(rows_of(index, step))
        return carry

    lax.fori_loop(0, total // step, one, 0)


def chain_gather(wire, place, refs, arrived=None):
    n = place.n_dp
    z = place.z
    width = len(refs(z))
    recv = wire.take(n * width)
    send = wire.take_send(2 * n * width)

    def copies(slot, up, dist):
        return [
            wire.copy_to(
                ref,
                ref,
                place.up if up else place.down,
                recv + slot * width + index,
                send + (2 * dist + (0 if up else 1)) * width + index,
            )
            for index, ref in enumerate(refs(slot))
        ]

    def start(slot, up, dist):
        for item in copies(slot, up, dist):
            item.start()

    def land(slot, up, dist):
        for item in copies(slot, up, dist):
            item.wait_recv()
        if arrived is not None:
            arrived(slot)

    def sent(slot, up, dist):
        for item in copies(slot, up, dist):
            item.wait_send()

    pl.when(z < n - 1)(lambda: start(z, True, 0))
    pl.when(z > 0)(lambda: start(z, False, 0))
    yield
    for dist in range(1, n):
        below, above = z - dist, z + dist

        @pl.when(below >= 0)
        def _():
            land(below, True, dist)
            pl.when(z < n - 1)(lambda: start(below, True, dist))

        @pl.when(above < n)
        def _():
            land(above, False, dist)
            pl.when(z > 0)(lambda: start(above, False, dist))

        yield
    for dist in range(n):
        below, above = z - dist, z + dist
        pl.when((below >= 0) & (z < n - 1))(lambda: sent(below, True, dist))
        pl.when((above < n) & (z > 0))(lambda: sent(above, False, dist))


def finish(*steps):
    for step in steps:
        for _ in step:
            pass


def plane_gather(wire, place, buf):
    rows = buf.shape[0] // 8
    half = buf.shape[1] // 2
    left, right = pl.ds(0, half), pl.ds(half, half)
    own = rows_of(place.block(place.c, place.y), rows)
    from_x = rows_of(place.block(place.cx, place.y), rows)
    from_y = rows_of(place.block(place.c, place.yn), rows)
    across = rows_of(place.block(place.cx, place.yn), rows)

    def go(where, lanes, device):
        ref = buf.at[where, lanes] if lanes is not None else buf.at[where, :]
        item = wire.copy(ref, ref, device)
        item.start()
        return item

    x_left = go(own, left, place.over_x)
    y_right = go(own, right, place.over_y)
    x_right = go(own, right, place.over_x)
    y_left = go(own, left, place.over_y)
    waits = [go(own, None, place.core)]
    yield
    x_left.wait_recv()
    far_left = go(from_x, left, place.over_y)
    y_right.wait_recv()
    far_right = go(from_y, right, place.over_x)
    yield
    x_right.wait_recv()
    waits.append(go(from_x, None, place.core))
    y_left.wait_recv()
    waits.append(go(from_y, None, place.core))
    yield
    far_left.wait_recv()
    far_right.wait_recv()
    waits.append(go(across, None, place.core))
    for item in waits:
        item.wait_recv()


def add_into(target, lanes, rows, extra):
    count = extra.shape[0]
    step = 16

    def one(index, carry):
        here = pl.ds(pl.multiple_of(rows + index * step, step), step)
        there = rows_of(index, step)
        total = target[here, lanes].astype(jnp.float32) + extra[there, :].astype(jnp.float32)
        target[here, lanes] = total.astype(target.dtype)
        return carry

    lax.fori_loop(0, count // step, one, 0)


def plane_reduce(wire, place, part, got_core, got_one, got_two):
    rows = part.shape[0] // 8
    half = part.shape[1] // 2
    left, right = pl.ds(0, half), pl.ds(half, half)
    chips = ((place.cx, place.yn), (place.cx, place.y), (place.c, place.yn), (place.c, place.y))
    starts = [place.block(c, y) * rows for c, y in chips]
    blocks = [pl.ds(pl.multiple_of(start, rows), rows) for start in starts]
    sibling = [
        rows_of(place.block(lax.bitwise_xor(c, jnp.int32(1)), y), rows) for c, y in chips
    ]
    swaps = []
    for index in range(4):
        item = wire.copy(part.at[sibling[index], :], got_core.at[index], place.core)
        item.start()
        swaps.append(item)
    whole = pl.ds(0, 2 * half)

    def one(index, lanes, slot, device):
        item = wire.copy(part.at[blocks[index], lanes], got_one.at[slot], device)
        item.start()
        return item

    swaps[0].wait_recv()
    add_into(part, whole, starts[0], got_core.at[0])
    far_x = one(0, left, 0, place.over_x)
    far_y = one(0, right, 2, place.over_y)
    swaps[1].wait_recv()
    add_into(part, whole, starts[1], got_core.at[1])
    near_x = one(1, left, 1, place.over_x)
    swaps[2].wait_recv()
    add_into(part, whole, starts[2], got_core.at[2])
    near_y = one(2, right, 3, place.over_y)
    yield
    swaps[3].wait_recv()
    add_into(part, whole, starts[3], got_core.at[3])
    far_x.wait_recv()
    add_into(part, left, starts[2], got_one.at[0])
    last_y = wire.copy(part.at[blocks[2], left], got_two.at[0], place.over_y)
    last_y.start()
    far_y.wait_recv()
    add_into(part, right, starts[1], got_one.at[2])
    last_x = wire.copy(part.at[blocks[1], right], got_two.at[1], place.over_x)
    last_x.start()
    yield
    near_x.wait_recv()
    near_y.wait_recv()
    last_x.wait_recv()
    last_y.wait_recv()


def plane_sum(place, part, got_one, got_two, here):
    rows = part.shape[0] // 8
    half = part.shape[1] // 2
    start = place.block(place.c, place.y) * rows + here.start
    at = pl.ds(pl.multiple_of(start, here.size), here.size)

    def value(ref):
        return ref.astype(jnp.float32)

    left = value(part[at, 0:half]) + value(got_one[1, here, :]) + value(got_two[0, here, :])
    right = value(part[at, half:]) + value(got_one[3, here, :]) + value(got_two[1, here, :])
    return jnp.concatenate([left, right], axis=1)


def forward_kernel(
    n_blocks, n_dp,
    tokens, small, ids, w_query, w_key, w_value, w_out, s_gate, s_up, s_down,
    bias, cosine, sine,
    attn_in, query, keys, values, attn, lse, hidden, moe_in,
    heads_weight, out_weight, gate_weight, up_weight, down_weight, smalls, all_ids,
    x_seq, partial, got_core, got_one, got_two, send, recv, local,
):
    place = Place(n_dp)
    wire = Wire(send, recv)
    inside = Local(local)
    z, c, y = place.z, place.c, place.y
    rows, width = tokens.shape
    seq = x_seq.shape[0]
    cols = query.shape[1]
    head_dim = cosine.shape[1]
    block = seq // n_blocks
    scale = 1.0 / math.sqrt(head_dim)
    n_ctx = 4
    share = w_query.shape[0]
    f32, low = jnp.float32, jnp.bfloat16

    others = [(dz, dc) for dz in range(n_dp) for dc in range(n_ctx) if dz or dc]

    def moved(dz, dc, y_to):
        return (lax.bitwise_xor(z, jnp.int32(dz)), lax.bitwise_xor(c, jnp.int32(dc)), y_to)

    barrier(
        [moved(dz, dc, y) for dz, dc in others] + [moved(dz, 0, place.yn) for dz in range(n_dp)]
    )

    mine = z * n_ctx + c
    my_rows = rows_of(mine, share)
    exchanges = []
    for dc in range(n_ctx):
        to = lax.bitwise_xor(c, jnp.int32(dc))
        lanes = pl.ds(pl.multiple_of(to * cols, cols), cols)
        pairs = [
            (weight.at[:, lanes], heads_weight.at[my_rows, pl.ds(index * cols, cols)])
            for index, weight in enumerate((w_query, w_key, w_value))
        ]
        pairs.append((w_out.at[rows_of(to, cols), :], out_weight.at[:, my_rows]))
        for src, dst in pairs:
            if dc == 0:
                exchanges.append(inside.start(src, dst))
            else:
                item = wire.copy(src, dst, moved(0, dc, y))
                item.start()
                exchanges.append(item)
    own_rows = rows_of(place.block(c, y), rows)
    here = inside.start(tokens, x_seq.at[own_rows, :])
    here.wait()
    tokens_in = plane_gather(wire, place, x_seq)
    next(tokens_in)
    small_copies = [inside.start(small, smalls.at[:, my_rows])]
    for dz, dc in others:
        item = wire.copy(small, smalls.at[:, my_rows], moved(dz, dc, y))
        item.start()
        small_copies.append(item)
    group = z * 2 + y
    small_copies.append(inside.start(ids, all_ids.at[group]))
    for dz in range(n_dp):
        for y_to in (y, place.yn):
            if dz or y_to is not y:
                item = wire.copy(ids, all_ids.at[group], moved(dz, 0, y_to))
                item.start()
                small_copies.append(item)
    for item in exchanges:
        item.wait_recv()

    def attention_blocks(slot):
        at = rows_of(slot, n_ctx * share)
        return [heads_weight.at[at, :], out_weight.at[:, at]]

    weights_in = chain_gather(wire, place, attention_blocks)
    next(weights_in)
    finish(tokens_in)
    for item in small_copies:
        item.wait_recv()

    gain_one = smalls[9:10, :].astype(f32)
    gain_two = smalls[10:11, :].astype(f32)

    def norm_one(at):
        x_float = x_seq[at, :].astype(f32)
        rstd = lax.rsqrt(jnp.mean(x_float * x_float, axis=1, keepdims=True) + EPS)
        attn_in[at, :] = (x_float * rstd * gain_one).astype(low)

    by_rows(seq, 64, norm_one)
    finish(weights_in)

    shared_pieces = []
    for dz in range(n_dp):
        to = lax.bitwise_xor(z, jnp.int32(dz))
        hidden_rows = rows_of(to, s_down.shape[0] // n_dp)
        pairs = [
            (s_gate.at[to], gate_weight.at[z, c]),
            (s_up.at[to], up_weight.at[z, c]),
            (s_down.at[hidden_rows, :], down_weight.at[:, my_rows]),
        ]
        for src, dst in pairs:
            if dz == 0:
                shared_pieces.append(inside.start(src, dst))
            else:
                item = wire.copy(src, dst, moved(dz, 0, y))
                item.start()
                shared_pieces.append(item)

    def project(at):
        pre = dot_f32(attn_in[at, :], heads_weight[...], 1, 0)
        cos = cosine[at, :]
        sin = sine[at, :]
        for index, kept in enumerate((query, keys, values)):
            for start in range(0, cols, head_dim):
                from_lane = index * cols + start
                part = pre[:, from_lane : from_lane + head_dim]
                part = part + bias[index : index + 1, start : start + head_dim]
                if index < 2:
                    part = part * cos + pltpu.roll(part, head_dim // 2, 1) * sin
                kept[at, start : start + head_dim] = part.astype(low)

    by_rows(seq, block, project)
    for start in range(0, cols, head_dim):
        lanes = slice(start, start + head_dim)
        for step in range(n_blocks):
            at = slice(step * block, (step + 1) * block)
            seen = slice(0, (step + 1) * block)
            scores = dot_f32(query[at, lanes], keys[seen, lanes], 1, 1) * scale
            top = jnp.max(scores, axis=1, keepdims=True)
            expo = jnp.exp(scores - top)
            total = jnp.sum(expo, axis=1, keepdims=True)
            probs = (expo / total).astype(low)
            attn[at, lanes] = dot_f32(probs, values[seen, lanes], 1, 0).astype(low)
            lse[at, lanes] = jnp.broadcast_to(top + jnp.log(total), (block, head_dim))

    def output(at):
        partial[at, :] = dot_f32(attn[at, :], out_weight[...], 1, 0).astype(low)

    by_rows(seq, block, output)
    finish(plane_reduce(wire, place, partial, got_core, got_one, got_two))

    def norm_two(at):
        start = place.block(c, y) * rows + at.start
        own = pl.ds(pl.multiple_of(start, at.size), at.size)
        total = x_seq[own, :].astype(f32) + plane_sum(place, partial, got_one, got_two, at)
        hidden[at, :] = total
        rstd = lax.rsqrt(jnp.mean(total * total, axis=1, keepdims=True) + EPS)
        got_core[0, at, :] = (total * rstd * gain_two).astype(low)

    by_rows(rows, 16, norm_two)
    at_group = rows_of(group, rows)
    here = inside.start(got_core.at[0], moe_in.at[at_group, :])
    here.wait()

    y_recv = wire.take(n_dp)
    y_send = wire.take_send(n_dp)

    def to_y(slot):
        at = rows_of(slot * 2 + y, rows)
        return wire.copy_to(
            moe_in.at[at, :], moe_in.at[at, :], place.over_y, y_recv + slot, y_send + slot
        )

    def from_y(slot):
        at = rows_of(slot * 2 + place.yn, rows)
        return wire.copy_to(
            moe_in.at[at, :], moe_in.at[at, :], place.over_y, y_recv + slot, y_send + slot
        )

    rows_chain = chain_gather(
        wire,
        place,
        lambda slot: [moe_in.at[rows_of(slot * 2 + y, rows), :]],
        arrived=lambda slot: to_y(slot).start(),
    )
    next(rows_chain)
    to_y(z).start()
    for item in shared_pieces:
        item.wait_recv()

    def shared_set(context):
        return [gate_weight.at[:, context], up_weight.at[:, context]] + [
            down_weight.at[:, rows_of(dz * n_ctx + context, share)] for dz in range(n_dp)
        ]

    over = []
    for ref in shared_set(c):
        item = wire.copy(ref, ref, place.over_x)
        item.start()
        over.append(item)
    close = []
    for ref in shared_set(c):
        item = wire.copy(ref, ref, place.core)
        item.start()
        close.append(item)
    finish(rows_chain)
    for item, ref in zip(over, shared_set(place.cx)):
        item.wait_recv()
        item = wire.copy(ref, ref, place.core)
        item.start()
        close.append(item)
    for item in close:
        item.wait_recv()
    for slot in range(n_dp):
        from_y(slot).wait_recv()
        to_y(slot).wait_send()
    wire.drain()


def attention_backward(
    n_blocks, d_out, w_out, heads_weight, query, keys, values, lse, cosine, sine,
    d_query_pre, d_key_pre, d_value_pre, d_bias, partial,
    d_attn, d_keys, d_values,
):
    rows, width = d_out.shape
    cols = query.shape[1]
    head_dim = cosine.shape[1]
    block = rows // n_blocks
    scale = 1.0 / math.sqrt(head_dim)

    def project(step, carry):
        here = pl.ds(pl.multiple_of(step * block, block), block)
        d_attn[here, :] = dot_f32(d_out[here, :], w_out[...], 1, 1).astype(jnp.bfloat16)
        return carry

    lax.fori_loop(0, n_blocks, project, 0)

    def back(part, here):
        return part * cosine[here, :] - pltpu.roll(part, head_dim // 2, 1) * sine[here, :]

    for start in range(0, cols, head_dim):
        lanes = slice(start, start + head_dim)
        d_keys[...] = jnp.zeros_like(d_keys)
        d_values[...] = jnp.zeros_like(d_values)
        for step in range(n_blocks):
            here = slice(step * block, (step + 1) * block)
            seen = slice(0, (step + 1) * block)
            q_here = query[here, lanes]
            k_seen = keys[seen, lanes]
            grad = d_attn[here, lanes]
            scores = dot_f32(q_here, k_seen, 1, 1) * scale
            probs = jnp.exp(scores - lse[here, start : start + 1])
            d_probs = dot_f32(grad, values[seen, lanes], 1, 1)
            delta = jnp.sum(probs * d_probs, axis=1, keepdims=True)
            d_scores = (probs * (d_probs - delta)).astype(jnp.bfloat16)
            d_query = dot_f32(d_scores, k_seen, 1, 0) * scale
            d_query_pre[here, lanes] = back(d_query, here).astype(jnp.bfloat16)
            d_keys[seen, :] += dot_f32(d_scores, q_here, 0, 0) * scale
            d_values[seen, :] += dot_f32(probs.astype(jnp.bfloat16), grad, 0, 0)
        every = slice(0, rows)
        d_key_pre[:, lanes] = back(d_keys[...], every).astype(jnp.bfloat16)
        d_value_pre[:, lanes] = d_values[...].astype(jnp.bfloat16)
    d_bias[...] = jnp.zeros_like(d_bias)
    for index, kept in enumerate((d_query_pre, d_key_pre, d_value_pre)):
        d_bias[index : index + 1, :] = jnp.sum(
            kept[...].astype(jnp.float32), axis=0, keepdims=True
        )

    def output(step, carry):
        here = pl.ds(pl.multiple_of(step * block, block), block)
        total = 0.0
        for index, kept in enumerate((d_query_pre, d_key_pre, d_value_pre)):
            weight = heads_weight[:, index * cols : (index + 1) * cols]
            total = total + dot_f32(kept[here, :], weight, 1, 1)
        partial[here, :] = total.astype(jnp.bfloat16)
        return carry

    lax.fori_loop(0, n_blocks, output, 0)


def tokens_plan(
    tokens,
    out_grad,
    expert_ids,
    norm1_gain,
    w_query,
    w_key,
    w_value,
    query_bias_heads,
    bias_key,
    bias_value,
    w_out,
    norm2_gain,
    w_router,
    shared_mix,
    shared_in_gate,
    shared_in_up,
    shared_down,
    expert_gate,
    expert_up,
    expert_down,
):
    low = jnp.bfloat16
    f32 = jnp.float32
    tok_rows, width = tokens.shape
    n_dp, n_ctx, n_half = (lax.axis_size(name) for name in (DP, CONTEXT, EXPERT))
    dp, ctx, half = (lax.axis_index(name) for name in (DP, CONTEXT, EXPERT))
    half_heads, head_dim = query_bias_heads.shape
    heads = half_heads // n_ctx
    cols = heads * head_dim
    seq_len = tok_rows * n_ctx * n_half
    n_blocks = seq_len // BLOCK
    n_experts = w_router.shape[1]
    n_group = n_dp * n_half
    my_expert = dp * n_half + half

    def heads_out(grad):
        mine = lax.psum_scatter(grad.astype(low), DP, scatter_dimension=0, tiled=True)
        return lax.all_to_all(mine, CONTEXT, split_axis=0, concat_axis=1, tiled=True).astype(f32)

    def heads_out_rows(grad):
        mine = lax.psum_scatter(grad.astype(low), DP, scatter_dimension=1, tiled=True)
        return lax.all_to_all(mine, CONTEXT, split_axis=1, concat_axis=0, tiled=True).astype(f32)

    def hidden_out(grad):
        split = grad.astype(low).reshape(n_dp, n_ctx, -1, grad.shape[1])
        mine = lax.psum_scatter(split, CONTEXT, scatter_dimension=1, tiled=True)
        mine = mine.reshape(width // n_ctx, -1)
        return lax.all_to_all(mine, DP, split_axis=0, concat_axis=1, tiled=True).astype(f32)

    def hidden_out_rows(grad):
        split = grad.astype(low).reshape(grad.shape[0], n_dp, n_ctx, -1)
        mine = lax.psum_scatter(split, CONTEXT, scatter_dimension=2, tiled=True)
        mine = mine.reshape(grad.shape[0], -1)
        return lax.all_to_all(mine, DP, split_axis=1, concat_axis=0, tiled=True).astype(f32)

    def plane_in(rows):
        return lax.all_gather(rows, (CONTEXT, EXPERT), axis=0, tiled=True)

    def plane_out(rows):
        return lax.psum_scatter(rows, (CONTEXT, EXPERT), scatter_dimension=0, tiled=True)

    def group_in(rows):
        return lax.all_gather(rows, (DP, EXPERT), axis=0, tiled=True)

    def group_out(rows):
        return lax.psum_scatter(rows, (DP, EXPERT), scatter_dimension=0, tiled=True)

    small = jnp.concatenate(
        [w_router.T, shared_mix[None], norm1_gain[None], norm2_gain[None]], axis=0
    )
    small = jnp.pad(small, ((0, 16 - small.shape[0]), (0, 0)))
    ids = jnp.pad(expert_ids.T, ((0, 8 - expert_ids.shape[1]), (0, 0)), constant_values=-1)
    hidden_units = shared_in_gate.shape[1] // n_dp

    def by_dp(weight):
        return weight.reshape(weight.shape[0], n_dp, hidden_units).transpose(1, 0, 2)

    biases = jnp.stack([query_bias_heads, bias_key, bias_value]).astype(f32)
    biases = lax.dynamic_slice_in_dim(biases, ctx * heads, heads, 1).reshape(3, cols)
    cosine, sine = rope_tables(jnp.arange(seq_len), head_dim)
    cosine = jnp.concatenate([cosine[:, 0], cosine[:, 0]], axis=1)
    sine = jnp.concatenate([-sine[:, 0], sine[:, 0]], axis=1)
    dy_group = group_in(out_grad)
    vmem = pl.BlockSpec(memory_space=pltpu.VMEM)
    anywhere = pl.BlockSpec(memory_space=pl.ANY)
    share = w_query.shape[0]
    half_width = width // 2
    (
        attn_in, query, keys, values, attn, lse, hidden_own, moe_in,
        heads_weight, wo, sg, su, sd, small, ids_group,
    ) = pl.pallas_call(
        lambda *refs: forward_kernel(n_blocks, n_dp, *refs),
        out_shape=[
            like((seq_len, width), low),
            like((seq_len, cols), low),
            like((seq_len, cols), low),
            like((seq_len, cols), low),
            like((seq_len, cols), low),
            like((seq_len, cols), f32),
            like((tok_rows, width), f32),
            like((n_group * tok_rows, width), low),
            like((width, 3 * cols), low),
            like((cols, width), low),
            like((n_dp, n_ctx, share, hidden_units), low),
            like((n_dp, n_ctx, share, hidden_units), low),
            like((hidden_units, width), low),
            like((16, width), low),
            like((n_group, 8, tok_rows), jnp.int32),
        ],
        in_specs=[anywhere] * 10 + [vmem] * 3,
        out_specs=[vmem] * 7 + [anywhere] + [vmem] * 2 + [anywhere] * 3 + [vmem, anywhere],
        scratch_shapes=[
            pltpu.VMEM((seq_len, width), low),
            pltpu.VMEM((seq_len, width), low),
            pltpu.VMEM((4, tok_rows, width), low),
            pltpu.VMEM((4, tok_rows, half_width), low),
            pltpu.VMEM((2, tok_rows, half_width), low),
            pltpu.SemaphoreType.DMA((144,)),
            pltpu.SemaphoreType.DMA((144,)),
            pltpu.SemaphoreType.DMA((16,)),
        ],
        name="forward",
        compiler_params=pltpu.CompilerParams(
            collective_id=1, has_side_effects=True, vmem_limit_bytes=60 * 2**20
        ),
    )(
        tokens, small, ids, w_query, w_key, w_value, w_out,
        by_dp(shared_in_gate), by_dp(shared_in_up), shared_down, biases, cosine, sine,
    )
    sg, su = sg.reshape(width, hidden_units), su.reshape(width, hidden_units)
    gain_one = small[n_experts + 1].astype(f32)
    gain_two = small[n_experts + 2].astype(f32)
    x_own = tokens.astype(f32)
    dy_own = out_grad.astype(f32)
    rstd_two = lax.rsqrt(jnp.mean(hidden_own * hidden_own, axis=1, keepdims=True) + EPS)
    normed_two = hidden_own * rstd_two
    moe_own = (normed_two * gain_two).astype(low)

    logits = mat_right(moe_in, small)
    router_probs = jax.nn.softmax(logits[:, :n_experts], axis=1)
    mix = jax.nn.sigmoid(logits[:, n_experts])
    hit = jnp.any(ids_group == my_expert, axis=1)
    gate = jnp.sum(
        jnp.where(jnp.arange(n_experts)[None, :] == my_expert, router_probs, 0.0), axis=1
    )
    place = jnp.cumsum(hit.astype(jnp.int32), axis=1) - 1
    chosen = (hit[:, None, :] & (place[:, None, :] == jnp.arange(CAP)[None, :, None]))
    pick = chosen.astype(low)
    gate_rows = jnp.sum(jnp.where(chosen, gate.reshape(n_group, 1, tok_rows), 0.0), axis=2)

    def to_rows(group):
        return jnp.einsum(
            "sct,std->scd", pick, group.reshape(n_group, tok_rows, -1), preferred_element_type=f32
        ).astype(low).reshape(n_group * CAP, -1)

    def to_tokens(rows):
        return jnp.einsum(
            "sct,scd->std", pick, rows.reshape(n_group, CAP, -1), preferred_element_type=f32
        ).reshape(n_group * tok_rows, -1)

    rows_in = to_rows(moe_in)
    dy_rows = to_rows(dy_group)
    grads_in = (gate_rows.reshape(-1, 1) * dy_rows.astype(f32)).astype(low)
    gate_weight, up_weight, down_weight = expert_gate[0], expert_up[0], expert_down[0]
    e_gate = jnp.dot(rows_in, gate_weight, preferred_element_type=f32)
    e_up = jnp.dot(rows_in, up_weight, preferred_element_type=f32)
    e_silu = jax.nn.silu(e_gate)
    e_hidden = (e_silu * e_up).astype(low)
    e_out = jnp.dot(e_hidden, down_weight, preferred_element_type=f32).astype(low)
    d_hidden = mat_right(grads_in, down_weight)
    d_gate = (d_hidden * e_up * silu_slope(e_gate)).astype(low)
    d_up = (d_hidden * e_silu).astype(low)
    d_in = (mat_right(d_gate, gate_weight) + mat_right(d_up, up_weight)).astype(low)

    s_gate = jnp.dot(moe_in, sg, preferred_element_type=f32)
    s_up = jnp.dot(moe_in, su, preferred_element_type=f32)
    s_silu = jax.nn.silu(s_gate)
    s_hidden = (s_silu * s_up).astype(low)
    shared = jnp.dot(s_hidden, sd, preferred_element_type=f32)
    dy_float = dy_group.astype(f32)
    d_shared = (mix[:, None] * dy_float).astype(low)
    d_shidden = mat_right(d_shared, sd)
    d_sgate = (d_shidden * s_up * silu_slope(s_gate)).astype(low)
    d_sup = (d_shidden * s_silu).astype(low)

    moe_part = (gate[:, None] * to_tokens(e_out) + mix[:, None] * shared).astype(low)
    d_in_part = (to_tokens(d_in) + mat_right(d_sgate, sg) + mat_right(d_sup, su)).astype(low)
    d_gate_rows = jnp.sum(e_out.astype(f32) * dy_rows.astype(f32), axis=1).reshape(n_group, CAP)
    d_gate_tok = jnp.sum(jnp.where(chosen, d_gate_rows[:, :, None], 0.0), axis=1).reshape(-1)
    shared_dot = jnp.sum(shared * dy_float, axis=1)
    scalars = jnp.concatenate(
        [
            jnp.where(jnp.arange(n_experts)[None, :] == my_expert, d_gate_tok[:, None], 0.0),
            shared_dot[:, None],
        ],
        axis=1,
    )
    scalars = group_out(scalars)
    d_in_own = group_out(d_in_part).astype(f32)
    moe_sum = group_out(moe_part).astype(f32)
    mixed = (hidden_own + moe_sum).astype(low)

    own = my_expert * tok_rows
    probs_own = lax.dynamic_slice_in_dim(router_probs, own, tok_rows, 0)
    mix_own = lax.dynamic_slice_in_dim(mix, own, tok_rows, 0)
    d_rprobs = scalars[:, :n_experts]
    d_logits = probs_own * (d_rprobs - jnp.sum(probs_own * d_rprobs, axis=1, keepdims=True))
    d_mixlogit = scalars[:, n_experts] * mix_own * (1.0 - mix_own)
    d_side = jnp.concatenate([d_logits, d_mixlogit[:, None]], axis=1)
    moe_own_float = moe_own.astype(f32)
    side_grad = jnp.dot(d_side.T, moe_own_float, precision=HIGH)
    d_moe_in = d_in_own + jnp.dot(
        d_side, small[: n_experts + 1].astype(f32), precision=HIGH
    )
    gain_two_grad = jnp.sum(d_moe_in * normed_two, axis=0)
    d_norm_two = d_moe_in * gain_two
    d_hidden_own = dy_own + rstd_two * (
        d_norm_two - normed_two * jnp.mean(d_norm_two * normed_two, axis=1, keepdims=True)
    )
    d_proj = plane_in(d_hidden_own.astype(low))

    d_q_pre, d_k_pre, d_v_pre, d_bias, d_partial = pl.pallas_call(
        lambda *refs: attention_backward(n_blocks, *refs),
        out_shape=[
            like((seq_len, cols), low),
            like((seq_len, cols), low),
            like((seq_len, cols), low),
            like((8, cols), f32),
            like((seq_len, width), low),
        ],
        in_specs=whole_vmem(9),
        out_specs=whole_vmem(5),
        scratch_shapes=[
            pltpu.VMEM((seq_len, cols), low),
            pltpu.VMEM((seq_len, head_dim), f32),
            pltpu.VMEM((seq_len, head_dim), f32),
        ],
        name="attention_backward",
        compiler_params=pltpu.CompilerParams(vmem_limit_bytes=56 * 2**20),
    )(d_proj, wo, heads_weight, query, keys, values, lse, cosine, sine)
    d_attn_in = plane_out(d_partial).astype(f32)
    rstd_one = lax.rsqrt(jnp.mean(x_own * x_own, axis=1, keepdims=True) + EPS)
    normed_one = x_own * rstd_one
    d_norm_one = d_attn_in * gain_one
    gain_one_grad = jnp.sum(d_attn_in * normed_one, axis=0)
    input_grad = (
        d_hidden_own
        + rstd_one
        * (d_norm_one - normed_one * jnp.mean(d_norm_one * normed_one, axis=1, keepdims=True))
    ).astype(low)

    routed = [
        lax.psum_scatter(
            grad[None].astype(low), CONTEXT, scatter_dimension=dim, tiled=True
        ).astype(f32)
        for grad, dim in (
            (left_operand(rows_in, d_gate), 1),
            (left_operand(rows_in, d_up), 1),
            (left_operand(e_hidden, grads_in), 2),
        )
    ]
    grad_sgate = hidden_out(left_operand(moe_in, d_sgate))
    grad_sup = hidden_out(left_operand(moe_in, d_sup))
    grad_sdown = hidden_out_rows(left_operand(s_hidden, d_shared))
    grad_out = heads_out_rows(left_operand(attn, d_proj))
    grad_query = heads_out(left_operand(attn_in, d_q_pre))
    grad_key = heads_out(left_operand(attn_in, d_k_pre))
    grad_value = heads_out(left_operand(attn_in, d_v_pre))

    all_bias = jnp.zeros((n_half, 3, half_heads, head_dim), f32)
    all_bias = lax.dynamic_update_slice(
        all_bias, d_bias[:3].reshape(1, 3, heads, head_dim), (half, 0, ctx * heads, 0)
    )
    rest = jnp.concatenate(
        [
            side_grad,
            gain_one_grad[None],
            gain_two_grad[None],
            all_bias.reshape(-1, width),
        ],
        axis=0,
    )
    rest = lax.psum(rest, (DP, CONTEXT, EXPERT))
    share = width // (n_dp * n_ctx)
    place = dp * n_ctx + ctx
    mine = lax.dynamic_slice_in_dim(rest[: n_experts + 3], place * share, share, 1)
    bias_sum = rest[n_experts + 3 :].reshape(n_half, 3, half_heads, head_dim)
    bias_share = head_dim // (n_dp * n_ctx)
    bias_sum = lax.dynamic_slice(
        bias_sum, (half, 0, 0, place * bias_share), (1, 3, half_heads, bias_share)
    )[0]
    return (
        mixed,
        input_grad,
        mine[n_experts + 1],
        grad_query,
        grad_key,
        grad_value,
        bias_sum[0],
        bias_sum[1],
        bias_sum[2],
        grad_out,
        mine[n_experts + 2],
        mine[:n_experts].T,
        mine[n_experts],
        grad_sgate,
        grad_sup,
        grad_sdown,
        routed[0],
        routed[1],
        routed[2],
    )


def on_device(*arrays):
    sizes = [lax.axis_size(name) for name in (DP, CONTEXT, EXPERT)]
    if sizes == [4, 4, 2] and arrays[7].shape[0] % sizes[1] == 0:
        return tokens_plan(*arrays)
    return weights_plan(*arrays)


def solution(mesh):
    placed = (
        P((DP, CONTEXT, EXPERT), None),
        P((DP, CONTEXT, EXPERT), None),
        P((DP, CONTEXT, EXPERT), None),
        P((DP, CONTEXT)),
        P((DP, CONTEXT), EXPERT),
        P((DP, CONTEXT), EXPERT),
        P((DP, CONTEXT), EXPERT),
        P(EXPERT, None),
        P(EXPERT, None),
        P(EXPERT, None),
        P(EXPERT, (DP, CONTEXT)),
        P((DP, CONTEXT)),
        P((DP, CONTEXT), None),
        P((DP, CONTEXT)),
        P((DP, CONTEXT), EXPERT),
        P((DP, CONTEXT), EXPERT),
        P(EXPERT, (DP, CONTEXT)),
        P((DP, EXPERT), None, None),
        P((DP, EXPERT), None, None),
        P((DP, EXPERT), None, None),
    )
    return jax.shard_map(
        on_device,
        mesh=mesh,
        in_specs=placed,
        out_specs=(
            P((DP, CONTEXT, EXPERT), None),
            P((DP, CONTEXT, EXPERT), None),
            P((DP, CONTEXT)),
            P((DP, CONTEXT), EXPERT),
            P((DP, CONTEXT), EXPERT),
            P((DP, CONTEXT), EXPERT),
            P(EXPERT, (DP, CONTEXT)),
            P(EXPERT, (DP, CONTEXT)),
            P(EXPERT, (DP, CONTEXT)),
            P(EXPERT, (DP, CONTEXT)),
            P((DP, CONTEXT)),
            P((DP, CONTEXT), None),
            P((DP, CONTEXT)),
            P((DP, CONTEXT), EXPERT),
            P((DP, CONTEXT), EXPERT),
            P(EXPERT, (DP, CONTEXT)),
            P((DP, EXPERT), CONTEXT, None),
            P((DP, EXPERT), CONTEXT, None),
            P((DP, EXPERT), None, CONTEXT),
        ),
        check_vma=False,
    )
```

```python
import math

import jax
import jax.numpy as jnp
from jax import lax
from jax.experimental import pallas as pl
from jax.experimental.pallas import tpu as pltpu
from jax.sharding import PartitionSpec as P

DP, CONTEXT, EXPERT = "dp", "context", "expert"
BLOCK = 256
CAP = 96


EPS = 1e-06
THETA = 1000000.0
HIGH = lax.Precision.HIGHEST


def rope_tables(positions, head_dim):
    half = head_dim // 2
    freq = THETA ** (-(2.0 * jnp.arange(half, dtype=jnp.float32)) / head_dim)
    angle = positions.astype(jnp.float32)[:, None] * freq[None, :]
    return (jnp.cos(angle)[:, None, :], jnp.sin(angle)[:, None, :])


def rotate(values, cosine, sine):
    half = values.shape[-1] // 2
    first = values[..., :half]
    second = values[..., half:]
    return jnp.concatenate(
        [first * cosine - second * sine, second * cosine + first * sine], axis=-1
    )


def rotate_back(values, cosine, sine):
    half = values.shape[-1] // 2
    first = values[..., :half]
    second = values[..., half:]
    return jnp.concatenate(
        [first * cosine + second * sine, second * cosine - first * sine], axis=-1
    )


def to_groups(matrix, groups, group_size, head_dim):
    return matrix.reshape(matrix.shape[0], groups, group_size, head_dim).transpose(1, 2, 0, 3)


def from_groups(stacked):
    return stacked.transpose(2, 0, 1, 3).reshape(stacked.shape[2], -1)


def silu_slope(values):
    sigma = jax.nn.sigmoid(values)
    return sigma * (1.0 + values * (1.0 - sigma))


def left_operand(left, right):
    return jnp.dot(left.T, right, preferred_element_type=jnp.float32)


def mat_right(left, right):
    return jnp.dot(left, right.T, preferred_element_type=jnp.float32)


def weights_plan(
    tokens,
    out_grad,
    expert_ids,
    norm1_gain,
    w_query,
    w_key,
    w_value,
    query_bias_heads,
    bias_key,
    bias_value,
    w_out,
    norm2_gain,
    w_router,
    shared_mix,
    shared_in_gate,
    shared_in_up,
    shared_down,
    expert_gate,
    expert_up,
    expert_down,
):
    tok_rows = tokens.shape[0]
    width = tokens.shape[1]
    my_half = lax.axis_index(EXPERT)
    my_piece = lax.axis_index(CONTEXT)
    n_pieces = lax.axis_size(CONTEXT)
    local_heads = query_bias_heads.shape[0]
    head_dim = query_bias_heads.shape[1]
    group_size = 2
    groups = local_heads // group_size
    score_scale = 1.0 / math.sqrt(head_dim)
    (
        full_query,
        full_key,
        full_value,
        full_out,
        full_sgate,
        full_sup,
        full_sdown,
        full_router,
        full_mix,
        full_gain_one,
        full_gain_two,
    ) = (
        lax.all_gather(w_query, (DP, CONTEXT), axis=0, tiled=True),
        lax.all_gather(w_key, (DP, CONTEXT), axis=0, tiled=True),
        lax.all_gather(w_value, (DP, CONTEXT), axis=0, tiled=True),
        lax.all_gather(w_out, (DP, CONTEXT), axis=1, tiled=True),
        lax.all_gather(shared_in_gate, (DP, CONTEXT), axis=0, tiled=True),
        lax.all_gather(shared_in_up, (DP, CONTEXT), axis=0, tiled=True),
        lax.all_gather(shared_down, (DP, CONTEXT), axis=1, tiled=True),
        lax.all_gather(w_router, (DP, CONTEXT), axis=0, tiled=True),
        lax.all_gather(shared_mix, (DP, CONTEXT), axis=0, tiled=True),
        lax.all_gather(norm1_gain, (DP, CONTEXT), axis=0, tiled=True),
        lax.all_gather(norm2_gain, (DP, CONTEXT), axis=0, tiled=True),
    )
    x_piece, dy_piece = (
        lax.all_gather(tokens, EXPERT, axis=0, tiled=True),
        lax.all_gather(out_grad, EXPERT, axis=0, tiled=True),
    )
    piece_rows = x_piece.shape[0]
    seq_len = piece_rows * n_pieces
    own_start = my_half * tok_rows
    positions = my_piece * piece_rows + jnp.arange(piece_rows)
    cosine, sine = rope_tables(positions, head_dim)
    query_blocks = positions // BLOCK
    key_blocks = jnp.arange(seq_len) // BLOCK
    visible = key_blocks[None, :] <= query_blocks[:, None]
    x_float = x_piece.astype(jnp.float32)
    rstd_one = lax.rsqrt(jnp.mean(x_float * x_float, axis=1, keepdims=True) + EPS)
    normed_one = x_float * rstd_one
    gain_one = full_gain_one.astype(jnp.float32)
    attn_in = (normed_one * gain_one).astype(jnp.bfloat16)
    q_pre = jnp.dot(
        attn_in, full_query, preferred_element_type=jnp.float32
    ) + query_bias_heads.astype(jnp.float32).reshape(-1)
    k_pre = jnp.dot(attn_in, full_key, preferred_element_type=jnp.float32) + bias_key.astype(
        jnp.float32
    ).reshape(-1)
    v_pre = jnp.dot(attn_in, full_value, preferred_element_type=jnp.float32) + bias_value.astype(
        jnp.float32
    ).reshape(-1)
    q_rot = (
        rotate(q_pre.reshape(piece_rows, local_heads, head_dim), cosine, sine)
        .reshape(piece_rows, -1)
        .astype(jnp.bfloat16)
    )
    k_rot = (
        rotate(k_pre.reshape(piece_rows, local_heads, head_dim), cosine, sine)
        .reshape(piece_rows, -1)
        .astype(jnp.bfloat16)
    )
    v_low = v_pre.astype(jnp.bfloat16)
    keys_all, values_all = (
        lax.all_gather(k_rot, CONTEXT, axis=0, tiled=True),
        lax.all_gather(v_low, CONTEXT, axis=0, tiled=True),
    )
    query_grp = to_groups(q_rot, groups, group_size, head_dim)
    keys_grp = to_groups(keys_all, groups, group_size, head_dim)
    values_grp = to_groups(values_all, groups, group_size, head_dim)

    def attend_group(args):
        group_query, group_keys, group_values = args
        scores = (
            jnp.einsum("hqd,hkd->hqk", group_query, group_keys, preferred_element_type=jnp.float32)
            * score_scale
        )
        scores = jnp.where(visible[None], scores, -jnp.inf)
        row_top = jnp.max(scores, axis=2, keepdims=True)
        expo = jnp.exp(scores - row_top)
        totals = jnp.sum(expo, axis=2, keepdims=True)
        probs = (expo / totals).astype(jnp.bfloat16)
        result = jnp.einsum("hqk,hkd->hqd", probs, group_values, preferred_element_type=jnp.float32)
        return (result, row_top[..., 0] + jnp.log(totals[..., 0]))

    attn_grp, lse_grp = lax.map(attend_group, (query_grp, keys_grp, values_grp))
    attn_low = from_groups(attn_grp).astype(jnp.bfloat16)
    out_partial = jnp.dot(attn_low, full_out, preferred_element_type=jnp.float32)
    out_full = lax.psum(out_partial, EXPERT)
    hidden_one = x_float + out_full
    rstd_two = lax.rsqrt(jnp.mean(hidden_one * hidden_one, axis=1, keepdims=True) + EPS)
    normed_two = hidden_one * rstd_two
    gain_two = full_gain_two.astype(jnp.float32)
    moe_in = (normed_two * gain_two).astype(jnp.bfloat16)
    mix = jax.nn.sigmoid(jnp.dot(moe_in, full_mix, preferred_element_type=jnp.float32))
    s_gate = jnp.dot(moe_in, full_sgate, preferred_element_type=jnp.float32)
    s_up = jnp.dot(moe_in, full_sup, preferred_element_type=jnp.float32)
    s_silu = jax.nn.silu(s_gate)
    s_hidden = (s_silu * s_up).astype(jnp.bfloat16)
    shared_own = lax.psum_scatter(
        jnp.dot(s_hidden, full_sdown, preferred_element_type=jnp.float32),
        EXPERT,
        scatter_dimension=0,
        tiled=True,
    )
    moe_own = lax.dynamic_slice_in_dim(moe_in, own_start, tok_rows, 0)
    hidden_own = lax.dynamic_slice_in_dim(hidden_one, own_start, tok_rows, 0)
    mix_own = lax.dynamic_slice_in_dim(mix, own_start, tok_rows, 0)
    dy_own = out_grad.astype(jnp.float32)
    n_experts = full_router.shape[1]
    router_probs = jax.nn.softmax(
        jnp.dot(moe_own, full_router, preferred_element_type=jnp.float32), axis=1
    )
    picked = (expert_ids[:, :, None] == jnp.arange(n_experts)[None, None, :]).astype(jnp.float32)
    gates = jnp.sum(picked * router_probs[:, None, :], axis=2)
    route_hot = (
        (expert_ids[:, :, None] == jnp.arange(n_experts)[None, None, :])
        .astype(jnp.int32)
        .reshape(-1, n_experts)
    )
    earlier = jnp.cumsum(route_hot, axis=0) - route_hot
    slots = jnp.sum(earlier * route_hot, axis=1)
    places = expert_ids.reshape(-1) * CAP + slots
    route_rows = jnp.repeat(moe_own, expert_ids.shape[1], axis=0)
    route_grads = (
        gates.reshape(-1)[:, None] * jnp.repeat(dy_own, expert_ids.shape[1], axis=0)
    ).astype(jnp.bfloat16)
    send_rows = (
        jnp.zeros((n_experts * CAP, width), jnp.bfloat16)
        .at[places]
        .set(route_rows)
        .reshape(n_experts, CAP, width)
    )
    send_grads = (
        jnp.zeros((n_experts * CAP, width), jnp.bfloat16)
        .at[places]
        .set(route_grads)
        .reshape(n_experts, CAP, width)
    )
    gate_weight = expert_gate[0]
    up_weight = expert_up[0]
    down_weight = expert_down[0]
    rows_in = lax.all_to_all(send_rows, (DP, EXPERT), split_axis=0, concat_axis=0, tiled=True)
    grads_in = lax.all_to_all(send_grads, (DP, EXPERT), split_axis=0, concat_axis=0, tiled=True)
    sources = rows_in.shape[0]
    items = rows_in.shape[1]
    flat_in = rows_in.reshape(-1, width)
    flat_grad = grads_in.reshape(-1, width)
    e_gate = jnp.dot(flat_in, gate_weight, preferred_element_type=jnp.float32)
    e_up = jnp.dot(flat_in, up_weight, preferred_element_type=jnp.float32)
    e_silu = jax.nn.silu(e_gate)
    e_hidden = (e_silu * e_up).astype(jnp.bfloat16)
    e_out = jnp.dot(e_hidden, down_weight, preferred_element_type=jnp.float32).astype(jnp.bfloat16)
    d_hidden = mat_right(flat_grad, down_weight)
    d_gate = (d_hidden * e_up * silu_slope(e_gate)).astype(jnp.bfloat16)
    d_up = (d_hidden * e_silu).astype(jnp.bfloat16)
    d_in = (mat_right(d_gate, gate_weight) + mat_right(d_up, up_weight)).astype(jnp.bfloat16)
    back_out = lax.all_to_all(
        e_out.reshape(sources, items, width),
        (DP, EXPERT),
        split_axis=0,
        concat_axis=0,
        tiled=True,
    )
    back_in = lax.all_to_all(
        d_in.reshape(sources, items, width),
        (DP, EXPERT),
        split_axis=0,
        concat_axis=0,
        tiled=True,
    )
    back_out, back_in, rows_seen, grads_seen, hidden_seen, dgate_seen, duplicate_visits = (
        back_out,
        back_in,
        rows_in,
        grads_in,
        e_hidden.reshape(sources, items, -1),
        d_gate.reshape(sources, items, -1),
        d_up.reshape(sources, items, -1),
    )
    flattened_rows = rows_seen.reshape(-1, width)
    routed_gate_gradient = left_operand(
        flattened_rows, dgate_seen.reshape(flattened_rows.shape[0], -1)
    )
    routed_up_gradient = left_operand(
        flattened_rows, duplicate_visits.reshape(flattened_rows.shape[0], -1)
    )
    routed_down_gradient = left_operand(
        hidden_seen.reshape(flattened_rows.shape[0], -1), grads_seen.reshape(-1, width)
    )
    routed_gate_gradient, routed_up_gradient, routed_down_gradient = (
        lax.psum_scatter(
            routed_gate_gradient[None].astype(jnp.bfloat16),
            CONTEXT,
            scatter_dimension=1,
            tiled=True,
        ).astype(jnp.float32),
        lax.psum_scatter(
            routed_up_gradient[None].astype(jnp.bfloat16),
            CONTEXT,
            scatter_dimension=1,
            tiled=True,
        ).astype(jnp.float32),
        lax.psum_scatter(
            routed_down_gradient[None].astype(jnp.bfloat16),
            CONTEXT,
            scatter_dimension=2,
            tiled=True,
        ).astype(jnp.float32),
    )
    route_out = back_out.reshape(-1, width)[places].astype(jnp.float32).reshape(tok_rows, -1, width)
    route_din = back_in.reshape(-1, width)[places].astype(jnp.float32).reshape(tok_rows, -1, width)
    moe_sum = jnp.sum(gates[:, :, None] * route_out, axis=1)
    mixed = (hidden_own + moe_sum + mix_own[:, None] * shared_own).astype(jnp.bfloat16)
    d_gates = jnp.sum(route_out * dy_own[:, None, :], axis=2)
    d_rprobs = jnp.sum(picked * d_gates[:, :, None], axis=1)
    d_logits = router_probs * (d_rprobs - jnp.sum(router_probs * d_rprobs, axis=1, keepdims=True))
    moe_own_float = moe_own.astype(jnp.float32)
    router_part = jnp.dot(moe_own_float.T, d_logits, precision=HIGH)
    d_mixlogit = jnp.sum(shared_own * dy_own, axis=1) * mix_own * (1.0 - mix_own)
    mix_part = jnp.dot(moe_own_float.T, d_mixlogit, precision=HIGH)
    d_in_own = (
        jnp.sum(route_din, axis=1)
        + jnp.dot(d_logits, full_router.astype(jnp.float32).T, precision=HIGH)
        + d_mixlogit[:, None] * full_mix.astype(jnp.float32)[None, :]
    )
    dy_float = dy_piece.astype(jnp.float32)
    d_shared = (mix[:, None] * dy_float).astype(jnp.bfloat16)
    grad_sdown = left_operand(s_hidden, d_shared)
    d_shidden = mat_right(d_shared, full_sdown)
    d_sgate = (d_shidden * s_up * silu_slope(s_gate)).astype(jnp.bfloat16)
    d_sup = (d_shidden * s_silu).astype(jnp.bfloat16)
    grad_sgate = left_operand(moe_in, d_sgate)
    grad_sup = left_operand(moe_in, d_sup)
    d_in_part = mat_right(d_sgate, full_sgate) + mat_right(d_sup, full_sup)
    d_in_part = lax.dynamic_update_slice_in_dim(
        d_in_part,
        lax.dynamic_slice_in_dim(d_in_part, own_start, tok_rows, 0) + d_in_own,
        own_start,
        0,
    )
    d_moe_in, router_grad, mix_grad = lax.psum((d_in_part, router_part, mix_part), EXPERT)
    d_norm_two = d_moe_in * gain_two
    gain_two_grad = jnp.sum(d_moe_in * normed_two, axis=0)
    d_hidden_one = dy_float + rstd_two * (
        d_norm_two - normed_two * jnp.mean(d_norm_two * normed_two, axis=1, keepdims=True)
    )
    d_proj = d_hidden_one.astype(jnp.bfloat16)
    grad_out = left_operand(attn_low, d_proj)
    d_attn = mat_right(d_proj, full_out).astype(jnp.bfloat16)
    dattn_grp = to_groups(d_attn, groups, group_size, head_dim)

    def query_side(args):
        group_query, group_keys, group_values, group_lse, group_attention_gradient = args
        scores = (
            jnp.einsum("hqd,hkd->hqk", group_query, group_keys, preferred_element_type=jnp.float32)
            * score_scale
        )
        probs = jnp.where(
            visible[None],
            jnp.exp(jnp.where(visible[None], scores, 0.0) - group_lse[..., None]),
            0.0,
        )
        d_probs = jnp.einsum(
            "hqd,hkd->hqk",
            group_attention_gradient,
            group_values,
            preferred_element_type=jnp.float32,
        )
        delta = jnp.sum(probs * d_probs, axis=2)
        d_scores = (probs * (d_probs - delta[..., None])).astype(jnp.bfloat16)
        d_query = (
            jnp.einsum("hqk,hkd->hqd", d_scores, group_keys, preferred_element_type=jnp.float32)
            * score_scale
        )
        return (probs, d_scores, d_query, delta)

    def both_sides(args):
        probs, d_scores, d_query, delta = query_side(args)
        d_key = (
            jnp.einsum("hqk,hqd->hkd", d_scores, args[0], preferred_element_type=jnp.float32)
            * score_scale
        )
        d_value = jnp.einsum(
            "hqk,hqd->hkd", probs.astype(jnp.bfloat16), args[4], preferred_element_type=jnp.float32
        )
        return (d_query, d_key, d_value)

    dq_grp, dk_grp, dv_grp = lax.map(
        both_sides, (query_grp, keys_grp, values_grp, lse_grp, dattn_grp)
    )
    d_query = from_groups(dq_grp)
    d_key_own, d_value_own = (
        lax.psum_scatter(from_groups(dk_grp), CONTEXT, scatter_dimension=0, tiled=True),
        lax.psum_scatter(from_groups(dv_grp), CONTEXT, scatter_dimension=0, tiled=True),
    )
    d_q_pre = (
        rotate_back(d_query.reshape(piece_rows, local_heads, head_dim), cosine, sine)
        .reshape(piece_rows, -1)
        .astype(jnp.bfloat16)
    )
    d_k_pre = (
        rotate_back(d_key_own.reshape(piece_rows, local_heads, head_dim), cosine, sine)
        .reshape(piece_rows, -1)
        .astype(jnp.bfloat16)
    )
    d_v_pre = d_value_own.astype(jnp.bfloat16)
    grad_bq = jnp.sum(d_q_pre.astype(jnp.float32), axis=0).reshape(local_heads, head_dim)
    grad_bk = jnp.sum(d_k_pre.astype(jnp.float32), axis=0).reshape(local_heads, head_dim)
    grad_bv = jnp.sum(d_v_pre.astype(jnp.float32), axis=0).reshape(local_heads, head_dim)
    grad_query = left_operand(attn_in, d_q_pre)
    grad_key = left_operand(attn_in, d_k_pre)
    grad_value = left_operand(attn_in, d_v_pre)
    d_attn_in = (
        mat_right(d_q_pre, full_query)
        + mat_right(d_k_pre, full_key)
        + mat_right(d_v_pre, full_value)
    )
    d_attn_in = lax.psum(d_attn_in.astype(jnp.bfloat16), EXPERT).astype(jnp.float32)
    d_norm_one = d_attn_in * gain_one
    gain_one_grad = jnp.sum(d_attn_in * normed_one, axis=0)
    d_x = d_hidden_one + rstd_one * (
        d_norm_one - normed_one * jnp.mean(d_norm_one * normed_one, axis=1, keepdims=True)
    )
    input_grad = lax.dynamic_slice_in_dim(d_x, own_start, tok_rows, 0).astype(jnp.bfloat16)
    (
        grad_query,
        grad_key,
        grad_value,
        grad_out,
        grad_sgate,
        grad_sup,
        grad_sdown,
        router_grad,
        mix_grad,
        gain_one_grad,
        gain_two_grad,
        grad_bq,
        grad_bk,
        grad_bv,
    ) = (
        lax.psum_scatter(grad_query, (DP, CONTEXT), scatter_dimension=0, tiled=True),
        lax.psum_scatter(grad_key, (DP, CONTEXT), scatter_dimension=0, tiled=True),
        lax.psum_scatter(grad_value, (DP, CONTEXT), scatter_dimension=0, tiled=True),
        lax.psum_scatter(grad_out, (DP, CONTEXT), scatter_dimension=1, tiled=True),
        lax.psum_scatter(grad_sgate, (DP, CONTEXT), scatter_dimension=0, tiled=True),
        lax.psum_scatter(grad_sup, (DP, CONTEXT), scatter_dimension=0, tiled=True),
        lax.psum_scatter(grad_sdown, (DP, CONTEXT), scatter_dimension=1, tiled=True),
        lax.psum_scatter(router_grad, (DP, CONTEXT), scatter_dimension=0, tiled=True),
        lax.psum_scatter(mix_grad, (DP, CONTEXT), scatter_dimension=0, tiled=True),
        lax.psum_scatter(gain_one_grad, (DP, CONTEXT), scatter_dimension=0, tiled=True),
        lax.psum_scatter(gain_two_grad, (DP, CONTEXT), scatter_dimension=0, tiled=True),
        lax.psum_scatter(grad_bq, (DP, CONTEXT), scatter_dimension=1, tiled=True),
        lax.psum_scatter(grad_bk, (DP, CONTEXT), scatter_dimension=1, tiled=True),
        lax.psum_scatter(grad_bv, (DP, CONTEXT), scatter_dimension=1, tiled=True),
    )
    return (
        mixed,
        input_grad,
        gain_one_grad,
        grad_query,
        grad_key,
        grad_value,
        grad_bq,
        grad_bk,
        grad_bv,
        grad_out,
        gain_two_grad,
        router_grad,
        mix_grad,
        grad_sgate,
        grad_sup,
        grad_sdown,
        routed_gate_gradient,
        routed_up_gradient,
        routed_down_gradient,
    )


def dot_f32(left, right, left_dim, right_dim):
    return lax.dot_general(
        left, right, (((left_dim,), (right_dim,)), ((), ())), preferred_element_type=jnp.float32
    )


def whole_vmem(count):
    return [pl.BlockSpec(memory_space=pltpu.VMEM)] * count


def like(shape, dtype):
    return jax.ShapeDtypeStruct(shape, dtype)


MESH_ID = pl.DeviceIdType.MESH


class Wire:
    def __init__(self, send, recv):
        self.send = send
        self.recv = recv
        self.sent = 0
        self.received = 0
        self.own = []

    def copy(self, src, dst, device):
        out = self.copy_to(src, dst, device, self.take(1), self.take_send(1))
        self.own.append(out)
        return out

    def take(self, count):
        self.received += count
        assert self.received <= self.recv.shape[0], self.received
        return self.received - count

    def take_send(self, count):
        self.sent += count
        assert self.sent <= self.send.shape[0], self.sent
        return self.sent - count

    def copy_to(self, src, dst, device, recv_slot, send_slot):
        return pltpu.make_async_remote_copy(
            src_ref=src,
            dst_ref=dst,
            send_sem=self.send.at[send_slot],
            recv_sem=self.recv.at[recv_slot],
            device_id=device,
            device_id_type=MESH_ID,
        )

    def drain(self, some=None):
        for item in self.own if some is None else some:
            item.wait_send()
        done = {id(item) for item in some} if some is not None else None
        self.own = [] if done is None else [item for item in self.own if id(item) not in done]


class Local:
    def __init__(self, sems):
        self.sems = sems
        self.count = 0

    def start(self, src, dst):
        assert self.count < self.sems.shape[0], self.count
        item = pltpu.make_async_copy(src, dst, self.sems.at[self.count])
        self.count += 1
        item.start()
        return item


class Place:
    def __init__(self, n_dp):
        self.n_dp = n_dp
        self.z = lax.axis_index(DP)
        self.c = lax.axis_index(CONTEXT)
        self.y = lax.axis_index(EXPERT)
        self.cx = lax.bitwise_xor(self.c, jnp.int32(2))
        self.cs = lax.bitwise_xor(self.c, jnp.int32(1))
        self.cd = lax.bitwise_xor(self.c, jnp.int32(3))
        self.yn = lax.bitwise_xor(self.y, jnp.int32(1))
        self.core = (self.z, self.cs, self.y)
        self.over_x = (self.z, self.cx, self.y)
        self.over_y = (self.z, self.c, self.yn)
        self.up = (self.z + 1, self.c, self.y)
        self.down = (self.z - 1, self.c, self.y)

    def block(self, c, y):
        return c * 2 + y


def barrier(devices):
    sem = pltpu.get_barrier_semaphore()
    for device in devices:
        pl.semaphore_signal(sem, inc=1, device_id=device, device_id_type=MESH_ID)
    pl.semaphore_wait(sem, len(devices))


def rows_of(index, count):
    return pl.ds(pl.multiple_of(index * count, count), count)


def by_rows(total, step, body):
    def one(index, carry):
        body(rows_of(index, step))
        return carry

    lax.fori_loop(0, total // step, one, 0)


def chain_gather(wire, place, refs, arrived=None):
    n = place.n_dp
    z = place.z
    width = len(refs(z))
    recv = wire.take(n * width)
    send = wire.take_send(2 * n * width)

    def copies(slot, up, dist):
        return [
            wire.copy_to(
                ref,
                ref,
                place.up if up else place.down,
                recv + slot * width + index,
                send + (2 * dist + (0 if up else 1)) * width + index,
            )
            for index, ref in enumerate(refs(slot))
        ]

    def start(slot, up, dist):
        for item in copies(slot, up, dist):
            item.start()

    def land(slot, up, dist):
        for item in copies(slot, up, dist):
            item.wait_recv()
        if arrived is not None:
            arrived(slot)

    def sent(slot, up, dist):
        for item in copies(slot, up, dist):
            item.wait_send()

    pl.when(z < n - 1)(lambda: start(z, True, 0))
    pl.when(z > 0)(lambda: start(z, False, 0))
    yield
    for dist in range(1, n):
        below, above = z - dist, z + dist

        @pl.when(below >= 0)
        def _():
            land(below, True, dist)
            pl.when(z < n - 1)(lambda: start(below, True, dist))

        @pl.when(above < n)
        def _():
            land(above, False, dist)
            pl.when(z > 0)(lambda: start(above, False, dist))

        yield
    for dist in range(n):
        below, above = z - dist, z + dist
        pl.when((below >= 0) & (z < n - 1))(lambda: sent(below, True, dist))
        pl.when((above < n) & (z > 0))(lambda: sent(above, False, dist))


def finish(*steps):
    for step in steps:
        for _ in step:
            pass


def plane_gather(wire, place, buf):
    rows = buf.shape[0] // 8
    half = buf.shape[1] // 2
    left, right = pl.ds(0, half), pl.ds(half, half)
    own = rows_of(place.block(place.c, place.y), rows)
    from_x = rows_of(place.block(place.cx, place.y), rows)
    from_y = rows_of(place.block(place.c, place.yn), rows)
    across = rows_of(place.block(place.cx, place.yn), rows)

    def go(where, lanes, device):
        ref = buf.at[where, lanes] if lanes is not None else buf.at[where, :]
        item = wire.copy(ref, ref, device)
        item.start()
        return item

    x_left = go(own, left, place.over_x)
    y_right = go(own, right, place.over_y)
    x_right = go(own, right, place.over_x)
    y_left = go(own, left, place.over_y)
    waits = [go(own, None, place.core)]
    yield
    x_left.wait_recv()
    far_left = go(from_x, left, place.over_y)
    y_right.wait_recv()
    far_right = go(from_y, right, place.over_x)
    yield
    x_right.wait_recv()
    waits.append(go(from_x, None, place.core))
    y_left.wait_recv()
    waits.append(go(from_y, None, place.core))
    yield
    far_left.wait_recv()
    far_right.wait_recv()
    waits.append(go(across, None, place.core))
    for item in waits:
        item.wait_recv()


def add_into(target, lanes, rows, extra):
    count = extra.shape[0]
    step = 16

    def one(index, carry):
        here = pl.ds(pl.multiple_of(rows + index * step, step), step)
        there = rows_of(index, step)
        total = target[here, lanes].astype(jnp.float32) + extra[there, :].astype(jnp.float32)
        target[here, lanes] = total.astype(target.dtype)
        return carry

    lax.fori_loop(0, count // step, one, 0)


def plane_reduce(wire, place, part, got_core, got_one, got_two):
    rows = part.shape[0] // 8
    half = part.shape[1] // 2
    left, right = pl.ds(0, half), pl.ds(half, half)
    chips = ((place.cx, place.yn), (place.cx, place.y), (place.c, place.yn), (place.c, place.y))
    starts = [place.block(c, y) * rows for c, y in chips]
    blocks = [pl.ds(pl.multiple_of(start, rows), rows) for start in starts]
    sibling = [
        rows_of(place.block(lax.bitwise_xor(c, jnp.int32(1)), y), rows) for c, y in chips
    ]
    swaps = []
    for index in range(4):
        item = wire.copy(part.at[sibling[index], :], got_core.at[index], place.core)
        item.start()
        swaps.append(item)
    whole = pl.ds(0, 2 * half)

    def one(index, lanes, slot, device):
        item = wire.copy(part.at[blocks[index], lanes], got_one.at[slot], device)
        item.start()
        return item

    swaps[0].wait_recv()
    add_into(part, whole, starts[0], got_core.at[0])
    far_x = one(0, left, 0, place.over_x)
    far_y = one(0, right, 2, place.over_y)
    swaps[1].wait_recv()
    add_into(part, whole, starts[1], got_core.at[1])
    near_x = one(1, left, 1, place.over_x)
    swaps[2].wait_recv()
    add_into(part, whole, starts[2], got_core.at[2])
    near_y = one(2, right, 3, place.over_y)
    yield
    swaps[3].wait_recv()
    add_into(part, whole, starts[3], got_core.at[3])
    far_x.wait_recv()
    add_into(part, left, starts[2], got_one.at[0])
    last_y = wire.copy(part.at[blocks[2], left], got_two.at[0], place.over_y)
    last_y.start()
    far_y.wait_recv()
    add_into(part, right, starts[1], got_one.at[2])
    last_x = wire.copy(part.at[blocks[1], right], got_two.at[1], place.over_x)
    last_x.start()
    yield
    near_x.wait_recv()
    near_y.wait_recv()
    last_x.wait_recv()
    last_y.wait_recv()


def plane_sum(place, part, got_one, got_two, here):
    rows = part.shape[0] // 8
    half = part.shape[1] // 2
    start = place.block(place.c, place.y) * rows + here.start
    at = pl.ds(pl.multiple_of(start, here.size), here.size)

    def value(ref):
        return ref.astype(jnp.float32)

    left = value(part[at, 0:half]) + value(got_one[1, here, :]) + value(got_two[0, here, :])
    right = value(part[at, half:]) + value(got_one[3, here, :]) + value(got_two[1, here, :])
    return jnp.concatenate([left, right], axis=1)


def forward_kernel(
    n_blocks, n_dp,
    tokens, small, ids, w_query, w_key, w_value, w_out, s_gate, s_up, s_down,
    bias, cosine, sine,
    attn_in, query, keys, values, attn, lse, hidden, moe_in,
    heads_weight, out_weight, gate_weight, up_weight, down_weight, smalls, all_ids,
    x_seq, partial, got_core, got_one, got_two, send, recv, local,
):
    place = Place(n_dp)
    wire = Wire(send, recv)
    inside = Local(local)
    z, c, y = place.z, place.c, place.y
    rows, width = tokens.shape
    seq = x_seq.shape[0]
    cols = query.shape[1]
    head_dim = cosine.shape[1]
    block = seq // n_blocks
    scale = 1.0 / math.sqrt(head_dim)
    n_ctx = 4
    share = w_query.shape[0]
    f32, low = jnp.float32, jnp.bfloat16

    others = [(dz, dc) for dz in range(n_dp) for dc in range(n_ctx) if dz or dc]

    def moved(dz, dc, y_to):
        return (lax.bitwise_xor(z, jnp.int32(dz)), lax.bitwise_xor(c, jnp.int32(dc)), y_to)

    barrier(
        [moved(dz, dc, y) for dz, dc in others] + [moved(dz, 0, place.yn) for dz in range(n_dp)]
    )

    mine = z * n_ctx + c
    my_rows = rows_of(mine, share)
    exchanges = []
    for dc in range(n_ctx):
        to = lax.bitwise_xor(c, jnp.int32(dc))
        lanes = pl.ds(pl.multiple_of(to * cols, cols), cols)
        pairs = [
            (weight.at[:, lanes], heads_weight.at[my_rows, pl.ds(index * cols, cols)])
            for index, weight in enumerate((w_query, w_key, w_value))
        ]
        pairs.append((w_out.at[rows_of(to, cols), :], out_weight.at[:, my_rows]))
        for src, dst in pairs:
            if dc == 0:
                exchanges.append(inside.start(src, dst))
            else:
                item = wire.copy(src, dst, moved(0, dc, y))
                item.start()
                exchanges.append(item)
    own_rows = rows_of(place.block(c, y), rows)
    here = inside.start(tokens, x_seq.at[own_rows, :])
    here.wait()
    tokens_in = plane_gather(wire, place, x_seq)
    next(tokens_in)
    small_copies = [inside.start(small, smalls.at[:, my_rows])]
    for dz, dc in others:
        item = wire.copy(small, smalls.at[:, my_rows], moved(dz, dc, y))
        item.start()
        small_copies.append(item)
    group = z * 2 + y
    small_copies.append(inside.start(ids, all_ids.at[group]))
    for dz in range(n_dp):
        for y_to in (y, place.yn):
            if dz or y_to is not y:
                item = wire.copy(ids, all_ids.at[group], moved(dz, 0, y_to))
                item.start()
                small_copies.append(item)
    for item in exchanges:
        item.wait_recv()

    def attention_blocks(slot):
        at = rows_of(slot, n_ctx * share)
        return [heads_weight.at[at, :], out_weight.at[:, at]]

    weights_in = chain_gather(wire, place, attention_blocks)
    next(weights_in)
    finish(tokens_in)
    for item in small_copies:
        item.wait_recv()

    gain_one = smalls[9:10, :].astype(f32)
    gain_two = smalls[10:11, :].astype(f32)

    def norm_one(at):
        x_float = x_seq[at, :].astype(f32)
        rstd = lax.rsqrt(jnp.mean(x_float * x_float, axis=1, keepdims=True) + EPS)
        attn_in[at, :] = (x_float * rstd * gain_one).astype(low)

    by_rows(seq, 64, norm_one)
    finish(weights_in)

    shared_pieces = []
    for dz in range(n_dp):
        to = lax.bitwise_xor(z, jnp.int32(dz))
        hidden_rows = rows_of(to, s_down.shape[0] // n_dp)
        pairs = [
            (s_gate.at[to], gate_weight.at[z, c]),
            (s_up.at[to], up_weight.at[z, c]),
            (s_down.at[hidden_rows, :], down_weight.at[:, my_rows]),
        ]
        for src, dst in pairs:
            if dz == 0:
                shared_pieces.append(inside.start(src, dst))
            else:
                item = wire.copy(src, dst, moved(dz, 0, y))
                item.start()
                shared_pieces.append(item)

    def project(at):
        pre = dot_f32(attn_in[at, :], heads_weight[...], 1, 0)
        cos = cosine[at, :]
        sin = sine[at, :]
        for index, kept in enumerate((query, keys, values)):
            for start in range(0, cols, head_dim):
                from_lane = index * cols + start
                part = pre[:, from_lane : from_lane + head_dim]
                part = part + bias[index : index + 1, start : start + head_dim]
                if index < 2:
                    part = part * cos + pltpu.roll(part, head_dim // 2, 1) * sin
                kept[at, start : start + head_dim] = part.astype(low)

    by_rows(seq, block, project)
    for start in range(0, cols, head_dim):
        lanes = slice(start, start + head_dim)
        for step in range(n_blocks):
            at = slice(step * block, (step + 1) * block)
            seen = slice(0, (step + 1) * block)
            scores = dot_f32(query[at, lanes], keys[seen, lanes], 1, 1) * scale
            top = jnp.max(scores, axis=1, keepdims=True)
            expo = jnp.exp(scores - top)
            total = jnp.sum(expo, axis=1, keepdims=True)
            probs = (expo / total).astype(low)
            attn[at, lanes] = dot_f32(probs, values[seen, lanes], 1, 0).astype(low)
            lse[at, lanes] = jnp.broadcast_to(top + jnp.log(total), (block, head_dim))

    def output(at):
        partial[at, :] = dot_f32(attn[at, :], out_weight[...], 1, 0).astype(low)

    by_rows(seq, block, output)
    finish(plane_reduce(wire, place, partial, got_core, got_one, got_two))

    def norm_two(at):
        start = place.block(c, y) * rows + at.start
        own = pl.ds(pl.multiple_of(start, at.size), at.size)
        total = x_seq[own, :].astype(f32) + plane_sum(place, partial, got_one, got_two, at)
        hidden[at, :] = total
        rstd = lax.rsqrt(jnp.mean(total * total, axis=1, keepdims=True) + EPS)
        got_core[0, at, :] = (total * rstd * gain_two).astype(low)

    by_rows(rows, 16, norm_two)
    at_group = rows_of(group, rows)
    here = inside.start(got_core.at[0], moe_in.at[at_group, :])
    here.wait()

    y_recv = wire.take(n_dp)
    y_send = wire.take_send(n_dp)

    def to_y(slot):
        at = rows_of(slot * 2 + y, rows)
        return wire.copy_to(
            moe_in.at[at, :], moe_in.at[at, :], place.over_y, y_recv + slot, y_send + slot
        )

    def from_y(slot):
        at = rows_of(slot * 2 + place.yn, rows)
        return wire.copy_to(
            moe_in.at[at, :], moe_in.at[at, :], place.over_y, y_recv + slot, y_send + slot
        )

    rows_chain = chain_gather(
        wire,
        place,
        lambda slot: [moe_in.at[rows_of(slot * 2 + y, rows), :]],
        arrived=lambda slot: to_y(slot).start(),
    )
    next(rows_chain)
    to_y(z).start()
    for item in shared_pieces:
        item.wait_recv()

    def shared_set(context):
        return [gate_weight.at[:, context], up_weight.at[:, context]] + [
            down_weight.at[:, rows_of(dz * n_ctx + context, share)] for dz in range(n_dp)
        ]

    over = []
    for ref in shared_set(c):
        item = wire.copy(ref, ref, place.over_x)
        item.start()
        over.append(item)
    close = []
    for ref in shared_set(c):
        item = wire.copy(ref, ref, place.core)
        item.start()
        close.append(item)
    finish(rows_chain)
    for item, ref in zip(over, shared_set(place.cx)):
        item.wait_recv()
        item = wire.copy(ref, ref, place.core)
        item.start()
        close.append(item)
    for item in close:
        item.wait_recv()
    for slot in range(n_dp):
        from_y(slot).wait_recv()
        to_y(slot).wait_send()
    wire.drain()


def chain_reduce(wire, place, parts):
    n = place.n_dp
    z = place.z
    count = len(parts)
    recv = wire.take(2 * n * count)
    send = wire.take_send(2 * n * count)

    def copies(target, up):
        out = []
        for index, (block, below, above) in enumerate(parts):
            slot = (2 * target + (0 if up else 1)) * count + index
            landing = below if up else above
            out.append(
                wire.copy_to(
                    block(target),
                    landing.at[target],
                    place.up if up else place.down,
                    recv + slot,
                    send + slot,
                )
            )
        return out

    def collect(target, up):
        for item, (block, below, above) in zip(copies(target, up), parts):
            item.wait_recv()
            add_block(block(target), (below if up else above).at[target])

    def pass_on(target, up):
        more = (z > 0) if up else (z < n - 1)
        pl.when(more)(lambda: collect(target, up))
        for item in copies(target, up):
            item.start()

    for step in range(n - 1):
        high, low = n - 1 - step, step

        @pl.when(z < n // 2)
        def _():
            pl.when(z < high)(lambda: pass_on(high, True))
            pl.when(z > low)(lambda: pass_on(low, False))

        @pl.when(z >= n // 2)
        def _():
            pl.when(z > low)(lambda: pass_on(low, False))
            pl.when(z < high)(lambda: pass_on(high, True))

        yield
    pl.when(z > 0)(lambda: collect(z, True))
    pl.when(z < n - 1)(lambda: collect(z, False))
    for target in range(n):

        @pl.when(z < target)
        def _():
            for item in copies(target, True):
                item.wait_send()

        @pl.when(z > target)
        def _():
            for item in copies(target, False):
                item.wait_send()


def add_block(target, extra):
    step = 16

    def one(index, carry):
        here = rows_of(index, step)
        total = target[here, :].astype(jnp.float32) + extra[here, :].astype(jnp.float32)
        target[here, :] = total.astype(target.dtype)
        return carry

    lax.fori_loop(0, extra.shape[0] // step, one, 0)


class Adder:
    def __init__(self, sems):
        self.sems = sems

    def run(self, buf, chunks):
        def load(index):
            first, second, _ = chunks[index]
            slot = index % 2
            items = [
                pltpu.make_async_copy(first, buf.at[0, slot], self.sems.at[3 * slot]),
                pltpu.make_async_copy(second, buf.at[1, slot], self.sems.at[3 * slot + 1]),
            ]
            for item in items:
                item.start()
            return items

        stores = [None, None]
        loads = load(0)
        for index, (_, _, target) in enumerate(chunks):
            slot = index % 2
            after = load(index + 1) if index + 1 < len(chunks) else None
            for item in loads:
                item.wait()
            loads = after
            if stores[slot] is not None:
                stores[slot].wait()
            total, first, second = buf.at[2, slot], buf.at[0, slot], buf.at[1, slot]

            def one(step, carry):
                here = rows_of(step, 16)
                value = first[here, :].astype(jnp.float32) + second[here, :].astype(jnp.float32)
                total[here, :] = value.astype(total.dtype)
                return carry

            lax.fori_loop(0, total.shape[0] // 16, one, 0)
            stores[slot] = pltpu.make_async_copy(total, target, self.sems.at[3 * slot + 2])
            stores[slot].start()
        for item in stores:
            if item is not None:
                item.wait()


def backward_kernel(
    n_blocks, n_dp,
    d_in_part, scalars, g_sgate, g_sup, g_sdown, g_egate, g_eup, g_edown,
    hidden, out_grad, tokens, smalls, probs, mix,
    heads_weight, w_out, query, keys, values, attn, lse, attn_in, cosine, sine,
    input_grad, heads_grad, out_weight_grad, small_grad, bias_grad,
    t_sgate, t_sup, t_sdown, r_egate, r_eup, r_edown, x_egate, x_eup, x_edown,
    k_sgate, k_sup, k_sdown, r_sgate, r_sup, r_sdown, x_sgate, x_sup, x_sdown,
    s_sgate, s_sup, s_sdown, k_egate, k_eup, k_edown,
    partial, got_y, got_z, got_scalars, d_hidden, side, moe_own, terms, acc,
    proj, d_attn, d_qkv, d_keys, d_values, got_core, got_one, got_two,
    g_heads, g_out, heads_below, heads_above, out_below, out_above, out_block,
    stage, landed, over_y, wide_buf, tall_buf, gate_buf, down_buf, send, recv, local, adds,
):
    place = Place(n_dp)
    wire = Wire(send, recv)
    inside = Local(local)
    adder = Adder(adds)
    z, c, y = place.z, place.c, place.y
    rows, width = tokens.shape
    seq = proj.shape[0]
    cols = query.shape[1]
    head_dim = cosine.shape[1]
    block = seq // n_blocks
    scale = 1.0 / math.sqrt(head_dim)
    n_ctx = 4
    share = width // (n_dp * n_ctx)
    n_experts = probs.shape[0]
    f32, low = jnp.float32, jnp.bfloat16
    core = lax.rem(c, 2)
    others = [(dz, dc) for dz in range(n_dp) for dc in range(n_ctx) if dz or dc]

    def moved(dz, dc, y_to):
        return (lax.bitwise_xor(z, jnp.int32(dz)), lax.bitwise_xor(c, jnp.int32(dc)), y_to)

    fill = inside.start(d_in_part, partial)
    barrier(
        [moved(dz, dc, y) for dz, dc in others] + [moved(dz, 0, place.yn) for dz in range(n_dp)]
    )
    fill.wait()

    def group_rows(dz, y_of):
        return rows_of(lax.bitwise_xor(z, jnp.int32(dz)) * 2 + y_of, rows)

    order = (2, 3, 1, 0)
    y_swaps = {}
    for dz in order:
        item = wire.copy(partial.at[group_rows(dz, place.yn), :], got_y.at[dz], place.over_y)
        item.start()
        y_swaps[dz] = item
    group = z * 2 + y
    scalar_items = []
    for dz in range(n_dp):
        for y_to in (y, place.yn):
            target = lax.bitwise_xor(z, jnp.int32(dz)) * 2 + y_to
            if dz == 0 and y_to is y:
                item = inside.start(scalars.at[target], got_scalars.at[group])
            else:
                item = wire.copy(
                    scalars.at[target], got_scalars.at[group], moved(dz, 0, y_to)
                )
                item.start()
            scalar_items.append(item)

    def piece(dx, sibling):
        side_of = lax.bitwise_xor(lax.div(c, 2), jnp.int32(dx))
        return side_of * 2 + (1 - core if sibling else core)

    piece_cols = g_edown.shape[1] // n_ctx

    def shared_blocks(dx, dz, sibling):
        index = dz * n_ctx + piece(dx, sibling)
        return [g_sgate.at[index], g_sup.at[index], g_sdown.at[:, rows_of(index, share)]]

    def routed_pieces(dx, sibling):
        index = piece(dx, sibling)
        return [g_egate.at[index], g_eup.at[index], g_edown.at[:, rows_of(index, piece_cols)]]

    shared_core = []
    for dx in (1, 0):
        for dz in range(n_dp):
            for src, dst in zip(shared_blocks(dx, dz, True), (k_sgate, k_sup, k_sdown)):
                item = wire.copy(src, dst.at[dx, dz], place.core)
                item.start()
                shared_core.append(item)
    routed_core = []
    for index, dst in enumerate((k_egate, k_eup, k_edown)):
        for dx in (1, 0):
            item = wire.copy(routed_pieces(dx, True)[index], dst.at[dx], place.core)
            item.start()
            routed_core.append(item)

    for item in shared_core:
        item.wait_recv()
    shared_over = []
    for index, (buf, kept, total, got) in enumerate(
        (
            (gate_buf, k_sgate, r_sgate, x_sgate),
            (gate_buf, k_sup, r_sup, x_sup),
            (down_buf, k_sdown, r_sdown, x_sdown),
        )
    ):
        adder.run(
            buf,
            [
                (shared_blocks(dx, dz, False)[index], kept.at[dx, dz], total.at[dx, dz])
                for dx in (1, 0)
                for dz in range(n_dp)
            ],
        )
        item = wire.copy(total.at[1], got, place.over_x)
        item.start()
        shared_over.append(item)

    z_swaps = []

    def over_dp(dz):
        y_swaps[dz].wait_recv()
        target = lax.bitwise_xor(z, jnp.int32(dz)) * 2 + y
        add_into(partial, pl.ds(0, width), target * rows, got_y.at[dz])
        if dz:
            item = wire.copy(
                partial.at[rows_of(target, rows), :], got_z.at[dz - 1], moved(dz, 0, y)
            )
            item.start()
            z_swaps.append(item)

    def routed_sum(index):
        for item in routed_core[2 * index : 2 * index + 2]:
            item.wait_recv()
        kept = (k_egate, k_eup, k_edown)[index]
        total = (r_egate, r_eup, r_edown)[index]
        buf = tall_buf if index == 2 else wide_buf
        step = buf.shape[2]
        chunks = []
        for dx in (1, 0):
            mine = routed_pieces(dx, False)[index]
            for start in range(0, mine.shape[0], step):
                at = pl.ds(start, step)
                chunks.append((mine.at[at, :], kept.at[dx, at, :], total.at[dx, at, :]))
        adder.run(buf, chunks)

    over_dp(2)
    routed_sum(0)
    over_dp(3)
    routed_sum(1)
    over_dp(1)
    routed_sum(2)
    over_dp(0)

    for item in scalar_items:
        item.wait_recv()
    d_rprobs = got_scalars[:, 0, :]
    probs_own = probs[...]
    d_logits = probs_own * (d_rprobs - jnp.sum(probs_own * d_rprobs, axis=0, keepdims=True))
    shared_dot = jnp.sum(got_scalars[:, 1, :], axis=0, keepdims=True)
    d_mix = shared_dot * mix[...] * (1.0 - mix[...])
    d_side = jnp.concatenate(
        [d_logits, jnp.broadcast_to(d_mix, (16 - n_experts, rows))], axis=0
    )
    row_of = lax.broadcasted_iota(jnp.int32, d_side.shape, 0)
    d_side = jnp.where(row_of <= n_experts, d_side, 0.0)
    first = d_side.astype(low)
    rest = d_side - first.astype(f32)
    second = rest.astype(low)
    third = (rest - second.astype(f32)).astype(low)
    terms[...] = jnp.concatenate([first, second, third], axis=0)
    side[...] = dot_f32(terms[...], jnp.concatenate([smalls[...]] * 3, axis=0), 0, 0)
    gain_one = smalls[n_experts + 1 : n_experts + 2, :].astype(f32)
    gain_two = smalls[n_experts + 2 : n_experts + 3, :].astype(f32)
    acc[...] = jnp.zeros_like(acc)
    for item in z_swaps:
        item.wait_recv()
    own_plane = place.block(c, y) * rows

    def norm_two(at):
        mine = pl.ds(pl.multiple_of(group * rows + at.start, at.size), at.size)
        d_moe = side[at, :] + partial[mine, :].astype(f32)
        for dz in range(n_dp - 1):
            d_moe = d_moe + got_z[dz, at, :].astype(f32)
        total = hidden[at, :]
        rstd = lax.rsqrt(jnp.mean(total * total, axis=1, keepdims=True) + EPS)
        normed = total * rstd
        acc[0] += d_moe * normed
        d_norm = d_moe * gain_two
        back = out_grad[at, :].astype(f32) + rstd * (
            d_norm - normed * jnp.mean(d_norm * normed, axis=1, keepdims=True)
        )
        d_hidden[at, :] = back
        moe_own[at, :] = (normed * gain_two).astype(low)
        proj[pl.ds(pl.multiple_of(own_plane + at.start, at.size), at.size), :] = back.astype(low)

    by_rows(rows, 16, norm_two)
    proj_in = plane_gather(wire, place, proj)
    next(proj_in)
    side[0:48, :] = dot_f32(terms[...], moe_own[...], 1, 0)
    next(proj_in)
    next(proj_in)

    shared_last = []
    for index, (buf, total, got, ready, target) in enumerate(
        (
            (gate_buf, r_sgate, x_sgate, s_sgate, t_sgate),
            (gate_buf, r_sup, x_sup, s_sup, t_sup),
            (down_buf, r_sdown, x_sdown, s_sdown, t_sdown),
        )
    ):
        shared_over[index].wait_recv()
        adder.run(buf, [(total.at[0, dz], got.at[dz], ready.at[dz]) for dz in range(n_dp)])
        for dz in (2, 3, 1, 0):
            to = lax.bitwise_xor(z, jnp.int32(dz))
            if dz:
                item = wire.copy(ready.at[to], target.at[z], moved(dz, 0, y))
                item.start()
            else:
                item = inside.start(ready.at[to], target.at[z])
            shared_last.append(item)
        if index == 0:
            finish(proj_in)

    def go_over_x(index):
        total = (r_egate, r_eup, r_edown)[index]
        got = (x_egate, x_eup, x_edown)[index]
        item = wire.copy(total.at[1], got, place.over_x)
        item.start()
        return item

    routed_over = [go_over_x(0)]
    by_share = n_ctx * share

    def out_weight(target):
        at = rows_of(target, by_share)
        g_out[:, at] = dot_f32(attn[...], proj[:, at], 0, 0).astype(low)

    def each(count, body):
        def one(index, carry):
            body(index)
            return carry

        lax.fori_loop(0, count, one, 0)

    each(n_dp, out_weight)
    out_chain = chain_reduce(
        wire, place, [(lambda t: g_out.at[:, rows_of(t, by_share)], out_below, out_above)]
    )
    next(out_chain)

    def project(at):
        d_attn[at, :] = dot_f32(proj[at, :], w_out[...], 1, 1).astype(low)

    by_rows(seq, block, project)

    def turn(part, at):
        return part * cosine[at, :] - pltpu.roll(part, head_dim // 2, 1) * sine[at, :]

    every = slice(0, seq)
    for start in range(0, cols, head_dim):
        lanes = slice(start, start + head_dim)
        d_keys[...] = jnp.zeros_like(d_keys)
        d_values[...] = jnp.zeros_like(d_values)
        for step in range(n_blocks):
            at = slice(step * block, (step + 1) * block)
            seen = slice(0, (step + 1) * block)
            q_here = query[at, lanes]
            k_seen = keys[seen, lanes]
            grad = d_attn[at, lanes]
            scores = dot_f32(q_here, k_seen, 1, 1) * scale
            weights = jnp.exp(scores - lse[at, start : start + 1])
            d_probs = dot_f32(grad, values[seen, lanes], 1, 1)
            delta = jnp.sum(weights * d_probs, axis=1, keepdims=True)
            d_scores = (weights * (d_probs - delta)).astype(low)
            d_query = dot_f32(d_scores, k_seen, 1, 0) * scale
            d_qkv[at, lanes] = turn(d_query, at).astype(low)
            d_keys[seen, :] += dot_f32(d_scores, q_here, 0, 0) * scale
            d_values[seen, :] += dot_f32(weights.astype(low), grad, 0, 0)
        d_qkv[:, cols + start : cols + start + head_dim] = turn(d_keys[...], every).astype(low)
        d_qkv[:, 2 * cols + start : 2 * cols + start + head_dim] = d_values[...].astype(low)

    wire.drain(list(y_swaps.values()) + z_swaps)

    def output(at):
        partial[at, :] = dot_f32(d_qkv[at, :], heads_weight[...], 1, 1).astype(low)

    by_rows(seq, block, output)
    reduce = plane_reduce(wire, place, partial, got_core, got_one, got_two)
    next(reduce)

    def heads_weights(target):
        at = rows_of(target, by_share)
        g_heads[at, :] = dot_f32(attn_in[:, at], d_qkv[...], 0, 0).astype(low)

    each(n_dp // 2, heads_weights)
    next(reduce)
    each(n_dp // 2, lambda index: heads_weights(index + n_dp // 2))
    heads_chain = chain_reduce(
        wire,
        place,
        [(lambda t: g_heads.at[rows_of(t, by_share), :], heads_below, heads_above)],
    )
    next(heads_chain)
    finish(reduce)
    routed_over += [go_over_x(1), go_over_x(2)]

    def norm_one(at):
        d_attn_in = plane_sum(place, partial, got_one, got_two, at)
        x_float = tokens[at, :].astype(f32)
        rstd = lax.rsqrt(jnp.mean(x_float * x_float, axis=1, keepdims=True) + EPS)
        normed = x_float * rstd
        acc[1] += d_attn_in * normed
        d_norm = d_attn_in * gain_one
        input_grad[at, :] = (
            d_hidden[at, :]
            + rstd * (d_norm - normed * jnp.mean(d_norm * normed, axis=1, keepdims=True))
        ).astype(low)

    by_rows(rows, 16, norm_one)

    side_grad = side[0:16, :] + side[16:32, :] + side[32:48, :]
    row_of = lax.broadcasted_iota(jnp.int32, side_grad.shape, 0)
    gain_one_grad = jnp.sum(acc[1], axis=0, keepdims=True)
    gain_two_grad = jnp.sum(acc[0], axis=0, keepdims=True)
    small_rows = jnp.where(
        row_of == n_experts + 1,
        gain_one_grad,
        jnp.where(row_of == n_experts + 2, gain_two_grad, side_grad),
    )
    bias_sums = jnp.sum(d_qkv[...].astype(f32), axis=0, keepdims=True)
    bias_rows = [
        bias_sums[:, start : start + head_dim] for start in range(0, 3 * cols, head_dim)
    ]
    bias_rows += [jnp.zeros((8 - len(bias_rows), head_dim), f32)]
    bias_rows = jnp.concatenate(bias_rows, axis=0)
    for target in range(n_dp * n_ctx):
        stage[target, 0:16, :] = small_rows[:, target * share : (target + 1) * share]
        stage[target, 16:24, :] = bias_rows
    mine = z * n_ctx + c
    small_items = [inside.start(stage.at[mine], landed.at[mine])]
    for dz, dc in others:
        target = lax.bitwise_xor(z, jnp.int32(dz)) * n_ctx + lax.bitwise_xor(c, jnp.int32(dc))
        item = wire.copy(stage.at[target], landed.at[mine], moved(dz, dc, y))
        item.start()
        small_items.append(item)
    next(out_chain)
    next(heads_chain)
    for item in small_items:
        item.wait_recv()
    total = landed[0, 0:16, :]
    for source in range(1, n_dp * n_ctx):
        total = total + landed[source, 0:16, :]
    over_y[0] = total
    swap = wire.copy(over_y.at[0], over_y.at[1], place.over_y)
    swap.start()
    for context in range(n_ctx):
        sums = landed[context, 16:24, :]
        for source in range(1, n_dp):
            sums = sums + landed[source * n_ctx + context, 16:24, :]
        bias_grad[context] = sums
    finish(out_chain)
    finish(heads_chain)

    out_block[...] = g_out[:, rows_of(z, by_share)]
    last = []
    for dc in range(n_ctx):
        to = lax.bitwise_xor(c, jnp.int32(dc))
        pairs = [
            (
                g_heads.at[pl.ds(pl.multiple_of(z * by_share + to * share, share), share), :],
                heads_grad.at[c],
            ),
            (out_block.at[:, rows_of(to, share)], out_weight_grad.at[c]),
        ]
        for src, dst in pairs:
            if dc:
                item = wire.copy(src, dst, moved(0, dc, y))
                item.start()
            else:
                item = inside.start(src, dst)
            last.append(item)
    swap.wait_recv()
    small_grad[...] = over_y[0] + over_y[1]
    for item in last + shared_last + routed_over:
        item.wait_recv()
    wire.drain()


def tokens_plan(
    tokens,
    out_grad,
    expert_ids,
    norm1_gain,
    w_query,
    w_key,
    w_value,
    query_bias_heads,
    bias_key,
    bias_value,
    w_out,
    norm2_gain,
    w_router,
    shared_mix,
    shared_in_gate,
    shared_in_up,
    shared_down,
    expert_gate,
    expert_up,
    expert_down,
):
    low = jnp.bfloat16
    f32 = jnp.float32
    tok_rows, width = tokens.shape
    n_dp, n_ctx, n_half = (lax.axis_size(name) for name in (DP, CONTEXT, EXPERT))
    dp, ctx, half = (lax.axis_index(name) for name in (DP, CONTEXT, EXPERT))
    half_heads, head_dim = query_bias_heads.shape
    heads = half_heads // n_ctx
    cols = heads * head_dim
    seq_len = tok_rows * n_ctx * n_half
    n_blocks = seq_len // BLOCK
    n_experts = w_router.shape[1]
    n_group = n_dp * n_half
    my_expert = dp * n_half + half

    def group_in(rows):
        return lax.all_gather(rows, (DP, EXPERT), axis=0, tiled=True)

    def group_out(rows):
        return lax.psum_scatter(rows, (DP, EXPERT), scatter_dimension=0, tiled=True)

    small = jnp.concatenate(
        [w_router.T, shared_mix[None], norm1_gain[None], norm2_gain[None]], axis=0
    )
    small = jnp.pad(small, ((0, 16 - small.shape[0]), (0, 0)))
    ids = jnp.pad(expert_ids.T, ((0, 8 - expert_ids.shape[1]), (0, 0)), constant_values=-1)
    hidden_units = shared_in_gate.shape[1] // n_dp

    def by_dp(weight):
        return weight.reshape(weight.shape[0], n_dp, hidden_units).transpose(1, 0, 2)

    biases = jnp.stack([query_bias_heads, bias_key, bias_value]).astype(f32)
    biases = lax.dynamic_slice_in_dim(biases, ctx * heads, heads, 1).reshape(3, cols)
    cosine, sine = rope_tables(jnp.arange(seq_len), head_dim)
    cosine = jnp.concatenate([cosine[:, 0], cosine[:, 0]], axis=1)
    sine = jnp.concatenate([-sine[:, 0], sine[:, 0]], axis=1)
    dy_group = group_in(out_grad)
    vmem = pl.BlockSpec(memory_space=pltpu.VMEM)
    anywhere = pl.BlockSpec(memory_space=pl.ANY)
    share = w_query.shape[0]
    half_width = width // 2
    (
        attn_in, query, keys, values, attn, lse, hidden_own, moe_in,
        heads_weight, wo, sg, su, sd, small, ids_group,
    ) = pl.pallas_call(
        lambda *refs: forward_kernel(n_blocks, n_dp, *refs),
        out_shape=[
            like((seq_len, width), low),
            like((seq_len, cols), low),
            like((seq_len, cols), low),
            like((seq_len, cols), low),
            like((seq_len, cols), low),
            like((seq_len, cols), f32),
            like((tok_rows, width), f32),
            like((n_group * tok_rows, width), low),
            like((width, 3 * cols), low),
            like((cols, width), low),
            like((n_dp, n_ctx, share, hidden_units), low),
            like((n_dp, n_ctx, share, hidden_units), low),
            like((hidden_units, width), low),
            like((16, width), low),
            like((n_group, 8, tok_rows), jnp.int32),
        ],
        in_specs=[anywhere] * 10 + [vmem] * 3,
        out_specs=[vmem] * 7 + [anywhere] + [vmem] * 2 + [anywhere] * 3 + [vmem, anywhere],
        scratch_shapes=[
            pltpu.VMEM((seq_len, width), low),
            pltpu.VMEM((seq_len, width), low),
            pltpu.VMEM((4, tok_rows, width), low),
            pltpu.VMEM((4, tok_rows, half_width), low),
            pltpu.VMEM((2, tok_rows, half_width), low),
            pltpu.SemaphoreType.DMA((144,)),
            pltpu.SemaphoreType.DMA((144,)),
            pltpu.SemaphoreType.DMA((16,)),
        ],
        name="forward",
        compiler_params=pltpu.CompilerParams(
            collective_id=1, has_side_effects=True, vmem_limit_bytes=60 * 2**20
        ),
    )(
        tokens, small, ids, w_query, w_key, w_value, w_out,
        by_dp(shared_in_gate), by_dp(shared_in_up), shared_down, biases, cosine, sine,
    )
    sg, su = sg.reshape(width, hidden_units), su.reshape(width, hidden_units)
    gain_one = small[n_experts + 1].astype(f32)
    gain_two = small[n_experts + 2].astype(f32)
    x_own = tokens.astype(f32)
    dy_own = out_grad.astype(f32)
    rstd_two = lax.rsqrt(jnp.mean(hidden_own * hidden_own, axis=1, keepdims=True) + EPS)
    normed_two = hidden_own * rstd_two
    moe_own = (normed_two * gain_two).astype(low)

    logits = mat_right(moe_in, small)
    router_probs = jax.nn.softmax(logits[:, :n_experts], axis=1)
    mix = jax.nn.sigmoid(logits[:, n_experts])
    hit = jnp.any(ids_group == my_expert, axis=1)
    gate = jnp.sum(
        jnp.where(jnp.arange(n_experts)[None, :] == my_expert, router_probs, 0.0), axis=1
    )
    place = jnp.cumsum(hit.astype(jnp.int32), axis=1) - 1
    chosen = (hit[:, None, :] & (place[:, None, :] == jnp.arange(CAP)[None, :, None]))
    pick = chosen.astype(low)
    gate_rows = jnp.sum(jnp.where(chosen, gate.reshape(n_group, 1, tok_rows), 0.0), axis=2)

    def to_rows(group):
        return jnp.einsum(
            "sct,std->scd", pick, group.reshape(n_group, tok_rows, -1), preferred_element_type=f32
        ).astype(low).reshape(n_group * CAP, -1)

    def to_tokens(rows):
        return jnp.einsum(
            "sct,scd->std", pick, rows.reshape(n_group, CAP, -1), preferred_element_type=f32
        ).reshape(n_group * tok_rows, -1)

    rows_in = to_rows(moe_in)
    dy_rows = to_rows(dy_group)
    grads_in = (gate_rows.reshape(-1, 1) * dy_rows.astype(f32)).astype(low)
    gate_weight, up_weight, down_weight = expert_gate[0], expert_up[0], expert_down[0]
    e_gate = jnp.dot(rows_in, gate_weight, preferred_element_type=f32)
    e_up = jnp.dot(rows_in, up_weight, preferred_element_type=f32)
    e_silu = jax.nn.silu(e_gate)
    e_hidden = (e_silu * e_up).astype(low)
    e_out = jnp.dot(e_hidden, down_weight, preferred_element_type=f32).astype(low)
    d_hidden = mat_right(grads_in, down_weight)
    d_gate = (d_hidden * e_up * silu_slope(e_gate)).astype(low)
    d_up = (d_hidden * e_silu).astype(low)
    d_in = (mat_right(d_gate, gate_weight) + mat_right(d_up, up_weight)).astype(low)

    s_gate = jnp.dot(moe_in, sg, preferred_element_type=f32)
    s_up = jnp.dot(moe_in, su, preferred_element_type=f32)
    s_silu = jax.nn.silu(s_gate)
    s_hidden = (s_silu * s_up).astype(low)
    shared = jnp.dot(s_hidden, sd, preferred_element_type=f32)
    dy_float = dy_group.astype(f32)
    d_shared = (mix[:, None] * dy_float).astype(low)
    d_shidden = mat_right(d_shared, sd)
    d_sgate = (d_shidden * s_up * silu_slope(s_gate)).astype(low)
    d_sup = (d_shidden * s_silu).astype(low)

    moe_part = (gate[:, None] * to_tokens(e_out) + mix[:, None] * shared).astype(low)
    d_in_part = (to_tokens(d_in) + mat_right(d_sgate, sg) + mat_right(d_sup, su)).astype(low)
    d_gate_rows = jnp.sum(e_out.astype(f32) * dy_rows.astype(f32), axis=1).reshape(n_group, CAP)
    d_gate_tok = jnp.sum(jnp.where(chosen, d_gate_rows[:, :, None], 0.0), axis=1).reshape(-1)
    shared_dot = jnp.sum(shared * dy_float, axis=1)
    scalars = jnp.stack([d_gate_tok, shared_dot]).reshape(2, n_group, tok_rows).transpose(1, 0, 2)
    scalars = jnp.pad(scalars, ((0, 0), (0, 6), (0, 0)))
    moe_sum = group_out(moe_part).astype(f32)
    mixed = (hidden_own + moe_sum).astype(low)

    own = my_expert * tok_rows
    probs_own = lax.dynamic_slice_in_dim(router_probs, own, tok_rows, 0).T
    mix_own = lax.dynamic_slice_in_dim(mix, own, tok_rows, 0)[None]
    g_sgate = left_operand(moe_in, d_sgate).astype(low).reshape(-1, share, hidden_units)
    g_sup = left_operand(moe_in, d_sup).astype(low).reshape(-1, share, hidden_units)
    g_sdown = left_operand(s_hidden, d_shared).astype(low)
    g_egate = left_operand(rows_in, d_gate).astype(low).reshape(n_ctx, width // n_ctx, -1)
    g_eup = left_operand(rows_in, d_up).astype(low).reshape(n_ctx, width // n_ctx, -1)
    g_edown = left_operand(e_hidden, grads_in).astype(low)
    units = g_edown.shape[0]
    by_share = n_ctx * share
    e_wide = (width // n_ctx, units)
    e_tall = (units, width // n_ctx)
    s_wide = (share, hidden_units)
    s_tall = (hidden_units, share)
    s_kinds = (s_wide, s_wide, s_tall)
    e_kinds = (e_wide, e_wide, e_tall)
    results = pl.pallas_call(
        lambda *refs: backward_kernel(n_blocks, n_dp, *refs),
        out_shape=[
            like((tok_rows, width), low),
            like((n_ctx, share, 3 * cols), low),
            like((n_ctx, cols, share), low),
            like((16, share), f32),
            like((n_ctx, 8, head_dim), f32),
        ]
        + [like((n_dp, *kind), low) for kind in s_kinds]
        + [like((2, *kind), low) for kind in e_kinds]
        + [like(kind, low) for kind in e_kinds]
        + [like((2, n_dp, *kind), low) for kind in s_kinds]
        + [like((2, n_dp, *kind), low) for kind in s_kinds]
        + [like((n_dp, *kind), low) for kind in s_kinds]
        + [like((n_dp, *kind), low) for kind in s_kinds]
        + [like((2, *kind), low) for kind in e_kinds],
        in_specs=[anywhere] * 8 + [vmem] * 16,
        out_specs=[vmem] + [anywhere] * 2 + [vmem] * 2 + [anywhere] * 24,
        scratch_shapes=[
            pltpu.VMEM((seq_len, width), low),
            pltpu.VMEM((n_dp, tok_rows, width), low),
            pltpu.VMEM((n_dp - 1, tok_rows, width), low),
            pltpu.VMEM((n_group, 8, tok_rows), f32),
            pltpu.VMEM((tok_rows, width), f32),
            pltpu.VMEM((tok_rows, width), f32),
            pltpu.VMEM((tok_rows, width), low),
            pltpu.VMEM((48, tok_rows), low),
            pltpu.VMEM((2, 16, width), f32),
            pltpu.VMEM((seq_len, width), low),
            pltpu.VMEM((seq_len, cols), low),
            pltpu.VMEM((seq_len, 3 * cols), low),
            pltpu.VMEM((seq_len, head_dim), f32),
            pltpu.VMEM((seq_len, head_dim), f32),
            pltpu.VMEM((4, tok_rows, width), low),
            pltpu.VMEM((4, tok_rows, half_width), low),
            pltpu.VMEM((2, tok_rows, half_width), low),
            pltpu.VMEM((width, 3 * cols), low),
            pltpu.VMEM((cols, width), low),
            pltpu.VMEM((n_dp, by_share, 3 * cols), low),
            pltpu.VMEM((n_dp, by_share, 3 * cols), low),
            pltpu.VMEM((n_dp, cols, by_share), low),
            pltpu.VMEM((n_dp, cols, by_share), low),
            pltpu.VMEM((cols, by_share), low),
            pltpu.VMEM((n_dp * n_ctx, 24, share), f32),
            pltpu.VMEM((n_dp * n_ctx, 24, share), f32),
            pltpu.VMEM((2, 16, share), f32),
            pltpu.VMEM((3, 2, 128, units), low),
            pltpu.VMEM((3, 2, units // 4, width // n_ctx), low),
            pltpu.VMEM((3, 2, *s_wide), low),
            pltpu.VMEM((3, 2, *s_tall), low),
            pltpu.SemaphoreType.DMA((160,)),
            pltpu.SemaphoreType.DMA((160,)),
            pltpu.SemaphoreType.DMA((16,)),
            pltpu.SemaphoreType.DMA((6,)),
        ],
        name="backward",
        compiler_params=pltpu.CompilerParams(
            collective_id=2, has_side_effects=True, vmem_limit_bytes=63 * 2**20
        ),
    )(
        d_in_part, scalars, g_sgate, g_sup, g_sdown, g_egate, g_eup, g_edown,
        hidden_own, out_grad, tokens, small, probs_own, mix_own,
        heads_weight, wo, query, keys, values, attn, lse, attn_in, cosine, sine,
    )
    input_grad, heads_grad, out_weight_grad, small_grad, bias_grad = results[:5]
    s_done, e_own, e_other = results[5:8], results[8:11], results[11:14]
    grad_sgate, grad_sup = (
        grad.transpose(1, 0, 2).reshape(share, -1).astype(f32) for grad in s_done[:2]
    )
    grad_sdown = s_done[2].reshape(-1, share).astype(f32)
    routed = [
        (mine[0].astype(f32) + other.astype(f32))[None] for mine, other in zip(e_own, e_other)
    ]
    heads_grad = heads_grad.reshape(n_ctx, share, 3, cols).transpose(2, 1, 0, 3)
    heads_grad = heads_grad.reshape(3, share, -1).astype(f32)
    grad_out = out_weight_grad.reshape(-1, share).astype(f32)
    bias_sum = bias_grad[:, : 3 * heads].reshape(n_ctx, 3, heads, head_dim)
    bias_sum = bias_sum.transpose(1, 0, 2, 3).reshape(3, half_heads, head_dim)
    bias_share = head_dim // (n_dp * n_ctx)
    bias_sum = lax.dynamic_slice_in_dim(bias_sum, (dp * n_ctx + ctx) * bias_share, bias_share, 2)
    return (
        mixed,
        input_grad,
        small_grad[n_experts + 1],
        heads_grad[0],
        heads_grad[1],
        heads_grad[2],
        bias_sum[0],
        bias_sum[1],
        bias_sum[2],
        grad_out,
        small_grad[n_experts + 2],
        small_grad[:n_experts].T,
        small_grad[n_experts],
        grad_sgate,
        grad_sup,
        grad_sdown,
        routed[0],
        routed[1],
        routed[2],
    )


def on_device(*arrays):
    sizes = [lax.axis_size(name) for name in (DP, CONTEXT, EXPERT)]
    if sizes == [4, 4, 2] and arrays[7].shape[0] % sizes[1] == 0:
        return tokens_plan(*arrays)
    return weights_plan(*arrays)


def solution(mesh):
    placed = (
        P((DP, CONTEXT, EXPERT), None),
        P((DP, CONTEXT, EXPERT), None),
        P((DP, CONTEXT, EXPERT), None),
        P((DP, CONTEXT)),
        P((DP, CONTEXT), EXPERT),
        P((DP, CONTEXT), EXPERT),
        P((DP, CONTEXT), EXPERT),
        P(EXPERT, None),
        P(EXPERT, None),
        P(EXPERT, None),
        P(EXPERT, (DP, CONTEXT)),
        P((DP, CONTEXT)),
        P((DP, CONTEXT), None),
        P((DP, CONTEXT)),
        P((DP, CONTEXT), EXPERT),
        P((DP, CONTEXT), EXPERT),
        P(EXPERT, (DP, CONTEXT)),
        P((DP, EXPERT), None, None),
        P((DP, EXPERT), None, None),
        P((DP, EXPERT), None, None),
    )
    return jax.shard_map(
        on_device,
        mesh=mesh,
        in_specs=placed,
        out_specs=(
            P((DP, CONTEXT, EXPERT), None),
            P((DP, CONTEXT, EXPERT), None),
            P((DP, CONTEXT)),
            P((DP, CONTEXT), EXPERT),
            P((DP, CONTEXT), EXPERT),
            P((DP, CONTEXT), EXPERT),
            P(EXPERT, (DP, CONTEXT)),
            P(EXPERT, (DP, CONTEXT)),
            P(EXPERT, (DP, CONTEXT)),
            P(EXPERT, (DP, CONTEXT)),
            P((DP, CONTEXT)),
            P((DP, CONTEXT), None),
            P((DP, CONTEXT)),
            P((DP, CONTEXT), EXPERT),
            P((DP, CONTEXT), EXPERT),
            P(EXPERT, (DP, CONTEXT)),
            P((DP, EXPERT), CONTEXT, None),
            P((DP, EXPERT), CONTEXT, None),
            P((DP, EXPERT), None, CONTEXT),
        ),
        check_vma=False,
    )
```

```python
import math

import jax
import jax.numpy as jnp
import numpy as np
from jax import lax
from jax.experimental import pallas as pl
from jax.experimental.pallas import tpu as pltpu
from jax.sharding import PartitionSpec as P

DP, CONTEXT, EXPERT = "dp", "context", "expert"
BLOCK = 256
CAP = 96


EPS = 1e-06
THETA = 1000000.0
HIGH = lax.Precision.HIGHEST


def rope_tables(positions, head_dim):
    half = head_dim // 2
    freq = THETA ** (-(2.0 * jnp.arange(half, dtype=jnp.float32)) / head_dim)
    angle = positions.astype(jnp.float32)[:, None] * freq[None, :]
    return (jnp.cos(angle)[:, None, :], jnp.sin(angle)[:, None, :])


def rotate(values, cosine, sine):
    half = values.shape[-1] // 2
    first = values[..., :half]
    second = values[..., half:]
    return jnp.concatenate(
        [first * cosine - second * sine, second * cosine + first * sine], axis=-1
    )


def rotate_back(values, cosine, sine):
    half = values.shape[-1] // 2
    first = values[..., :half]
    second = values[..., half:]
    return jnp.concatenate(
        [first * cosine + second * sine, second * cosine - first * sine], axis=-1
    )


def to_groups(matrix, groups, group_size, head_dim):
    return matrix.reshape(matrix.shape[0], groups, group_size, head_dim).transpose(1, 2, 0, 3)


def from_groups(stacked):
    return stacked.transpose(2, 0, 1, 3).reshape(stacked.shape[2], -1)


def silu_slope(values):
    sigma = jax.nn.sigmoid(values)
    return sigma * (1.0 + values * (1.0 - sigma))


def left_operand(left, right):
    return jnp.dot(left.T, right, preferred_element_type=jnp.float32)


def mat_right(left, right):
    return jnp.dot(left, right.T, preferred_element_type=jnp.float32)


def weights_plan(
    tokens,
    out_grad,
    expert_ids,
    norm1_gain,
    w_query,
    w_key,
    w_value,
    query_bias_heads,
    bias_key,
    bias_value,
    w_out,
    norm2_gain,
    w_router,
    shared_mix,
    shared_in_gate,
    shared_in_up,
    shared_down,
    expert_gate,
    expert_up,
    expert_down,
):
    tok_rows = tokens.shape[0]
    width = tokens.shape[1]
    my_half = lax.axis_index(EXPERT)
    my_piece = lax.axis_index(CONTEXT)
    n_pieces = lax.axis_size(CONTEXT)
    local_heads = query_bias_heads.shape[0]
    head_dim = query_bias_heads.shape[1]
    group_size = 2
    groups = local_heads // group_size
    score_scale = 1.0 / math.sqrt(head_dim)
    (
        full_query,
        full_key,
        full_value,
        full_out,
        full_sgate,
        full_sup,
        full_sdown,
        full_router,
        full_mix,
        full_gain_one,
        full_gain_two,
    ) = (
        lax.all_gather(w_query, (DP, CONTEXT), axis=0, tiled=True),
        lax.all_gather(w_key, (DP, CONTEXT), axis=0, tiled=True),
        lax.all_gather(w_value, (DP, CONTEXT), axis=0, tiled=True),
        lax.all_gather(w_out, (DP, CONTEXT), axis=1, tiled=True),
        lax.all_gather(shared_in_gate, (DP, CONTEXT), axis=0, tiled=True),
        lax.all_gather(shared_in_up, (DP, CONTEXT), axis=0, tiled=True),
        lax.all_gather(shared_down, (DP, CONTEXT), axis=1, tiled=True),
        lax.all_gather(w_router, (DP, CONTEXT), axis=0, tiled=True),
        lax.all_gather(shared_mix, (DP, CONTEXT), axis=0, tiled=True),
        lax.all_gather(norm1_gain, (DP, CONTEXT), axis=0, tiled=True),
        lax.all_gather(norm2_gain, (DP, CONTEXT), axis=0, tiled=True),
    )
    x_piece, dy_piece = (
        lax.all_gather(tokens, EXPERT, axis=0, tiled=True),
        lax.all_gather(out_grad, EXPERT, axis=0, tiled=True),
    )
    piece_rows = x_piece.shape[0]
    seq_len = piece_rows * n_pieces
    own_start = my_half * tok_rows
    positions = my_piece * piece_rows + jnp.arange(piece_rows)
    cosine, sine = rope_tables(positions, head_dim)
    query_blocks = positions // BLOCK
    key_blocks = jnp.arange(seq_len) // BLOCK
    visible = key_blocks[None, :] <= query_blocks[:, None]
    x_float = x_piece.astype(jnp.float32)
    rstd_one = lax.rsqrt(jnp.mean(x_float * x_float, axis=1, keepdims=True) + EPS)
    normed_one = x_float * rstd_one
    gain_one = full_gain_one.astype(jnp.float32)
    attn_in = (normed_one * gain_one).astype(jnp.bfloat16)
    q_pre = jnp.dot(
        attn_in, full_query, preferred_element_type=jnp.float32
    ) + query_bias_heads.astype(jnp.float32).reshape(-1)
    k_pre = jnp.dot(attn_in, full_key, preferred_element_type=jnp.float32) + bias_key.astype(
        jnp.float32
    ).reshape(-1)
    v_pre = jnp.dot(attn_in, full_value, preferred_element_type=jnp.float32) + bias_value.astype(
        jnp.float32
    ).reshape(-1)
    q_rot = (
        rotate(q_pre.reshape(piece_rows, local_heads, head_dim), cosine, sine)
        .reshape(piece_rows, -1)
        .astype(jnp.bfloat16)
    )
    k_rot = (
        rotate(k_pre.reshape(piece_rows, local_heads, head_dim), cosine, sine)
        .reshape(piece_rows, -1)
        .astype(jnp.bfloat16)
    )
    v_low = v_pre.astype(jnp.bfloat16)
    keys_all, values_all = (
        lax.all_gather(k_rot, CONTEXT, axis=0, tiled=True),
        lax.all_gather(v_low, CONTEXT, axis=0, tiled=True),
    )
    query_grp = to_groups(q_rot, groups, group_size, head_dim)
    keys_grp = to_groups(keys_all, groups, group_size, head_dim)
    values_grp = to_groups(values_all, groups, group_size, head_dim)

    def attend_group(args):
        group_query, group_keys, group_values = args
        scores = (
            jnp.einsum("hqd,hkd->hqk", group_query, group_keys, preferred_element_type=jnp.float32)
            * score_scale
        )
        scores = jnp.where(visible[None], scores, -jnp.inf)
        row_top = jnp.max(scores, axis=2, keepdims=True)
        expo = jnp.exp(scores - row_top)
        totals = jnp.sum(expo, axis=2, keepdims=True)
        probs = (expo / totals).astype(jnp.bfloat16)
        result = jnp.einsum("hqk,hkd->hqd", probs, group_values, preferred_element_type=jnp.float32)
        return (result, row_top[..., 0] + jnp.log(totals[..., 0]))

    attn_grp, lse_grp = lax.map(attend_group, (query_grp, keys_grp, values_grp))
    attn_low = from_groups(attn_grp).astype(jnp.bfloat16)
    out_partial = jnp.dot(attn_low, full_out, preferred_element_type=jnp.float32)
    out_full = lax.psum(out_partial, EXPERT)
    hidden_one = x_float + out_full
    rstd_two = lax.rsqrt(jnp.mean(hidden_one * hidden_one, axis=1, keepdims=True) + EPS)
    normed_two = hidden_one * rstd_two
    gain_two = full_gain_two.astype(jnp.float32)
    moe_in = (normed_two * gain_two).astype(jnp.bfloat16)
    mix = jax.nn.sigmoid(jnp.dot(moe_in, full_mix, preferred_element_type=jnp.float32))
    s_gate = jnp.dot(moe_in, full_sgate, preferred_element_type=jnp.float32)
    s_up = jnp.dot(moe_in, full_sup, preferred_element_type=jnp.float32)
    s_silu = jax.nn.silu(s_gate)
    s_hidden = (s_silu * s_up).astype(jnp.bfloat16)
    shared_own = lax.psum_scatter(
        jnp.dot(s_hidden, full_sdown, preferred_element_type=jnp.float32),
        EXPERT,
        scatter_dimension=0,
        tiled=True,
    )
    moe_own = lax.dynamic_slice_in_dim(moe_in, own_start, tok_rows, 0)
    hidden_own = lax.dynamic_slice_in_dim(hidden_one, own_start, tok_rows, 0)
    mix_own = lax.dynamic_slice_in_dim(mix, own_start, tok_rows, 0)
    dy_own = out_grad.astype(jnp.float32)
    n_experts = full_router.shape[1]
    router_probs = jax.nn.softmax(
        jnp.dot(moe_own, full_router, preferred_element_type=jnp.float32), axis=1
    )
    picked = (expert_ids[:, :, None] == jnp.arange(n_experts)[None, None, :]).astype(jnp.float32)
    gates = jnp.sum(picked * router_probs[:, None, :], axis=2)
    route_hot = (
        (expert_ids[:, :, None] == jnp.arange(n_experts)[None, None, :])
        .astype(jnp.int32)
        .reshape(-1, n_experts)
    )
    earlier = jnp.cumsum(route_hot, axis=0) - route_hot
    slots = jnp.sum(earlier * route_hot, axis=1)
    places = expert_ids.reshape(-1) * CAP + slots
    route_rows = jnp.repeat(moe_own, expert_ids.shape[1], axis=0)
    route_grads = (
        gates.reshape(-1)[:, None] * jnp.repeat(dy_own, expert_ids.shape[1], axis=0)
    ).astype(jnp.bfloat16)
    send_rows = (
        jnp.zeros((n_experts * CAP, width), jnp.bfloat16)
        .at[places]
        .set(route_rows)
        .reshape(n_experts, CAP, width)
    )
    send_grads = (
        jnp.zeros((n_experts * CAP, width), jnp.bfloat16)
        .at[places]
        .set(route_grads)
        .reshape(n_experts, CAP, width)
    )
    gate_weight = expert_gate[0]
    up_weight = expert_up[0]
    down_weight = expert_down[0]
    rows_in = lax.all_to_all(send_rows, (DP, EXPERT), split_axis=0, concat_axis=0, tiled=True)
    grads_in = lax.all_to_all(send_grads, (DP, EXPERT), split_axis=0, concat_axis=0, tiled=True)
    sources = rows_in.shape[0]
    items = rows_in.shape[1]
    flat_in = rows_in.reshape(-1, width)
    flat_grad = grads_in.reshape(-1, width)
    e_gate = jnp.dot(flat_in, gate_weight, preferred_element_type=jnp.float32)
    e_up = jnp.dot(flat_in, up_weight, preferred_element_type=jnp.float32)
    e_silu = jax.nn.silu(e_gate)
    e_hidden = (e_silu * e_up).astype(jnp.bfloat16)
    e_out = jnp.dot(e_hidden, down_weight, preferred_element_type=jnp.float32).astype(jnp.bfloat16)
    d_hidden = mat_right(flat_grad, down_weight)
    d_gate = (d_hidden * e_up * silu_slope(e_gate)).astype(jnp.bfloat16)
    d_up = (d_hidden * e_silu).astype(jnp.bfloat16)
    d_in = (mat_right(d_gate, gate_weight) + mat_right(d_up, up_weight)).astype(jnp.bfloat16)
    back_out = lax.all_to_all(
        e_out.reshape(sources, items, width),
        (DP, EXPERT),
        split_axis=0,
        concat_axis=0,
        tiled=True,
    )
    back_in = lax.all_to_all(
        d_in.reshape(sources, items, width),
        (DP, EXPERT),
        split_axis=0,
        concat_axis=0,
        tiled=True,
    )
    back_out, back_in, rows_seen, grads_seen, hidden_seen, dgate_seen, duplicate_visits = (
        back_out,
        back_in,
        rows_in,
        grads_in,
        e_hidden.reshape(sources, items, -1),
        d_gate.reshape(sources, items, -1),
        d_up.reshape(sources, items, -1),
    )
    flattened_rows = rows_seen.reshape(-1, width)
    routed_gate_gradient = left_operand(
        flattened_rows, dgate_seen.reshape(flattened_rows.shape[0], -1)
    )
    routed_up_gradient = left_operand(
        flattened_rows, duplicate_visits.reshape(flattened_rows.shape[0], -1)
    )
    routed_down_gradient = left_operand(
        hidden_seen.reshape(flattened_rows.shape[0], -1), grads_seen.reshape(-1, width)
    )
    routed_gate_gradient, routed_up_gradient, routed_down_gradient = (
        lax.psum_scatter(
            routed_gate_gradient[None].astype(jnp.bfloat16),
            CONTEXT,
            scatter_dimension=1,
            tiled=True,
        ).astype(jnp.float32),
        lax.psum_scatter(
            routed_up_gradient[None].astype(jnp.bfloat16),
            CONTEXT,
            scatter_dimension=1,
            tiled=True,
        ).astype(jnp.float32),
        lax.psum_scatter(
            routed_down_gradient[None].astype(jnp.bfloat16),
            CONTEXT,
            scatter_dimension=2,
            tiled=True,
        ).astype(jnp.float32),
    )
    route_out = back_out.reshape(-1, width)[places].astype(jnp.float32).reshape(tok_rows, -1, width)
    route_din = back_in.reshape(-1, width)[places].astype(jnp.float32).reshape(tok_rows, -1, width)
    moe_sum = jnp.sum(gates[:, :, None] * route_out, axis=1)
    mixed = (hidden_own + moe_sum + mix_own[:, None] * shared_own).astype(jnp.bfloat16)
    d_gates = jnp.sum(route_out * dy_own[:, None, :], axis=2)
    d_rprobs = jnp.sum(picked * d_gates[:, :, None], axis=1)
    d_logits = router_probs * (d_rprobs - jnp.sum(router_probs * d_rprobs, axis=1, keepdims=True))
    moe_own_float = moe_own.astype(jnp.float32)
    router_part = jnp.dot(moe_own_float.T, d_logits, precision=HIGH)
    d_mixlogit = jnp.sum(shared_own * dy_own, axis=1) * mix_own * (1.0 - mix_own)
    mix_part = jnp.dot(moe_own_float.T, d_mixlogit, precision=HIGH)
    d_in_own = (
        jnp.sum(route_din, axis=1)
        + jnp.dot(d_logits, full_router.astype(jnp.float32).T, precision=HIGH)
        + d_mixlogit[:, None] * full_mix.astype(jnp.float32)[None, :]
    )
    dy_float = dy_piece.astype(jnp.float32)
    d_shared = (mix[:, None] * dy_float).astype(jnp.bfloat16)
    grad_sdown = left_operand(s_hidden, d_shared)
    d_shidden = mat_right(d_shared, full_sdown)
    d_sgate = (d_shidden * s_up * silu_slope(s_gate)).astype(jnp.bfloat16)
    d_sup = (d_shidden * s_silu).astype(jnp.bfloat16)
    grad_sgate = left_operand(moe_in, d_sgate)
    grad_sup = left_operand(moe_in, d_sup)
    d_in_part = mat_right(d_sgate, full_sgate) + mat_right(d_sup, full_sup)
    d_in_part = lax.dynamic_update_slice_in_dim(
        d_in_part,
        lax.dynamic_slice_in_dim(d_in_part, own_start, tok_rows, 0) + d_in_own,
        own_start,
        0,
    )
    d_moe_in, router_grad, mix_grad = lax.psum((d_in_part, router_part, mix_part), EXPERT)
    d_norm_two = d_moe_in * gain_two
    gain_two_grad = jnp.sum(d_moe_in * normed_two, axis=0)
    d_hidden_one = dy_float + rstd_two * (
        d_norm_two - normed_two * jnp.mean(d_norm_two * normed_two, axis=1, keepdims=True)
    )
    d_proj = d_hidden_one.astype(jnp.bfloat16)
    grad_out = left_operand(attn_low, d_proj)
    d_attn = mat_right(d_proj, full_out).astype(jnp.bfloat16)
    dattn_grp = to_groups(d_attn, groups, group_size, head_dim)

    def query_side(args):
        group_query, group_keys, group_values, group_lse, group_attention_gradient = args
        scores = (
            jnp.einsum("hqd,hkd->hqk", group_query, group_keys, preferred_element_type=jnp.float32)
            * score_scale
        )
        probs = jnp.where(
            visible[None],
            jnp.exp(jnp.where(visible[None], scores, 0.0) - group_lse[..., None]),
            0.0,
        )
        d_probs = jnp.einsum(
            "hqd,hkd->hqk",
            group_attention_gradient,
            group_values,
            preferred_element_type=jnp.float32,
        )
        delta = jnp.sum(probs * d_probs, axis=2)
        d_scores = (probs * (d_probs - delta[..., None])).astype(jnp.bfloat16)
        d_query = (
            jnp.einsum("hqk,hkd->hqd", d_scores, group_keys, preferred_element_type=jnp.float32)
            * score_scale
        )
        return (probs, d_scores, d_query, delta)

    def both_sides(args):
        probs, d_scores, d_query, delta = query_side(args)
        d_key = (
            jnp.einsum("hqk,hqd->hkd", d_scores, args[0], preferred_element_type=jnp.float32)
            * score_scale
        )
        d_value = jnp.einsum(
            "hqk,hqd->hkd", probs.astype(jnp.bfloat16), args[4], preferred_element_type=jnp.float32
        )
        return (d_query, d_key, d_value)

    dq_grp, dk_grp, dv_grp = lax.map(
        both_sides, (query_grp, keys_grp, values_grp, lse_grp, dattn_grp)
    )
    d_query = from_groups(dq_grp)
    d_key_own, d_value_own = (
        lax.psum_scatter(from_groups(dk_grp), CONTEXT, scatter_dimension=0, tiled=True),
        lax.psum_scatter(from_groups(dv_grp), CONTEXT, scatter_dimension=0, tiled=True),
    )
    d_q_pre = (
        rotate_back(d_query.reshape(piece_rows, local_heads, head_dim), cosine, sine)
        .reshape(piece_rows, -1)
        .astype(jnp.bfloat16)
    )
    d_k_pre = (
        rotate_back(d_key_own.reshape(piece_rows, local_heads, head_dim), cosine, sine)
        .reshape(piece_rows, -1)
        .astype(jnp.bfloat16)
    )
    d_v_pre = d_value_own.astype(jnp.bfloat16)
    grad_bq = jnp.sum(d_q_pre.astype(jnp.float32), axis=0).reshape(local_heads, head_dim)
    grad_bk = jnp.sum(d_k_pre.astype(jnp.float32), axis=0).reshape(local_heads, head_dim)
    grad_bv = jnp.sum(d_v_pre.astype(jnp.float32), axis=0).reshape(local_heads, head_dim)
    grad_query = left_operand(attn_in, d_q_pre)
    grad_key = left_operand(attn_in, d_k_pre)
    grad_value = left_operand(attn_in, d_v_pre)
    d_attn_in = (
        mat_right(d_q_pre, full_query)
        + mat_right(d_k_pre, full_key)
        + mat_right(d_v_pre, full_value)
    )
    d_attn_in = lax.psum(d_attn_in.astype(jnp.bfloat16), EXPERT).astype(jnp.float32)
    d_norm_one = d_attn_in * gain_one
    gain_one_grad = jnp.sum(d_attn_in * normed_one, axis=0)
    d_x = d_hidden_one + rstd_one * (
        d_norm_one - normed_one * jnp.mean(d_norm_one * normed_one, axis=1, keepdims=True)
    )
    input_grad = lax.dynamic_slice_in_dim(d_x, own_start, tok_rows, 0).astype(jnp.bfloat16)
    (
        grad_query,
        grad_key,
        grad_value,
        grad_out,
        grad_sgate,
        grad_sup,
        grad_sdown,
        router_grad,
        mix_grad,
        gain_one_grad,
        gain_two_grad,
        grad_bq,
        grad_bk,
        grad_bv,
    ) = (
        lax.psum_scatter(grad_query, (DP, CONTEXT), scatter_dimension=0, tiled=True),
        lax.psum_scatter(grad_key, (DP, CONTEXT), scatter_dimension=0, tiled=True),
        lax.psum_scatter(grad_value, (DP, CONTEXT), scatter_dimension=0, tiled=True),
        lax.psum_scatter(grad_out, (DP, CONTEXT), scatter_dimension=1, tiled=True),
        lax.psum_scatter(grad_sgate, (DP, CONTEXT), scatter_dimension=0, tiled=True),
        lax.psum_scatter(grad_sup, (DP, CONTEXT), scatter_dimension=0, tiled=True),
        lax.psum_scatter(grad_sdown, (DP, CONTEXT), scatter_dimension=1, tiled=True),
        lax.psum_scatter(router_grad, (DP, CONTEXT), scatter_dimension=0, tiled=True),
        lax.psum_scatter(mix_grad, (DP, CONTEXT), scatter_dimension=0, tiled=True),
        lax.psum_scatter(gain_one_grad, (DP, CONTEXT), scatter_dimension=0, tiled=True),
        lax.psum_scatter(gain_two_grad, (DP, CONTEXT), scatter_dimension=0, tiled=True),
        lax.psum_scatter(grad_bq, (DP, CONTEXT), scatter_dimension=1, tiled=True),
        lax.psum_scatter(grad_bk, (DP, CONTEXT), scatter_dimension=1, tiled=True),
        lax.psum_scatter(grad_bv, (DP, CONTEXT), scatter_dimension=1, tiled=True),
    )
    return (
        mixed,
        input_grad,
        gain_one_grad,
        grad_query,
        grad_key,
        grad_value,
        grad_bq,
        grad_bk,
        grad_bv,
        grad_out,
        gain_two_grad,
        router_grad,
        mix_grad,
        grad_sgate,
        grad_sup,
        grad_sdown,
        routed_gate_gradient,
        routed_up_gradient,
        routed_down_gradient,
    )


def dot_f32(left, right, left_dim, right_dim):
    return lax.dot_general(
        left, right, (((left_dim,), (right_dim,)), ((), ())), preferred_element_type=jnp.float32
    )


def whole_vmem(count):
    return [pl.BlockSpec(memory_space=pltpu.VMEM)] * count


def like(shape, dtype):
    return jax.ShapeDtypeStruct(shape, dtype)


MESH_ID = pl.DeviceIdType.MESH


class Wire:
    def __init__(self, send, recv):
        self.send = send
        self.recv = recv
        self.sent = 0
        self.received = 0
        self.own = []

    def copy(self, src, dst, device):
        out = self.copy_to(src, dst, device, self.take(1), self.take_send(1))
        self.own.append(out)
        return out

    def take(self, count):
        self.received += count
        assert self.received <= self.recv.shape[0], self.received
        return self.received - count

    def take_send(self, count):
        self.sent += count
        assert self.sent <= self.send.shape[0], self.sent
        return self.sent - count

    def copy_to(self, src, dst, device, recv_slot, send_slot):
        return pltpu.make_async_remote_copy(
            src_ref=src,
            dst_ref=dst,
            send_sem=self.send.at[send_slot],
            recv_sem=self.recv.at[recv_slot],
            device_id=device,
            device_id_type=MESH_ID,
        )

    def drain(self, some=None):
        for item in self.own if some is None else some:
            item.wait_send()
        done = {id(item) for item in some} if some is not None else None
        self.own = [] if done is None else [item for item in self.own if id(item) not in done]


class Local:
    def __init__(self, sems):
        self.sems = sems
        self.count = 0

    def start(self, src, dst):
        assert self.count < self.sems.shape[0], self.count
        item = pltpu.make_async_copy(src, dst, self.sems.at[self.count])
        self.count += 1
        item.start()
        return item


class Phases:
    def __init__(self):
        self.scope = None

    def go(self, name):
        if self.scope is not None:
            self.scope.__exit__(None, None, None)
        self.scope = jax.named_scope(name) if name else None
        if name:
            self.scope.__enter__()


class Place:
    def __init__(self, n_dp):
        self.n_dp = n_dp
        self.z = lax.axis_index(DP)
        self.c = lax.axis_index(CONTEXT)
        self.y = lax.axis_index(EXPERT)
        self.cx = lax.bitwise_xor(self.c, jnp.int32(2))
        self.cs = lax.bitwise_xor(self.c, jnp.int32(1))
        self.cd = lax.bitwise_xor(self.c, jnp.int32(3))
        self.yn = lax.bitwise_xor(self.y, jnp.int32(1))
        self.core = (self.z, self.cs, self.y)
        self.over_x = (self.z, self.cx, self.y)
        self.over_y = (self.z, self.c, self.yn)
        self.up = (self.z + 1, self.c, self.y)
        self.down = (self.z - 1, self.c, self.y)

    def block(self, c, y):
        return c * 2 + y


def barrier(devices):
    sem = pltpu.get_barrier_semaphore()
    for device in devices:
        pl.semaphore_signal(sem, inc=1, device_id=device, device_id_type=MESH_ID)
    pl.semaphore_wait(sem, len(devices))


def rows_of(index, count):
    return pl.ds(pl.multiple_of(index * count, count), count)


def by_rows(total, step, body):
    def one(index, carry):
        body(rows_of(index, step))
        return carry

    lax.fori_loop(0, total // step, one, 0)


def chain_gather(wire, place, refs, arrived=None, own=None):
    n = place.n_dp
    z = place.z
    width = len(refs(z))
    recv = wire.take(n * width)
    send = wire.take_send(2 * n * width)

    def copies(slot, up, dist):
        return [
            wire.copy_to(
                own[index] if own is not None and dist == 0 else ref,
                ref,
                place.up if up else place.down,
                recv + slot * width + index,
                send + (2 * dist + (0 if up else 1)) * width + index,
            )
            for index, ref in enumerate(refs(slot))
        ]

    def start(slot, up, dist):
        for item in copies(slot, up, dist):
            item.start()

    def land(slot, up, dist):
        for item in copies(slot, up, dist):
            item.wait_recv()
        if arrived is not None:
            arrived(slot)

    def sent(slot, up, dist):
        for item in copies(slot, up, dist):
            item.wait_send()

    pl.when(z < n - 1)(lambda: start(z, True, 0))
    pl.when(z > 0)(lambda: start(z, False, 0))
    yield
    for dist in range(1, n):
        below, above = z - dist, z + dist

        @pl.when(below >= 0)
        def _():
            land(below, True, dist)
            pl.when(z < n - 1)(lambda: start(below, True, dist))

        @pl.when(above < n)
        def _():
            land(above, False, dist)
            pl.when(z > 0)(lambda: start(above, False, dist))

        yield
    for dist in range(n):
        below, above = z - dist, z + dist
        pl.when((below >= 0) & (z < n - 1))(lambda: sent(below, True, dist))
        pl.when((above < n) & (z > 0))(lambda: sent(above, False, dist))


def finish(*steps):
    for step in steps:
        for _ in step:
            pass


def plane_gather(wire, place, buf):
    rows = buf.shape[0] // 8
    half = buf.shape[1] // 2
    left, right = pl.ds(0, half), pl.ds(half, half)
    own = rows_of(place.block(place.c, place.y), rows)
    from_x = rows_of(place.block(place.cx, place.y), rows)
    from_y = rows_of(place.block(place.c, place.yn), rows)
    across = rows_of(place.block(place.cx, place.yn), rows)

    def go(where, lanes, device):
        ref = buf.at[where, lanes] if lanes is not None else buf.at[where, :]
        item = wire.copy(ref, ref, device)
        item.start()
        return item

    x_left = go(own, left, place.over_x)
    y_right = go(own, right, place.over_y)
    x_right = go(own, right, place.over_x)
    y_left = go(own, left, place.over_y)
    waits = [go(own, None, place.core)]
    yield
    x_left.wait_recv()
    far_left = go(from_x, left, place.over_y)
    y_right.wait_recv()
    far_right = go(from_y, right, place.over_x)
    yield
    x_right.wait_recv()
    waits.append(go(from_x, None, place.core))
    y_left.wait_recv()
    waits.append(go(from_y, None, place.core))
    yield
    far_left.wait_recv()
    far_right.wait_recv()
    waits.append(go(across, None, place.core))
    for item in waits:
        item.wait_recv()


def add_into(target, lanes, rows, extra):
    count = extra.shape[0]
    step = 16

    def one(index, carry):
        here = pl.ds(pl.multiple_of(rows + index * step, step), step)
        there = rows_of(index, step)
        total = target[here, lanes].astype(jnp.float32) + extra[there, :].astype(jnp.float32)
        target[here, lanes] = total.astype(target.dtype)
        return carry

    lax.fori_loop(0, count // step, one, 0)


def plane_reduce(wire, place, part, got_core, got_one, got_two):
    rows = part.shape[0] // 8
    half = part.shape[1] // 2
    left, right = pl.ds(0, half), pl.ds(half, half)
    chips = ((place.cx, place.yn), (place.cx, place.y), (place.c, place.yn), (place.c, place.y))
    starts = [place.block(c, y) * rows for c, y in chips]
    blocks = [pl.ds(pl.multiple_of(start, rows), rows) for start in starts]
    sibling = [
        rows_of(place.block(lax.bitwise_xor(c, jnp.int32(1)), y), rows) for c, y in chips
    ]
    swaps = []
    for index in range(4):
        item = wire.copy(part.at[sibling[index], :], got_core.at[index], place.core)
        item.start()
        swaps.append(item)
    whole = pl.ds(0, 2 * half)

    def one(index, lanes, slot, device):
        item = wire.copy(part.at[blocks[index], lanes], got_one.at[slot], device)
        item.start()
        return item

    swaps[0].wait_recv()
    add_into(part, whole, starts[0], got_core.at[0])
    far_x = one(0, left, 0, place.over_x)
    far_y = one(0, right, 2, place.over_y)
    swaps[1].wait_recv()
    add_into(part, whole, starts[1], got_core.at[1])
    near_x = one(1, left, 1, place.over_x)
    swaps[2].wait_recv()
    add_into(part, whole, starts[2], got_core.at[2])
    near_y = one(2, right, 3, place.over_y)
    yield
    swaps[3].wait_recv()
    add_into(part, whole, starts[3], got_core.at[3])
    far_x.wait_recv()
    add_into(part, left, starts[2], got_one.at[0])
    last_y = wire.copy(part.at[blocks[2], left], got_two.at[0], place.over_y)
    last_y.start()
    far_y.wait_recv()
    add_into(part, right, starts[1], got_one.at[2])
    last_x = wire.copy(part.at[blocks[1], right], got_two.at[1], place.over_x)
    last_x.start()
    yield
    near_x.wait_recv()
    near_y.wait_recv()
    last_x.wait_recv()
    last_y.wait_recv()


def plane_sum(place, part, got_one, got_two, here):
    rows = part.shape[0] // 8
    half = part.shape[1] // 2
    start = place.block(place.c, place.y) * rows + here.start
    at = pl.ds(pl.multiple_of(start, here.size), here.size)

    def value(ref):
        return ref.astype(jnp.float32)

    left = value(part[at, 0:half]) + value(got_one[1, here, :]) + value(got_two[0, here, :])
    right = value(part[at, half:]) + value(got_one[3, here, :]) + value(got_two[1, here, :])
    return jnp.concatenate([left, right], axis=1)


def forward_kernel(
    n_blocks, n_dp,
    tokens, small, ids, w_query, w_key, w_value, w_out, s_gate, s_up, s_down,
    bias, cosine, sine,
    attn_in_to, query_to, keys_to, values_to, attn_to, lse_to, hidden_to, moe_in,
    heads_weight_to, out_weight_to, gate_weight, up_weight, down_weight, smalls, all_ids,
    x_seq, partial, got_core, got_one, got_two,
    attn_in, query, keys, values, attn, lse, hidden, heads_weight, out_weight, send, recv, local,
):
    place = Place(n_dp)
    wire = Wire(send, recv)
    inside = Local(local)
    z, c, y = place.z, place.c, place.y
    rows, width = tokens.shape
    seq = x_seq.shape[0]
    cols = query.shape[1]
    head_dim = cosine.shape[1]
    block = seq // n_blocks
    scale = 1.0 / math.sqrt(head_dim)
    n_ctx = 4
    share = w_query.shape[0]
    f32, low = jnp.float32, jnp.bfloat16

    others = [(dz, dc) for dz in range(n_dp) for dc in range(n_ctx) if dz or dc]
    phases = Phases()
    phases.go("entry")

    def moved(dz, dc, y_to):
        return (lax.bitwise_xor(z, jnp.int32(dz)), lax.bitwise_xor(c, jnp.int32(dc)), y_to)

    barrier(
        [moved(dz, dc, y) for dz, dc in others] + [moved(dz, 0, place.yn) for dz in range(n_dp)]
    )

    mine = z * n_ctx + c
    my_rows = rows_of(mine, share)
    group = z * 2 + y
    shared_pieces = [[], [], []]

    def shared_along_dp(index):
        for dz in (2, 3, 1, 0):
            to = lax.bitwise_xor(z, jnp.int32(dz))
            if index == 2:
                src = s_down.at[rows_of(to, s_down.shape[0] // n_dp), :]
                dst = down_weight.at[:, my_rows]
            else:
                src = (s_gate, s_up)[index].at[to]
                dst = (gate_weight, up_weight)[index].at[z, c]
            if dz == 0:
                item = inside.start(src, dst)
            else:
                item = wire.copy(src, dst, moved(dz, 0, y))
                item.start()
            shared_pieces[index].append(item)

    shared_along_dp(0)

    exchanges = []
    for dc in range(n_ctx):
        to = lax.bitwise_xor(c, jnp.int32(dc))
        lanes = pl.ds(pl.multiple_of(to * cols, cols), cols)
        pairs = [
            (weight.at[:, lanes], heads_weight.at[my_rows, pl.ds(index * cols, cols)])
            for index, weight in enumerate((w_query, w_key, w_value))
        ]
        pairs.append((w_out.at[rows_of(to, cols), :], out_weight.at[:, my_rows]))
        for src, dst in pairs:
            if dc == 0:
                exchanges.append(inside.start(src, dst))
            else:
                item = wire.copy(src, dst, moved(0, dc, y))
                item.start()
                exchanges.append(item)
    own_rows = rows_of(place.block(c, y), rows)
    here = inside.start(tokens, x_seq.at[own_rows, :])
    here.wait()
    small_copies = [inside.start(small, smalls.at[:, my_rows])]
    for dz, dc in others:
        item = wire.copy(small, smalls.at[:, my_rows], moved(dz, dc, y))
        item.start()
        small_copies.append(item)
    small_copies.append(inside.start(ids, all_ids.at[group]))
    for dz in range(n_dp):
        for y_to in (y, place.yn):
            if dz or y_to is not y:
                item = wire.copy(ids, all_ids.at[group], moved(dz, 0, y_to))
                item.start()
                small_copies.append(item)
    phases.go("exchanges")
    for item in exchanges:
        item.wait_recv()

    def from_place(slot):
        return rows_of(slot, n_ctx * share)

    weights_in = chain_gather(wire, place, lambda slot: [heads_weight.at[from_place(slot), :]])
    next(weights_in)
    phases.go("tokens")
    tokens_in = plane_gather(wire, place, x_seq)
    finish(tokens_in)
    next(weights_in)
    for item in small_copies:
        item.wait_recv()

    gain_one = smalls[9:10, :].astype(f32)
    gain_two = smalls[10:11, :].astype(f32)

    def norm_one(at):
        x_float = x_seq[at, :].astype(f32)
        rstd = lax.rsqrt(jnp.mean(x_float * x_float, axis=1, keepdims=True) + EPS)
        attn_in[at, :] = (x_float * rstd * gain_one).astype(low)

    by_rows(seq, 64, norm_one)
    def shared_set(index, context):
        if index < 2:
            return [(gate_weight, up_weight)[index].at[:, context]]
        return [
            down_weight.at[:, rows_of(dz * n_ctx + context, share)] for dz in range(n_dp)
        ]

    over = [[], [], []]
    close = []

    def shared_over_x(index):
        for item in shared_pieces[index]:
            item.wait_recv()
        for ref in shared_set(index, c):
            item = wire.copy(ref, ref, place.over_x)
            item.start()
            over[index].append(item)
        for ref in shared_set(index, c):
            item = wire.copy(ref, ref, place.core)
            item.start()
            close.append(item)

    def shared_close(index):
        for item, ref in zip(over[index], shared_set(index, place.cx)):
            item.wait_recv()
            item = wire.copy(ref, ref, place.core)
            item.start()
            close.append(item)

    shared_over_x(0)
    phases.go("heads_weights")
    finish(weights_in)
    phases.go("attention")
    out_in = chain_gather(wire, place, lambda slot: [out_weight.at[:, from_place(slot)]])
    next(out_in)

    def project(at):
        pre = dot_f32(attn_in[at, :], heads_weight[...], 1, 0)
        cos = cosine[at, :]
        sin = sine[at, :]
        for index, kept in enumerate((query, keys, values)):
            for start in range(0, cols, head_dim):
                from_lane = index * cols + start
                part = pre[:, from_lane : from_lane + head_dim]
                part = part + bias[index : index + 1, start : start + head_dim]
                if index < 2:
                    part = part * cos + pltpu.roll(part, head_dim // 2, 1) * sin
                kept[at, start : start + head_dim] = part.astype(low)

    by_rows(seq, block, project)
    next(out_in)
    for start in range(0, cols, head_dim):
        lanes = slice(start, start + head_dim)
        for step in range(n_blocks):
            at = slice(step * block, (step + 1) * block)
            seen = slice(0, (step + 1) * block)
            scores = dot_f32(query[at, lanes], keys[seen, lanes], 1, 1) * scale
            top = jnp.max(scores, axis=1, keepdims=True)
            expo = jnp.exp(scores - top)
            total = jnp.sum(expo, axis=1, keepdims=True)
            probs = (expo / total).astype(low)
            attn[at, lanes] = dot_f32(probs, values[seen, lanes], 1, 0).astype(low)
            lse[at, lanes] = jnp.broadcast_to(top + jnp.log(total), (block, head_dim))
        if start == 0:
            next(out_in)
    phases.go("out_weights")
    finish(out_in)
    shared_along_dp(1)
    shared_along_dp(2)
    phases.go("attention_out")

    def output(at):
        partial[at, :] = dot_f32(attn[at, :], out_weight[...], 1, 0).astype(low)

    by_rows(seq, block, output)
    stores = [
        inside.start(src, dst)
        for src, dst in (
            (attn_in, attn_in_to), (query, query_to), (keys, keys_to), (values, values_to),
            (attn, attn_to), (lse, lse_to), (heads_weight, heads_weight_to),
            (out_weight, out_weight_to),
        )
    ]
    phases.go("sum_in_plane")
    reduce = plane_reduce(wire, place, partial, got_core, got_one, got_two)
    next(reduce)

    next(reduce)
    finish(reduce)
    phases.go("norm_two")

    def norm_two(at):
        start = place.block(c, y) * rows + at.start
        own = pl.ds(pl.multiple_of(start, at.size), at.size)
        total = x_seq[own, :].astype(f32) + plane_sum(place, partial, got_one, got_two, at)
        hidden[at, :] = total
        rstd = lax.rsqrt(jnp.mean(total * total, axis=1, keepdims=True) + EPS)
        got_core[0, at, :] = (total * rstd * gain_two).astype(low)

    by_rows(rows, 16, norm_two)
    stores.append(inside.start(hidden, hidden_to))
    at_group = rows_of(group, rows)
    here = inside.start(got_core.at[0], moe_in.at[at_group, :])
    here.wait()

    y_recv = wire.take(n_dp)
    y_send = wire.take_send(n_dp)

    def to_y(slot):
        at = rows_of(slot * 2 + y, rows)
        return wire.copy_to(
            moe_in.at[at, :], moe_in.at[at, :], place.over_y, y_recv + slot, y_send + slot
        )

    def from_y(slot):
        at = rows_of(slot * 2 + place.yn, rows)
        return wire.copy_to(
            moe_in.at[at, :], moe_in.at[at, :], place.over_y, y_recv + slot, y_send + slot
        )

    rows_chain = chain_gather(
        wire,
        place,
        lambda slot: [moe_in.at[rows_of(slot * 2 + y, rows), :]],
        arrived=lambda slot: to_y(slot).start(),
    )
    next(rows_chain)
    to_y(z).start()
    phases.go("rows_one")
    next(rows_chain)
    phases.go("shared_one")
    shared_over_x(1)
    phases.go("rows_two")
    next(rows_chain)
    phases.go("shared_two")
    shared_over_x(2)
    phases.go("rows_three")
    finish(rows_chain)
    phases.go("shared_close")
    for index in range(3):
        shared_close(index)
    for item in close:
        item.wait_recv()
    phases.go("rows_over_y")
    for slot in range(n_dp):
        from_y(slot).wait_recv()
        to_y(slot).wait_send()
    for item in stores:
        item.wait()
    wire.drain()
    phases.go(None)


def chain_reduce(wire, place, parts):
    n = place.n_dp
    z = place.z
    count = len(parts)
    recv = wire.take(2 * n * count)
    send = wire.take_send(2 * n * count)

    def copies(target, up):
        out = []
        for index, (block, below, above) in enumerate(parts):
            slot = (2 * target + (0 if up else 1)) * count + index
            landing = below if up else above
            out.append(
                wire.copy_to(
                    block(target),
                    landing.at[target],
                    place.up if up else place.down,
                    recv + slot,
                    send + slot,
                )
            )
        return out

    def collect(target, up):
        for item, (block, below, above) in zip(copies(target, up), parts):
            item.wait_recv()
            add_block(block(target), (below if up else above).at[target])

    def pass_on(target, up):
        collect(target, up)
        for item in copies(target, up):
            item.start()

    def first(target, up):
        for item in copies(target, up):
            item.start()

    @pl.when(z == 0)
    def _():
        for target in range(n - 1, 0, -1):
            first(target, True)

    @pl.when(z == n - 1)
    def _():
        for target in range(n - 1):
            first(target, False)

    yield
    for step in range(n - 1):
        high, low = n - 1 - step, step

        @pl.when((z > 0) & (z < n // 2))
        def _():
            pl.when(z < high)(lambda: pass_on(high, True))
            pl.when(z > low)(lambda: pass_on(low, False))

        @pl.when((z >= n // 2) & (z < n - 1))
        def _():
            pl.when(z > low)(lambda: pass_on(low, False))
            pl.when(z < high)(lambda: pass_on(high, True))

        yield
    pl.when(z > 0)(lambda: collect(z, True))
    pl.when(z < n - 1)(lambda: collect(z, False))
    for target in range(n):

        @pl.when(z < target)
        def _():
            for item in copies(target, True):
                item.wait_send()

        @pl.when(z > target)
        def _():
            for item in copies(target, False):
                item.wait_send()


def add_block(target, extra):
    step = 16

    def one(index, carry):
        here = rows_of(index, step)
        total = target[here, :].astype(jnp.float32) + extra[here, :].astype(jnp.float32)
        target[here, :] = total.astype(target.dtype)
        return carry

    lax.fori_loop(0, extra.shape[0] // step, one, 0)


class Adder:
    def __init__(self, sems):
        self.sems = sems

    def run(self, buf, chunks):
        def load(index):
            first, second, _ = chunks[index]
            slot = index % 2
            items = [
                pltpu.make_async_copy(first, buf.at[0, slot], self.sems.at[3 * slot]),
                pltpu.make_async_copy(second, buf.at[1, slot], self.sems.at[3 * slot + 1]),
            ]
            for item in items:
                item.start()
            return items

        stores = [None, None]
        loads = load(0)
        for index, (_, _, target) in enumerate(chunks):
            slot = index % 2
            after = load(index + 1) if index + 1 < len(chunks) else None
            for item in loads:
                item.wait()
            loads = after
            if stores[slot] is not None:
                stores[slot].wait()
            total, first, second = buf.at[2, slot], buf.at[0, slot], buf.at[1, slot]

            def one(step, carry):
                here = rows_of(step, 16)
                value = first[here, :].astype(jnp.float32) + second[here, :].astype(jnp.float32)
                total[here, :] = value.astype(total.dtype)
                return carry

            lax.fori_loop(0, total.shape[0] // 16, one, 0)
            stores[slot] = pltpu.make_async_copy(total, target, self.sems.at[3 * slot + 2])
            stores[slot].start()
        for item in stores:
            if item is not None:
                item.wait()


def backward_kernel(
    n_blocks, n_dp,
    d_in_part, scalars, k_sgate, k_sup, k_sdown, x_sgate, x_sup, x_sdown, g_egate, g_eup, g_edown,
    hidden_in, out_grad_in, tokens_in, smalls, probs, mix,
    heads_weight_in, w_out_in, query_in, keys_in, values_in, attn_from, lse_in, attn_in_from,
    cosine_in, sine_in,
    input_grad, heads_grad, out_weight_grad, small_grad, bias_grad,
    t_sgate, t_sup, t_sdown, r_egate, r_eup, r_edown, x_egate, x_eup, x_edown,
    s_sgate, s_sup, s_sdown, k_egate, k_eup, k_edown,
    partial, got_y, got_z, got_scalars, d_hidden, side, moe_own, terms, acc,
    proj, d_attn, d_qkv, d_keys, d_values, got_core, got_one, got_two,
    g_heads, g_out, heads_below, heads_above, out_below, out_above, out_block,
    stage, landed, over_y, wide_buf, tall_buf, gate_buf, down_buf,
    hidden, out_grad, tokens, heads_weight, w_out, query, keys, values, attn, lse, attn_in,
    cosine, sine, send, recv, local, adds,
):
    place = Place(n_dp)
    wire = Wire(send, recv)
    inside = Local(local)
    adder = Adder(adds)
    z, c, y = place.z, place.c, place.y
    rows, width = tokens.shape
    seq = proj.shape[0]
    cols = query.shape[1]
    head_dim = cosine.shape[1]
    block = seq // n_blocks
    scale = 1.0 / math.sqrt(head_dim)
    n_ctx = 4
    share = width // (n_dp * n_ctx)
    n_experts = probs.shape[0]
    f32, low = jnp.float32, jnp.bfloat16
    core = lax.rem(c, 2)
    others = [(dz, dc) for dz in range(n_dp) for dc in range(n_ctx) if dz or dc]

    def moved(dz, dc, y_to):
        return (lax.bitwise_xor(z, jnp.int32(dz)), lax.bitwise_xor(c, jnp.int32(dc)), y_to)

    phases = Phases()
    phases.go("entry")
    fill = inside.start(d_in_part, partial)
    barrier(
        [moved(dz, dc, y) for dz, dc in others] + [moved(dz, 0, place.yn) for dz in range(n_dp)]
    )
    fill.wait()

    def group_rows(dz, y_of):
        return rows_of(lax.bitwise_xor(z, jnp.int32(dz)) * 2 + y_of, rows)

    order = (2, 3, 1, 0)
    y_swaps = {}
    for dz in order:
        item = wire.copy(partial.at[group_rows(dz, place.yn), :], got_y.at[dz], place.over_y)
        item.start()
        y_swaps[dz] = item
    group = z * 2 + y
    scalar_items = []
    for dz in range(n_dp):
        for y_to in (y, place.yn):
            target = lax.bitwise_xor(z, jnp.int32(dz)) * 2 + y_to
            if dz == 0 and y_to is y:
                item = inside.start(scalars.at[target], got_scalars.at[group])
            else:
                item = wire.copy(
                    scalars.at[target], got_scalars.at[group], moved(dz, 0, y_to)
                )
                item.start()
            scalar_items.append(item)

    def piece(dx, sibling):
        side_of = lax.bitwise_xor(lax.div(c, 2), jnp.int32(dx))
        return side_of * 2 + (1 - core if sibling else core)

    piece_cols = g_edown.shape[1] // n_ctx

    def routed_pieces(dx, sibling):
        index = piece(dx, sibling)
        return [g_egate.at[index], g_eup.at[index], g_edown.at[:, rows_of(index, piece_cols)]]

    routed_core = []
    for index, dst in enumerate((k_egate, k_eup, k_edown)):
        for dx in (1, 0):
            item = wire.copy(routed_pieces(dx, True)[index], dst.at[dx], place.core)
            item.start()
            routed_core.append(item)

    z_swaps = []

    def over_dp(dz):
        y_swaps[dz].wait_recv()
        target = lax.bitwise_xor(z, jnp.int32(dz)) * 2 + y
        add_into(partial, pl.ds(0, width), target * rows, got_y.at[dz])
        if dz:
            item = wire.copy(
                partial.at[rows_of(target, rows), :], got_z.at[dz - 1], moved(dz, 0, y)
            )
            item.start()
            z_swaps.append(item)

    def routed_sum(index):
        for item in routed_core[2 * index : 2 * index + 2]:
            item.wait_recv()
        kept = (k_egate, k_eup, k_edown)[index]
        total = (r_egate, r_eup, r_edown)[index]
        buf = tall_buf if index == 2 else wide_buf
        step = buf.shape[2]
        chunks = []
        for dx in (1, 0):
            mine = routed_pieces(dx, False)[index]
            for start in range(0, mine.shape[0], step):
                at = pl.ds(start, step)
                chunks.append((mine.at[at, :], kept.at[dx, at, :], total.at[dx, at, :]))
        adder.run(buf, chunks)

    def go_over_x(index, part=0, parts=1):
        total = (r_egate, r_eup, r_edown)[index]
        got = (x_egate, x_eup, x_edown)[index]
        count = got.shape[0] // parts
        at = pl.ds(part * count, count)
        item = wire.copy(total.at[1, at, :], got.at[at, :], place.over_x)
        item.start()
        return item

    def part_of(ref, dz):
        size = ref.shape[0] // n_dp
        return ref.at[pl.ds(dz * size, size), :]

    def shared_ready(index):
        buf = down_buf if index == 2 else gate_buf
        kept = (k_sgate, k_sup, k_sdown)[index]
        got = (x_sgate, x_sup, x_sdown)[index]
        ready = (s_sgate, s_sup, s_sdown)[index]
        adder.run(buf, [(part_of(kept, dz), part_of(got, dz), ready.at[dz]) for dz in range(n_dp)])

    shared_last = []

    def shared_along_dp(index):
        ready = (s_sgate, s_sup, s_sdown)[index]
        target = (t_sgate, t_sup, t_sdown)[index]
        for dz in (2, 3, 1, 0):
            to = lax.bitwise_xor(z, jnp.int32(dz))
            if dz:
                item = wire.copy(ready.at[to], target.at[z], moved(dz, 0, y))
                item.start()
            else:
                item = inside.start(ready.at[to], target.at[z])
            shared_last.append(item)

    loads = [
        inside.start(src, dst)
        for src, dst in (
            (hidden_in, hidden), (out_grad_in, out_grad), (tokens_in, tokens), (attn_from, attn),
            (w_out_in, w_out), (query_in, query), (keys_in, keys), (values_in, values),
            (lse_in, lse), (cosine_in, cosine), (sine_in, sine), (heads_weight_in, heads_weight),
            (attn_in_from, attn_in),
        )
    ]
    phases.go("routed_gate")
    routed_sum(0)
    routed_over = [go_over_x(0)]
    phases.go("over_dp_two")
    over_dp(2)
    phases.go("routed_up")
    routed_sum(1)
    routed_over.append(go_over_x(1, 0, 2))
    phases.go("over_dp_three")
    over_dp(3)
    phases.go("routed_down")
    routed_sum(2)
    phases.go("over_dp_one")
    over_dp(1)
    phases.go("shared_ready")
    shared_ready(0)
    shared_ready(1)
    phases.go("over_dp_own")
    over_dp(0)
    phases.go("shared_ready_last")
    shared_ready(2)

    phases.go("router")
    for item in scalar_items:
        item.wait_recv()
    d_rprobs = got_scalars[:, 0, :]
    probs_own = probs[...]
    d_logits = probs_own * (d_rprobs - jnp.sum(probs_own * d_rprobs, axis=0, keepdims=True))
    shared_dot = jnp.sum(got_scalars[:, 1, :], axis=0, keepdims=True)
    d_mix = shared_dot * mix[...] * (1.0 - mix[...])
    d_side = jnp.concatenate(
        [d_logits, jnp.broadcast_to(d_mix, (16 - n_experts, rows))], axis=0
    )
    row_of = lax.broadcasted_iota(jnp.int32, d_side.shape, 0)
    d_side = jnp.where(row_of <= n_experts, d_side, 0.0)
    first = d_side.astype(low)
    rest = d_side - first.astype(f32)
    second = rest.astype(low)
    third = (rest - second.astype(f32)).astype(low)
    terms[...] = jnp.concatenate([first, second, third], axis=0)
    side[...] = dot_f32(terms[...], jnp.concatenate([smalls[...]] * 3, axis=0), 0, 0)
    gain_one = smalls[n_experts + 1 : n_experts + 2, :].astype(f32)
    gain_two = smalls[n_experts + 2 : n_experts + 3, :].astype(f32)
    acc[...] = jnp.zeros_like(acc)
    phases.go("wait_sums")
    for item in z_swaps:
        item.wait_recv()
    own_plane = place.block(c, y) * rows

    def norm_two(at):
        mine = pl.ds(pl.multiple_of(group * rows + at.start, at.size), at.size)
        d_moe = side[at, :] + partial[mine, :].astype(f32)
        for dz in range(n_dp - 1):
            d_moe = d_moe + got_z[dz, at, :].astype(f32)
        total = hidden[at, :]
        rstd = lax.rsqrt(jnp.mean(total * total, axis=1, keepdims=True) + EPS)
        normed = total * rstd
        acc[0] += d_moe * normed
        d_norm = d_moe * gain_two
        back = out_grad[at, :].astype(f32) + rstd * (
            d_norm - normed * jnp.mean(d_norm * normed, axis=1, keepdims=True)
        )
        d_hidden[at, :] = back
        moe_own[at, :] = (normed * gain_two).astype(low)
        proj[pl.ds(pl.multiple_of(own_plane + at.start, at.size), at.size), :] = back.astype(low)

    phases.go("norm_two")
    for item in loads:
        item.wait()
    by_rows(rows, 16, norm_two)
    phases.go("gather_in_plane")
    proj_in = plane_gather(wire, place, proj)
    next(proj_in)
    side[0:48, :] = dot_f32(terms[...], moe_own[...], 1, 0)

    for index in range(3):
        shared_along_dp(index)
    phases.go("gather_relay")
    next(proj_in)
    phases.go("gather_close")
    next(proj_in)
    phases.go("gather_end")
    finish(proj_in)

    phases.go("attention")
    routed_over.append(go_over_x(1, 1, 2))
    by_share = n_ctx * share

    def out_weight(target):
        at = rows_of(target, by_share)
        g_out[:, at] = dot_f32(attn[...], proj[:, at], 0, 0).astype(low)

    def each(count, body):
        def one(index, carry):
            body(index)
            return carry

        lax.fori_loop(0, count, one, 0)

    each(n_dp, out_weight)
    out_chain = chain_reduce(
        wire, place, [(lambda t: g_out.at[:, rows_of(t, by_share)], out_below, out_above)]
    )
    next(out_chain)

    def project(at):
        d_attn[at, :] = dot_f32(proj[at, :], w_out[...], 1, 1).astype(low)

    by_rows(seq, block, project)

    def turn(part, at):
        return part * cosine[at, :] - pltpu.roll(part, head_dim // 2, 1) * sine[at, :]

    every = slice(0, seq)
    for start in range(0, cols, head_dim):
        lanes = slice(start, start + head_dim)
        d_keys[...] = jnp.zeros_like(d_keys)
        d_values[...] = jnp.zeros_like(d_values)
        for step in range(n_blocks):
            at = slice(step * block, (step + 1) * block)
            seen = slice(0, (step + 1) * block)
            q_here = query[at, lanes]
            k_seen = keys[seen, lanes]
            grad = d_attn[at, lanes]
            scores = dot_f32(q_here, k_seen, 1, 1) * scale
            weights = jnp.exp(scores - lse[at, start : start + 1])
            d_probs = dot_f32(grad, values[seen, lanes], 1, 1)
            delta = jnp.sum(weights * d_probs, axis=1, keepdims=True)
            d_scores = (weights * (d_probs - delta)).astype(low)
            d_query = dot_f32(d_scores, k_seen, 1, 0) * scale
            d_qkv[at, lanes] = turn(d_query, at).astype(low)
            d_keys[seen, :] += dot_f32(d_scores, q_here, 0, 0) * scale
            d_values[seen, :] += dot_f32(weights.astype(low), grad, 0, 0)
        d_qkv[:, cols + start : cols + start + head_dim] = turn(d_keys[...], every).astype(low)
        d_qkv[:, 2 * cols + start : 2 * cols + start + head_dim] = d_values[...].astype(low)

    phases.go("attention_in_grad")
    wire.drain(list(y_swaps.values()) + z_swaps)

    def output(at):
        partial[at, :] = dot_f32(d_qkv[at, :], heads_weight[...], 1, 1).astype(low)

    by_rows(seq, block, output)
    phases.go("sum_in_plane")
    reduce = plane_reduce(wire, place, partial, got_core, got_one, got_two)
    next(reduce)

    def heads_weights(target):
        at = rows_of(target, by_share)
        g_heads[at, :] = dot_f32(attn_in[:, at], d_qkv[...], 0, 0).astype(low)

    each(n_dp // 2, heads_weights)
    next(reduce)
    next(out_chain)
    each(n_dp // 2, lambda index: heads_weights(index + n_dp // 2))
    heads_chain = chain_reduce(
        wire,
        place,
        [(lambda t: g_heads.at[rows_of(t, by_share), :], heads_below, heads_above)],
    )
    next(heads_chain)
    phases.go("sum_in_plane_end")
    finish(reduce)
    routed_over.append(go_over_x(2))

    def norm_one(at):
        d_attn_in = plane_sum(place, partial, got_one, got_two, at)
        x_float = tokens[at, :].astype(f32)
        rstd = lax.rsqrt(jnp.mean(x_float * x_float, axis=1, keepdims=True) + EPS)
        normed = x_float * rstd
        acc[1] += d_attn_in * normed
        d_norm = d_attn_in * gain_one
        input_grad[at, :] = (
            d_hidden[at, :]
            + rstd * (d_norm - normed * jnp.mean(d_norm * normed, axis=1, keepdims=True))
        ).astype(low)

    phases.go("norm_one")
    by_rows(rows, 16, norm_one)

    side_grad = side[0:16, :] + side[16:32, :] + side[32:48, :]
    row_of = lax.broadcasted_iota(jnp.int32, side_grad.shape, 0)
    gain_one_grad = jnp.sum(acc[1], axis=0, keepdims=True)
    gain_two_grad = jnp.sum(acc[0], axis=0, keepdims=True)
    small_rows = jnp.where(
        row_of == n_experts + 1,
        gain_one_grad,
        jnp.where(row_of == n_experts + 2, gain_two_grad, side_grad),
    )
    bias_sums = jnp.sum(d_qkv[...].astype(f32), axis=0, keepdims=True)
    bias_rows = [
        bias_sums[:, start : start + head_dim] for start in range(0, 3 * cols, head_dim)
    ]
    bias_rows += [jnp.zeros((8 - len(bias_rows), head_dim), f32)]
    bias_rows = jnp.concatenate(bias_rows, axis=0)
    for target in range(n_dp * n_ctx):
        stage[target, 0:16, :] = small_rows[:, target * share : (target + 1) * share]
        stage[target, 16:24, :] = bias_rows
    mine = z * n_ctx + c
    small_items = [inside.start(stage.at[mine], landed.at[mine])]
    for dz, dc in others:
        target = lax.bitwise_xor(z, jnp.int32(dz)) * n_ctx + lax.bitwise_xor(c, jnp.int32(dc))
        item = wire.copy(stage.at[target], landed.at[mine], moved(dz, dc, y))
        item.start()
        small_items.append(item)
    phases.go("chains")
    finish(out_chain)
    phases.go("heads_chain")
    finish(heads_chain)
    phases.go("last")

    out_block[...] = g_out[:, rows_of(z, by_share)]
    last = []
    for dc in range(n_ctx):
        to = lax.bitwise_xor(c, jnp.int32(dc))
        pairs = [
            (
                g_heads.at[pl.ds(pl.multiple_of(z * by_share + to * share, share), share), :],
                heads_grad.at[c],
            ),
            (out_block.at[:, rows_of(to, share)], out_weight_grad.at[c]),
        ]
        for src, dst in pairs:
            if dc:
                item = wire.copy(src, dst, moved(0, dc, y))
                item.start()
            else:
                item = inside.start(src, dst)
            last.append(item)

    phases.go("small")
    for item in small_items:
        item.wait_recv()
    total = landed[0, 0:16, :]
    for source in range(1, n_dp * n_ctx):
        total = total + landed[source, 0:16, :]
    over_y[0] = total
    swap = wire.copy(over_y.at[0], over_y.at[1], place.over_y)
    swap.start()
    for context in range(n_ctx):
        sums = landed[context, 16:24, :]
        for source in range(1, n_dp):
            sums = sums + landed[source * n_ctx + context, 16:24, :]
        bias_grad[context] = sums
    swap.wait_recv()
    small_grad[...] = over_y[0] + over_y[1]
    phases.go("wait_all")
    for item in last + shared_last + routed_over:
        item.wait_recv()
    wire.drain()
    phases.go(None)


def moe_forward(
    n_dp, out_grad, moe_in, smalls, ids, s_gate_in, s_up_in, s_down_in, e_gate, e_up, e_down,
    cols, pick, s_slope, s_silu, s_hidden, e_slope, e_silu, e_hidden, rows_in, part, e_out, shared,
    dy_group,
    x, wg, wu, wd, v_slope, v_silu, v_hidden, r_slope, r_silu, r_hidden, rows, out, sh,
    s_gate, s_up, s_down, send, recv, local,
):
    place_here = Place(n_dp)
    wire = Wire(send, recv)
    z, c, y = place_here.z, place_here.c, place_here.y
    f32, low = jnp.float32, jnp.bfloat16
    inside = Local(local)
    n_experts = ids.shape[0]
    tok_rows = ids.shape[2]
    phases = Phases()
    phases.go("entry")
    mine = z * 2 + y

    def block_of(slot):
        return dy_group.at[rows_of(slot * 2 + y, tok_rows), :]

    y_recv = wire.take(n_dp)
    y_send = wire.take_send(n_dp)

    def over_y(slot):
        ref = block_of(slot)
        return wire.copy_to(ref, ref, place_here.over_y, y_recv + slot, y_send + slot)

    loads = [
        inside.start(src, dst)
        for src, dst in ((moe_in, x), (s_gate_in, s_gate), (s_up_in, s_up), (s_down_in, s_down))
    ]
    near = [(lax.bitwise_xor(z, jnp.int32(dz)), c, y) for dz in range(1, n_dp)]
    barrier(near + [place_here.over_y])
    dy_chain = chain_gather(
        wire,
        place_here,
        lambda slot: [block_of(slot)],
        arrived=lambda slot: over_y(slot).start(),
        own=[out_grad],
    )
    next(dy_chain)

    def own_over_y():
        return wire.copy_to(
            out_grad, block_of(z), place_here.over_y, y_recv + z, y_send + z
        )

    own_over_y().start()
    own = inside.start(out_grad, block_of(z))
    loads += [inside.start(src, dst) for src, dst in ((e_gate, wg), (e_up, wu), (e_down, wd))]
    hit = jnp.concatenate(
        [jnp.any(ids[s] == mine, axis=0, keepdims=True).astype(f32) for s in range(n_experts)], axis=0
    )
    upto = (
        lax.broadcasted_iota(jnp.int32, (tok_rows, tok_rows), 0)
        <= lax.broadcasted_iota(jnp.int32, (tok_rows, tok_rows), 1)
    ).astype(low)
    place = dot_f32(hit.astype(low), upto, 1, 0) - 1.0
    slots = lax.broadcasted_iota(jnp.int32, (CAP, tok_rows), 0).astype(f32)
    for s in range(n_experts):
        chosen = (hit[s : s + 1] > 0.5) & (place[s : s + 1] == slots)
        pick[s] = jnp.where(chosen, 1.0, 0.0).astype(low)
    phases.go("x_wait")
    for item in loads[:4]:
        item.wait()

    def gated(g, u):
        sigma = 1.0 / (1.0 + jnp.exp(-g))
        silu = g * sigma
        return u * (sigma * (1.0 + g * (1.0 - sigma))), silu, silu * u

    def shared_tile(at):
        here = x[at, :]
        logits = dot_f32(here, smalls[...], 1, 1)
        lane = lax.broadcasted_iota(jnp.int32, logits.shape, 1)
        routed = lane < n_experts
        top = jnp.max(jnp.where(routed, logits, -jnp.inf), axis=1, keepdims=True)
        expo = jnp.where(routed, jnp.exp(jnp.where(routed, logits, top) - top), 0.0)
        probs = expo / jnp.sum(expo, axis=1, keepdims=True)
        mix = jnp.sum(jnp.where(lane == n_experts, logits, 0.0), axis=1, keepdims=True)
        mix = 1.0 / (1.0 + jnp.exp(-mix))
        gate = jnp.sum(jnp.where(lane == mine, probs, 0.0), axis=1, keepdims=True)
        cols[at, 0:16] = jnp.where(
            routed, probs, jnp.where(lane == n_experts, mix, jnp.where(lane == n_experts + 1, gate, 0.0))
        )
        slope, silu, hidden = gated(dot_f32(here, s_gate[...], 1, 0), dot_f32(here, s_up[...], 1, 0))
        v_slope[at, :] = slope.astype(low)
        v_silu[at, :] = silu.astype(low)
        v_hidden[at, :] = hidden.astype(low)
        sh[at, :] = dot_f32(v_hidden[at, :], s_down[...], 1, 0).astype(low)

    phases.go("shared")
    by_rows(x.shape[0], 512, shared_tile)
    next(dy_chain)
    stores = [
        inside.start(src, dst)
        for src, dst in ((v_slope, s_slope), (v_silu, s_silu), (v_hidden, s_hidden), (sh, shared))
    ]

    def gather(s, carry):
        block = x[rows_of(s, tok_rows), :]
        rows[rows_of(s, CAP), :] = dot_f32(pick[s], block, 1, 0).astype(low)
        return carry

    phases.go("gather")
    lax.fori_loop(0, n_experts, gather, 0)
    stores.append(inside.start(rows, rows_in))
    phases.go("w_wait")
    for item in loads[4:]:
        item.wait()

    def routed_tile(at):
        here = rows[at, :]
        slope, silu, hidden = gated(dot_f32(here, wg[...], 1, 0), dot_f32(here, wu[...], 1, 0))
        r_slope[at, :] = slope.astype(low)
        r_silu[at, :] = silu.astype(low)
        r_hidden[at, :] = hidden.astype(low)
        out[at, :] = dot_f32(r_hidden[at, :], wd[...], 1, 0).astype(low)

    phases.go("routed")
    routed_tile(pl.ds(0, 384))
    phases.go("dy_two")
    next(dy_chain)
    phases.go("routed_end")
    routed_tile(pl.ds(384, 384))
    phases.go("dy_three")
    next(dy_chain)
    stores.append(inside.start(out, e_out))
    stores += [
        inside.start(src, dst)
        for src, dst in ((r_slope, e_slope), (r_silu, e_silu), (r_hidden, e_hidden))
    ]

    def scatter(s, carry):
        at = rows_of(s, tok_rows)
        back = dot_f32(pick[s], out[rows_of(s, CAP), :], 0, 0)
        mix = cols[at, n_experts : n_experts + 1]
        gate = cols[at, n_experts + 1 : n_experts + 2]
        x[at, :] = (gate * back + mix * sh[at, :].astype(f32)).astype(low)
        return carry

    phases.go("scatter")
    lax.fori_loop(0, n_experts, scatter, 0)
    phases.go("stores")
    stores.append(inside.start(x, part))
    for item in stores:
        item.wait()
    phases.go("over_y")
    finish(dy_chain)
    for slot in range(n_dp):
        over_y(slot).wait_recv()
        over_y(slot).wait_send()
    own.wait()
    phases.go(None)


def shared_backward(
    n_dp, dy_group, cols, pick, s_gate_in, s_up_in, s_down_in, s_slope_in, s_silu_in,
    s_hidden, e_out, shared, moe_in,
    grads_in, part, scalars, keep_gate, keep_up, keep_down, give_gate, give_up, give_down,
    dy, out, sh, tok, d_sh, rows, grads, total, x, hidden,
    g_gate, g_up, g_down, got_gate, got_up, got_down,
    s_gate, s_up, s_down, s_slope, s_silu, sums, send, recv, local, slots,
):
    f32, low = jnp.float32, jnp.bfloat16
    inside = Local(local)
    wire = Wire(send, recv)
    place = Place(n_dp)
    n_experts = pick.shape[0]
    tok_rows = pick.shape[2]
    units = s_gate.shape[1]
    lanes = grads.shape[1] // 2
    share = g_gate.shape[1]
    n_ctx = 4
    core = lax.rem(place.c, 2)
    chip = lax.div(place.c, 2)
    phases = Phases()
    phases.go("entry")

    depth = dy.shape[0]

    def fetch(index):
        slot = index % depth
        at = pl.ds(index * tok_rows, tok_rows)
        items = [
            pltpu.make_async_copy(src, dst.at[slot], slots.at[3 * slot + k])
            for k, (src, dst) in enumerate(
                (
                    (dy_group.at[at, :], dy),
                    (e_out.at[pl.ds(index * CAP, CAP), :], out),
                    (shared.at[at, :], sh),
                )
            )
        ]
        for item in items:
            item.start()
        return items

    coming = [fetch(index) for index in range(depth - 1)]
    loads = [
        inside.start(src, dst)
        for src, dst in (
            (s_down_in, s_down), (s_slope_in, s_slope), (s_silu_in, s_silu),
            (s_gate_in, s_gate), (s_up_in, s_up), (moe_in, x), (s_hidden, hidden),
        )
    ]
    barrier([place.core])
    grads[...] = jnp.zeros_like(grads)
    sums[...] = jnp.zeros_like(sums)
    for index in range(n_experts):
        slot = index % depth
        if index + depth - 1 < n_experts:
            coming.append(fetch(index + depth - 1))
        for item in coming[index]:
            item.wait()
        tok[...] = dot_f32(pick[index], out[slot], 0, 0)

        def chunk(at):
            here = pl.ds(pl.multiple_of(index * tok_rows + at.start, at.size), at.size)
            grad = dy[slot, at, :].astype(f32)
            mix = cols[here, n_experts : n_experts + 1]
            gate = cols[here, n_experts + 1 : n_experts + 2]
            d_sh[here, :] = (mix * grad).astype(low)
            sums[at, 0:1] = jnp.sum(tok[at, :] * grad, axis=1, keepdims=True)
            sums[at, 1:2] = jnp.sum(sh[slot, at, :].astype(f32) * grad, axis=1, keepdims=True)
            dy[slot, at, :] = (gate * grad).astype(low)

        by_rows(tok_rows, 32, chunk)
        scalars[index] = jnp.transpose(sums[...])[0:8, :]
        rows[pl.ds(index * CAP, CAP), :] = dot_f32(pick[index], dy[slot], 1, 0).astype(low)
    stores = [inside.start(rows, grads_in)]

    def shared_tile(at):
        d_hidden = dot_f32(d_sh[at, :], s_down[...], 1, 1)
        d_gate = (d_hidden * s_slope[at, :].astype(f32)).astype(low)
        d_up = (d_hidden * s_silu[at, :].astype(f32)).astype(low)
        grads[at, 0:units] = d_gate
        grads[at, lanes : lanes + units] = d_up
        total[at, :] = (dot_f32(d_gate, s_gate[...], 1, 1) + dot_f32(d_up, s_up[...], 1, 1)).astype(low)

    for item in loads[:5]:
        item.wait()
    phases.go("shared")
    by_rows(d_sh.shape[0], 512, shared_tile)
    stores.append(inside.start(total, part))
    for item in loads[5:]:
        item.wait()
    phases.go("in_grads")

    def block_index(dx, dz, sibling):
        side = lax.bitwise_xor(chip, jnp.int32(dx)) * 2
        return dz * n_ctx + side + (1 - core if sibling else core)

    sent = {}

    def to_sibling(dz, mats):
        for dx in (1, 0):
            for grad, got in mats:
                item = wire.copy(grad.at[block_index(dx, dz, True)], got.at[dx, dz], place.core)
                item.start()
                sent.setdefault(dz, []).append(item)

    step = n_ctx * share
    for dz in range(n_dp):
        product = dot_f32(x[:, dz * step : (dz + 1) * step], grads[...], 0, 0)
        for k in range(n_ctx):
            here = slice(k * share, (k + 1) * share)
            g_gate[dz * n_ctx + k] = product[here, 0:units].astype(low)
            g_up[dz * n_ctx + k] = product[here, lanes : lanes + units].astype(low)
        to_sibling(dz, ((g_gate, got_gate), (g_up, got_up)))
    phases.go("down_grads")
    down = {}
    for dz in range(n_dp):
        product = dot_f32(hidden[...], d_sh[:, dz * step : (dz + 1) * step], 0, 0)
        for k in range(n_ctx):
            g_down[dz * n_ctx + k] = product[:, k * share : (k + 1) * share].astype(low)
        for dx in (1, 0):
            item = wire.copy(g_down.at[block_index(dx, dz, True)], got_down.at[dx, dz], place.core)
            item.start()
            down.setdefault(dz, []).append(item)
    phases.go("sums")

    def collect(dx, dz, grad, got, out_ref):
        mine = block_index(dx, dz, False)
        add_block(grad.at[mine], got.at[dx, dz])
        size = grad.shape[1]
        stores.append(inside.start(grad.at[mine], out_ref.at[pl.ds(dz * size, size), :]))

    for dz in range(n_dp):
        for item in sent[dz]:
            item.wait_recv()
        for dx, outs in ((1, (give_gate, give_up)), (0, (keep_gate, keep_up))):
            for grad, got, out_ref in zip((g_gate, g_up), (got_gate, got_up), outs):
                collect(dx, dz, grad, got, out_ref)
    for dz in range(n_dp):
        for item in down[dz]:
            item.wait_recv()
        for dx, out_ref in ((1, give_down), (0, keep_down)):
            collect(dx, dz, g_down, got_down, out_ref)
    phases.go("stores")
    for item in stores:
        item.wait()
    wire.drain()
    phases.go(None)


def routed_backward(
    grads_in, rows_in, e_gate, e_up, e_down, slope_in, silu_in, hidden_in, pick, shared_part,
    part, o_gate, o_up, o_down,
    wg, wu, wd, grads, rows, slope, silu, hidden, d_hid, d_in, total, buf_gate, buf_up, buf_down,
    local, stores,
):
    f32, low = jnp.float32, jnp.bfloat16
    inside = Local(local)
    n_experts = pick.shape[0]
    tok_rows = pick.shape[2]
    units = wg.shape[1]
    phases = Phases()
    phases.go("entry")
    loads = [
        inside.start(src, dst)
        for src, dst in (
            (grads_in, grads), (e_down, wd), (slope_in, slope), (silu_in, silu),
            (e_gate, wg), (e_up, wu), (shared_part, total), (rows_in, rows), (hidden_in, hidden),
        )
    ]
    for item in loads[:4]:
        item.wait()
    phases.go("routed")
    half = grads.shape[0] // 2

    def routed_tile(at, wait):
        d_hidden = dot_f32(grads[at, :], wd[...], 1, 1)
        d_gate = (d_hidden * slope[at, :].astype(f32)).astype(low)
        d_up = (d_hidden * silu[at, :].astype(f32)).astype(low)
        d_hid[at, 0:units] = d_gate
        d_hid[at, units : 2 * units] = d_up
        for item in wait:
            item.wait()
        d_in[at, :] = (dot_f32(d_gate, wg[...], 1, 1) + dot_f32(d_up, wu[...], 1, 1)).astype(low)

    routed_tile(pl.ds(0, half), loads[4:6])
    routed_tile(pl.ds(half, half), [])
    for item in loads[6:]:
        item.wait()
    phases.go("to_tokens")

    def to_tokens(s, carry):
        at = rows_of(s, tok_rows)
        back = dot_f32(pick[s], d_in[rows_of(s, CAP), :], 0, 0)
        total[at, :] = (back + total[at, :].astype(f32)).astype(low)
        return carry

    lax.fori_loop(0, n_experts, to_tokens, 0)
    done = inside.start(total, part)
    phases.go("in_grads")

    def products(first, steps, size, outs, product):
        def copy(index, k):
            slot = lax.rem(index, 2)
            buf, target = outs[k]
            return pltpu.make_async_copy(buf.at[slot], target(index), stores.at[slot, first + k])

        def one(index, carry):
            for k in range(len(outs)):

                @pl.when(index >= 2)
                def _():
                    copy(index - 2, k).wait()

            value = product(rows_of(index, size))
            for k, (buf, _) in enumerate(outs):
                width = buf.shape[2]
                buf[lax.rem(index, 2)] = value[:, k * width : (k + 1) * width].astype(low)
                copy(index, k).start()
            return carry

        lax.fori_loop(0, steps, one, 0)
        for k in range(len(outs)):
            for last in (steps - 2, steps - 1):
                copy(jnp.int32(last), k).wait()

    tall = buf_gate.shape[1]
    products(
        0,
        rows.shape[1] // tall,
        tall,
        [
            (buf_gate, lambda index: o_gate.at[rows_of(index, tall), :]),
            (buf_up, lambda index: o_up.at[rows_of(index, tall), :]),
        ],
        lambda at: dot_f32(rows[:, at], d_hid[...], 0, 0),
    )
    phases.go("down_grads")
    wide = buf_down.shape[2]
    products(
        2,
        grads.shape[1] // wide,
        wide,
        [(buf_down, lambda index: o_down.at[:, rows_of(index, wide)])],
        lambda at: dot_f32(hidden[...], grads[:, at], 0, 0),
    )
    phases.go("stores")
    done.wait()
    phases.go(None)


def finish_grads(n_ctx, *refs):
    (
        t_gate, t_up, t_down, own_gate, own_up, own_down, far_gate, far_up, far_down, heads, out_weight,
        o_sgate, o_sup, o_sdown, o_egate, o_eup, o_edown, o_query, o_key, o_value, o_out,
    ) = refs
    f32 = jnp.float32
    n_dp, share, units = t_gate.shape
    for source, target in ((t_gate, o_sgate), (t_up, o_sup)):
        target[...] = jnp.concatenate([source[k].astype(f32) for k in range(n_dp)], axis=1)
    for k in range(n_dp):
        o_sdown[k * units : (k + 1) * units, :] = t_down[k].astype(f32)
    for own, far, target in (
        (own_gate, far_gate, o_egate), (own_up, far_up, o_eup), (own_down, far_down, o_edown),
    ):

        def add(at):
            target[at, :] = own[at, :].astype(f32) + far[at, :].astype(f32)

        by_rows(target.shape[0], 32, add)
    cols = heads.shape[2] // 3
    for k, target in enumerate((o_query, o_key, o_value)):
        for c in range(n_ctx):
            target[:, c * cols : (c + 1) * cols] = heads[c, :, k * cols : (k + 1) * cols].astype(f32)
    for c in range(n_ctx):
        o_out[c * cols : (c + 1) * cols, :] = out_weight[c].astype(f32)


def whole_tables(seq_len, head_dim):
    half = head_dim // 2
    freq = np.float32(THETA) ** (-(2.0 * np.arange(half, dtype=np.float32)) / np.float32(head_dim))
    angle = np.arange(seq_len, dtype=np.float32)[:, None] * freq.astype(np.float32)[None, :]
    cosine, sine = np.cos(angle), np.sin(angle)
    return (
        jnp.asarray(np.concatenate([cosine, cosine], axis=1), jnp.float32),
        jnp.asarray(np.concatenate([-sine, sine], axis=1), jnp.float32),
    )


def tokens_plan(
    tokens,
    out_grad,
    expert_ids,
    norm1_gain,
    w_query,
    w_key,
    w_value,
    query_bias_heads,
    bias_key,
    bias_value,
    w_out,
    norm2_gain,
    w_router,
    shared_mix,
    shared_in_gate,
    shared_in_up,
    shared_down,
    expert_gate,
    expert_up,
    expert_down,
):
    low = jnp.bfloat16
    f32 = jnp.float32
    tok_rows, width = tokens.shape
    n_dp, n_ctx, n_half = (lax.axis_size(name) for name in (DP, CONTEXT, EXPERT))
    dp, ctx, half = (lax.axis_index(name) for name in (DP, CONTEXT, EXPERT))
    half_heads, head_dim = query_bias_heads.shape
    heads = half_heads // n_ctx
    cols = heads * head_dim
    seq_len = tok_rows * n_ctx * n_half
    n_blocks = seq_len // BLOCK
    n_experts = w_router.shape[1]
    n_group = n_dp * n_half
    my_expert = dp * n_half + half

    def group_out(rows):
        return lax.psum_scatter(rows, (DP, EXPERT), scatter_dimension=0, tiled=True)

    small = jnp.concatenate(
        [w_router.T, shared_mix[None], norm1_gain[None], norm2_gain[None]], axis=0
    )
    small = jnp.pad(small, ((0, 16 - small.shape[0]), (0, 0)))
    ids = jnp.pad(expert_ids.T, ((0, 8 - expert_ids.shape[1]), (0, 0)), constant_values=-1)
    hidden_units = shared_in_gate.shape[1] // n_dp

    def by_dp(weight):
        return weight.reshape(weight.shape[0], n_dp, hidden_units).transpose(1, 0, 2)

    biases = jnp.stack([query_bias_heads, bias_key, bias_value]).astype(f32)
    biases = lax.dynamic_slice_in_dim(biases, ctx * heads, heads, 1).reshape(3, cols)
    cosine, sine = whole_tables(seq_len, head_dim)
    vmem = pl.BlockSpec(memory_space=pltpu.VMEM)
    anywhere = pl.BlockSpec(memory_space=pl.ANY)
    share = w_query.shape[0]
    half_width = width // 2
    (
        attn_in, query, keys, values, attn, lse, hidden_own, moe_in,
        heads_weight, wo, sg, su, sd, small, ids_group,
    ) = pl.pallas_call(
        lambda *refs: forward_kernel(n_blocks, n_dp, *refs),
        out_shape=[
            like((seq_len, width), low),
            like((seq_len, cols), low),
            like((seq_len, cols), low),
            like((seq_len, cols), low),
            like((seq_len, cols), low),
            like((seq_len, cols), f32),
            like((tok_rows, width), f32),
            like((n_group * tok_rows, width), low),
            like((width, 3 * cols), low),
            like((cols, width), low),
            like((n_dp, n_ctx, share, hidden_units), low),
            like((n_dp, n_ctx, share, hidden_units), low),
            like((hidden_units, width), low),
            like((16, width), low),
            like((n_group, 8, tok_rows), jnp.int32),
        ],
        in_specs=[anywhere] * 10 + [vmem] * 3,
        out_specs=[anywhere] * 13 + [vmem, anywhere],
        scratch_shapes=[
            pltpu.VMEM((seq_len, width), low),
            pltpu.VMEM((seq_len, width), low),
            pltpu.VMEM((4, tok_rows, width), low),
            pltpu.VMEM((4, tok_rows, half_width), low),
            pltpu.VMEM((2, tok_rows, half_width), low),
            pltpu.VMEM((seq_len, width), low),
            pltpu.VMEM((seq_len, cols), low),
            pltpu.VMEM((seq_len, cols), low),
            pltpu.VMEM((seq_len, cols), low),
            pltpu.VMEM((seq_len, cols), low),
            pltpu.VMEM((seq_len, cols), f32),
            pltpu.VMEM((tok_rows, width), f32),
            pltpu.VMEM((width, 3 * cols), low),
            pltpu.VMEM((cols, width), low),
            pltpu.SemaphoreType.DMA((144,)),
            pltpu.SemaphoreType.DMA((144,)),
            pltpu.SemaphoreType.DMA((32,)),
        ],
        name="forward",
        compiler_params=pltpu.CompilerParams(
            collective_id=1, has_side_effects=True, vmem_limit_bytes=60 * 2**20
        ),
    )(
        tokens, small, ids, w_query, w_key, w_value, w_out,
        by_dp(shared_in_gate), by_dp(shared_in_up), shared_down, biases, cosine, sine,
    )
    sg, su = sg.reshape(width, hidden_units), su.reshape(width, hidden_units)
    units = expert_gate.shape[2]
    s_weights = [
        pltpu.VMEM((width, hidden_units), low),
        pltpu.VMEM((width, hidden_units), low),
        pltpu.VMEM((hidden_units, width), low),
    ]
    gate_weight, up_weight, down_weight = expert_gate[0], expert_up[0], expert_down[0]
    slots = n_group * CAP
    group_rows = n_group * tok_rows
    (
        token_cols, pick, s_slope, s_silu, s_hidden, e_slope, e_silu, e_hidden, rows_in,
        moe_part, e_out, shared, dy_group,
    ) = pl.pallas_call(
        lambda *refs: moe_forward(n_dp, *refs),
        out_shape=[
            like((group_rows, 128), f32),
            like((n_group, CAP, tok_rows), low),
        ]
        + [like((group_rows, hidden_units), low)] * 3
        + [like((slots, units), low)] * 3
        + [
            like((slots, width), low),
            like((group_rows, width), low),
            like((slots, width), low),
            like((group_rows, width), low),
            like((group_rows, width), low),
        ],
        in_specs=[anywhere] * 2 + [vmem] * 2 + [anywhere] * 6,
        out_specs=[vmem] * 2 + [anywhere] * 11,
        scratch_shapes=[
            pltpu.VMEM((group_rows, width), low),
            pltpu.VMEM((width, units), low),
            pltpu.VMEM((width, units), low),
            pltpu.VMEM((units, width), low),
        ]
        + [pltpu.VMEM((group_rows, hidden_units), low)] * 3
        + [pltpu.VMEM((slots, units), low)] * 3
        + [pltpu.VMEM((slots, width), low)] * 2
        + [pltpu.VMEM((group_rows, width), low)]
        + s_weights
        + [pltpu.SemaphoreType.DMA((16,))] * 2
        + [pltpu.SemaphoreType.DMA((24,))],
        name="moe_forward",
        compiler_params=pltpu.CompilerParams(
            collective_id=3, has_side_effects=True, vmem_limit_bytes=63 * 2**20
        ),
        cost_estimate=pl.CostEstimate(
            flops=6 * width * (group_rows * hidden_units + slots * units),
            bytes_accessed=2 * (9 * width * units + 4 * group_rows * width),
            transcendentals=0,
        ),
    )(out_grad, moe_in, small, ids_group, sg, su, sd, gate_weight, up_weight, down_weight)
    lanes = -(-hidden_units // 128) * 128
    block_kinds = [(n_dp, share, hidden_units)] * 2 + [(n_dp, hidden_units, share)]
    shared_all = [(n_dp * n_ctx, share, hidden_units)] * 2 + [(n_dp * n_ctx, hidden_units, share)]
    results = pl.pallas_call(
        lambda *refs: shared_backward(n_dp, *refs),
        out_shape=[
            like((slots, width), low),
            like((group_rows, width), low),
            like((n_group, 8, tok_rows), f32),
        ]
        + [like((kind[0] * kind[1], kind[2]), low) for kind in block_kinds] * 2,
        in_specs=[anywhere] + [vmem] * 2 + [anywhere] * 9,
        out_specs=[anywhere] * 2 + [vmem] + [anywhere] * 6,
        scratch_shapes=[
            pltpu.VMEM((4, tok_rows, width), low),
            pltpu.VMEM((4, CAP, width), low),
            pltpu.VMEM((4, tok_rows, width), low),
            pltpu.VMEM((tok_rows, width), f32),
            pltpu.VMEM((group_rows, width), low),
            pltpu.VMEM((slots, width), low),
            pltpu.VMEM((group_rows, 2 * lanes), low),
            pltpu.VMEM((group_rows, width), low),
            pltpu.VMEM((group_rows, width), low),
            pltpu.VMEM((group_rows, hidden_units), low),
        ]
        + [pltpu.VMEM(kind, low) for kind in shared_all]
        + [pltpu.VMEM((2, *kind), low) for kind in block_kinds]
        + s_weights
        + [pltpu.VMEM((group_rows, hidden_units), low)] * 2
        + [pltpu.VMEM((tok_rows, 128), f32)]
        + [pltpu.SemaphoreType.DMA((32,))] * 2
        + [pltpu.SemaphoreType.DMA((48,)), pltpu.SemaphoreType.DMA((12,))],
        name="shared_backward",
        compiler_params=pltpu.CompilerParams(
            collective_id=4, has_side_effects=True, vmem_limit_bytes=63 * 2**20
        ),
        cost_estimate=pl.CostEstimate(
            flops=12 * width * group_rows * hidden_units,
            bytes_accessed=2 * (9 * width * hidden_units + 8 * group_rows * width),
            transcendentals=0,
        ),
    )(
        dy_group, token_cols, pick, sg, su, sd, s_slope, s_silu, s_hidden, e_out, shared, moe_in,
    )
    grads_in, shared_part, scalars = results[:3]
    keep = results[3:6]
    over_x = [(index, index ^ 2) for index in range(n_ctx)]
    got = [lax.ppermute(item, CONTEXT, over_x) for item in results[6:9]]
    quarter = width // n_ctx
    d_in_part, g_egate, g_eup, g_edown = pl.pallas_call(
        routed_backward,
        out_shape=[
            like((group_rows, width), low),
            like((width, units), low),
            like((width, units), low),
            like((units, width), low),
        ],
        in_specs=[anywhere] * 8 + [vmem] + [anywhere],
        out_specs=[anywhere] * 4,
        scratch_shapes=[
            pltpu.VMEM((width, units), low),
            pltpu.VMEM((width, units), low),
            pltpu.VMEM((units, width), low),
            pltpu.VMEM((slots, width), low),
            pltpu.VMEM((slots, width), low),
            pltpu.VMEM((slots, units), low),
            pltpu.VMEM((slots, units), low),
            pltpu.VMEM((slots, units), low),
            pltpu.VMEM((slots, 2 * units), low),
            pltpu.VMEM((slots, width), low),
            pltpu.VMEM((group_rows, width), low),
            pltpu.VMEM((2, quarter // 2, units), low),
            pltpu.VMEM((2, quarter // 2, units), low),
            pltpu.VMEM((2, units, quarter), low),
            pltpu.SemaphoreType.DMA((16,)),
            pltpu.SemaphoreType.DMA((2, 3)),
        ],
        name="routed_backward",
        compiler_params=pltpu.CompilerParams(vmem_limit_bytes=63 * 2**20),
        cost_estimate=pl.CostEstimate(
            flops=12 * width * slots * units,
            bytes_accessed=2 * (12 * width * units + 4 * group_rows * width),
            transcendentals=0,
        ),
    )(
        grads_in, rows_in, gate_weight, up_weight, down_weight, e_slope, e_silu, e_hidden, pick,
        shared_part,
    )
    g_egate = g_egate.reshape(n_ctx, quarter, units)
    g_eup = g_eup.reshape(n_ctx, quarter, units)
    moe_sum = group_out(moe_part).astype(f32)
    mixed = (hidden_own + moe_sum).astype(low)

    own_cols = lax.dynamic_slice_in_dim(token_cols, my_expert * tok_rows, tok_rows, 0)
    probs_own = own_cols[:, :n_experts].T
    mix_own = own_cols[:, n_experts][None]
    by_share = n_ctx * share
    e_wide = (width // n_ctx, units)
    e_tall = (units, width // n_ctx)
    s_wide = (share, hidden_units)
    s_tall = (hidden_units, share)
    s_kinds = (s_wide, s_wide, s_tall)
    e_kinds = (e_wide, e_wide, e_tall)
    results = pl.pallas_call(
        lambda *refs: backward_kernel(n_blocks, n_dp, *refs),
        out_shape=[
            like((tok_rows, width), low),
            like((n_ctx, share, 3 * cols), low),
            like((n_ctx, cols, share), low),
            like((16, share), f32),
            like((n_ctx, 8, head_dim), f32),
        ]
        + [like((n_dp, *kind), low) for kind in s_kinds]
        + [like((2, *kind), low) for kind in e_kinds]
        + [like(kind, low) for kind in e_kinds]
        + [like((n_dp, *kind), low) for kind in s_kinds]
        + [like((2, *kind), low) for kind in e_kinds],
        in_specs=[anywhere] * 14 + [vmem] * 3 + [anywhere] * 10,
        out_specs=[vmem] + [anywhere] * 2 + [vmem] * 2 + [anywhere] * 15,
        scratch_shapes=[
            pltpu.VMEM((seq_len, width), low),
            pltpu.VMEM((n_dp, tok_rows, width), low),
            pltpu.VMEM((n_dp - 1, tok_rows, width), low),
            pltpu.VMEM((n_group, 8, tok_rows), f32),
            pltpu.VMEM((tok_rows, width), f32),
            pltpu.VMEM((tok_rows, width), f32),
            pltpu.VMEM((tok_rows, width), low),
            pltpu.VMEM((48, tok_rows), low),
            pltpu.VMEM((2, 16, width), f32),
            pltpu.VMEM((seq_len, width), low),
            pltpu.VMEM((seq_len, cols), low),
            pltpu.VMEM((seq_len, 3 * cols), low),
            pltpu.VMEM((seq_len, head_dim), f32),
            pltpu.VMEM((seq_len, head_dim), f32),
            pltpu.VMEM((4, tok_rows, width), low),
            pltpu.VMEM((4, tok_rows, half_width), low),
            pltpu.VMEM((2, tok_rows, half_width), low),
            pltpu.VMEM((width, 3 * cols), low),
            pltpu.VMEM((cols, width), low),
            pltpu.VMEM((n_dp, by_share, 3 * cols), low),
            pltpu.VMEM((n_dp, by_share, 3 * cols), low),
            pltpu.VMEM((n_dp, cols, by_share), low),
            pltpu.VMEM((n_dp, cols, by_share), low),
            pltpu.VMEM((cols, by_share), low),
            pltpu.VMEM((n_dp * n_ctx, 24, share), f32),
            pltpu.VMEM((n_dp * n_ctx, 24, share), f32),
            pltpu.VMEM((2, 16, share), f32),
            pltpu.VMEM((3, 2, 128, units), low),
            pltpu.VMEM((3, 2, units // 4, width // n_ctx), low),
            pltpu.VMEM((3, 2, *s_wide), low),
            pltpu.VMEM((3, 2, *s_tall), low),
            pltpu.VMEM((tok_rows, width), f32),
            pltpu.VMEM((tok_rows, width), low),
            pltpu.VMEM((tok_rows, width), low),
            pltpu.VMEM((width, 3 * cols), low),
            pltpu.VMEM((cols, width), low),
            pltpu.VMEM((seq_len, cols), low),
            pltpu.VMEM((seq_len, cols), low),
            pltpu.VMEM((seq_len, cols), low),
            pltpu.VMEM((seq_len, cols), low),
            pltpu.VMEM((seq_len, cols), f32),
            pltpu.VMEM((seq_len, width), low),
            pltpu.VMEM((seq_len, head_dim), f32),
            pltpu.VMEM((seq_len, head_dim), f32),
            pltpu.SemaphoreType.DMA((160,)),
            pltpu.SemaphoreType.DMA((160,)),
            pltpu.SemaphoreType.DMA((32,)),
            pltpu.SemaphoreType.DMA((6,)),
        ],
        name="backward",
        compiler_params=pltpu.CompilerParams(
            collective_id=2, has_side_effects=True, vmem_limit_bytes=63 * 2**20
        ),
    )(
        d_in_part, scalars, *keep, *got, g_egate, g_eup, g_edown,
        hidden_own, out_grad, tokens, small, probs_own, mix_own,
        heads_weight, wo, query, keys, values, attn, lse, attn_in, cosine, sine,
    )
    input_grad, heads_grad, out_weight_grad, small_grad, bias_grad = results[:5]
    s_done, e_own, e_other = results[5:8], results[8:11], results[11:14]
    finished = pl.pallas_call(
        lambda *refs: finish_grads(n_ctx, *refs),
        out_shape=[
            like((share, n_dp * hidden_units), f32),
            like((share, n_dp * hidden_units), f32),
            like((n_dp * hidden_units, share), f32),
            like(e_wide, f32),
            like(e_wide, f32),
            like(e_tall, f32),
            like((share, n_ctx * cols), f32),
            like((share, n_ctx * cols), f32),
            like((share, n_ctx * cols), f32),
            like((n_ctx * cols, share), f32),
        ],
        grid=(1,),
        in_specs=[pl.BlockSpec((n_dp, *kind), lambda i: (0, 0, 0)) for kind in s_kinds]
        + [pl.BlockSpec((None, *kind), lambda i: (0, 0, 0)) for kind in e_kinds]
        + [pl.BlockSpec(kind, lambda i: (0, 0)) for kind in e_kinds]
        + [
            pl.BlockSpec(heads_grad.shape, lambda i: (0, 0, 0)),
            pl.BlockSpec(out_weight_grad.shape, lambda i: (0, 0, 0)),
        ],
        out_specs=[
            pl.BlockSpec((share, n_dp * hidden_units), lambda i: (0, 0)),
            pl.BlockSpec((share, n_dp * hidden_units), lambda i: (0, 0)),
            pl.BlockSpec((n_dp * hidden_units, share), lambda i: (0, 0)),
            pl.BlockSpec(e_wide, lambda i: (0, 0)),
            pl.BlockSpec(e_wide, lambda i: (0, 0)),
            pl.BlockSpec(e_tall, lambda i: (0, 0)),
            pl.BlockSpec((share, n_ctx * cols), lambda i: (0, 0)),
            pl.BlockSpec((share, n_ctx * cols), lambda i: (0, 0)),
            pl.BlockSpec((share, n_ctx * cols), lambda i: (0, 0)),
            pl.BlockSpec((n_ctx * cols, share), lambda i: (0, 0)),
        ],
        name="finish_grads",
        compiler_params=pltpu.CompilerParams(vmem_limit_bytes=63 * 2**20),
    )(*s_done, *e_own, *e_other, heads_grad, out_weight_grad)
    grad_sgate, grad_sup, grad_sdown = finished[:3]
    routed = [item[None] for item in finished[3:6]]
    heads_grad = finished[6:9]
    grad_out = finished[9]
    bias_sum = bias_grad[:, : 3 * heads].reshape(n_ctx, 3, heads, head_dim)
    bias_sum = bias_sum.transpose(1, 0, 2, 3).reshape(3, half_heads, head_dim)
    bias_share = head_dim // (n_dp * n_ctx)
    bias_sum = lax.dynamic_slice_in_dim(bias_sum, (dp * n_ctx + ctx) * bias_share, bias_share, 2)
    return (
        mixed,
        input_grad,
        small_grad[n_experts + 1],
        heads_grad[0],
        heads_grad[1],
        heads_grad[2],
        bias_sum[0],
        bias_sum[1],
        bias_sum[2],
        grad_out,
        small_grad[n_experts + 2],
        small_grad[:n_experts].T,
        small_grad[n_experts],
        grad_sgate,
        grad_sup,
        grad_sdown,
        routed[0],
        routed[1],
        routed[2],
    )


def on_device(*arrays):
    sizes = [lax.axis_size(name) for name in (DP, CONTEXT, EXPERT)]
    if sizes == [4, 4, 2] and arrays[7].shape[0] % sizes[1] == 0:
        return tokens_plan(*arrays)
    return weights_plan(*arrays)


def solution(mesh):
    placed = (
        P((DP, CONTEXT, EXPERT), None),
        P((DP, CONTEXT, EXPERT), None),
        P((DP, CONTEXT, EXPERT), None),
        P((DP, CONTEXT)),
        P((DP, CONTEXT), EXPERT),
        P((DP, CONTEXT), EXPERT),
        P((DP, CONTEXT), EXPERT),
        P(EXPERT, None),
        P(EXPERT, None),
        P(EXPERT, None),
        P(EXPERT, (DP, CONTEXT)),
        P((DP, CONTEXT)),
        P((DP, CONTEXT), None),
        P((DP, CONTEXT)),
        P((DP, CONTEXT), EXPERT),
        P((DP, CONTEXT), EXPERT),
        P(EXPERT, (DP, CONTEXT)),
        P((DP, EXPERT), None, None),
        P((DP, EXPERT), None, None),
        P((DP, EXPERT), None, None),
    )
    return jax.shard_map(
        on_device,
        mesh=mesh,
        in_specs=placed,
        out_specs=(
            P((DP, CONTEXT, EXPERT), None),
            P((DP, CONTEXT, EXPERT), None),
            P((DP, CONTEXT)),
            P((DP, CONTEXT), EXPERT),
            P((DP, CONTEXT), EXPERT),
            P((DP, CONTEXT), EXPERT),
            P(EXPERT, (DP, CONTEXT)),
            P(EXPERT, (DP, CONTEXT)),
            P(EXPERT, (DP, CONTEXT)),
            P(EXPERT, (DP, CONTEXT)),
            P((DP, CONTEXT)),
            P((DP, CONTEXT), None),
            P((DP, CONTEXT)),
            P((DP, CONTEXT), EXPERT),
            P((DP, CONTEXT), EXPERT),
            P(EXPERT, (DP, CONTEXT)),
            P((DP, EXPERT), CONTEXT, None),
            P((DP, EXPERT), CONTEXT, None),
            P((DP, EXPERT), None, CONTEXT),
        ),
        check_vma=False,
    )
```

```python
import math

import jax
import jax.numpy as jnp
import numpy as np
from jax import lax
from jax.experimental import pallas as pl
from jax.experimental.pallas import tpu as pltpu
from jax.sharding import PartitionSpec as P

DP, CONTEXT, EXPERT = "dp", "context", "expert"
BLOCK = 256
CAP = 96


EPS = 1e-06
THETA = 1000000.0
HIGH = lax.Precision.HIGHEST


def rope_tables(positions, head_dim):
    half = head_dim // 2
    freq = THETA ** (-(2.0 * jnp.arange(half, dtype=jnp.float32)) / head_dim)
    angle = positions.astype(jnp.float32)[:, None] * freq[None, :]
    return (jnp.cos(angle)[:, None, :], jnp.sin(angle)[:, None, :])


def rotate(values, cosine, sine):
    half = values.shape[-1] // 2
    first = values[..., :half]
    second = values[..., half:]
    return jnp.concatenate(
        [first * cosine - second * sine, second * cosine + first * sine], axis=-1
    )


def rotate_back(values, cosine, sine):
    half = values.shape[-1] // 2
    first = values[..., :half]
    second = values[..., half:]
    return jnp.concatenate(
        [first * cosine + second * sine, second * cosine - first * sine], axis=-1
    )


def to_groups(matrix, groups, group_size, head_dim):
    return matrix.reshape(matrix.shape[0], groups, group_size, head_dim).transpose(1, 2, 0, 3)


def from_groups(stacked):
    return stacked.transpose(2, 0, 1, 3).reshape(stacked.shape[2], -1)


def silu_slope(values):
    sigma = jax.nn.sigmoid(values)
    return sigma * (1.0 + values * (1.0 - sigma))


def left_operand(left, right):
    return jnp.dot(left.T, right, preferred_element_type=jnp.float32)


def mat_right(left, right):
    return jnp.dot(left, right.T, preferred_element_type=jnp.float32)


def weights_plan(
    tokens,
    out_grad,
    expert_ids,
    norm1_gain,
    w_query,
    w_key,
    w_value,
    query_bias_heads,
    bias_key,
    bias_value,
    w_out,
    norm2_gain,
    w_router,
    shared_mix,
    shared_in_gate,
    shared_in_up,
    shared_down,
    expert_gate,
    expert_up,
    expert_down,
):
    tok_rows = tokens.shape[0]
    width = tokens.shape[1]
    my_half = lax.axis_index(EXPERT)
    my_piece = lax.axis_index(CONTEXT)
    n_pieces = lax.axis_size(CONTEXT)
    local_heads = query_bias_heads.shape[0]
    head_dim = query_bias_heads.shape[1]
    group_size = 2
    groups = local_heads // group_size
    score_scale = 1.0 / math.sqrt(head_dim)
    (
        full_query,
        full_key,
        full_value,
        full_out,
        full_sgate,
        full_sup,
        full_sdown,
        full_router,
        full_mix,
        full_gain_one,
        full_gain_two,
    ) = (
        lax.all_gather(w_query, (DP, CONTEXT), axis=0, tiled=True),
        lax.all_gather(w_key, (DP, CONTEXT), axis=0, tiled=True),
        lax.all_gather(w_value, (DP, CONTEXT), axis=0, tiled=True),
        lax.all_gather(w_out, (DP, CONTEXT), axis=1, tiled=True),
        lax.all_gather(shared_in_gate, (DP, CONTEXT), axis=0, tiled=True),
        lax.all_gather(shared_in_up, (DP, CONTEXT), axis=0, tiled=True),
        lax.all_gather(shared_down, (DP, CONTEXT), axis=1, tiled=True),
        lax.all_gather(w_router, (DP, CONTEXT), axis=0, tiled=True),
        lax.all_gather(shared_mix, (DP, CONTEXT), axis=0, tiled=True),
        lax.all_gather(norm1_gain, (DP, CONTEXT), axis=0, tiled=True),
        lax.all_gather(norm2_gain, (DP, CONTEXT), axis=0, tiled=True),
    )
    x_piece, dy_piece = (
        lax.all_gather(tokens, EXPERT, axis=0, tiled=True),
        lax.all_gather(out_grad, EXPERT, axis=0, tiled=True),
    )
    piece_rows = x_piece.shape[0]
    seq_len = piece_rows * n_pieces
    own_start = my_half * tok_rows
    positions = my_piece * piece_rows + jnp.arange(piece_rows)
    cosine, sine = rope_tables(positions, head_dim)
    query_blocks = positions // BLOCK
    key_blocks = jnp.arange(seq_len) // BLOCK
    visible = key_blocks[None, :] <= query_blocks[:, None]
    x_float = x_piece.astype(jnp.float32)
    rstd_one = lax.rsqrt(jnp.mean(x_float * x_float, axis=1, keepdims=True) + EPS)
    normed_one = x_float * rstd_one
    gain_one = full_gain_one.astype(jnp.float32)
    attn_in = (normed_one * gain_one).astype(jnp.bfloat16)
    q_pre = jnp.dot(
        attn_in, full_query, preferred_element_type=jnp.float32
    ) + query_bias_heads.astype(jnp.float32).reshape(-1)
    k_pre = jnp.dot(attn_in, full_key, preferred_element_type=jnp.float32) + bias_key.astype(
        jnp.float32
    ).reshape(-1)
    v_pre = jnp.dot(attn_in, full_value, preferred_element_type=jnp.float32) + bias_value.astype(
        jnp.float32
    ).reshape(-1)
    q_rot = (
        rotate(q_pre.reshape(piece_rows, local_heads, head_dim), cosine, sine)
        .reshape(piece_rows, -1)
        .astype(jnp.bfloat16)
    )
    k_rot = (
        rotate(k_pre.reshape(piece_rows, local_heads, head_dim), cosine, sine)
        .reshape(piece_rows, -1)
        .astype(jnp.bfloat16)
    )
    v_low = v_pre.astype(jnp.bfloat16)
    keys_all, values_all = (
        lax.all_gather(k_rot, CONTEXT, axis=0, tiled=True),
        lax.all_gather(v_low, CONTEXT, axis=0, tiled=True),
    )
    query_grp = to_groups(q_rot, groups, group_size, head_dim)
    keys_grp = to_groups(keys_all, groups, group_size, head_dim)
    values_grp = to_groups(values_all, groups, group_size, head_dim)

    def attend_group(args):
        group_query, group_keys, group_values = args
        scores = (
            jnp.einsum("hqd,hkd->hqk", group_query, group_keys, preferred_element_type=jnp.float32)
            * score_scale
        )
        scores = jnp.where(visible[None], scores, -jnp.inf)
        row_top = jnp.max(scores, axis=2, keepdims=True)
        expo = jnp.exp(scores - row_top)
        totals = jnp.sum(expo, axis=2, keepdims=True)
        probs = (expo / totals).astype(jnp.bfloat16)
        result = jnp.einsum("hqk,hkd->hqd", probs, group_values, preferred_element_type=jnp.float32)
        return (result, row_top[..., 0] + jnp.log(totals[..., 0]))

    attn_grp, lse_grp = lax.map(attend_group, (query_grp, keys_grp, values_grp))
    attn_low = from_groups(attn_grp).astype(jnp.bfloat16)
    out_partial = jnp.dot(attn_low, full_out, preferred_element_type=jnp.float32)
    out_full = lax.psum(out_partial, EXPERT)
    hidden_one = x_float + out_full
    rstd_two = lax.rsqrt(jnp.mean(hidden_one * hidden_one, axis=1, keepdims=True) + EPS)
    normed_two = hidden_one * rstd_two
    gain_two = full_gain_two.astype(jnp.float32)
    moe_in = (normed_two * gain_two).astype(jnp.bfloat16)
    mix = jax.nn.sigmoid(jnp.dot(moe_in, full_mix, preferred_element_type=jnp.float32))
    s_gate = jnp.dot(moe_in, full_sgate, preferred_element_type=jnp.float32)
    s_up = jnp.dot(moe_in, full_sup, preferred_element_type=jnp.float32)
    s_silu = jax.nn.silu(s_gate)
    s_hidden = (s_silu * s_up).astype(jnp.bfloat16)
    shared_own = lax.psum_scatter(
        jnp.dot(s_hidden, full_sdown, preferred_element_type=jnp.float32),
        EXPERT,
        scatter_dimension=0,
        tiled=True,
    )
    moe_own = lax.dynamic_slice_in_dim(moe_in, own_start, tok_rows, 0)
    hidden_own = lax.dynamic_slice_in_dim(hidden_one, own_start, tok_rows, 0)
    mix_own = lax.dynamic_slice_in_dim(mix, own_start, tok_rows, 0)
    dy_own = out_grad.astype(jnp.float32)
    n_experts = full_router.shape[1]
    router_probs = jax.nn.softmax(
        jnp.dot(moe_own, full_router, preferred_element_type=jnp.float32), axis=1
    )
    picked = (expert_ids[:, :, None] == jnp.arange(n_experts)[None, None, :]).astype(jnp.float32)
    gates = jnp.sum(picked * router_probs[:, None, :], axis=2)
    route_hot = (
        (expert_ids[:, :, None] == jnp.arange(n_experts)[None, None, :])
        .astype(jnp.int32)
        .reshape(-1, n_experts)
    )
    earlier = jnp.cumsum(route_hot, axis=0) - route_hot
    slots = jnp.sum(earlier * route_hot, axis=1)
    places = expert_ids.reshape(-1) * CAP + slots
    route_rows = jnp.repeat(moe_own, expert_ids.shape[1], axis=0)
    route_grads = (
        gates.reshape(-1)[:, None] * jnp.repeat(dy_own, expert_ids.shape[1], axis=0)
    ).astype(jnp.bfloat16)
    send_rows = (
        jnp.zeros((n_experts * CAP, width), jnp.bfloat16)
        .at[places]
        .set(route_rows)
        .reshape(n_experts, CAP, width)
    )
    send_grads = (
        jnp.zeros((n_experts * CAP, width), jnp.bfloat16)
        .at[places]
        .set(route_grads)
        .reshape(n_experts, CAP, width)
    )
    gate_weight = expert_gate[0]
    up_weight = expert_up[0]
    down_weight = expert_down[0]
    rows_in = lax.all_to_all(send_rows, (DP, EXPERT), split_axis=0, concat_axis=0, tiled=True)
    grads_in = lax.all_to_all(send_grads, (DP, EXPERT), split_axis=0, concat_axis=0, tiled=True)
    sources = rows_in.shape[0]
    items = rows_in.shape[1]
    flat_in = rows_in.reshape(-1, width)
    flat_grad = grads_in.reshape(-1, width)
    e_gate = jnp.dot(flat_in, gate_weight, preferred_element_type=jnp.float32)
    e_up = jnp.dot(flat_in, up_weight, preferred_element_type=jnp.float32)
    e_silu = jax.nn.silu(e_gate)
    e_hidden = (e_silu * e_up).astype(jnp.bfloat16)
    e_out = jnp.dot(e_hidden, down_weight, preferred_element_type=jnp.float32).astype(jnp.bfloat16)
    d_hidden = mat_right(flat_grad, down_weight)
    d_gate = (d_hidden * e_up * silu_slope(e_gate)).astype(jnp.bfloat16)
    d_up = (d_hidden * e_silu).astype(jnp.bfloat16)
    d_in = (mat_right(d_gate, gate_weight) + mat_right(d_up, up_weight)).astype(jnp.bfloat16)
    back_out = lax.all_to_all(
        e_out.reshape(sources, items, width),
        (DP, EXPERT),
        split_axis=0,
        concat_axis=0,
        tiled=True,
    )
    back_in = lax.all_to_all(
        d_in.reshape(sources, items, width),
        (DP, EXPERT),
        split_axis=0,
        concat_axis=0,
        tiled=True,
    )
    back_out, back_in, rows_seen, grads_seen, hidden_seen, dgate_seen, duplicate_visits = (
        back_out,
        back_in,
        rows_in,
        grads_in,
        e_hidden.reshape(sources, items, -1),
        d_gate.reshape(sources, items, -1),
        d_up.reshape(sources, items, -1),
    )
    flattened_rows = rows_seen.reshape(-1, width)
    routed_gate_gradient = left_operand(
        flattened_rows, dgate_seen.reshape(flattened_rows.shape[0], -1)
    )
    routed_up_gradient = left_operand(
        flattened_rows, duplicate_visits.reshape(flattened_rows.shape[0], -1)
    )
    routed_down_gradient = left_operand(
        hidden_seen.reshape(flattened_rows.shape[0], -1), grads_seen.reshape(-1, width)
    )
    routed_gate_gradient, routed_up_gradient, routed_down_gradient = (
        lax.psum_scatter(
            routed_gate_gradient[None].astype(jnp.bfloat16),
            CONTEXT,
            scatter_dimension=1,
            tiled=True,
        ).astype(jnp.float32),
        lax.psum_scatter(
            routed_up_gradient[None].astype(jnp.bfloat16),
            CONTEXT,
            scatter_dimension=1,
            tiled=True,
        ).astype(jnp.float32),
        lax.psum_scatter(
            routed_down_gradient[None].astype(jnp.bfloat16),
            CONTEXT,
            scatter_dimension=2,
            tiled=True,
        ).astype(jnp.float32),
    )
    route_out = back_out.reshape(-1, width)[places].astype(jnp.float32).reshape(tok_rows, -1, width)
    route_din = back_in.reshape(-1, width)[places].astype(jnp.float32).reshape(tok_rows, -1, width)
    moe_sum = jnp.sum(gates[:, :, None] * route_out, axis=1)
    mixed = (hidden_own + moe_sum + mix_own[:, None] * shared_own).astype(jnp.bfloat16)
    d_gates = jnp.sum(route_out * dy_own[:, None, :], axis=2)
    d_rprobs = jnp.sum(picked * d_gates[:, :, None], axis=1)
    d_logits = router_probs * (d_rprobs - jnp.sum(router_probs * d_rprobs, axis=1, keepdims=True))
    moe_own_float = moe_own.astype(jnp.float32)
    router_part = jnp.dot(moe_own_float.T, d_logits, precision=HIGH)
    d_mixlogit = jnp.sum(shared_own * dy_own, axis=1) * mix_own * (1.0 - mix_own)
    mix_part = jnp.dot(moe_own_float.T, d_mixlogit, precision=HIGH)
    d_in_own = (
        jnp.sum(route_din, axis=1)
        + jnp.dot(d_logits, full_router.astype(jnp.float32).T, precision=HIGH)
        + d_mixlogit[:, None] * full_mix.astype(jnp.float32)[None, :]
    )
    dy_float = dy_piece.astype(jnp.float32)
    d_shared = (mix[:, None] * dy_float).astype(jnp.bfloat16)
    grad_sdown = left_operand(s_hidden, d_shared)
    d_shidden = mat_right(d_shared, full_sdown)
    d_sgate = (d_shidden * s_up * silu_slope(s_gate)).astype(jnp.bfloat16)
    d_sup = (d_shidden * s_silu).astype(jnp.bfloat16)
    grad_sgate = left_operand(moe_in, d_sgate)
    grad_sup = left_operand(moe_in, d_sup)
    d_in_part = mat_right(d_sgate, full_sgate) + mat_right(d_sup, full_sup)
    d_in_part = lax.dynamic_update_slice_in_dim(
        d_in_part,
        lax.dynamic_slice_in_dim(d_in_part, own_start, tok_rows, 0) + d_in_own,
        own_start,
        0,
    )
    d_moe_in, router_grad, mix_grad = lax.psum((d_in_part, router_part, mix_part), EXPERT)
    d_norm_two = d_moe_in * gain_two
    gain_two_grad = jnp.sum(d_moe_in * normed_two, axis=0)
    d_hidden_one = dy_float + rstd_two * (
        d_norm_two - normed_two * jnp.mean(d_norm_two * normed_two, axis=1, keepdims=True)
    )
    d_proj = d_hidden_one.astype(jnp.bfloat16)
    grad_out = left_operand(attn_low, d_proj)
    d_attn = mat_right(d_proj, full_out).astype(jnp.bfloat16)
    dattn_grp = to_groups(d_attn, groups, group_size, head_dim)

    def query_side(args):
        group_query, group_keys, group_values, group_lse, group_attention_gradient = args
        scores = (
            jnp.einsum("hqd,hkd->hqk", group_query, group_keys, preferred_element_type=jnp.float32)
            * score_scale
        )
        probs = jnp.where(
            visible[None],
            jnp.exp(jnp.where(visible[None], scores, 0.0) - group_lse[..., None]),
            0.0,
        )
        d_probs = jnp.einsum(
            "hqd,hkd->hqk",
            group_attention_gradient,
            group_values,
            preferred_element_type=jnp.float32,
        )
        delta = jnp.sum(probs * d_probs, axis=2)
        d_scores = (probs * (d_probs - delta[..., None])).astype(jnp.bfloat16)
        d_query = (
            jnp.einsum("hqk,hkd->hqd", d_scores, group_keys, preferred_element_type=jnp.float32)
            * score_scale
        )
        return (probs, d_scores, d_query, delta)

    def both_sides(args):
        probs, d_scores, d_query, delta = query_side(args)
        d_key = (
            jnp.einsum("hqk,hqd->hkd", d_scores, args[0], preferred_element_type=jnp.float32)
            * score_scale
        )
        d_value = jnp.einsum(
            "hqk,hqd->hkd", probs.astype(jnp.bfloat16), args[4], preferred_element_type=jnp.float32
        )
        return (d_query, d_key, d_value)

    dq_grp, dk_grp, dv_grp = lax.map(
        both_sides, (query_grp, keys_grp, values_grp, lse_grp, dattn_grp)
    )
    d_query = from_groups(dq_grp)
    d_key_own, d_value_own = (
        lax.psum_scatter(from_groups(dk_grp), CONTEXT, scatter_dimension=0, tiled=True),
        lax.psum_scatter(from_groups(dv_grp), CONTEXT, scatter_dimension=0, tiled=True),
    )
    d_q_pre = (
        rotate_back(d_query.reshape(piece_rows, local_heads, head_dim), cosine, sine)
        .reshape(piece_rows, -1)
        .astype(jnp.bfloat16)
    )
    d_k_pre = (
        rotate_back(d_key_own.reshape(piece_rows, local_heads, head_dim), cosine, sine)
        .reshape(piece_rows, -1)
        .astype(jnp.bfloat16)
    )
    d_v_pre = d_value_own.astype(jnp.bfloat16)
    grad_bq = jnp.sum(d_q_pre.astype(jnp.float32), axis=0).reshape(local_heads, head_dim)
    grad_bk = jnp.sum(d_k_pre.astype(jnp.float32), axis=0).reshape(local_heads, head_dim)
    grad_bv = jnp.sum(d_v_pre.astype(jnp.float32), axis=0).reshape(local_heads, head_dim)
    grad_query = left_operand(attn_in, d_q_pre)
    grad_key = left_operand(attn_in, d_k_pre)
    grad_value = left_operand(attn_in, d_v_pre)
    d_attn_in = (
        mat_right(d_q_pre, full_query)
        + mat_right(d_k_pre, full_key)
        + mat_right(d_v_pre, full_value)
    )
    d_attn_in = lax.psum(d_attn_in.astype(jnp.bfloat16), EXPERT).astype(jnp.float32)
    d_norm_one = d_attn_in * gain_one
    gain_one_grad = jnp.sum(d_attn_in * normed_one, axis=0)
    d_x = d_hidden_one + rstd_one * (
        d_norm_one - normed_one * jnp.mean(d_norm_one * normed_one, axis=1, keepdims=True)
    )
    input_grad = lax.dynamic_slice_in_dim(d_x, own_start, tok_rows, 0).astype(jnp.bfloat16)
    (
        grad_query,
        grad_key,
        grad_value,
        grad_out,
        grad_sgate,
        grad_sup,
        grad_sdown,
        router_grad,
        mix_grad,
        gain_one_grad,
        gain_two_grad,
        grad_bq,
        grad_bk,
        grad_bv,
    ) = (
        lax.psum_scatter(grad_query, (DP, CONTEXT), scatter_dimension=0, tiled=True),
        lax.psum_scatter(grad_key, (DP, CONTEXT), scatter_dimension=0, tiled=True),
        lax.psum_scatter(grad_value, (DP, CONTEXT), scatter_dimension=0, tiled=True),
        lax.psum_scatter(grad_out, (DP, CONTEXT), scatter_dimension=1, tiled=True),
        lax.psum_scatter(grad_sgate, (DP, CONTEXT), scatter_dimension=0, tiled=True),
        lax.psum_scatter(grad_sup, (DP, CONTEXT), scatter_dimension=0, tiled=True),
        lax.psum_scatter(grad_sdown, (DP, CONTEXT), scatter_dimension=1, tiled=True),
        lax.psum_scatter(router_grad, (DP, CONTEXT), scatter_dimension=0, tiled=True),
        lax.psum_scatter(mix_grad, (DP, CONTEXT), scatter_dimension=0, tiled=True),
        lax.psum_scatter(gain_one_grad, (DP, CONTEXT), scatter_dimension=0, tiled=True),
        lax.psum_scatter(gain_two_grad, (DP, CONTEXT), scatter_dimension=0, tiled=True),
        lax.psum_scatter(grad_bq, (DP, CONTEXT), scatter_dimension=1, tiled=True),
        lax.psum_scatter(grad_bk, (DP, CONTEXT), scatter_dimension=1, tiled=True),
        lax.psum_scatter(grad_bv, (DP, CONTEXT), scatter_dimension=1, tiled=True),
    )
    return (
        mixed,
        input_grad,
        gain_one_grad,
        grad_query,
        grad_key,
        grad_value,
        grad_bq,
        grad_bk,
        grad_bv,
        grad_out,
        gain_two_grad,
        router_grad,
        mix_grad,
        grad_sgate,
        grad_sup,
        grad_sdown,
        routed_gate_gradient,
        routed_up_gradient,
        routed_down_gradient,
    )


def dot_f32(left, right, left_dim, right_dim):
    return lax.dot_general(
        left, right, (((left_dim,), (right_dim,)), ((), ())), preferred_element_type=jnp.float32
    )


def whole_vmem(count):
    return [pl.BlockSpec(memory_space=pltpu.VMEM)] * count


def like(shape, dtype):
    return jax.ShapeDtypeStruct(shape, dtype)


MESH_ID = pl.DeviceIdType.MESH


class Wire:
    def __init__(self, send, recv):
        self.send = send
        self.recv = recv
        self.sent = 0
        self.received = 0
        self.own = []

    def copy(self, src, dst, device):
        out = self.copy_to(src, dst, device, self.take(1), self.take_send(1))
        self.own.append(out)
        return out

    def take(self, count):
        self.received += count
        assert self.received <= self.recv.shape[0], self.received
        return self.received - count

    def take_send(self, count):
        self.sent += count
        assert self.sent <= self.send.shape[0], self.sent
        return self.sent - count

    def copy_to(self, src, dst, device, recv_slot, send_slot):
        return pltpu.make_async_remote_copy(
            src_ref=src,
            dst_ref=dst,
            send_sem=self.send.at[send_slot],
            recv_sem=self.recv.at[recv_slot],
            device_id=device,
            device_id_type=MESH_ID,
        )

    def drain(self, some=None):
        for item in self.own if some is None else some:
            item.wait_send()
        done = {id(item) for item in some} if some is not None else None
        self.own = [] if done is None else [item for item in self.own if id(item) not in done]


class Local:
    def __init__(self, sems):
        self.sems = sems
        self.count = 0

    def start(self, src, dst):
        assert self.count < self.sems.shape[0], self.count
        item = pltpu.make_async_copy(src, dst, self.sems.at[self.count])
        self.count += 1
        item.start()
        return item


class Phases:
    def __init__(self):
        self.scope = None

    def go(self, name):
        if self.scope is not None:
            self.scope.__exit__(None, None, None)
        self.scope = jax.named_scope(name) if name else None
        if name:
            self.scope.__enter__()


class Place:
    def __init__(self, n_dp):
        self.n_dp = n_dp
        self.z = lax.axis_index(DP)
        self.c = lax.axis_index(CONTEXT)
        self.y = lax.axis_index(EXPERT)
        self.cx = lax.bitwise_xor(self.c, jnp.int32(2))
        self.cs = lax.bitwise_xor(self.c, jnp.int32(1))
        self.cd = lax.bitwise_xor(self.c, jnp.int32(3))
        self.yn = lax.bitwise_xor(self.y, jnp.int32(1))
        self.core = (self.z, self.cs, self.y)
        self.over_x = (self.z, self.cx, self.y)
        self.over_y = (self.z, self.c, self.yn)
        self.up = (self.z + 1, self.c, self.y)
        self.down = (self.z - 1, self.c, self.y)

    def block(self, c, y):
        return c * 2 + y


def barrier(devices):
    sem = pltpu.get_barrier_semaphore()
    for device in devices:
        pl.semaphore_signal(sem, inc=1, device_id=device, device_id_type=MESH_ID)
    pl.semaphore_wait(sem, len(devices))


def rows_of(index, count):
    return pl.ds(pl.multiple_of(index * count, count), count)


def by_rows(total, step, body):
    def one(index, carry):
        body(rows_of(index, step))
        return carry

    lax.fori_loop(0, total // step, one, 0)


def chain_gather(wire, place, refs, arrived=None, begun=False):
    n = place.n_dp
    z = place.z
    width = len(refs(z))
    recv = wire.take(n * width)
    send = wire.take_send(2 * n * width)

    def copies(slot, up, dist):
        return [
            wire.copy_to(
                ref,
                ref,
                place.up if up else place.down,
                recv + slot * width + index,
                send + (2 * dist + (0 if up else 1)) * width + index,
            )
            for index, ref in enumerate(refs(slot))
        ]

    def start(slot, up, dist):
        for item in copies(slot, up, dist):
            item.start()

    def land(slot, up, dist):
        if dist > 1 or not begun:
            for item in copies(slot, up, dist):
                item.wait_recv()
        if arrived is not None:
            arrived(slot)

    def sent(slot, up, dist):
        for item in copies(slot, up, dist):
            item.wait_send()

    if not begun:
        pl.when(z < n - 1)(lambda: start(z, True, 0))
        pl.when(z > 0)(lambda: start(z, False, 0))
        yield
    for dist in range(1, n):
        below, above = z - dist, z + dist

        @pl.when(below >= 0)
        def _():
            land(below, True, dist)
            pl.when(z < n - 1)(lambda: start(below, True, dist))

        @pl.when(above < n)
        def _():
            land(above, False, dist)
            pl.when(z > 0)(lambda: start(above, False, dist))

        yield
    for dist in range(1 if begun else 0, n):
        below, above = z - dist, z + dist
        pl.when((below >= 0) & (z < n - 1))(lambda: sent(below, True, dist))
        pl.when((above < n) & (z > 0))(lambda: sent(above, False, dist))


def finish(*steps):
    for step in steps:
        for _ in step:
            pass


def plane_gather(wire, place, buf):
    rows = buf.shape[0] // 8
    half = buf.shape[1] // 2
    left, right = pl.ds(0, half), pl.ds(half, half)
    own = rows_of(place.block(place.c, place.y), rows)
    from_x = rows_of(place.block(place.cx, place.y), rows)
    from_y = rows_of(place.block(place.c, place.yn), rows)
    across = rows_of(place.block(place.cx, place.yn), rows)

    def go(where, lanes, device):
        ref = buf.at[where, lanes] if lanes is not None else buf.at[where, :]
        item = wire.copy(ref, ref, device)
        item.start()
        return item

    x_left = go(own, left, place.over_x)
    y_right = go(own, right, place.over_y)
    x_right = go(own, right, place.over_x)
    y_left = go(own, left, place.over_y)
    waits = [go(own, None, place.core)]
    yield
    x_left.wait_recv()
    far_left = go(from_x, left, place.over_y)
    y_right.wait_recv()
    far_right = go(from_y, right, place.over_x)
    yield
    x_right.wait_recv()
    waits.append(go(from_x, None, place.core))
    y_left.wait_recv()
    waits.append(go(from_y, None, place.core))
    yield
    far_left.wait_recv()
    far_right.wait_recv()
    waits.append(go(across, None, place.core))
    for item in waits:
        item.wait_recv()


def add_into(target, lanes, rows, extra):
    count = extra.shape[0]
    step = 16

    def one(index, carry):
        here = pl.ds(pl.multiple_of(rows + index * step, step), step)
        there = rows_of(index, step)
        total = target[here, lanes].astype(jnp.float32) + extra[there, :].astype(jnp.float32)
        target[here, lanes] = total.astype(target.dtype)
        return carry

    lax.fori_loop(0, count // step, one, 0)


def plane_reduce(wire, place, part, got_core, got_one, got_two):
    rows = part.shape[0] // 8
    half = part.shape[1] // 2
    left, right = pl.ds(0, half), pl.ds(half, half)
    chips = ((place.cx, place.yn), (place.cx, place.y), (place.c, place.yn), (place.c, place.y))
    starts = [place.block(c, y) * rows for c, y in chips]
    blocks = [pl.ds(pl.multiple_of(start, rows), rows) for start in starts]
    sibling = [
        rows_of(place.block(lax.bitwise_xor(c, jnp.int32(1)), y), rows) for c, y in chips
    ]
    swaps = []
    for index in range(4):
        item = wire.copy(part.at[sibling[index], :], got_core.at[index], place.core)
        item.start()
        swaps.append(item)
    whole = pl.ds(0, 2 * half)

    def one(index, lanes, slot, device):
        item = wire.copy(part.at[blocks[index], lanes], got_one.at[slot], device)
        item.start()
        return item

    swaps[0].wait_recv()
    add_into(part, whole, starts[0], got_core.at[0])
    far_x = one(0, left, 0, place.over_x)
    far_y = one(0, right, 2, place.over_y)
    swaps[1].wait_recv()
    add_into(part, whole, starts[1], got_core.at[1])
    near_x = one(1, left, 1, place.over_x)
    swaps[2].wait_recv()
    add_into(part, whole, starts[2], got_core.at[2])
    near_y = one(2, right, 3, place.over_y)
    yield
    swaps[3].wait_recv()
    add_into(part, whole, starts[3], got_core.at[3])
    far_x.wait_recv()
    add_into(part, left, starts[2], got_one.at[0])
    last_y = wire.copy(part.at[blocks[2], left], got_two.at[0], place.over_y)
    last_y.start()
    far_y.wait_recv()
    add_into(part, right, starts[1], got_one.at[2])
    last_x = wire.copy(part.at[blocks[1], right], got_two.at[1], place.over_x)
    last_x.start()
    yield
    near_x.wait_recv()
    near_y.wait_recv()
    last_x.wait_recv()
    last_y.wait_recv()


def plane_sum(place, part, got_one, got_two, here):
    rows = part.shape[0] // 8
    half = part.shape[1] // 2
    start = place.block(place.c, place.y) * rows + here.start
    at = pl.ds(pl.multiple_of(start, here.size), here.size)

    def value(ref):
        return ref.astype(jnp.float32)

    left = value(part[at, 0:half]) + value(got_one[1, here, :]) + value(got_two[0, here, :])
    right = value(part[at, half:]) + value(got_one[3, here, :]) + value(got_two[1, here, :])
    return jnp.concatenate([left, right], axis=1)


def forward_kernel(
    n_blocks, n_dp,
    tokens, out_grad, small, ids, w_query, w_key, w_value, w_out, s_gate, s_up, s_down,
    bias, cosine, sine,
    attn_in_to, query_to, keys_to, values_to, attn_to, lse_to, hidden_to, moe_in,
    heads_weight_to, out_weight_to, gate_weight, up_weight, down_weight, smalls, all_ids, dy_group,
    x_seq, partial, got_core, got_one, got_two,
    attn_in, query, keys, values, attn, lse, hidden, heads_weight, out_weight,
    shared_raw, shared_packed, send, recv, local,
):
    place = Place(n_dp)
    wire = Wire(send, recv)
    inside = Local(local)
    z, c, y = place.z, place.c, place.y
    rows, width = tokens.shape
    seq = x_seq.shape[0]
    cols = query.shape[1]
    head_dim = cosine.shape[1]
    block = seq // n_blocks
    scale = 1.0 / math.sqrt(head_dim)
    n_ctx = 4
    share = w_query.shape[0]
    f32, low = jnp.float32, jnp.bfloat16

    others = [(dz, dc) for dz in range(n_dp) for dc in range(n_ctx) if dz or dc]
    phases = Phases()
    phases.go("entry")
    raw_in = [inside.start(src, shared_raw.at[k]) for k, src in enumerate((s_gate, s_up))]

    def moved(dz, dc, y_to):
        return (lax.bitwise_xor(z, jnp.int32(dz)), lax.bitwise_xor(c, jnp.int32(dc)), y_to)

    barrier(
        [moved(dz, dc, y) for dz, dc in others] + [moved(dz, 0, place.yn) for dz in range(n_dp)]
    )

    mine = z * n_ctx + c
    my_rows = rows_of(mine, share)
    group = z * 2 + y
    shared_pieces = [[], [], []]

    units = gate_weight.shape[3]

    def pack(index):
        raw_in[index].wait()
        for part in range(n_dp):
            shared_packed[index, part] = shared_raw[index, :, part * units : (part + 1) * units]

    def shared_along_dp(index):
        if index < 2:
            pack(index)
        for dz in (2, 3, 1, 0):
            to = lax.bitwise_xor(z, jnp.int32(dz))
            if index == 2:
                src = s_down.at[rows_of(to, s_down.shape[0] // n_dp), :]
                dst = down_weight.at[:, my_rows]
            else:
                src = shared_packed.at[index, to]
                dst = (gate_weight, up_weight)[index].at[z, c]
            if dz == 0:
                item = inside.start(src, dst)
            else:
                item = wire.copy(src, dst, moved(dz, 0, y))
                item.start()
            shared_pieces[index].append(item)

    shared_along_dp(0)

    exchanges = []
    for dc in range(n_ctx):
        to = lax.bitwise_xor(c, jnp.int32(dc))
        lanes = pl.ds(pl.multiple_of(to * cols, cols), cols)
        pairs = [
            (weight.at[:, lanes], heads_weight.at[my_rows, pl.ds(index * cols, cols)])
            for index, weight in enumerate((w_query, w_key, w_value))
        ]
        pairs.append((w_out.at[rows_of(to, cols), :], out_weight.at[:, my_rows]))
        for src, dst in pairs:
            if dc == 0:
                exchanges.append(inside.start(src, dst))
            else:
                item = wire.copy(src, dst, moved(0, dc, y))
                item.start()
                exchanges.append(item)
    own_rows = rows_of(place.block(c, y), rows)
    here = inside.start(tokens, x_seq.at[own_rows, :])
    here.wait()
    small_copies = [inside.start(small, smalls.at[:, my_rows])]
    for dz, dc in others:
        item = wire.copy(small, smalls.at[:, my_rows], moved(dz, dc, y))
        item.start()
        small_copies.append(item)
    small_copies.append(inside.start(ids, all_ids.at[group]))
    for dz in range(n_dp):
        for y_to in (y, place.yn):
            if dz or y_to is not y:
                item = wire.copy(ids, all_ids.at[group], moved(dz, 0, y_to))
                item.start()
                small_copies.append(item)
    def dy_rows(slot, half):
        return dy_group.at[rows_of(slot * 2 + half, rows), :]

    stores = [inside.start(out_grad, dy_rows(z, y))]
    dy_over_y = wire.copy(out_grad, dy_rows(z, y), place.over_y)
    dy_over_y.start()
    phases.go("exchanges")
    for item in exchanges:
        item.wait_recv()

    def from_place(slot):
        return rows_of(slot, n_ctx * share)

    weights_in = chain_gather(wire, place, lambda slot: [heads_weight.at[from_place(slot), :]])
    next(weights_in)
    phases.go("tokens")
    tokens_in = plane_gather(wire, place, x_seq)
    finish(tokens_in)
    next(weights_in)
    for item in small_copies:
        item.wait_recv()

    gain_one = smalls[9:10, :].astype(f32)
    gain_two = smalls[10:11, :].astype(f32)

    def norm_one(at):
        x_float = x_seq[at, :].astype(f32)
        rstd = lax.rsqrt(jnp.mean(x_float * x_float, axis=1, keepdims=True) + EPS)
        attn_in[at, :] = (x_float * rstd * gain_one).astype(low)

    by_rows(seq, 64, norm_one)
    def shared_set(index, context):
        if index < 2:
            return [(gate_weight, up_weight)[index].at[:, context]]
        return [
            down_weight.at[:, rows_of(dz * n_ctx + context, share)] for dz in range(n_dp)
        ]

    over = [[], [], []]
    close = []

    def shared_over_x(index):
        for item in shared_pieces[index]:
            item.wait_recv()
        for ref in shared_set(index, c):
            item = wire.copy(ref, ref, place.over_x)
            item.start()
            over[index].append(item)
        for ref in shared_set(index, c):
            item = wire.copy(ref, ref, place.core)
            item.start()
            close.append(item)

    def shared_close(index):
        for item, ref in zip(over[index], shared_set(index, place.cx)):
            item.wait_recv()
            item = wire.copy(ref, ref, place.core)
            item.start()
            close.append(item)

    shared_over_x(0)
    phases.go("heads_weights")
    finish(weights_in)
    phases.go("attention")
    out_in = chain_gather(wire, place, lambda slot: [out_weight.at[:, from_place(slot)]])
    next(out_in)

    def project(at):
        pre = dot_f32(attn_in[at, :], heads_weight[...], 1, 0)
        cos = cosine[at, :]
        sin = sine[at, :]
        for index, kept in enumerate((query, keys, values)):
            for start in range(0, cols, head_dim):
                from_lane = index * cols + start
                part = pre[:, from_lane : from_lane + head_dim]
                part = part + bias[index : index + 1, start : start + head_dim]
                if index < 2:
                    part = part * cos + pltpu.roll(part, head_dim // 2, 1) * sin
                kept[at, start : start + head_dim] = part.astype(low)

    by_rows(seq, block, project)
    next(out_in)
    for start in range(0, cols, head_dim):
        lanes = slice(start, start + head_dim)
        for step in range(n_blocks):
            at = slice(step * block, (step + 1) * block)
            seen = slice(0, (step + 1) * block)
            scores = dot_f32(query[at, lanes], keys[seen, lanes], 1, 1) * scale
            top = jnp.max(scores, axis=1, keepdims=True)
            expo = jnp.exp(scores - top)
            total = jnp.sum(expo, axis=1, keepdims=True)
            probs = (expo / total).astype(low)
            attn[at, lanes] = dot_f32(probs, values[seen, lanes], 1, 0).astype(low)
            lse[at, lanes] = jnp.broadcast_to(top + jnp.log(total), (block, head_dim))
        if start == 0:
            next(out_in)
    phases.go("out_weights")
    finish(out_in)
    shared_along_dp(1)
    shared_along_dp(2)
    phases.go("attention_out")

    def output(at):
        partial[at, :] = dot_f32(attn[at, :], out_weight[...], 1, 0).astype(low)

    by_rows(seq, block, output)
    stores += [
        inside.start(src, dst)
        for src, dst in (
            (attn_in, attn_in_to), (query, query_to), (keys, keys_to), (values, values_to),
            (attn, attn_to), (lse, lse_to), (heads_weight, heads_weight_to),
            (out_weight, out_weight_to),
        )
    ]
    phases.go("sum_in_plane")
    reduce = plane_reduce(wire, place, partial, got_core, got_one, got_two)
    next(reduce)

    next(reduce)
    finish(reduce)
    phases.go("norm_two")

    def norm_two(at):
        start = place.block(c, y) * rows + at.start
        own = pl.ds(pl.multiple_of(start, at.size), at.size)
        total = x_seq[own, :].astype(f32) + plane_sum(place, partial, got_one, got_two, at)
        hidden[at, :] = total
        rstd = lax.rsqrt(jnp.mean(total * total, axis=1, keepdims=True) + EPS)
        got_core[0, at, :] = (total * rstd * gain_two).astype(low)

    by_rows(rows, 16, norm_two)
    stores.append(inside.start(hidden, hidden_to))
    at_group = rows_of(group, rows)
    here = inside.start(got_core.at[0], moe_in.at[at_group, :])
    here.wait()

    half_width = width // 2
    y_recv = wire.take(2 * n_dp)
    y_send = wire.take_send(2 * n_dp)

    def moe_block(slot, half, part):
        return moe_in.at[rows_of(slot * 2 + half, rows), pl.ds(part * half_width, half_width)]

    def to_y(slot, part, half=None):
        ref = moe_block(slot, y if half is None else half, part)
        sem = 2 * slot + part
        return wire.copy_to(ref, ref, place.over_y, y_recv + sem, y_send + sem)

    chains = [
        chain_gather(
            wire,
            place,
            lambda slot, part=part: [moe_block(slot, y, part)],
            arrived=lambda slot, part=part: to_y(slot, part).start(),
        )
        for part in range(2)
    ]
    for part in range(2):
        next(chains[part])
        to_y(z, part).start()
    phases.go("shared_one")
    shared_over_x(1)
    phases.go("rows_one")
    for chain in chains:
        next(chain)
    phases.go("shared_two")
    shared_over_x(2)
    phases.go("rows_two")
    for chain in chains:
        next(chain)
    phases.go("rows_three")
    for chain in chains:
        next(chain)
    dy_recv = wire.take(2)
    dy_send = wire.take_send(2)

    def dy_step(up):
        ref = dy_rows(z, y)
        to = place.up if up else place.down
        return wire.copy_to(out_grad, ref, to, dy_recv + (0 if up else 1), dy_send + (0 if up else 1))

    pl.when(z < n_dp - 1)(lambda: dy_step(True).start())
    pl.when(z > 0)(lambda: dy_step(False).start())
    finish(*chains)
    phases.go("shared_close")
    for index in range(3):
        shared_close(index)
    for item in close:
        item.wait_recv()
    phases.go("rows_over_y")
    for slot in range(n_dp):
        for part in range(2):
            to_y(slot, part, place.yn).wait_recv()
            to_y(slot, part).wait_send()
    phases.go("dy")
    dy_over_y.wait_recv()

    @pl.when(z > 0)
    def _():
        dy_step(True).wait_recv()
        dy_step(False).wait_send()

    @pl.when(z < n_dp - 1)
    def _():
        dy_step(False).wait_recv()
        dy_step(True).wait_send()

    for item in stores:
        item.wait()
    wire.drain()
    phases.go(None)


def chain_reduce(wire, place, parts):
    n = place.n_dp
    z = place.z
    count = len(parts)
    recv = wire.take(2 * n * count)
    send = wire.take_send(2 * n * count)

    def copies(target, up):
        out = []
        for index, (block, below, above) in enumerate(parts):
            slot = (2 * target + (0 if up else 1)) * count + index
            landing = below if up else above
            out.append(
                wire.copy_to(
                    block(target),
                    landing.at[target],
                    place.up if up else place.down,
                    recv + slot,
                    send + slot,
                )
            )
        return out

    def collect(target, up):
        for item, (block, below, above) in zip(copies(target, up), parts):
            item.wait_recv()
            add_block(block(target), (below if up else above).at[target])

    def pass_on(target, up):
        collect(target, up)
        for item in copies(target, up):
            item.start()

    def first(target, up):
        for item in copies(target, up):
            item.start()

    @pl.when(z == 0)
    def _():
        for target in range(n - 1, 0, -1):
            first(target, True)

    @pl.when(z == n - 1)
    def _():
        for target in range(n - 1):
            first(target, False)

    yield
    for step in range(n - 1):
        high, low = n - 1 - step, step

        @pl.when((z > 0) & (z < n // 2))
        def _():
            pl.when(z < high)(lambda: pass_on(high, True))
            pl.when(z > low)(lambda: pass_on(low, False))

        @pl.when((z >= n // 2) & (z < n - 1))
        def _():
            pl.when(z > low)(lambda: pass_on(low, False))
            pl.when(z < high)(lambda: pass_on(high, True))

        yield
    pl.when(z > 0)(lambda: collect(z, True))
    pl.when(z < n - 1)(lambda: collect(z, False))
    for target in range(n):

        @pl.when(z < target)
        def _():
            for item in copies(target, True):
                item.wait_send()

        @pl.when(z > target)
        def _():
            for item in copies(target, False):
                item.wait_send()


def add_block(target, extra):
    step = 16

    def one(index, carry):
        here = rows_of(index, step)
        total = target[here, :].astype(jnp.float32) + extra[here, :].astype(jnp.float32)
        target[here, :] = total.astype(target.dtype)
        return carry

    lax.fori_loop(0, extra.shape[0] // step, one, 0)


class Adder:
    def __init__(self, sems):
        self.sems = sems

    def run(self, buf, chunks):
        def load(index):
            first, second, _ = chunks[index]
            slot = index % 2
            items = [
                pltpu.make_async_copy(first, buf.at[0, slot], self.sems.at[3 * slot]),
                pltpu.make_async_copy(second, buf.at[1, slot], self.sems.at[3 * slot + 1]),
            ]
            for item in items:
                item.start()
            return items

        stores = [None, None]
        loads = load(0)
        for index, (_, _, target) in enumerate(chunks):
            slot = index % 2
            after = load(index + 1) if index + 1 < len(chunks) else None
            for item in loads:
                item.wait()
            loads = after
            if stores[slot] is not None:
                stores[slot].wait()
            total, first, second = buf.at[2, slot], buf.at[0, slot], buf.at[1, slot]

            def one(step, carry):
                here = rows_of(step, 16)
                value = first[here, :].astype(jnp.float32) + second[here, :].astype(jnp.float32)
                total[here, :] = value.astype(total.dtype)
                return carry

            lax.fori_loop(0, total.shape[0] // 16, one, 0)
            stores[slot] = pltpu.make_async_copy(total, target, self.sems.at[3 * slot + 2])
            stores[slot].start()
        for item in stores:
            if item is not None:
                item.wait()


def backward_kernel(
    n_blocks, n_dp,
    own_sum, got_scalars, k_sup, k_sdown, x_sup, x_sdown, r_eup, r_edown,
    hidden_in, out_grad_in, tokens_in, smalls, probs, mix,
    heads_weight_in, w_out_in, query_in, keys_in, values_in, attn_from, lse_in, attn_in_from,
    cosine_in, sine_in,
    input_grad, heads_grad, out_weight_grad, small_grad, bias_grad,
    t_sup, t_sdown, x_eup, x_edown, s_sup, s_sdown,
    partial, d_hidden, side, moe_own, terms, acc,
    proj, d_attn, d_qkv, d_keys, d_values, got_core, got_one, got_two,
    g_heads, g_out, heads_below, heads_above, out_below, out_above, out_block,
    stage, landed, over_y, gate_buf, down_buf,
    hidden, out_grad, tokens, heads_weight, w_out, query, keys, values, attn, lse, attn_in,
    cosine, sine, send, recv, local, adds,
):
    place = Place(n_dp)
    wire = Wire(send, recv)
    inside = Local(local)
    adder = Adder(adds)
    z, c, y = place.z, place.c, place.y
    rows, width = tokens.shape
    seq = proj.shape[0]
    cols = query.shape[1]
    head_dim = cosine.shape[1]
    block = seq // n_blocks
    scale = 1.0 / math.sqrt(head_dim)
    n_ctx = 4
    share = width // (n_dp * n_ctx)
    n_experts = probs.shape[0]
    f32, low = jnp.float32, jnp.bfloat16
    core = lax.rem(c, 2)
    others = [(dz, dc) for dz in range(n_dp) for dc in range(n_ctx) if dz or dc]

    def moved(dz, dc, y_to):
        return (lax.bitwise_xor(z, jnp.int32(dz)), lax.bitwise_xor(c, jnp.int32(dc)), y_to)

    phases = Phases()
    phases.go("entry")
    barrier(
        [moved(dz, dc, y) for dz, dc in others] + [moved(dz, 0, place.yn) for dz in range(n_dp)]
    )
    def go_over_x(index, part=0, parts=1):
        total = (r_eup, r_edown)[index]
        got = (x_eup, x_edown)[index]
        count = got.shape[0] // parts
        at = pl.ds(part * count, count)
        item = wire.copy(total.at[at, :], got.at[at, :], place.over_x)
        item.start()
        return item

    def part_of(ref, dz):
        size = ref.shape[0] // n_dp
        return ref.at[pl.ds(dz * size, size), :]

    def shared_ready(index):
        buf = (gate_buf, down_buf)[index]
        kept = (k_sup, k_sdown)[index]
        got = (x_sup, x_sdown)[index]
        ready = (s_sup, s_sdown)[index]
        adder.run(buf, [(part_of(kept, dz), part_of(got, dz), ready.at[dz]) for dz in range(n_dp)])

    shared_last = []

    def shared_along_dp(index):
        ready = (s_sup, s_sdown)[index]
        target = (t_sup, t_sdown)[index]
        for dz in (2, 3, 1, 0):
            to = lax.bitwise_xor(z, jnp.int32(dz))
            if dz:
                item = wire.copy(ready.at[to], target.at[z], moved(dz, 0, y))
                item.start()
            else:
                item = inside.start(ready.at[to], target.at[z])
            shared_last.append(item)

    loads = [
        inside.start(src, dst)
        for src, dst in (
            (hidden_in, hidden), (out_grad_in, out_grad), (tokens_in, tokens), (attn_from, attn),
            (w_out_in, w_out), (query_in, query), (keys_in, keys), (values_in, values),
            (lse_in, lse), (cosine_in, cosine), (sine_in, sine), (heads_weight_in, heads_weight),
            (attn_in_from, attn_in),
        )
    ]
    phases.go("router")
    d_rprobs = got_scalars[:, 0, :]
    probs_own = probs[...]
    d_logits = probs_own * (d_rprobs - jnp.sum(probs_own * d_rprobs, axis=0, keepdims=True))
    shared_dot = jnp.sum(got_scalars[:, 1, :], axis=0, keepdims=True)
    d_mix = shared_dot * mix[...] * (1.0 - mix[...])
    d_side = jnp.concatenate(
        [d_logits, jnp.broadcast_to(d_mix, (16 - n_experts, rows))], axis=0
    )
    row_of = lax.broadcasted_iota(jnp.int32, d_side.shape, 0)
    d_side = jnp.where(row_of <= n_experts, d_side, 0.0)
    first = d_side.astype(low)
    rest = d_side - first.astype(f32)
    second = rest.astype(low)
    third = (rest - second.astype(f32)).astype(low)
    terms[...] = jnp.concatenate([first, second, third], axis=0)
    side[...] = dot_f32(terms[...], jnp.concatenate([smalls[...]] * 3, axis=0), 0, 0)
    gain_one = smalls[n_experts + 1 : n_experts + 2, :].astype(f32)
    gain_two = smalls[n_experts + 2 : n_experts + 3, :].astype(f32)
    acc[...] = jnp.zeros_like(acc)
    own_plane = place.block(c, y) * rows

    def norm_two(at):
        d_moe = side[at, :] + own_sum[at, :]
        total = hidden[at, :]
        rstd = lax.rsqrt(jnp.mean(total * total, axis=1, keepdims=True) + EPS)
        normed = total * rstd
        acc[0] += d_moe * normed
        d_norm = d_moe * gain_two
        back = out_grad[at, :].astype(f32) + rstd * (
            d_norm - normed * jnp.mean(d_norm * normed, axis=1, keepdims=True)
        )
        d_hidden[at, :] = back
        moe_own[at, :] = (normed * gain_two).astype(low)
        proj[pl.ds(pl.multiple_of(own_plane + at.start, at.size), at.size), :] = back.astype(low)

    phases.go("norm_two")
    for item in loads[:3]:
        item.wait()
    by_rows(rows, 16, norm_two)
    phases.go("gather_in_plane")
    proj_in = plane_gather(wire, place, proj)
    next(proj_in)
    side[0:48, :] = dot_f32(terms[...], moe_own[...], 1, 0)

    phases.go("shared_up")
    shared_ready(0)
    shared_along_dp(0)
    phases.go("gather_relay")
    next(proj_in)
    phases.go("shared_down")
    shared_ready(1)
    shared_along_dp(1)
    phases.go("gather_close")
    next(proj_in)
    phases.go("gather_end")
    finish(proj_in)

    phases.go("attention")
    routed_over = [go_over_x(0, 0, 2)]
    for item in loads[3:]:
        item.wait()
    by_share = n_ctx * share

    def out_weight(target):
        at = rows_of(target, by_share)
        g_out[:, at] = dot_f32(attn[...], proj[:, at], 0, 0).astype(low)

    def each(count, body):
        def one(index, carry):
            body(index)
            return carry

        lax.fori_loop(0, count, one, 0)

    each(n_dp, out_weight)
    out_chain = chain_reduce(
        wire, place, [(lambda t: g_out.at[:, rows_of(t, by_share)], out_below, out_above)]
    )
    next(out_chain)

    def project(at):
        d_attn[at, :] = dot_f32(proj[at, :], w_out[...], 1, 1).astype(low)

    by_rows(seq, block, project)

    def turn(part, at):
        return part * cosine[at, :] - pltpu.roll(part, head_dim // 2, 1) * sine[at, :]

    every = slice(0, seq)
    for start in range(0, cols, head_dim):
        lanes = slice(start, start + head_dim)
        d_keys[...] = jnp.zeros_like(d_keys)
        d_values[...] = jnp.zeros_like(d_values)
        for step in range(n_blocks):
            at = slice(step * block, (step + 1) * block)
            seen = slice(0, (step + 1) * block)
            q_here = query[at, lanes]
            k_seen = keys[seen, lanes]
            grad = d_attn[at, lanes]
            scores = dot_f32(q_here, k_seen, 1, 1) * scale
            weights = jnp.exp(scores - lse[at, start : start + 1])
            d_probs = dot_f32(grad, values[seen, lanes], 1, 1)
            delta = jnp.sum(weights * d_probs, axis=1, keepdims=True)
            d_scores = (weights * (d_probs - delta)).astype(low)
            d_query = dot_f32(d_scores, k_seen, 1, 0) * scale
            d_qkv[at, lanes] = turn(d_query, at).astype(low)
            d_keys[seen, :] += dot_f32(d_scores, q_here, 0, 0) * scale
            d_values[seen, :] += dot_f32(weights.astype(low), grad, 0, 0)
        d_qkv[:, cols + start : cols + start + head_dim] = turn(d_keys[...], every).astype(low)
        d_qkv[:, 2 * cols + start : 2 * cols + start + head_dim] = d_values[...].astype(low)

    phases.go("attention_in_grad")

    def output(at):
        partial[at, :] = dot_f32(d_qkv[at, :], heads_weight[...], 1, 1).astype(low)

    by_rows(seq, block, output)
    phases.go("sum_in_plane")
    reduce = plane_reduce(wire, place, partial, got_core, got_one, got_two)
    next(reduce)

    def heads_weights(target):
        at = rows_of(target, by_share)
        g_heads[at, :] = dot_f32(attn_in[:, at], d_qkv[...], 0, 0).astype(low)

    each(n_dp // 2, heads_weights)
    next(reduce)
    each(n_dp // 2, lambda index: heads_weights(index + n_dp // 2))
    heads_chain = chain_reduce(
        wire,
        place,
        [(lambda t: g_heads.at[rows_of(t, by_share), :], heads_below, heads_above)],
    )
    next(heads_chain)
    phases.go("sum_in_plane_end")
    finish(reduce)
    routed_over += [go_over_x(0, 1, 2), go_over_x(1)]

    def norm_one(at):
        d_attn_in = plane_sum(place, partial, got_one, got_two, at)
        x_float = tokens[at, :].astype(f32)
        rstd = lax.rsqrt(jnp.mean(x_float * x_float, axis=1, keepdims=True) + EPS)
        normed = x_float * rstd
        acc[1] += d_attn_in * normed
        d_norm = d_attn_in * gain_one
        input_grad[at, :] = (
            d_hidden[at, :]
            + rstd * (d_norm - normed * jnp.mean(d_norm * normed, axis=1, keepdims=True))
        ).astype(low)

    phases.go("norm_one")
    by_rows(rows, 16, norm_one)

    side_grad = side[0:16, :] + side[16:32, :] + side[32:48, :]
    row_of = lax.broadcasted_iota(jnp.int32, side_grad.shape, 0)
    gain_one_grad = jnp.sum(acc[1], axis=0, keepdims=True)
    gain_two_grad = jnp.sum(acc[0], axis=0, keepdims=True)
    small_rows = jnp.where(
        row_of == n_experts + 1,
        gain_one_grad,
        jnp.where(row_of == n_experts + 2, gain_two_grad, side_grad),
    )
    bias_sums = jnp.sum(d_qkv[...].astype(f32), axis=0, keepdims=True)
    bias_rows = [
        bias_sums[:, start : start + head_dim] for start in range(0, 3 * cols, head_dim)
    ]
    bias_rows += [jnp.zeros((8 - len(bias_rows), head_dim), f32)]
    bias_rows = jnp.concatenate(bias_rows, axis=0)
    for target in range(n_dp * n_ctx):
        stage[target, 0:16, :] = small_rows[:, target * share : (target + 1) * share]
        stage[target, 16:24, :] = bias_rows
    mine = z * n_ctx + c
    small_items = [inside.start(stage.at[mine], landed.at[mine])]
    for dz, dc in others:
        target = lax.bitwise_xor(z, jnp.int32(dz)) * n_ctx + lax.bitwise_xor(c, jnp.int32(dc))
        item = wire.copy(stage.at[target], landed.at[mine], moved(dz, dc, y))
        item.start()
        small_items.append(item)
    phases.go("chains")
    finish(out_chain)
    phases.go("heads_chain")
    finish(heads_chain)
    phases.go("last")

    out_block[...] = g_out[:, rows_of(z, by_share)]
    last = []
    for dc in range(n_ctx):
        to = lax.bitwise_xor(c, jnp.int32(dc))
        pairs = [
            (
                g_heads.at[pl.ds(pl.multiple_of(z * by_share + to * share, share), share), :],
                heads_grad.at[c],
            ),
            (out_block.at[:, rows_of(to, share)], out_weight_grad.at[c]),
        ]
        for src, dst in pairs:
            if dc:
                item = wire.copy(src, dst, moved(0, dc, y))
                item.start()
            else:
                item = inside.start(src, dst)
            last.append(item)

    phases.go("small")
    for item in small_items:
        item.wait_recv()
    total = landed[0, 0:16, :]
    for source in range(1, n_dp * n_ctx):
        total = total + landed[source, 0:16, :]
    over_y[0] = total
    swap = wire.copy(over_y.at[0], over_y.at[1], place.over_y)
    swap.start()
    for context in range(n_ctx):
        sums = landed[context, 16:24, :]
        for source in range(1, n_dp):
            sums = sums + landed[source * n_ctx + context, 16:24, :]
        bias_grad[context] = sums
    swap.wait_recv()
    small_grad[...] = over_y[0] + over_y[1]
    phases.go("wait_all")
    for item in last + shared_last + routed_over:
        item.wait_recv()
    wire.drain()
    phases.go(None)


def moe_forward(
    n_dp, dy_begun, moe_in, smalls, ids, s_gate_in, s_up_in, s_down_in, e_gate, e_up, e_down,
    cols, pick, s_slope, s_silu, s_hidden, e_slope, e_silu, e_hidden, rows_in, part, e_out, shared,
    dy_group,
    x, wg, wu, wd, v_slope, v_silu, v_hidden, r_slope, r_silu, r_hidden, rows, out, sh,
    s_gate, s_up, s_down, send, recv, local,
):
    place_here = Place(n_dp)
    wire = Wire(send, recv)
    z, c, y = place_here.z, place_here.c, place_here.y
    f32, low = jnp.float32, jnp.bfloat16
    inside = Local(local)
    n_experts = ids.shape[0]
    tok_rows = ids.shape[2]
    phases = Phases()
    phases.go("entry")
    mine = z * 2 + y

    def block_of(slot):
        return dy_group.at[rows_of(slot * 2 + y, tok_rows), :]

    y_recv = wire.take(n_dp)
    y_send = wire.take_send(n_dp)

    def over_y(slot):
        ref = block_of(slot)
        return wire.copy_to(ref, ref, place_here.over_y, y_recv + slot, y_send + slot)

    loads = [
        inside.start(src, dst)
        for src, dst in ((moe_in, x), (s_gate_in, s_gate), (s_up_in, s_up), (s_down_in, s_down))
    ]
    near = [(lax.bitwise_xor(z, jnp.int32(dz)), c, y) for dz in range(1, n_dp)]
    barrier(near + [place_here.over_y])
    dy_chain = chain_gather(
        wire,
        place_here,
        lambda slot: [block_of(slot)],
        arrived=lambda slot: over_y(slot).start(),
        begun=True,
    )
    next(dy_chain)
    loads += [inside.start(src, dst) for src, dst in ((e_gate, wg), (e_up, wu), (e_down, wd))]
    hit = jnp.concatenate(
        [jnp.any(ids[s] == mine, axis=0, keepdims=True).astype(f32) for s in range(n_experts)], axis=0
    )
    upto = (
        lax.broadcasted_iota(jnp.int32, (tok_rows, tok_rows), 0)
        <= lax.broadcasted_iota(jnp.int32, (tok_rows, tok_rows), 1)
    ).astype(low)
    place = dot_f32(hit.astype(low), upto, 1, 0) - 1.0
    slots = lax.broadcasted_iota(jnp.int32, (CAP, tok_rows), 0).astype(f32)
    for s in range(n_experts):
        chosen = (hit[s : s + 1] > 0.5) & (place[s : s + 1] == slots)
        pick[s] = jnp.where(chosen, 1.0, 0.0).astype(low)
    phases.go("x_wait")
    for item in loads[:4]:
        item.wait()

    def gated(g, u):
        sigma = 1.0 / (1.0 + jnp.exp(-g))
        silu = g * sigma
        return u * (sigma * (1.0 + g * (1.0 - sigma))), silu, silu * u

    def shared_tile(at):
        here = x[at, :]
        logits = dot_f32(here, smalls[...], 1, 1)
        lane = lax.broadcasted_iota(jnp.int32, logits.shape, 1)
        routed = lane < n_experts
        top = jnp.max(jnp.where(routed, logits, -jnp.inf), axis=1, keepdims=True)
        expo = jnp.where(routed, jnp.exp(jnp.where(routed, logits, top) - top), 0.0)
        probs = expo / jnp.sum(expo, axis=1, keepdims=True)
        mix = jnp.sum(jnp.where(lane == n_experts, logits, 0.0), axis=1, keepdims=True)
        mix = 1.0 / (1.0 + jnp.exp(-mix))
        gate = jnp.sum(jnp.where(lane == mine, probs, 0.0), axis=1, keepdims=True)
        cols[at, 0:16] = jnp.where(
            routed, probs, jnp.where(lane == n_experts, mix, jnp.where(lane == n_experts + 1, gate, 0.0))
        )
        slope, silu, hidden = gated(dot_f32(here, s_gate[...], 1, 0), dot_f32(here, s_up[...], 1, 0))
        v_slope[at, :] = slope.astype(low)
        v_silu[at, :] = silu.astype(low)
        v_hidden[at, :] = hidden.astype(low)
        sh[at, :] = dot_f32(v_hidden[at, :], s_down[...], 1, 0).astype(low)

    phases.go("shared")
    by_rows(x.shape[0], 512, shared_tile)
    phases.go("dy_two")
    next(dy_chain)
    stores = [
        inside.start(src, dst)
        for src, dst in ((v_slope, s_slope), (v_silu, s_silu), (v_hidden, s_hidden), (sh, shared))
    ]

    def gather(s, carry):
        block = x[rows_of(s, tok_rows), :]
        rows[rows_of(s, CAP), :] = dot_f32(pick[s], block, 1, 0).astype(low)
        return carry

    phases.go("gather")
    lax.fori_loop(0, n_experts, gather, 0)
    stores.append(inside.start(rows, rows_in))
    phases.go("w_wait")
    for item in loads[4:]:
        item.wait()

    def routed_tile(at):
        here = rows[at, :]
        slope, silu, hidden = gated(dot_f32(here, wg[...], 1, 0), dot_f32(here, wu[...], 1, 0))
        r_slope[at, :] = slope.astype(low)
        r_silu[at, :] = silu.astype(low)
        r_hidden[at, :] = hidden.astype(low)
        out[at, :] = dot_f32(r_hidden[at, :], wd[...], 1, 0).astype(low)

    phases.go("routed")
    routed_tile(pl.ds(0, 384))
    phases.go("dy_three")
    next(dy_chain)
    phases.go("routed_end")
    routed_tile(pl.ds(384, 384))
    stores.append(inside.start(out, e_out))
    stores += [
        inside.start(src, dst)
        for src, dst in ((r_slope, e_slope), (r_silu, e_silu), (r_hidden, e_hidden))
    ]

    def scatter(s, carry):
        at = rows_of(s, tok_rows)
        back = dot_f32(pick[s], out[rows_of(s, CAP), :], 0, 0)
        mix = cols[at, n_experts : n_experts + 1]
        gate = cols[at, n_experts + 1 : n_experts + 2]
        x[at, :] = (gate * back + mix * sh[at, :].astype(f32)).astype(low)
        return carry

    phases.go("scatter")
    lax.fori_loop(0, n_experts, scatter, 0)
    phases.go("stores")
    stores.append(inside.start(x, part))
    for item in stores:
        item.wait()
    phases.go("over_y")
    finish(dy_chain)
    for slot in range(n_dp):

        @pl.when(z != slot)
        def _():
            over_y(slot).wait_recv()
            over_y(slot).wait_send()

    phases.go(None)


def shared_backward(
    n_dp, dy_group, cols, pick, s_gate_in, s_up_in, s_down_in, s_slope_in, s_silu_in,
    s_hidden, e_out, shared, moe_in,
    grads_in, part, scalars, keep_gate, keep_up, keep_down, give_gate, give_up, give_down,
    dy, out, sh, d_sh, rows, grads, total, x, hidden,
    g_gate, g_up, g_down, got_gate, got_up, got_down,
    s_gate, s_up, s_down, s_slope, s_silu, sums, picked, slot_sums, send, recv, local, slots,
):
    f32, low = jnp.float32, jnp.bfloat16
    inside = Local(local)
    wire = Wire(send, recv)
    place = Place(n_dp)
    n_experts = pick.shape[0]
    tok_rows = pick.shape[2]
    units = s_gate.shape[1]
    lanes = grads.shape[1] // 2
    share = g_gate.shape[1]
    n_ctx = 4
    core = lax.rem(place.c, 2)
    chip = lax.div(place.c, 2)
    phases = Phases()
    phases.go("entry")

    depth = dy.shape[0]

    def fetch(index):
        slot = index % depth
        at = pl.ds(index * tok_rows, tok_rows)
        items = [
            pltpu.make_async_copy(src, dst.at[slot], slots.at[3 * slot + k])
            for k, (src, dst) in enumerate(
                (
                    (dy_group.at[at, :], dy),
                    (e_out.at[pl.ds(index * CAP, CAP), :], out),
                    (shared.at[at, :], sh),
                )
            )
        ]
        for item in items:
            item.start()
        return items

    coming = [fetch(index) for index in range(depth - 1)]
    loads = [
        inside.start(src, dst)
        for src, dst in (
            (s_down_in, s_down), (s_slope_in, s_slope), (s_silu_in, s_silu),
            (s_gate_in, s_gate), (s_up_in, s_up), (moe_in, x), (s_hidden, hidden),
        )
    ]
    barrier([place.core])
    grads[...] = jnp.zeros_like(grads)
    sums[...] = jnp.zeros_like(sums)
    for index in range(n_experts):
        slot = index % depth
        if index + depth - 1 < n_experts:
            coming.append(fetch(index + depth - 1))
        for item in coming[index]:
            item.wait()
        here = pl.ds(index * tok_rows, tok_rows)
        chosen = pick[index].astype(f32)
        gate = jnp.transpose(cols[here, :])[n_experts + 1 : n_experts + 2, :]
        gate = jnp.sum(chosen * gate, axis=1, keepdims=True)
        picked[...] = dot_f32(pick[index], dy[slot], 1, 0)

        def slot_rows(at):
            grad = picked[at, :]
            this = out[slot, at, :].astype(f32)
            slot_sums[at, 0:1] = jnp.sum(this * grad, axis=1, keepdims=True)

        by_rows(CAP, 32, slot_rows)
        rows[pl.ds(index * CAP, CAP), :] = (gate * picked[...]).astype(low)
        d_gate = jnp.sum(chosen * slot_sums[:, 0:1], axis=0, keepdims=True)

        def chunk(at):
            there = pl.ds(pl.multiple_of(index * tok_rows + at.start, at.size), at.size)
            grad = dy[slot, at, :].astype(f32)
            mix = cols[there, n_experts : n_experts + 1]
            d_sh[there, :] = (mix * grad).astype(low)
            sums[at, 0:1] = jnp.sum(sh[slot, at, :].astype(f32) * grad, axis=1, keepdims=True)

        by_rows(tok_rows, 32, chunk)
        shared_dot = jnp.transpose(sums[...])[0:1, :]
        row_of = lax.broadcasted_iota(jnp.int32, (8, tok_rows), 0)
        scalars[index] = jnp.where(row_of == 0, d_gate, jnp.where(row_of == 1, shared_dot, 0.0))
    stores = [inside.start(rows, grads_in)]

    def shared_tile(at):
        d_hidden = dot_f32(d_sh[at, :], s_down[...], 1, 1)
        d_gate = (d_hidden * s_slope[at, :].astype(f32)).astype(low)
        d_up = (d_hidden * s_silu[at, :].astype(f32)).astype(low)
        grads[at, 0:units] = d_gate
        grads[at, lanes : lanes + units] = d_up
        total[at, :] = (dot_f32(d_gate, s_gate[...], 1, 1) + dot_f32(d_up, s_up[...], 1, 1)).astype(low)

    for item in loads[:5]:
        item.wait()
    phases.go("shared")
    by_rows(d_sh.shape[0], 512, shared_tile)
    stores.append(inside.start(total, part))
    for item in loads[5:]:
        item.wait()
    phases.go("in_grads")

    def block_index(dx, dz, sibling):
        side = lax.bitwise_xor(chip, jnp.int32(dx)) * 2
        return dz * n_ctx + side + (1 - core if sibling else core)

    sent = {}

    def to_sibling(dz, mats):
        for dx in (1, 0):
            for grad, got in mats:
                item = wire.copy(grad.at[block_index(dx, dz, True)], got.at[dx, dz], place.core)
                item.start()
                sent.setdefault(dz, []).append(item)

    step = n_ctx * share
    for dz in range(n_dp):
        product = dot_f32(x[:, dz * step : (dz + 1) * step], grads[...], 0, 0)
        for k in range(n_ctx):
            here = slice(k * share, (k + 1) * share)
            g_gate[dz * n_ctx + k] = product[here, 0:units].astype(low)
            g_up[dz * n_ctx + k] = product[here, lanes : lanes + units].astype(low)
        to_sibling(dz, ((g_gate, got_gate), (g_up, got_up)))
    phases.go("down_grads")
    down = {}
    for dz in range(n_dp):
        product = dot_f32(hidden[...], d_sh[:, dz * step : (dz + 1) * step], 0, 0)
        for k in range(n_ctx):
            g_down[dz * n_ctx + k] = product[:, k * share : (k + 1) * share].astype(low)
        for dx in (1, 0):
            item = wire.copy(g_down.at[block_index(dx, dz, True)], got_down.at[dx, dz], place.core)
            item.start()
            down.setdefault(dz, []).append(item)
    phases.go("sums")

    def collect(dx, dz, grad, got, out_ref):
        mine = block_index(dx, dz, False)
        add_block(grad.at[mine], got.at[dx, dz])
        size = grad.shape[1]
        stores.append(inside.start(grad.at[mine], out_ref.at[pl.ds(dz * size, size), :]))

    for dz in range(n_dp):
        for item in sent[dz]:
            item.wait_recv()
        for dx, outs in ((1, (give_gate, give_up)), (0, (keep_gate, keep_up))):
            for grad, got, out_ref in zip((g_gate, g_up), (got_gate, got_up), outs):
                collect(dx, dz, grad, got, out_ref)
    for dz in range(n_dp):
        for item in down[dz]:
            item.wait_recv()
        for dx, out_ref in ((1, give_down), (0, keep_down)):
            collect(dx, dz, g_down, got_down, out_ref)
    phases.go("stores")
    for item in stores:
        item.wait()
    wire.drain()
    phases.go(None)


def routed_backward(
    n_dp, grads_in, rows_in, e_gate, e_up, e_down, slope_in, silu_in, hidden_in, shared_part, scalars,
    keep_sgate, give_sgate, give_sup, give_sdown, pick,
    own_sum, got_scalars, t_sgate, x_sup, x_sdown,
    keep_gate, keep_up, keep_down, give_up, give_down, x_gate,
    wg, wu, wd, grads, rows, slope, silu, hidden, d_hid, d_in, total,
    got_gate, got_up, got_down, got_y, got_dp, x_sgate, sum_sgate, send, recv, local,
):
    f32, low = jnp.float32, jnp.bfloat16
    inside = Local(local)
    wire = Wire(send, recv)
    place = Place(n_dp)
    z, c, y = place.z, place.c, place.y
    n_experts = pick.shape[0]
    tok_rows = pick.shape[2]
    units = wg.shape[1]
    width = rows.shape[1]
    core = lax.rem(c, 2)
    chip = lax.div(c, 2)
    group = z * 2 + y
    phases = Phases()
    phases.go("entry")
    loads = [
        inside.start(src, dst)
        for src, dst in (
            (grads_in, grads), (e_down, wd), (slope_in, slope), (silu_in, silu),
            (e_gate, wg), (e_up, wu), (shared_part, total), (rows_in, rows), (hidden_in, hidden),
            (keep_sgate, sum_sgate),
        )
    ]

    def near(dz, y_to):
        return (lax.bitwise_xor(z, jnp.int32(dz)), c, y_to)

    members = [(dz, y_to) for dz in range(n_dp) for y_to in (y, place.yn) if dz or y_to is not y]
    barrier([place.core, place.over_x] + [near(dz, y_to) for dz, y_to in members])

    over_x = []
    for src, dst in ((give_sgate, x_sgate), (give_sup, x_sup), (give_sdown, x_sdown)):
        item = wire.copy(src, dst, place.over_x)
        item.start()
        over_x.append(item)
    scalar_items = [inside.start(scalars.at[group], got_scalars.at[group])]
    for dz, y_to in members:
        target = lax.bitwise_xor(z, jnp.int32(dz)) * 2 + y_to
        item = wire.copy(scalars.at[target], got_scalars.at[group], near(dz, y_to))
        item.start()
        scalar_items.append(item)
    for item in loads[:4]:
        item.wait()
    phases.go("routed")
    half = grads.shape[0] // 2

    def routed_tile(at, wait):
        d_hidden = dot_f32(grads[at, :], wd[...], 1, 1)
        d_gate = (d_hidden * slope[at, :].astype(f32)).astype(low)
        d_up = (d_hidden * silu[at, :].astype(f32)).astype(low)
        d_hid[at, 0:units] = d_gate
        d_hid[at, units : 2 * units] = d_up
        for item in wait:
            item.wait()
        d_in[at, :] = (dot_f32(d_gate, wg[...], 1, 1) + dot_f32(d_up, wu[...], 1, 1)).astype(low)

    routed_tile(pl.ds(0, half), loads[4:6])
    routed_tile(pl.ds(half, half), [])
    for item in loads[6:]:
        item.wait()
    phases.go("to_tokens")

    def to_tokens(s, carry):
        at = rows_of(s, tok_rows)
        back = dot_f32(pick[s], d_in[rows_of(s, CAP), :], 0, 0)
        total[at, :] = (back + total[at, :].astype(f32)).astype(low)
        return carry

    lax.fori_loop(0, n_experts, to_tokens, 0)

    orders = ((3, 2, 1, 0), (3, 0, 2, 1), (0, 3, 1, 2), (0, 1, 2, 3))
    lower = 1 - lax.div(z, 2)
    order = (
        3 * lower,
        lower * (2 - 2 * z) + (1 - lower) * (7 - 2 * z),
        1 + lax.rem(z, 2),
        z,
    )
    y_swaps = []
    for step in range(n_dp):
        from_row = order[step] * 2 + place.yn
        item = wire.copy(total.at[rows_of(from_row, tok_rows), :], got_y.at[step], place.over_y)
        item.start()
        y_swaps.append(item)
    dp_recv = wire.take(2 * n_dp)
    dp_send = wire.take_send(2 * n_dp)

    def along(target, up):
        slot = target - 1 if up else n_dp - 1 + target
        return wire.copy_to(
            total.at[pl.ds(pl.multiple_of((target * 2 + y) * tok_rows, tok_rows), tok_rows), :],
            got_dp.at[slot],
            place.up if up else place.down,
            dp_recv + slot,
            dp_send + slot,
        )

    def add_from(target, up):
        along(target, up).wait_recv()
        slot = target - 1 if up else n_dp - 1 + target
        add_into(total, pl.ds(0, width), (target * 2 + y) * tok_rows, got_dp.at[slot])

    def over_dp(step):
        y_swaps[step].wait_recv()
        add_into(total, pl.ds(0, width), (order[step] * 2 + y) * tok_rows, got_y.at[step])
        for here in range(n_dp):
            target = orders[here][step]

            @pl.when(z == here)
            def _():
                if target == here:
                    if here > 0:
                        add_from(target, True)
                    if here < n_dp - 1:
                        add_from(target, False)
                else:
                    up = target > here
                    if 0 < here < n_dp - 1:
                        add_from(target, up)
                    along(target, up).start()

    phases.go("shared_gate")
    over_x[0].wait_recv()
    add_block(sum_sgate, x_sgate)
    size = t_sgate.shape[1]
    along_dp = []
    for dz in (2, 3, 1, 0):
        to = lax.bitwise_xor(z, jnp.int32(dz))
        src = sum_sgate.at[rows_of(to, size), :]
        if dz:
            item = wire.copy(src, t_sgate.at[z], near(dz, y))
            item.start()
        else:
            item = inside.start(src, t_sgate.at[z])
        along_dp.append(item)

    def piece(dx, sibling):
        return lax.bitwise_xor(chip, jnp.int32(dx)) * 2 + (1 - core if sibling else core)

    quarter = width // 4
    tile = quarter // 2

    def in_grads(index):
        def one(part, carry):
            at = pl.ds(pl.multiple_of(index * quarter + part * tile, tile), tile)
            value = dot_f32(rows[:, at], d_hid[...], 0, 0)
            wg[at, :] = value[:, 0:units].astype(low)
            wu[at, :] = value[:, units : 2 * units].astype(low)
            return carry

        lax.fori_loop(0, 2, one, 0)

    def down_grads(index):
        at = rows_of(index, quarter)
        wd[:, at] = dot_f32(hidden[...], grads[:, at], 0, 0).astype(low)

    phases.go("in_grads")
    sent = {}
    for dx in (1, 0):
        index = piece(dx, True)
        in_grads(index)
        at = rows_of(index, quarter)
        sent[dx] = [
            wire.copy(wg.at[at, :], got_gate.at[dx], place.core),
            wire.copy(wu.at[at, :], got_up.at[dx], place.core),
        ]
        for item in sent[dx]:
            item.start()
    for dx in (1, 0):
        in_grads(piece(dx, False))
    phases.go("gate_sums")

    def finish_piece(grad, dx, got, target):
        at = rows_of(piece(dx, False), quarter)
        add_block(grad.at[at, :], got.at[dx])
        if target is not None:
            stores.append(inside.start(grad.at[at, :], target))
        return grad.at[at, :]

    stores = []
    sent[1][0].wait_recv()
    gate_over = wire.copy(finish_piece(wg, 1, got_gate, None), x_gate, place.over_x)
    gate_over.start()
    phases.go("over_dp_one")
    over_dp(0)
    phases.go("down_grads")
    down = {}
    for dx in (1, 0):
        index = piece(dx, True)
        down_grads(index)
        down[dx] = wire.copy(wd.at[:, rows_of(index, quarter)], got_down.at[dx], place.core)
        down[dx].start()
    for dx in (1, 0):
        down_grads(piece(dx, False))
    phases.go("over_dp_two")
    over_dp(1)
    phases.go("sums")
    sent[1][1].wait_recv()
    finish_piece(wu, 1, got_up, give_up)
    for item in sent[0]:
        item.wait_recv()
    finish_piece(wg, 0, got_gate, keep_gate)
    finish_piece(wu, 0, got_up, keep_up)
    for dx, target in ((1, give_down), (0, keep_down)):
        down[dx].wait_recv()
        at = rows_of(piece(dx, False), quarter)
        add_into(wd, at, 0, got_down.at[dx])
        stores.append(inside.start(wd.at[:, at], target))
    phases.go("over_dp_three")
    over_dp(2)
    phases.go("over_dp_own")
    over_dp(3)
    for here in range(n_dp):

        @pl.when(z == here)
        def _():
            for target in range(n_dp):
                if target != here:
                    along(target, target > here).wait_send()


    def add_up(at):
        mine = pl.ds(pl.multiple_of(group * tok_rows + at.start, at.size), at.size)
        own_sum[at, :] = total[mine, :].astype(f32)

    by_rows(tok_rows, 16, add_up)
    phases.go("wait_all")
    for item in stores:
        item.wait()
    for item in over_x[1:] + scalar_items + along_dp + [gate_over]:
        item.wait_recv()
    wire.drain()
    phases.go(None)


def finish_grads(n_ctx, *refs):
    (
        t_gate, t_up, t_down, own_gate, own_up, own_down,
        far_gate, far_up, far_down, heads, out_weight, hidden, moe_sum,
        o_sgate, o_sup, o_sdown, o_egate, o_eup, o_edown, o_query, o_key, o_value, o_out, o_mixed,
    ) = refs
    f32 = jnp.float32
    n_dp, share, units = t_gate.shape
    for source, target in ((t_gate, o_sgate), (t_up, o_sup)):
        target[...] = jnp.concatenate([source[k].astype(f32) for k in range(n_dp)], axis=1)
    for k in range(n_dp):
        o_sdown[k * units : (k + 1) * units, :] = t_down[k].astype(f32)
    for own, far, target in (
        (own_gate, far_gate, o_egate), (own_up, far_up, o_eup), (own_down, far_down, o_edown),
    ):

        def add(at):
            target[at, :] = own[at, :].astype(f32) + far[at, :].astype(f32)

        by_rows(target.shape[0], 32, add)
    o_mixed[...] = (hidden[...] + moe_sum[...].astype(f32)).astype(o_mixed.dtype)
    cols = heads.shape[2] // 3
    for k, target in enumerate((o_query, o_key, o_value)):
        for c in range(n_ctx):
            target[:, c * cols : (c + 1) * cols] = heads[c, :, k * cols : (k + 1) * cols].astype(f32)
    for c in range(n_ctx):
        o_out[c * cols : (c + 1) * cols, :] = out_weight[c].astype(f32)


def whole_tables(seq_len, head_dim):
    half = head_dim // 2
    freq = np.float32(THETA) ** (-(2.0 * np.arange(half, dtype=np.float32)) / np.float32(head_dim))
    angle = np.arange(seq_len, dtype=np.float32)[:, None] * freq.astype(np.float32)[None, :]
    cosine, sine = np.cos(angle), np.sin(angle)
    return (
        jnp.asarray(np.concatenate([cosine, cosine], axis=1), jnp.float32),
        jnp.asarray(np.concatenate([-sine, sine], axis=1), jnp.float32),
    )


def tokens_plan(
    tokens,
    out_grad,
    expert_ids,
    norm1_gain,
    w_query,
    w_key,
    w_value,
    query_bias_heads,
    bias_key,
    bias_value,
    w_out,
    norm2_gain,
    w_router,
    shared_mix,
    shared_in_gate,
    shared_in_up,
    shared_down,
    expert_gate,
    expert_up,
    expert_down,
):
    low = jnp.bfloat16
    f32 = jnp.float32
    tok_rows, width = tokens.shape
    n_dp, n_ctx, n_half = (lax.axis_size(name) for name in (DP, CONTEXT, EXPERT))
    dp, ctx, half = (lax.axis_index(name) for name in (DP, CONTEXT, EXPERT))
    half_heads, head_dim = query_bias_heads.shape
    heads = half_heads // n_ctx
    cols = heads * head_dim
    seq_len = tok_rows * n_ctx * n_half
    n_blocks = seq_len // BLOCK
    n_experts = w_router.shape[1]
    n_group = n_dp * n_half
    my_expert = dp * n_half + half

    def group_out(rows):
        return lax.psum_scatter(rows, (DP, EXPERT), scatter_dimension=0, tiled=True)

    small = jnp.concatenate(
        [w_router.T, shared_mix[None], norm1_gain[None], norm2_gain[None]], axis=0
    )
    small = jnp.pad(small, ((0, 16 - small.shape[0]), (0, 0)))
    ids = jnp.pad(expert_ids.T, ((0, 8 - expert_ids.shape[1]), (0, 0)), constant_values=-1)
    hidden_units = shared_in_gate.shape[1] // n_dp

    biases = jnp.stack([query_bias_heads, bias_key, bias_value]).astype(f32)
    biases = lax.dynamic_slice_in_dim(biases, ctx * heads, heads, 1).reshape(3, cols)
    cosine, sine = whole_tables(seq_len, head_dim)
    vmem = pl.BlockSpec(memory_space=pltpu.VMEM)
    anywhere = pl.BlockSpec(memory_space=pl.ANY)
    share = w_query.shape[0]
    half_width = width // 2
    (
        attn_in, query, keys, values, attn, lse, hidden_own, moe_in,
        heads_weight, wo, sg, su, sd, small, ids_group, dy_begun,
    ) = pl.pallas_call(
        lambda *refs: forward_kernel(n_blocks, n_dp, *refs),
        out_shape=[
            like((seq_len, width), low),
            like((seq_len, cols), low),
            like((seq_len, cols), low),
            like((seq_len, cols), low),
            like((seq_len, cols), low),
            like((seq_len, cols), f32),
            like((tok_rows, width), f32),
            like((n_group * tok_rows, width), low),
            like((width, 3 * cols), low),
            like((cols, width), low),
            like((n_dp, n_ctx, share, hidden_units), low),
            like((n_dp, n_ctx, share, hidden_units), low),
            like((hidden_units, width), low),
            like((16, width), low),
            like((n_group, 8, tok_rows), jnp.int32),
            like((n_group * tok_rows, width), low),
        ],
        in_specs=[anywhere] * 11 + [vmem] * 3,
        out_specs=[anywhere] * 13 + [vmem] + [anywhere] * 2,
        scratch_shapes=[
            pltpu.VMEM((seq_len, width), low),
            pltpu.VMEM((seq_len, width), low),
            pltpu.VMEM((4, tok_rows, width), low),
            pltpu.VMEM((4, tok_rows, half_width), low),
            pltpu.VMEM((2, tok_rows, half_width), low),
            pltpu.VMEM((seq_len, width), low),
            pltpu.VMEM((seq_len, cols), low),
            pltpu.VMEM((seq_len, cols), low),
            pltpu.VMEM((seq_len, cols), low),
            pltpu.VMEM((seq_len, cols), low),
            pltpu.VMEM((seq_len, cols), f32),
            pltpu.VMEM((tok_rows, width), f32),
            pltpu.VMEM((width, 3 * cols), low),
            pltpu.VMEM((cols, width), low),
            pltpu.VMEM((2, share, n_dp * hidden_units), low),
            pltpu.VMEM((2, n_dp, share, hidden_units), low),
            pltpu.SemaphoreType.DMA((160,)),
            pltpu.SemaphoreType.DMA((160,)),
            pltpu.SemaphoreType.DMA((32,)),
        ],
        name="forward",
        compiler_params=pltpu.CompilerParams(
            collective_id=1, has_side_effects=True, vmem_limit_bytes=60 * 2**20
        ),
    )(
        tokens, out_grad, small, ids, w_query, w_key, w_value, w_out,
        shared_in_gate, shared_in_up, shared_down, biases, cosine, sine,
    )
    sg, su = sg.reshape(width, hidden_units), su.reshape(width, hidden_units)
    units = expert_gate.shape[2]
    s_weights = [
        pltpu.VMEM((width, hidden_units), low),
        pltpu.VMEM((width, hidden_units), low),
        pltpu.VMEM((hidden_units, width), low),
    ]
    gate_weight, up_weight, down_weight = expert_gate[0], expert_up[0], expert_down[0]
    slots = n_group * CAP
    group_rows = n_group * tok_rows
    (
        token_cols, pick, s_slope, s_silu, s_hidden, e_slope, e_silu, e_hidden, rows_in,
        moe_part, e_out, shared, dy_group,
    ) = pl.pallas_call(
        lambda *refs: moe_forward(n_dp, *refs),
        out_shape=[
            like((group_rows, 128), f32),
            like((n_group, CAP, tok_rows), low),
        ]
        + [like((group_rows, hidden_units), low)] * 3
        + [like((slots, units), low)] * 3
        + [
            like((slots, width), low),
            like((group_rows, width), low),
            like((slots, width), low),
            like((group_rows, width), low),
            like((group_rows, width), low),
        ],
        in_specs=[anywhere] * 2 + [vmem] * 2 + [anywhere] * 6,
        out_specs=[vmem] * 2 + [anywhere] * 11,
        scratch_shapes=[
            pltpu.VMEM((group_rows, width), low),
            pltpu.VMEM((width, units), low),
            pltpu.VMEM((width, units), low),
            pltpu.VMEM((units, width), low),
        ]
        + [pltpu.VMEM((group_rows, hidden_units), low)] * 3
        + [pltpu.VMEM((slots, units), low)] * 3
        + [pltpu.VMEM((slots, width), low)] * 2
        + [pltpu.VMEM((group_rows, width), low)]
        + s_weights
        + [pltpu.SemaphoreType.DMA((16,))] * 2
        + [pltpu.SemaphoreType.DMA((24,))],
        name="moe_forward",
        compiler_params=pltpu.CompilerParams(
            collective_id=3, has_side_effects=True, vmem_limit_bytes=63 * 2**20
        ),
        cost_estimate=pl.CostEstimate(
            flops=6 * width * (group_rows * hidden_units + slots * units),
            bytes_accessed=2 * (9 * width * units + 4 * group_rows * width),
            transcendentals=0,
        ),
        input_output_aliases={0: 12},
    )(dy_begun, moe_in, small, ids_group, sg, su, sd, gate_weight, up_weight, down_weight)
    lanes = -(-hidden_units // 128) * 128
    block_kinds = [(n_dp, share, hidden_units)] * 2 + [(n_dp, hidden_units, share)]
    shared_all = [(n_dp * n_ctx, share, hidden_units)] * 2 + [(n_dp * n_ctx, hidden_units, share)]
    results = pl.pallas_call(
        lambda *refs: shared_backward(n_dp, *refs),
        out_shape=[
            like((slots, width), low),
            like((group_rows, width), low),
            like((n_group, 8, tok_rows), f32),
        ]
        + [like((kind[0] * kind[1], kind[2]), low) for kind in block_kinds] * 2,
        in_specs=[anywhere] + [vmem] * 2 + [anywhere] * 9,
        out_specs=[anywhere] * 2 + [vmem] + [anywhere] * 6,
        scratch_shapes=[
            pltpu.VMEM((4, tok_rows, width), low),
            pltpu.VMEM((4, CAP, width), low),
            pltpu.VMEM((4, tok_rows, width), low),
            pltpu.VMEM((group_rows, width), low),
            pltpu.VMEM((slots, width), low),
            pltpu.VMEM((group_rows, 2 * lanes), low),
            pltpu.VMEM((group_rows, width), low),
            pltpu.VMEM((group_rows, width), low),
            pltpu.VMEM((group_rows, hidden_units), low),
        ]
        + [pltpu.VMEM(kind, low) for kind in shared_all]
        + [pltpu.VMEM((2, *kind), low) for kind in block_kinds]
        + s_weights
        + [pltpu.VMEM((group_rows, hidden_units), low)] * 2
        + [
            pltpu.VMEM((tok_rows, 128), f32),
            pltpu.VMEM((CAP, width), f32),
            pltpu.VMEM((CAP, 128), f32),
        ]
        + [pltpu.SemaphoreType.DMA((32,))] * 2
        + [pltpu.SemaphoreType.DMA((48,)), pltpu.SemaphoreType.DMA((12,))],
        name="shared_backward",
        compiler_params=pltpu.CompilerParams(
            collective_id=4, has_side_effects=True, vmem_limit_bytes=63 * 2**20
        ),
        cost_estimate=pl.CostEstimate(
            flops=12 * width * group_rows * hidden_units,
            bytes_accessed=2 * (9 * width * hidden_units + 8 * group_rows * width),
            transcendentals=0,
        ),
    )(
        dy_group, token_cols, pick, sg, su, sd, s_slope, s_silu, s_hidden, e_out, shared, moe_in,
    )
    grads_in, shared_part, scalars = results[:3]
    keep = results[3:6]
    give = results[6:9]
    quarter = width // n_ctx
    e_wide, e_tall = (quarter, units), (units, quarter)
    flat_kinds = [(kind[0] * kind[1], kind[2]) for kind in block_kinds]
    (
        own_sum, got_scalars, t_sgate, x_sup, x_sdown,
        keep_gate, keep_up, keep_down, give_up, give_down, x_gate,
    ) = pl.pallas_call(
        lambda *refs: routed_backward(n_dp, *refs),
        out_shape=[like((tok_rows, width), f32), like((n_group, 8, tok_rows), f32)]
        + [like(block_kinds[0], low)]
        + [like(kind, low) for kind in flat_kinds[1:]]
        + [like(kind, low) for kind in (e_wide, e_wide, e_tall, e_wide, e_tall, e_wide)],
        in_specs=[anywhere] * 14 + [vmem],
        out_specs=[vmem] + [anywhere] * 10,
        scratch_shapes=[
            pltpu.VMEM((width, units), low),
            pltpu.VMEM((width, units), low),
            pltpu.VMEM((units, width), low),
            pltpu.VMEM((slots, width), low),
            pltpu.VMEM((slots, width), low),
            pltpu.VMEM((slots, units), low),
            pltpu.VMEM((slots, units), low),
            pltpu.VMEM((slots, units), low),
            pltpu.VMEM((slots, 2 * units), low),
            pltpu.VMEM((slots, width), low),
            pltpu.VMEM((group_rows, width), low),
            pltpu.VMEM((2, *e_wide), low),
            pltpu.VMEM((2, *e_wide), low),
            pltpu.VMEM((2, *e_tall), low),
            pltpu.VMEM((n_dp, tok_rows, width), low),
            pltpu.VMEM((2 * (n_dp - 1), tok_rows, width), low),
            pltpu.VMEM(flat_kinds[0], low),
            pltpu.VMEM(flat_kinds[0], low),
            pltpu.SemaphoreType.DMA((32,)),
            pltpu.SemaphoreType.DMA((32,)),
            pltpu.SemaphoreType.DMA((24,)),
        ],
        name="routed_backward",
        compiler_params=pltpu.CompilerParams(
            collective_id=5, has_side_effects=True, vmem_limit_bytes=63 * 2**20
        ),
        cost_estimate=pl.CostEstimate(
            flops=12 * width * slots * units,
            bytes_accessed=2 * (12 * width * units + 4 * group_rows * width),
            transcendentals=0,
        ),
    )(
        grads_in, rows_in, gate_weight, up_weight, down_weight, e_slope, e_silu, e_hidden,
        shared_part, scalars, keep[0], *give, pick,
    )
    moe_sum = group_out(moe_part)

    own_cols = lax.dynamic_slice_in_dim(token_cols, my_expert * tok_rows, tok_rows, 0)
    probs_own = own_cols[:, :n_experts].T
    mix_own = own_cols[:, n_experts][None]
    by_share = n_ctx * share
    s_wide = (share, hidden_units)
    s_tall = (hidden_units, share)
    s_kinds = (s_wide, s_wide, s_tall)
    e_kinds = (e_wide, e_wide, e_tall)
    results = pl.pallas_call(
        lambda *refs: backward_kernel(n_blocks, n_dp, *refs),
        out_shape=[
            like((tok_rows, width), low),
            like((n_ctx, share, 3 * cols), low),
            like((n_ctx, cols, share), low),
            like((16, share), f32),
            like((n_ctx, 8, head_dim), f32),
        ]
        + [like((n_dp, *kind), low) for kind in s_kinds[1:]]
        + [like(kind, low) for kind in e_kinds[1:]]
        + [like((n_dp, *kind), low) for kind in s_kinds[1:]],
        in_specs=[vmem] * 2 + [anywhere] * 9 + [vmem] * 3 + [anywhere] * 10,
        out_specs=[vmem] + [anywhere] * 2 + [vmem] * 2 + [anywhere] * 6,
        scratch_shapes=[
            pltpu.VMEM((seq_len, width), low),
            pltpu.VMEM((tok_rows, width), f32),
            pltpu.VMEM((tok_rows, width), f32),
            pltpu.VMEM((tok_rows, width), low),
            pltpu.VMEM((48, tok_rows), low),
            pltpu.VMEM((2, 16, width), f32),
            pltpu.VMEM((seq_len, width), low),
            pltpu.VMEM((seq_len, cols), low),
            pltpu.VMEM((seq_len, 3 * cols), low),
            pltpu.VMEM((seq_len, head_dim), f32),
            pltpu.VMEM((seq_len, head_dim), f32),
            pltpu.VMEM((4, tok_rows, width), low),
            pltpu.VMEM((4, tok_rows, half_width), low),
            pltpu.VMEM((2, tok_rows, half_width), low),
            pltpu.VMEM((width, 3 * cols), low),
            pltpu.VMEM((cols, width), low),
            pltpu.VMEM((n_dp, by_share, 3 * cols), low),
            pltpu.VMEM((n_dp, by_share, 3 * cols), low),
            pltpu.VMEM((n_dp, cols, by_share), low),
            pltpu.VMEM((n_dp, cols, by_share), low),
            pltpu.VMEM((cols, by_share), low),
            pltpu.VMEM((n_dp * n_ctx, 24, share), f32),
            pltpu.VMEM((n_dp * n_ctx, 24, share), f32),
            pltpu.VMEM((2, 16, share), f32),
            pltpu.VMEM((3, 2, *s_wide), low),
            pltpu.VMEM((3, 2, *s_tall), low),
            pltpu.VMEM((tok_rows, width), f32),
            pltpu.VMEM((tok_rows, width), low),
            pltpu.VMEM((tok_rows, width), low),
            pltpu.VMEM((width, 3 * cols), low),
            pltpu.VMEM((cols, width), low),
            pltpu.VMEM((seq_len, cols), low),
            pltpu.VMEM((seq_len, cols), low),
            pltpu.VMEM((seq_len, cols), low),
            pltpu.VMEM((seq_len, cols), low),
            pltpu.VMEM((seq_len, cols), f32),
            pltpu.VMEM((seq_len, width), low),
            pltpu.VMEM((seq_len, head_dim), f32),
            pltpu.VMEM((seq_len, head_dim), f32),
            pltpu.SemaphoreType.DMA((160,)),
            pltpu.SemaphoreType.DMA((160,)),
            pltpu.SemaphoreType.DMA((32,)),
            pltpu.SemaphoreType.DMA((6,)),
        ],
        name="backward",
        compiler_params=pltpu.CompilerParams(
            collective_id=2, has_side_effects=True, vmem_limit_bytes=63 * 2**20
        ),
    )(
        own_sum, got_scalars, *keep[1:], x_sup, x_sdown, give_up, give_down,
        hidden_own, out_grad, tokens, small, probs_own, mix_own,
        heads_weight, wo, query, keys, values, attn, lse, attn_in, cosine, sine,
    )
    input_grad, heads_grad, out_weight_grad, small_grad, bias_grad = results[:5]
    s_done = (t_sgate, *results[5:7])
    e_own, e_other = (keep_gate, keep_up, keep_down), (x_gate, *results[7:9])
    finished = pl.pallas_call(
        lambda *refs: finish_grads(n_ctx, *refs),
        out_shape=[
            like((share, n_dp * hidden_units), f32),
            like((share, n_dp * hidden_units), f32),
            like((n_dp * hidden_units, share), f32),
            like(e_wide, f32),
            like(e_wide, f32),
            like(e_tall, f32),
            like((share, n_ctx * cols), f32),
            like((share, n_ctx * cols), f32),
            like((share, n_ctx * cols), f32),
            like((n_ctx * cols, share), f32),
            like((tok_rows, width), low),
        ],
        grid=(1,),
        in_specs=[pl.BlockSpec((n_dp, *kind), lambda i: (0, 0, 0)) for kind in s_kinds]
        + [pl.BlockSpec(kind, lambda i: (0, 0)) for kind in e_kinds * 2]
        + [
            pl.BlockSpec(heads_grad.shape, lambda i: (0, 0, 0)),
            pl.BlockSpec(out_weight_grad.shape, lambda i: (0, 0, 0)),
            pl.BlockSpec((tok_rows, width), lambda i: (0, 0)),
            pl.BlockSpec((tok_rows, width), lambda i: (0, 0)),
        ],
        out_specs=[
            pl.BlockSpec((share, n_dp * hidden_units), lambda i: (0, 0)),
            pl.BlockSpec((share, n_dp * hidden_units), lambda i: (0, 0)),
            pl.BlockSpec((n_dp * hidden_units, share), lambda i: (0, 0)),
            pl.BlockSpec(e_wide, lambda i: (0, 0)),
            pl.BlockSpec(e_wide, lambda i: (0, 0)),
            pl.BlockSpec(e_tall, lambda i: (0, 0)),
            pl.BlockSpec((share, n_ctx * cols), lambda i: (0, 0)),
            pl.BlockSpec((share, n_ctx * cols), lambda i: (0, 0)),
            pl.BlockSpec((share, n_ctx * cols), lambda i: (0, 0)),
            pl.BlockSpec((n_ctx * cols, share), lambda i: (0, 0)),
            pl.BlockSpec((tok_rows, width), lambda i: (0, 0)),
        ],
        name="finish_grads",
        compiler_params=pltpu.CompilerParams(vmem_limit_bytes=63 * 2**20),
    )(*s_done, *e_own, *e_other, heads_grad, out_weight_grad, hidden_own, moe_sum)
    grad_sgate, grad_sup, grad_sdown = finished[:3]
    routed = [item[None] for item in finished[3:6]]
    heads_grad = finished[6:9]
    grad_out, mixed = finished[9:11]
    bias_sum = bias_grad[:, : 3 * heads].reshape(n_ctx, 3, heads, head_dim)
    bias_sum = bias_sum.transpose(1, 0, 2, 3).reshape(3, half_heads, head_dim)
    bias_share = head_dim // (n_dp * n_ctx)
    bias_sum = lax.dynamic_slice_in_dim(bias_sum, (dp * n_ctx + ctx) * bias_share, bias_share, 2)
    return (
        mixed,
        input_grad,
        small_grad[n_experts + 1],
        heads_grad[0],
        heads_grad[1],
        heads_grad[2],
        bias_sum[0],
        bias_sum[1],
        bias_sum[2],
        grad_out,
        small_grad[n_experts + 2],
        small_grad[:n_experts].T,
        small_grad[n_experts],
        grad_sgate,
        grad_sup,
        grad_sdown,
        routed[0],
        routed[1],
        routed[2],
    )


def on_device(*arrays):
    sizes = [lax.axis_size(name) for name in (DP, CONTEXT, EXPERT)]
    if sizes == [4, 4, 2] and arrays[7].shape[0] % sizes[1] == 0:
        return tokens_plan(*arrays)
    return weights_plan(*arrays)


def solution(mesh):
    placed = (
        P((DP, CONTEXT, EXPERT), None),
        P((DP, CONTEXT, EXPERT), None),
        P((DP, CONTEXT, EXPERT), None),
        P((DP, CONTEXT)),
        P((DP, CONTEXT), EXPERT),
        P((DP, CONTEXT), EXPERT),
        P((DP, CONTEXT), EXPERT),
        P(EXPERT, None),
        P(EXPERT, None),
        P(EXPERT, None),
        P(EXPERT, (DP, CONTEXT)),
        P((DP, CONTEXT)),
        P((DP, CONTEXT), None),
        P((DP, CONTEXT)),
        P((DP, CONTEXT), EXPERT),
        P((DP, CONTEXT), EXPERT),
        P(EXPERT, (DP, CONTEXT)),
        P((DP, EXPERT), None, None),
        P((DP, EXPERT), None, None),
        P((DP, EXPERT), None, None),
    )
    return jax.shard_map(
        on_device,
        mesh=mesh,
        in_specs=placed,
        out_specs=(
            P((DP, CONTEXT, EXPERT), None),
            P((DP, CONTEXT, EXPERT), None),
            P((DP, CONTEXT)),
            P((DP, CONTEXT), EXPERT),
            P((DP, CONTEXT), EXPERT),
            P((DP, CONTEXT), EXPERT),
            P(EXPERT, (DP, CONTEXT)),
            P(EXPERT, (DP, CONTEXT)),
            P(EXPERT, (DP, CONTEXT)),
            P(EXPERT, (DP, CONTEXT)),
            P((DP, CONTEXT)),
            P((DP, CONTEXT), None),
            P((DP, CONTEXT)),
            P((DP, CONTEXT), EXPERT),
            P((DP, CONTEXT), EXPERT),
            P(EXPERT, (DP, CONTEXT)),
            P((DP, EXPERT), CONTEXT, None),
            P((DP, EXPERT), CONTEXT, None),
            P((DP, EXPERT), None, CONTEXT),
        ),
        check_vma=False,
    )
```

```python
import math

import jax
import jax.numpy as jnp
import numpy as np
from jax import lax
from jax.experimental import pallas as pl
from jax.experimental.pallas import tpu as pltpu
from jax.sharding import PartitionSpec as P

DP, CONTEXT, EXPERT = "dp", "context", "expert"
BLOCK = 256
CAP = 96


EPS = 1e-06
THETA = 1000000.0
HIGH = lax.Precision.HIGHEST


def rope_tables(positions, head_dim):
    half = head_dim // 2
    freq = THETA ** (-(2.0 * jnp.arange(half, dtype=jnp.float32)) / head_dim)
    angle = positions.astype(jnp.float32)[:, None] * freq[None, :]
    return (jnp.cos(angle)[:, None, :], jnp.sin(angle)[:, None, :])


def rotate(values, cosine, sine):
    half = values.shape[-1] // 2
    first = values[..., :half]
    second = values[..., half:]
    return jnp.concatenate(
        [first * cosine - second * sine, second * cosine + first * sine], axis=-1
    )


def rotate_back(values, cosine, sine):
    half = values.shape[-1] // 2
    first = values[..., :half]
    second = values[..., half:]
    return jnp.concatenate(
        [first * cosine + second * sine, second * cosine - first * sine], axis=-1
    )


def to_groups(matrix, groups, group_size, head_dim):
    return matrix.reshape(matrix.shape[0], groups, group_size, head_dim).transpose(1, 2, 0, 3)


def from_groups(stacked):
    return stacked.transpose(2, 0, 1, 3).reshape(stacked.shape[2], -1)


def silu_slope(values):
    sigma = jax.nn.sigmoid(values)
    return sigma * (1.0 + values * (1.0 - sigma))


def left_operand(left, right):
    return jnp.dot(left.T, right, preferred_element_type=jnp.float32)


def mat_right(left, right):
    return jnp.dot(left, right.T, preferred_element_type=jnp.float32)


def weights_plan(
    tokens,
    out_grad,
    expert_ids,
    norm1_gain,
    w_query,
    w_key,
    w_value,
    query_bias_heads,
    bias_key,
    bias_value,
    w_out,
    norm2_gain,
    w_router,
    shared_mix,
    shared_in_gate,
    shared_in_up,
    shared_down,
    expert_gate,
    expert_up,
    expert_down,
):
    tok_rows = tokens.shape[0]
    width = tokens.shape[1]
    my_half = lax.axis_index(EXPERT)
    my_piece = lax.axis_index(CONTEXT)
    n_pieces = lax.axis_size(CONTEXT)
    local_heads = query_bias_heads.shape[0]
    head_dim = query_bias_heads.shape[1]
    group_size = 2
    groups = local_heads // group_size
    score_scale = 1.0 / math.sqrt(head_dim)
    (
        full_query,
        full_key,
        full_value,
        full_out,
        full_sgate,
        full_sup,
        full_sdown,
        full_router,
        full_mix,
        full_gain_one,
        full_gain_two,
    ) = (
        lax.all_gather(w_query, (DP, CONTEXT), axis=0, tiled=True),
        lax.all_gather(w_key, (DP, CONTEXT), axis=0, tiled=True),
        lax.all_gather(w_value, (DP, CONTEXT), axis=0, tiled=True),
        lax.all_gather(w_out, (DP, CONTEXT), axis=1, tiled=True),
        lax.all_gather(shared_in_gate, (DP, CONTEXT), axis=0, tiled=True),
        lax.all_gather(shared_in_up, (DP, CONTEXT), axis=0, tiled=True),
        lax.all_gather(shared_down, (DP, CONTEXT), axis=1, tiled=True),
        lax.all_gather(w_router, (DP, CONTEXT), axis=0, tiled=True),
        lax.all_gather(shared_mix, (DP, CONTEXT), axis=0, tiled=True),
        lax.all_gather(norm1_gain, (DP, CONTEXT), axis=0, tiled=True),
        lax.all_gather(norm2_gain, (DP, CONTEXT), axis=0, tiled=True),
    )
    x_piece, dy_piece = (
        lax.all_gather(tokens, EXPERT, axis=0, tiled=True),
        lax.all_gather(out_grad, EXPERT, axis=0, tiled=True),
    )
    piece_rows = x_piece.shape[0]
    seq_len = piece_rows * n_pieces
    own_start = my_half * tok_rows
    positions = my_piece * piece_rows + jnp.arange(piece_rows)
    cosine, sine = rope_tables(positions, head_dim)
    query_blocks = positions // BLOCK
    key_blocks = jnp.arange(seq_len) // BLOCK
    visible = key_blocks[None, :] <= query_blocks[:, None]
    x_float = x_piece.astype(jnp.float32)
    rstd_one = lax.rsqrt(jnp.mean(x_float * x_float, axis=1, keepdims=True) + EPS)
    normed_one = x_float * rstd_one
    gain_one = full_gain_one.astype(jnp.float32)
    attn_in = (normed_one * gain_one).astype(jnp.bfloat16)
    q_pre = jnp.dot(
        attn_in, full_query, preferred_element_type=jnp.float32
    ) + query_bias_heads.astype(jnp.float32).reshape(-1)
    k_pre = jnp.dot(attn_in, full_key, preferred_element_type=jnp.float32) + bias_key.astype(
        jnp.float32
    ).reshape(-1)
    v_pre = jnp.dot(attn_in, full_value, preferred_element_type=jnp.float32) + bias_value.astype(
        jnp.float32
    ).reshape(-1)
    q_rot = (
        rotate(q_pre.reshape(piece_rows, local_heads, head_dim), cosine, sine)
        .reshape(piece_rows, -1)
        .astype(jnp.bfloat16)
    )
    k_rot = (
        rotate(k_pre.reshape(piece_rows, local_heads, head_dim), cosine, sine)
        .reshape(piece_rows, -1)
        .astype(jnp.bfloat16)
    )
    v_low = v_pre.astype(jnp.bfloat16)
    keys_all, values_all = (
        lax.all_gather(k_rot, CONTEXT, axis=0, tiled=True),
        lax.all_gather(v_low, CONTEXT, axis=0, tiled=True),
    )
    query_grp = to_groups(q_rot, groups, group_size, head_dim)
    keys_grp = to_groups(keys_all, groups, group_size, head_dim)
    values_grp = to_groups(values_all, groups, group_size, head_dim)

    def attend_group(args):
        group_query, group_keys, group_values = args
        scores = (
            jnp.einsum("hqd,hkd->hqk", group_query, group_keys, preferred_element_type=jnp.float32)
            * score_scale
        )
        scores = jnp.where(visible[None], scores, -jnp.inf)
        row_top = jnp.max(scores, axis=2, keepdims=True)
        expo = jnp.exp(scores - row_top)
        totals = jnp.sum(expo, axis=2, keepdims=True)
        probs = (expo / totals).astype(jnp.bfloat16)
        result = jnp.einsum("hqk,hkd->hqd", probs, group_values, preferred_element_type=jnp.float32)
        return (result, row_top[..., 0] + jnp.log(totals[..., 0]))

    attn_grp, lse_grp = lax.map(attend_group, (query_grp, keys_grp, values_grp))
    attn_low = from_groups(attn_grp).astype(jnp.bfloat16)
    out_partial = jnp.dot(attn_low, full_out, preferred_element_type=jnp.float32)
    out_full = lax.psum(out_partial, EXPERT)
    hidden_one = x_float + out_full
    rstd_two = lax.rsqrt(jnp.mean(hidden_one * hidden_one, axis=1, keepdims=True) + EPS)
    normed_two = hidden_one * rstd_two
    gain_two = full_gain_two.astype(jnp.float32)
    moe_in = (normed_two * gain_two).astype(jnp.bfloat16)
    mix = jax.nn.sigmoid(jnp.dot(moe_in, full_mix, preferred_element_type=jnp.float32))
    s_gate = jnp.dot(moe_in, full_sgate, preferred_element_type=jnp.float32)
    s_up = jnp.dot(moe_in, full_sup, preferred_element_type=jnp.float32)
    s_silu = jax.nn.silu(s_gate)
    s_hidden = (s_silu * s_up).astype(jnp.bfloat16)
    shared_own = lax.psum_scatter(
        jnp.dot(s_hidden, full_sdown, preferred_element_type=jnp.float32),
        EXPERT,
        scatter_dimension=0,
        tiled=True,
    )
    moe_own = lax.dynamic_slice_in_dim(moe_in, own_start, tok_rows, 0)
    hidden_own = lax.dynamic_slice_in_dim(hidden_one, own_start, tok_rows, 0)
    mix_own = lax.dynamic_slice_in_dim(mix, own_start, tok_rows, 0)
    dy_own = out_grad.astype(jnp.float32)
    n_experts = full_router.shape[1]
    router_probs = jax.nn.softmax(
        jnp.dot(moe_own, full_router, preferred_element_type=jnp.float32), axis=1
    )
    picked = (expert_ids[:, :, None] == jnp.arange(n_experts)[None, None, :]).astype(jnp.float32)
    gates = jnp.sum(picked * router_probs[:, None, :], axis=2)
    route_hot = (
        (expert_ids[:, :, None] == jnp.arange(n_experts)[None, None, :])
        .astype(jnp.int32)
        .reshape(-1, n_experts)
    )
    earlier = jnp.cumsum(route_hot, axis=0) - route_hot
    slots = jnp.sum(earlier * route_hot, axis=1)
    places = expert_ids.reshape(-1) * CAP + slots
    route_rows = jnp.repeat(moe_own, expert_ids.shape[1], axis=0)
    route_grads = (
        gates.reshape(-1)[:, None] * jnp.repeat(dy_own, expert_ids.shape[1], axis=0)
    ).astype(jnp.bfloat16)
    send_rows = (
        jnp.zeros((n_experts * CAP, width), jnp.bfloat16)
        .at[places]
        .set(route_rows)
        .reshape(n_experts, CAP, width)
    )
    send_grads = (
        jnp.zeros((n_experts * CAP, width), jnp.bfloat16)
        .at[places]
        .set(route_grads)
        .reshape(n_experts, CAP, width)
    )
    gate_weight = expert_gate[0]
    up_weight = expert_up[0]
    down_weight = expert_down[0]
    rows_in = lax.all_to_all(send_rows, (DP, EXPERT), split_axis=0, concat_axis=0, tiled=True)
    grads_in = lax.all_to_all(send_grads, (DP, EXPERT), split_axis=0, concat_axis=0, tiled=True)
    sources = rows_in.shape[0]
    items = rows_in.shape[1]
    flat_in = rows_in.reshape(-1, width)
    flat_grad = grads_in.reshape(-1, width)
    e_gate = jnp.dot(flat_in, gate_weight, preferred_element_type=jnp.float32)
    e_up = jnp.dot(flat_in, up_weight, preferred_element_type=jnp.float32)
    e_silu = jax.nn.silu(e_gate)
    e_hidden = (e_silu * e_up).astype(jnp.bfloat16)
    e_out = jnp.dot(e_hidden, down_weight, preferred_element_type=jnp.float32).astype(jnp.bfloat16)
    d_hidden = mat_right(flat_grad, down_weight)
    d_gate = (d_hidden * e_up * silu_slope(e_gate)).astype(jnp.bfloat16)
    d_up = (d_hidden * e_silu).astype(jnp.bfloat16)
    d_in = (mat_right(d_gate, gate_weight) + mat_right(d_up, up_weight)).astype(jnp.bfloat16)
    back_out = lax.all_to_all(
        e_out.reshape(sources, items, width),
        (DP, EXPERT),
        split_axis=0,
        concat_axis=0,
        tiled=True,
    )
    back_in = lax.all_to_all(
        d_in.reshape(sources, items, width),
        (DP, EXPERT),
        split_axis=0,
        concat_axis=0,
        tiled=True,
    )
    back_out, back_in, rows_seen, grads_seen, hidden_seen, dgate_seen, duplicate_visits = (
        back_out,
        back_in,
        rows_in,
        grads_in,
        e_hidden.reshape(sources, items, -1),
        d_gate.reshape(sources, items, -1),
        d_up.reshape(sources, items, -1),
    )
    flattened_rows = rows_seen.reshape(-1, width)
    routed_gate_gradient = left_operand(
        flattened_rows, dgate_seen.reshape(flattened_rows.shape[0], -1)
    )
    routed_up_gradient = left_operand(
        flattened_rows, duplicate_visits.reshape(flattened_rows.shape[0], -1)
    )
    routed_down_gradient = left_operand(
        hidden_seen.reshape(flattened_rows.shape[0], -1), grads_seen.reshape(-1, width)
    )
    routed_gate_gradient, routed_up_gradient, routed_down_gradient = (
        lax.psum_scatter(
            routed_gate_gradient[None].astype(jnp.bfloat16),
            CONTEXT,
            scatter_dimension=1,
            tiled=True,
        ).astype(jnp.float32),
        lax.psum_scatter(
            routed_up_gradient[None].astype(jnp.bfloat16),
            CONTEXT,
            scatter_dimension=1,
            tiled=True,
        ).astype(jnp.float32),
        lax.psum_scatter(
            routed_down_gradient[None].astype(jnp.bfloat16),
            CONTEXT,
            scatter_dimension=2,
            tiled=True,
        ).astype(jnp.float32),
    )
    route_out = back_out.reshape(-1, width)[places].astype(jnp.float32).reshape(tok_rows, -1, width)
    route_din = back_in.reshape(-1, width)[places].astype(jnp.float32).reshape(tok_rows, -1, width)
    moe_sum = jnp.sum(gates[:, :, None] * route_out, axis=1)
    mixed = (hidden_own + moe_sum + mix_own[:, None] * shared_own).astype(jnp.bfloat16)
    d_gates = jnp.sum(route_out * dy_own[:, None, :], axis=2)
    d_rprobs = jnp.sum(picked * d_gates[:, :, None], axis=1)
    d_logits = router_probs * (d_rprobs - jnp.sum(router_probs * d_rprobs, axis=1, keepdims=True))
    moe_own_float = moe_own.astype(jnp.float32)
    router_part = jnp.dot(moe_own_float.T, d_logits, precision=HIGH)
    d_mixlogit = jnp.sum(shared_own * dy_own, axis=1) * mix_own * (1.0 - mix_own)
    mix_part = jnp.dot(moe_own_float.T, d_mixlogit, precision=HIGH)
    d_in_own = (
        jnp.sum(route_din, axis=1)
        + jnp.dot(d_logits, full_router.astype(jnp.float32).T, precision=HIGH)
        + d_mixlogit[:, None] * full_mix.astype(jnp.float32)[None, :]
    )
    dy_float = dy_piece.astype(jnp.float32)
    d_shared = (mix[:, None] * dy_float).astype(jnp.bfloat16)
    grad_sdown = left_operand(s_hidden, d_shared)
    d_shidden = mat_right(d_shared, full_sdown)
    d_sgate = (d_shidden * s_up * silu_slope(s_gate)).astype(jnp.bfloat16)
    d_sup = (d_shidden * s_silu).astype(jnp.bfloat16)
    grad_sgate = left_operand(moe_in, d_sgate)
    grad_sup = left_operand(moe_in, d_sup)
    d_in_part = mat_right(d_sgate, full_sgate) + mat_right(d_sup, full_sup)
    d_in_part = lax.dynamic_update_slice_in_dim(
        d_in_part,
        lax.dynamic_slice_in_dim(d_in_part, own_start, tok_rows, 0) + d_in_own,
        own_start,
        0,
    )
    d_moe_in, router_grad, mix_grad = lax.psum((d_in_part, router_part, mix_part), EXPERT)
    d_norm_two = d_moe_in * gain_two
    gain_two_grad = jnp.sum(d_moe_in * normed_two, axis=0)
    d_hidden_one = dy_float + rstd_two * (
        d_norm_two - normed_two * jnp.mean(d_norm_two * normed_two, axis=1, keepdims=True)
    )
    d_proj = d_hidden_one.astype(jnp.bfloat16)
    grad_out = left_operand(attn_low, d_proj)
    d_attn = mat_right(d_proj, full_out).astype(jnp.bfloat16)
    dattn_grp = to_groups(d_attn, groups, group_size, head_dim)

    def query_side(args):
        group_query, group_keys, group_values, group_lse, group_attention_gradient = args
        scores = (
            jnp.einsum("hqd,hkd->hqk", group_query, group_keys, preferred_element_type=jnp.float32)
            * score_scale
        )
        probs = jnp.where(
            visible[None],
            jnp.exp(jnp.where(visible[None], scores, 0.0) - group_lse[..., None]),
            0.0,
        )
        d_probs = jnp.einsum(
            "hqd,hkd->hqk",
            group_attention_gradient,
            group_values,
            preferred_element_type=jnp.float32,
        )
        delta = jnp.sum(probs * d_probs, axis=2)
        d_scores = (probs * (d_probs - delta[..., None])).astype(jnp.bfloat16)
        d_query = (
            jnp.einsum("hqk,hkd->hqd", d_scores, group_keys, preferred_element_type=jnp.float32)
            * score_scale
        )
        return (probs, d_scores, d_query, delta)

    def both_sides(args):
        probs, d_scores, d_query, delta = query_side(args)
        d_key = (
            jnp.einsum("hqk,hqd->hkd", d_scores, args[0], preferred_element_type=jnp.float32)
            * score_scale
        )
        d_value = jnp.einsum(
            "hqk,hqd->hkd", probs.astype(jnp.bfloat16), args[4], preferred_element_type=jnp.float32
        )
        return (d_query, d_key, d_value)

    dq_grp, dk_grp, dv_grp = lax.map(
        both_sides, (query_grp, keys_grp, values_grp, lse_grp, dattn_grp)
    )
    d_query = from_groups(dq_grp)
    d_key_own, d_value_own = (
        lax.psum_scatter(from_groups(dk_grp), CONTEXT, scatter_dimension=0, tiled=True),
        lax.psum_scatter(from_groups(dv_grp), CONTEXT, scatter_dimension=0, tiled=True),
    )
    d_q_pre = (
        rotate_back(d_query.reshape(piece_rows, local_heads, head_dim), cosine, sine)
        .reshape(piece_rows, -1)
        .astype(jnp.bfloat16)
    )
    d_k_pre = (
        rotate_back(d_key_own.reshape(piece_rows, local_heads, head_dim), cosine, sine)
        .reshape(piece_rows, -1)
        .astype(jnp.bfloat16)
    )
    d_v_pre = d_value_own.astype(jnp.bfloat16)
    grad_bq = jnp.sum(d_q_pre.astype(jnp.float32), axis=0).reshape(local_heads, head_dim)
    grad_bk = jnp.sum(d_k_pre.astype(jnp.float32), axis=0).reshape(local_heads, head_dim)
    grad_bv = jnp.sum(d_v_pre.astype(jnp.float32), axis=0).reshape(local_heads, head_dim)
    grad_query = left_operand(attn_in, d_q_pre)
    grad_key = left_operand(attn_in, d_k_pre)
    grad_value = left_operand(attn_in, d_v_pre)
    d_attn_in = (
        mat_right(d_q_pre, full_query)
        + mat_right(d_k_pre, full_key)
        + mat_right(d_v_pre, full_value)
    )
    d_attn_in = lax.psum(d_attn_in.astype(jnp.bfloat16), EXPERT).astype(jnp.float32)
    d_norm_one = d_attn_in * gain_one
    gain_one_grad = jnp.sum(d_attn_in * normed_one, axis=0)
    d_x = d_hidden_one + rstd_one * (
        d_norm_one - normed_one * jnp.mean(d_norm_one * normed_one, axis=1, keepdims=True)
    )
    input_grad = lax.dynamic_slice_in_dim(d_x, own_start, tok_rows, 0).astype(jnp.bfloat16)
    (
        grad_query,
        grad_key,
        grad_value,
        grad_out,
        grad_sgate,
        grad_sup,
        grad_sdown,
        router_grad,
        mix_grad,
        gain_one_grad,
        gain_two_grad,
        grad_bq,
        grad_bk,
        grad_bv,
    ) = (
        lax.psum_scatter(grad_query, (DP, CONTEXT), scatter_dimension=0, tiled=True),
        lax.psum_scatter(grad_key, (DP, CONTEXT), scatter_dimension=0, tiled=True),
        lax.psum_scatter(grad_value, (DP, CONTEXT), scatter_dimension=0, tiled=True),
        lax.psum_scatter(grad_out, (DP, CONTEXT), scatter_dimension=1, tiled=True),
        lax.psum_scatter(grad_sgate, (DP, CONTEXT), scatter_dimension=0, tiled=True),
        lax.psum_scatter(grad_sup, (DP, CONTEXT), scatter_dimension=0, tiled=True),
        lax.psum_scatter(grad_sdown, (DP, CONTEXT), scatter_dimension=1, tiled=True),
        lax.psum_scatter(router_grad, (DP, CONTEXT), scatter_dimension=0, tiled=True),
        lax.psum_scatter(mix_grad, (DP, CONTEXT), scatter_dimension=0, tiled=True),
        lax.psum_scatter(gain_one_grad, (DP, CONTEXT), scatter_dimension=0, tiled=True),
        lax.psum_scatter(gain_two_grad, (DP, CONTEXT), scatter_dimension=0, tiled=True),
        lax.psum_scatter(grad_bq, (DP, CONTEXT), scatter_dimension=1, tiled=True),
        lax.psum_scatter(grad_bk, (DP, CONTEXT), scatter_dimension=1, tiled=True),
        lax.psum_scatter(grad_bv, (DP, CONTEXT), scatter_dimension=1, tiled=True),
    )
    return (
        mixed,
        input_grad,
        gain_one_grad,
        grad_query,
        grad_key,
        grad_value,
        grad_bq,
        grad_bk,
        grad_bv,
        grad_out,
        gain_two_grad,
        router_grad,
        mix_grad,
        grad_sgate,
        grad_sup,
        grad_sdown,
        routed_gate_gradient,
        routed_up_gradient,
        routed_down_gradient,
    )


def dot_f32(left, right, left_dim, right_dim):
    return lax.dot_general(
        left, right, (((left_dim,), (right_dim,)), ((), ())), preferred_element_type=jnp.float32
    )


def whole_vmem(count):
    return [pl.BlockSpec(memory_space=pltpu.VMEM)] * count


def like(shape, dtype):
    return jax.ShapeDtypeStruct(shape, dtype)


MESH_ID = pl.DeviceIdType.MESH


class Wire:
    def __init__(self, send, recv):
        self.send = send
        self.recv = recv
        self.sent = 0
        self.received = 0
        self.own = []

    def copy(self, src, dst, device):
        out = self.copy_to(src, dst, device, self.take(1), self.take_send(1))
        self.own.append(out)
        return out

    def take(self, count):
        self.received += count
        assert self.received <= self.recv.shape[0], self.received
        return self.received - count

    def take_send(self, count):
        self.sent += count
        assert self.sent <= self.send.shape[0], self.sent
        return self.sent - count

    def copy_to(self, src, dst, device, recv_slot, send_slot):
        return pltpu.make_async_remote_copy(
            src_ref=src,
            dst_ref=dst,
            send_sem=self.send.at[send_slot],
            recv_sem=self.recv.at[recv_slot],
            device_id=device,
            device_id_type=MESH_ID,
        )

    def drain(self, some=None):
        for item in self.own if some is None else some:
            item.wait_send()
        done = {id(item) for item in some} if some is not None else None
        self.own = [] if done is None else [item for item in self.own if id(item) not in done]


class Local:
    def __init__(self, sems):
        self.sems = sems
        self.count = 0

    def start(self, src, dst):
        assert self.count < self.sems.shape[0], self.count
        item = pltpu.make_async_copy(src, dst, self.sems.at[self.count])
        self.count += 1
        item.start()
        return item


class Phases:
    def __init__(self):
        self.scope = None

    def go(self, name):
        if self.scope is not None:
            self.scope.__exit__(None, None, None)
        self.scope = jax.named_scope(name) if name else None
        if name:
            self.scope.__enter__()


class Place:
    def __init__(self, n_dp):
        self.n_dp = n_dp
        self.z = lax.axis_index(DP)
        self.c = lax.axis_index(CONTEXT)
        self.y = lax.axis_index(EXPERT)
        self.cx = lax.bitwise_xor(self.c, jnp.int32(2))
        self.cs = lax.bitwise_xor(self.c, jnp.int32(1))
        self.cd = lax.bitwise_xor(self.c, jnp.int32(3))
        self.yn = lax.bitwise_xor(self.y, jnp.int32(1))
        self.core = (self.z, self.cs, self.y)
        self.over_x = (self.z, self.cx, self.y)
        self.over_y = (self.z, self.c, self.yn)
        self.up = (self.z + 1, self.c, self.y)
        self.down = (self.z - 1, self.c, self.y)

    def block(self, c, y):
        return c * 2 + y


def barrier(devices):
    sem = pltpu.get_barrier_semaphore()
    for device in devices:
        pl.semaphore_signal(sem, inc=1, device_id=device, device_id_type=MESH_ID)
    pl.semaphore_wait(sem, len(devices))


def rows_of(index, count):
    return pl.ds(pl.multiple_of(index * count, count), count)


def by_rows(total, step, body):
    def one(index, carry):
        body(rows_of(index, step))
        return carry

    lax.fori_loop(0, total // step, one, 0)


def chain_gather(wire, place, refs, arrived=None, begun=False):
    n = place.n_dp
    z = place.z
    width = len(refs(z))
    recv = wire.take(n * width)
    send = wire.take_send(2 * n * width)

    def copies(slot, up, dist):
        return [
            wire.copy_to(
                ref,
                ref,
                place.up if up else place.down,
                recv + slot * width + index,
                send + (2 * dist + (0 if up else 1)) * width + index,
            )
            for index, ref in enumerate(refs(slot))
        ]

    def start(slot, up, dist):
        for item in copies(slot, up, dist):
            item.start()

    def land(slot, up, dist):
        if dist > 1 or not begun:
            for item in copies(slot, up, dist):
                item.wait_recv()
        if arrived is not None:
            arrived(slot)

    def sent(slot, up, dist):
        for item in copies(slot, up, dist):
            item.wait_send()

    if not begun:
        pl.when(z < n - 1)(lambda: start(z, True, 0))
        pl.when(z > 0)(lambda: start(z, False, 0))
        yield
    for dist in range(1, n):
        below, above = z - dist, z + dist

        @pl.when(below >= 0)
        def _():
            land(below, True, dist)
            pl.when(z < n - 1)(lambda: start(below, True, dist))

        @pl.when(above < n)
        def _():
            land(above, False, dist)
            pl.when(z > 0)(lambda: start(above, False, dist))

        yield
    for dist in range(1 if begun else 0, n):
        below, above = z - dist, z + dist
        pl.when((below >= 0) & (z < n - 1))(lambda: sent(below, True, dist))
        pl.when((above < n) & (z > 0))(lambda: sent(above, False, dist))


def finish(*steps):
    for step in steps:
        for _ in step:
            pass


def plane_gather(wire, place, buf):
    rows = buf.shape[0] // 8
    half = buf.shape[1] // 2
    left, right = pl.ds(0, half), pl.ds(half, half)
    own = rows_of(place.block(place.c, place.y), rows)
    from_x = rows_of(place.block(place.cx, place.y), rows)
    from_y = rows_of(place.block(place.c, place.yn), rows)
    across = rows_of(place.block(place.cx, place.yn), rows)

    def go(where, lanes, device):
        ref = buf.at[where, lanes] if lanes is not None else buf.at[where, :]
        item = wire.copy(ref, ref, device)
        item.start()
        return item

    x_left = go(own, left, place.over_x)
    y_right = go(own, right, place.over_y)
    x_right = go(own, right, place.over_x)
    y_left = go(own, left, place.over_y)
    waits = [go(own, None, place.core)]
    yield
    x_left.wait_recv()
    far_left = go(from_x, left, place.over_y)
    y_right.wait_recv()
    far_right = go(from_y, right, place.over_x)
    yield
    x_right.wait_recv()
    waits.append(go(from_x, None, place.core))
    y_left.wait_recv()
    waits.append(go(from_y, None, place.core))
    yield
    far_left.wait_recv()
    far_right.wait_recv()
    waits.append(go(across, None, place.core))
    for item in waits:
        item.wait_recv()


def add_into(target, lanes, rows, extra):
    count = extra.shape[0]
    step = 16

    def one(index, carry):
        here = pl.ds(pl.multiple_of(rows + index * step, step), step)
        there = rows_of(index, step)
        total = target[here, lanes].astype(jnp.float32) + extra[there, :].astype(jnp.float32)
        target[here, lanes] = total.astype(target.dtype)
        return carry

    lax.fori_loop(0, count // step, one, 0)


def plane_reduce(wire, place, part, got_core, got_one, got_two):
    rows = part.shape[0] // 8
    half = part.shape[1] // 2
    left, right = pl.ds(0, half), pl.ds(half, half)
    chips = ((place.cx, place.yn), (place.cx, place.y), (place.c, place.yn), (place.c, place.y))
    starts = [place.block(c, y) * rows for c, y in chips]
    blocks = [pl.ds(pl.multiple_of(start, rows), rows) for start in starts]
    sibling = [
        rows_of(place.block(lax.bitwise_xor(c, jnp.int32(1)), y), rows) for c, y in chips
    ]
    swaps = []
    for index in range(4):
        item = wire.copy(part.at[sibling[index], :], got_core.at[index], place.core)
        item.start()
        swaps.append(item)
    whole = pl.ds(0, 2 * half)

    def one(index, lanes, slot, device):
        item = wire.copy(part.at[blocks[index], lanes], got_one.at[slot], device)
        item.start()
        return item

    swaps[0].wait_recv()
    add_into(part, whole, starts[0], got_core.at[0])
    far_x = one(0, left, 0, place.over_x)
    far_y = one(0, right, 2, place.over_y)
    swaps[1].wait_recv()
    add_into(part, whole, starts[1], got_core.at[1])
    near_x = one(1, left, 1, place.over_x)
    swaps[2].wait_recv()
    add_into(part, whole, starts[2], got_core.at[2])
    near_y = one(2, right, 3, place.over_y)
    yield
    swaps[3].wait_recv()
    add_into(part, whole, starts[3], got_core.at[3])
    far_x.wait_recv()
    add_into(part, left, starts[2], got_one.at[0])
    last_y = wire.copy(part.at[blocks[2], left], got_two.at[0], place.over_y)
    last_y.start()
    far_y.wait_recv()
    add_into(part, right, starts[1], got_one.at[2])
    last_x = wire.copy(part.at[blocks[1], right], got_two.at[1], place.over_x)
    last_x.start()
    yield
    near_x.wait_recv()
    near_y.wait_recv()
    last_x.wait_recv()
    last_y.wait_recv()


def plane_sum(place, part, got_one, got_two, here):
    rows = part.shape[0] // 8
    half = part.shape[1] // 2
    start = place.block(place.c, place.y) * rows + here.start
    at = pl.ds(pl.multiple_of(start, here.size), here.size)

    def value(ref):
        return ref.astype(jnp.float32)

    left = value(part[at, 0:half]) + value(got_one[1, here, :]) + value(got_two[0, here, :])
    right = value(part[at, half:]) + value(got_one[3, here, :]) + value(got_two[1, here, :])
    return jnp.concatenate([left, right], axis=1)


def forward_kernel(
    n_blocks, n_dp,
    tokens, out_grad, small, ids, w_query, w_key, w_value, w_out, s_gate, s_up, s_down,
    bias, cosine, sine,
    attn_in_to, query_to, keys_to, values_to, attn_to, lse_to, hidden_to, moe_in,
    heads_weight_to, out_weight_to, gate_weight, up_weight, down_weight, smalls, all_ids, dy_group,
    x_seq, partial, got_core, got_one, got_two,
    attn_in, query, keys, values, attn, lse, hidden, heads_weight, out_weight,
    shared_raw, shared_packed, send, recv, local,
):
    place = Place(n_dp)
    wire = Wire(send, recv)
    inside = Local(local)
    z, c, y = place.z, place.c, place.y
    rows, width = tokens.shape
    seq = x_seq.shape[0]
    cols = query.shape[1]
    head_dim = cosine.shape[1]
    block = seq // n_blocks
    scale = 1.0 / math.sqrt(head_dim)
    n_ctx = 4
    share = w_query.shape[0]
    f32, low = jnp.float32, jnp.bfloat16

    others = [(dz, dc) for dz in range(n_dp) for dc in range(n_ctx) if dz or dc]
    phases = Phases()
    phases.go("entry")
    raw_in = [inside.start(src, shared_raw.at[k]) for k, src in enumerate((s_gate, s_up))]

    def moved(dz, dc, y_to):
        return (lax.bitwise_xor(z, jnp.int32(dz)), lax.bitwise_xor(c, jnp.int32(dc)), y_to)

    barrier(
        [moved(dz, dc, y) for dz, dc in others] + [moved(dz, 0, place.yn) for dz in range(n_dp)]
    )

    mine = z * n_ctx + c
    my_rows = rows_of(mine, share)
    group = z * 2 + y
    shared_pieces = [[], [], []]

    units = gate_weight.shape[3]

    def pack(index):
        raw_in[index].wait()
        for part in range(n_dp):
            shared_packed[index, part] = shared_raw[index, :, part * units : (part + 1) * units]

    def shared_along_dp(index):
        if index < 2:
            pack(index)
        for dz in (2, 3, 1, 0):
            to = lax.bitwise_xor(z, jnp.int32(dz))
            if index == 2:
                src = s_down.at[rows_of(to, s_down.shape[0] // n_dp), :]
                dst = down_weight.at[:, my_rows]
            else:
                src = shared_packed.at[index, to]
                dst = (gate_weight, up_weight)[index].at[z, c]
            if dz == 0:
                item = inside.start(src, dst)
            else:
                item = wire.copy(src, dst, moved(dz, 0, y))
                item.start()
            shared_pieces[index].append(item)

    shared_along_dp(0)

    exchanges = []
    for dc in range(n_ctx):
        to = lax.bitwise_xor(c, jnp.int32(dc))
        lanes = pl.ds(pl.multiple_of(to * cols, cols), cols)
        pairs = [
            (weight.at[:, lanes], heads_weight.at[my_rows, pl.ds(index * cols, cols)])
            for index, weight in enumerate((w_query, w_key, w_value))
        ]
        pairs.append((w_out.at[rows_of(to, cols), :], out_weight.at[:, my_rows]))
        for src, dst in pairs:
            if dc == 0:
                exchanges.append(inside.start(src, dst))
            else:
                item = wire.copy(src, dst, moved(0, dc, y))
                item.start()
                exchanges.append(item)
    own_rows = rows_of(place.block(c, y), rows)
    here = inside.start(tokens, x_seq.at[own_rows, :])
    here.wait()
    small_copies = [inside.start(small, smalls.at[:, my_rows])]
    for dz, dc in others:
        item = wire.copy(small, smalls.at[:, my_rows], moved(dz, dc, y))
        item.start()
        small_copies.append(item)
    small_copies.append(inside.start(ids, all_ids.at[group]))
    for dz in range(n_dp):
        for y_to in (y, place.yn):
            if dz or y_to is not y:
                item = wire.copy(ids, all_ids.at[group], moved(dz, 0, y_to))
                item.start()
                small_copies.append(item)
    def dy_rows(slot, half):
        return dy_group.at[rows_of(slot * 2 + half, rows), :]

    stores = [inside.start(out_grad, dy_rows(z, y))]
    dy_over_y = wire.copy(out_grad, dy_rows(z, y), place.over_y)
    dy_over_y.start()
    phases.go("exchanges")
    for item in exchanges:
        item.wait_recv()

    def from_place(slot):
        return rows_of(slot, n_ctx * share)

    weights_in = chain_gather(wire, place, lambda slot: [heads_weight.at[from_place(slot), :]])
    next(weights_in)
    phases.go("tokens")
    tokens_in = plane_gather(wire, place, x_seq)
    finish(tokens_in)
    next(weights_in)
    for item in small_copies:
        item.wait_recv()

    gain_one = smalls[9:10, :].astype(f32)
    gain_two = smalls[10:11, :].astype(f32)

    def norm_one(at):
        x_float = x_seq[at, :].astype(f32)
        rstd = lax.rsqrt(jnp.mean(x_float * x_float, axis=1, keepdims=True) + EPS)
        attn_in[at, :] = (x_float * rstd * gain_one).astype(low)

    by_rows(seq, 64, norm_one)
    def shared_set(index, context):
        if index < 2:
            return [(gate_weight, up_weight)[index].at[:, context]]
        return [
            down_weight.at[:, rows_of(dz * n_ctx + context, share)] for dz in range(n_dp)
        ]

    over = [[], [], []]
    close = []

    def shared_over_x(index):
        for item in shared_pieces[index]:
            item.wait_recv()
        for ref in shared_set(index, c):
            item = wire.copy(ref, ref, place.over_x)
            item.start()
            over[index].append(item)
        for ref in shared_set(index, c):
            item = wire.copy(ref, ref, place.core)
            item.start()
            close.append(item)

    def shared_close(index):
        for item, ref in zip(over[index], shared_set(index, place.cx)):
            item.wait_recv()
            item = wire.copy(ref, ref, place.core)
            item.start()
            close.append(item)

    shared_over_x(0)
    phases.go("heads_weights")
    finish(weights_in)
    phases.go("attention")
    out_in = chain_gather(wire, place, lambda slot: [out_weight.at[:, from_place(slot)]])
    next(out_in)

    def project(at):
        pre = dot_f32(attn_in[at, :], heads_weight[...], 1, 0)
        cos = cosine[at, :]
        sin = sine[at, :]
        for index, kept in enumerate((query, keys, values)):
            for start in range(0, cols, head_dim):
                from_lane = index * cols + start
                part = pre[:, from_lane : from_lane + head_dim]
                part = part + bias[index : index + 1, start : start + head_dim]
                if index < 2:
                    part = part * cos + pltpu.roll(part, head_dim // 2, 1) * sin
                kept[at, start : start + head_dim] = part.astype(low)

    by_rows(seq, block, project)
    next(out_in)
    for start in range(0, cols, head_dim):
        lanes = slice(start, start + head_dim)
        for step in range(n_blocks):
            at = slice(step * block, (step + 1) * block)
            seen = slice(0, (step + 1) * block)
            scores = dot_f32(query[at, lanes], keys[seen, lanes], 1, 1) * scale
            top = jnp.max(scores, axis=1, keepdims=True)
            expo = jnp.exp(scores - top)
            total = jnp.sum(expo, axis=1, keepdims=True)
            probs = (expo / total).astype(low)
            attn[at, lanes] = dot_f32(probs, values[seen, lanes], 1, 0).astype(low)
            lse[at, lanes] = jnp.broadcast_to(top + jnp.log(total), (block, head_dim))
        if start == 0:
            next(out_in)
    phases.go("out_weights")
    finish(out_in)
    shared_along_dp(1)
    shared_along_dp(2)
    phases.go("attention_out")

    def output(at):
        partial[at, :] = dot_f32(attn[at, :], out_weight[...], 1, 0).astype(low)

    by_rows(seq, block, output)
    stores += [
        inside.start(src, dst)
        for src, dst in (
            (attn_in, attn_in_to), (query, query_to), (keys, keys_to), (values, values_to),
            (attn, attn_to), (lse, lse_to), (heads_weight, heads_weight_to),
            (out_weight, out_weight_to),
        )
    ]
    phases.go("sum_in_plane")
    reduce = plane_reduce(wire, place, partial, got_core, got_one, got_two)
    next(reduce)

    next(reduce)
    finish(reduce)
    phases.go("norm_two")

    def norm_two(at):
        start = place.block(c, y) * rows + at.start
        own = pl.ds(pl.multiple_of(start, at.size), at.size)
        total = x_seq[own, :].astype(f32) + plane_sum(place, partial, got_one, got_two, at)
        hidden[at, :] = total
        rstd = lax.rsqrt(jnp.mean(total * total, axis=1, keepdims=True) + EPS)
        got_core[0, at, :] = (total * rstd * gain_two).astype(low)

    by_rows(rows, 16, norm_two)
    stores.append(inside.start(hidden, hidden_to))
    at_group = rows_of(group, rows)
    here = inside.start(got_core.at[0], moe_in.at[at_group, :])
    here.wait()

    half_width = width // 2
    y_recv = wire.take(2 * n_dp)
    y_send = wire.take_send(2 * n_dp)

    def moe_block(slot, half, part):
        return moe_in.at[rows_of(slot * 2 + half, rows), pl.ds(part * half_width, half_width)]

    def to_y(slot, part, half=None):
        ref = moe_block(slot, y if half is None else half, part)
        sem = 2 * slot + part
        return wire.copy_to(ref, ref, place.over_y, y_recv + sem, y_send + sem)

    chains = [
        chain_gather(
            wire,
            place,
            lambda slot, part=part: [moe_block(slot, y, part)],
            arrived=lambda slot, part=part: to_y(slot, part).start(),
        )
        for part in range(2)
    ]
    for part in range(2):
        next(chains[part])
        to_y(z, part).start()
    phases.go("shared_one")
    shared_over_x(1)
    phases.go("rows_one")
    for chain in chains:
        next(chain)
    phases.go("shared_two")
    shared_over_x(2)
    phases.go("rows_two")
    for chain in chains:
        next(chain)
    phases.go("rows_three")
    for chain in chains:
        next(chain)
    dy_recv = wire.take(2)
    dy_send = wire.take_send(2)

    def dy_step(up):
        ref = dy_rows(z, y)
        to = place.up if up else place.down
        return wire.copy_to(out_grad, ref, to, dy_recv + (0 if up else 1), dy_send + (0 if up else 1))

    pl.when(z < n_dp - 1)(lambda: dy_step(True).start())
    pl.when(z > 0)(lambda: dy_step(False).start())
    finish(*chains)
    phases.go("shared_close")
    for index in range(3):
        shared_close(index)
    for item in close:
        item.wait_recv()
    phases.go("rows_over_y")
    for slot in range(n_dp):
        for part in range(2):
            to_y(slot, part, place.yn).wait_recv()
            to_y(slot, part).wait_send()
    phases.go("dy")
    dy_over_y.wait_recv()

    @pl.when(z > 0)
    def _():
        dy_step(True).wait_recv()
        dy_step(False).wait_send()

    @pl.when(z < n_dp - 1)
    def _():
        dy_step(False).wait_recv()
        dy_step(True).wait_send()

    for item in stores:
        item.wait()
    wire.drain()
    phases.go(None)


def chain_reduce(wire, place, parts):
    n = place.n_dp
    z = place.z
    count = len(parts)
    recv = wire.take(2 * n * count)
    send = wire.take_send(2 * n * count)

    def copies(target, up):
        out = []
        for index, (block, below, above) in enumerate(parts):
            slot = (2 * target + (0 if up else 1)) * count + index
            landing = below if up else above
            out.append(
                wire.copy_to(
                    block(target),
                    landing.at[target],
                    place.up if up else place.down,
                    recv + slot,
                    send + slot,
                )
            )
        return out

    def collect(target, up):
        for item, (block, below, above) in zip(copies(target, up), parts):
            item.wait_recv()
            add_block(block(target), (below if up else above).at[target])

    def pass_on(target, up):
        collect(target, up)
        for item in copies(target, up):
            item.start()

    def first(target, up):
        for item in copies(target, up):
            item.start()

    @pl.when(z == 0)
    def _():
        for target in range(n - 1, 0, -1):
            first(target, True)

    @pl.when(z == n - 1)
    def _():
        for target in range(n - 1):
            first(target, False)

    yield
    for step in range(n - 1):
        high, low = n - 1 - step, step

        @pl.when((z > 0) & (z < n // 2))
        def _():
            pl.when(z < high)(lambda: pass_on(high, True))
            pl.when(z > low)(lambda: pass_on(low, False))

        @pl.when((z >= n // 2) & (z < n - 1))
        def _():
            pl.when(z > low)(lambda: pass_on(low, False))
            pl.when(z < high)(lambda: pass_on(high, True))

        yield
    pl.when(z > 0)(lambda: collect(z, True))
    pl.when(z < n - 1)(lambda: collect(z, False))
    for target in range(n):

        @pl.when(z < target)
        def _():
            for item in copies(target, True):
                item.wait_send()

        @pl.when(z > target)
        def _():
            for item in copies(target, False):
                item.wait_send()


def add_block(target, extra):
    step = 16

    def one(index, carry):
        here = rows_of(index, step)
        total = target[here, :].astype(jnp.float32) + extra[here, :].astype(jnp.float32)
        target[here, :] = total.astype(target.dtype)
        return carry

    lax.fori_loop(0, extra.shape[0] // step, one, 0)


class Adder:
    def __init__(self, sems):
        self.sems = sems

    def run(self, buf, chunks):
        def load(index):
            first, second, _ = chunks[index]
            slot = index % 2
            items = [
                pltpu.make_async_copy(first, buf.at[0, slot], self.sems.at[3 * slot]),
                pltpu.make_async_copy(second, buf.at[1, slot], self.sems.at[3 * slot + 1]),
            ]
            for item in items:
                item.start()
            return items

        stores = [None, None]
        loads = load(0)
        for index, (_, _, target) in enumerate(chunks):
            slot = index % 2
            after = load(index + 1) if index + 1 < len(chunks) else None
            for item in loads:
                item.wait()
            loads = after
            if stores[slot] is not None:
                stores[slot].wait()
            total, first, second = buf.at[2, slot], buf.at[0, slot], buf.at[1, slot]

            def one(step, carry):
                here = rows_of(step, 16)
                value = first[here, :].astype(jnp.float32) + second[here, :].astype(jnp.float32)
                total[here, :] = value.astype(total.dtype)
                return carry

            lax.fori_loop(0, total.shape[0] // 16, one, 0)
            stores[slot] = pltpu.make_async_copy(total, target, self.sems.at[3 * slot + 2])
            stores[slot].start()
        for item in stores:
            if item is not None:
                item.wait()


def backward_kernel(
    n_blocks, n_dp,
    own_sum, got_scalars, k_sup, k_sdown, x_sup, x_sdown, r_eup, r_edown,
    hidden_in, out_grad_in, tokens_in, smalls, probs, mix,
    heads_weight_in, w_out_in, query_in, keys_in, values_in, attn_from, lse_in, attn_in_from,
    cosine_in, sine_in,
    input_grad, heads_grad, out_weight_grad, small_grad, bias_grad,
    t_sup, t_sdown, x_eup, x_edown, s_sup, s_sdown,
    partial, d_hidden, side, moe_own, terms, acc,
    proj, d_attn, d_qkv, d_keys, d_values, got_core, got_one, got_two,
    g_heads, g_out, heads_below, heads_above, out_below, out_above, out_block,
    stage, landed, over_y, gate_buf, down_buf,
    hidden, out_grad, tokens, heads_weight, w_out, query, keys, values, attn, lse, attn_in,
    cosine, sine, send, recv, local, adds,
):
    place = Place(n_dp)
    wire = Wire(send, recv)
    inside = Local(local)
    adder = Adder(adds)
    z, c, y = place.z, place.c, place.y
    rows, width = tokens.shape
    seq = proj.shape[0]
    cols = query.shape[1]
    head_dim = cosine.shape[1]
    block = seq // n_blocks
    scale = 1.0 / math.sqrt(head_dim)
    n_ctx = 4
    share = width // (n_dp * n_ctx)
    n_experts = probs.shape[0]
    f32, low = jnp.float32, jnp.bfloat16
    core = lax.rem(c, 2)
    others = [(dz, dc) for dz in range(n_dp) for dc in range(n_ctx) if dz or dc]

    def moved(dz, dc, y_to):
        return (lax.bitwise_xor(z, jnp.int32(dz)), lax.bitwise_xor(c, jnp.int32(dc)), y_to)

    phases = Phases()
    phases.go("entry")
    barrier(
        [moved(dz, dc, y) for dz, dc in others] + [moved(dz, 0, place.yn) for dz in range(n_dp)]
    )
    def go_over_x(index, part=0, parts=1):
        total = (r_eup, r_edown)[index]
        got = (x_eup, x_edown)[index]
        count = got.shape[0] // parts
        at = pl.ds(part * count, count)
        item = wire.copy(total.at[at, :], got.at[at, :], place.over_x)
        item.start()
        return item

    def part_of(ref, dz):
        size = ref.shape[0] // n_dp
        return ref.at[pl.ds(dz * size, size), :]

    def shared_ready(index):
        buf = (gate_buf, down_buf)[index]
        kept = (k_sup, k_sdown)[index]
        got = (x_sup, x_sdown)[index]
        ready = (s_sup, s_sdown)[index]
        adder.run(buf, [(part_of(kept, dz), part_of(got, dz), ready.at[dz]) for dz in range(n_dp)])

    shared_last = []

    def shared_along_dp(index):
        ready = (s_sup, s_sdown)[index]
        target = (t_sup, t_sdown)[index]
        for dz in (2, 3, 1, 0):
            to = lax.bitwise_xor(z, jnp.int32(dz))
            if dz:
                item = wire.copy(ready.at[to], target.at[z], moved(dz, 0, y))
                item.start()
            else:
                item = inside.start(ready.at[to], target.at[z])
            shared_last.append(item)

    loads = [
        inside.start(src, dst)
        for src, dst in (
            (hidden_in, hidden), (out_grad_in, out_grad), (tokens_in, tokens), (attn_from, attn),
            (w_out_in, w_out), (query_in, query), (keys_in, keys), (values_in, values),
            (lse_in, lse), (cosine_in, cosine), (sine_in, sine), (heads_weight_in, heads_weight),
            (attn_in_from, attn_in),
        )
    ]
    phases.go("router")
    d_rprobs = got_scalars[:, 0, :]
    probs_own = probs[...]
    d_logits = probs_own * (d_rprobs - jnp.sum(probs_own * d_rprobs, axis=0, keepdims=True))
    shared_dot = jnp.sum(got_scalars[:, 1, :], axis=0, keepdims=True)
    d_mix = shared_dot * mix[...] * (1.0 - mix[...])
    d_side = jnp.concatenate(
        [d_logits, jnp.broadcast_to(d_mix, (16 - n_experts, rows))], axis=0
    )
    row_of = lax.broadcasted_iota(jnp.int32, d_side.shape, 0)
    d_side = jnp.where(row_of <= n_experts, d_side, 0.0)
    first = d_side.astype(low)
    rest = d_side - first.astype(f32)
    second = rest.astype(low)
    third = (rest - second.astype(f32)).astype(low)
    terms[...] = jnp.concatenate([first, second, third], axis=0)
    side[...] = dot_f32(terms[...], jnp.concatenate([smalls[...]] * 3, axis=0), 0, 0)
    gain_one = smalls[n_experts + 1 : n_experts + 2, :].astype(f32)
    gain_two = smalls[n_experts + 2 : n_experts + 3, :].astype(f32)
    acc[...] = jnp.zeros_like(acc)
    own_plane = place.block(c, y) * rows

    def norm_two(at):
        d_moe = side[at, :] + own_sum[at, :]
        total = hidden[at, :]
        rstd = lax.rsqrt(jnp.mean(total * total, axis=1, keepdims=True) + EPS)
        normed = total * rstd
        acc[0] += d_moe * normed
        d_norm = d_moe * gain_two
        back = out_grad[at, :].astype(f32) + rstd * (
            d_norm - normed * jnp.mean(d_norm * normed, axis=1, keepdims=True)
        )
        d_hidden[at, :] = back
        moe_own[at, :] = (normed * gain_two).astype(low)
        proj[pl.ds(pl.multiple_of(own_plane + at.start, at.size), at.size), :] = back.astype(low)

    phases.go("norm_two")
    for item in loads[:3]:
        item.wait()
    by_rows(rows, 16, norm_two)
    phases.go("gather_in_plane")
    proj_in = plane_gather(wire, place, proj)
    next(proj_in)
    side[0:48, :] = dot_f32(terms[...], moe_own[...], 1, 0)

    phases.go("shared_up")
    shared_ready(0)
    shared_along_dp(0)
    phases.go("gather_relay")
    next(proj_in)
    phases.go("shared_down")
    shared_ready(1)
    shared_along_dp(1)
    phases.go("gather_close")
    next(proj_in)
    phases.go("gather_end")
    finish(proj_in)

    phases.go("attention")
    routed_over = [go_over_x(0, part, 4) for part in range(3)]
    for item in loads[3:]:
        item.wait()
    by_share = n_ctx * share

    def out_weight(target):
        at = rows_of(target, by_share)
        g_out[:, at] = dot_f32(attn[...], proj[:, at], 0, 0).astype(low)

    def each(count, body):
        def one(index, carry):
            body(index)
            return carry

        lax.fori_loop(0, count, one, 0)

    each(n_dp, out_weight)
    out_chain = chain_reduce(
        wire, place, [(lambda t: g_out.at[:, rows_of(t, by_share)], out_below, out_above)]
    )
    next(out_chain)

    def project(at):
        d_attn[at, :] = dot_f32(proj[at, :], w_out[...], 1, 1).astype(low)

    by_rows(seq, block, project)

    def turn(part, at):
        return part * cosine[at, :] - pltpu.roll(part, head_dim // 2, 1) * sine[at, :]

    every = slice(0, seq)
    for start in range(0, cols, head_dim):
        lanes = slice(start, start + head_dim)
        d_keys[...] = jnp.zeros_like(d_keys)
        d_values[...] = jnp.zeros_like(d_values)
        for step in range(n_blocks):
            at = slice(step * block, (step + 1) * block)
            seen = slice(0, (step + 1) * block)
            q_here = query[at, lanes]
            k_seen = keys[seen, lanes]
            grad = d_attn[at, lanes]
            scores = dot_f32(q_here, k_seen, 1, 1) * scale
            weights = jnp.exp(scores - lse[at, start : start + 1])
            d_probs = dot_f32(grad, values[seen, lanes], 1, 1)
            delta = jnp.sum(weights * d_probs, axis=1, keepdims=True)
            d_scores = (weights * (d_probs - delta)).astype(low)
            d_query = dot_f32(d_scores, k_seen, 1, 0) * scale
            d_qkv[at, lanes] = turn(d_query, at).astype(low)
            d_keys[seen, :] += dot_f32(d_scores, q_here, 0, 0) * scale
            d_values[seen, :] += dot_f32(weights.astype(low), grad, 0, 0)
        d_qkv[:, cols + start : cols + start + head_dim] = turn(d_keys[...], every).astype(low)
        d_qkv[:, 2 * cols + start : 2 * cols + start + head_dim] = d_values[...].astype(low)

    phases.go("heads_grad")

    def heads_weights(target):
        at = rows_of(target, by_share)
        g_heads[at, :] = dot_f32(attn_in[:, at], d_qkv[...], 0, 0).astype(low)

    each(n_dp, heads_weights)
    heads_chain = chain_reduce(
        wire,
        place,
        [(lambda t: g_heads.at[rows_of(t, by_share), :], heads_below, heads_above)],
    )
    next(heads_chain)
    phases.go("attention_in_grad")

    def output(at):
        partial[at, :] = dot_f32(d_qkv[at, :], heads_weight[...], 1, 1).astype(low)

    by_rows(seq, block, output)
    phases.go("sum_in_plane")
    reduce = plane_reduce(wire, place, partial, got_core, got_one, got_two)
    next(reduce)
    next(out_chain)
    next(reduce)
    next(out_chain)
    phases.go("sum_in_plane_end")
    finish(reduce)
    routed_over += [go_over_x(0, 3, 4), go_over_x(1)]

    def norm_one(at):
        d_attn_in = plane_sum(place, partial, got_one, got_two, at)
        x_float = tokens[at, :].astype(f32)
        rstd = lax.rsqrt(jnp.mean(x_float * x_float, axis=1, keepdims=True) + EPS)
        normed = x_float * rstd
        acc[1] += d_attn_in * normed
        d_norm = d_attn_in * gain_one
        input_grad[at, :] = (
            d_hidden[at, :]
            + rstd * (d_norm - normed * jnp.mean(d_norm * normed, axis=1, keepdims=True))
        ).astype(low)

    phases.go("heads_chain_one")
    next(heads_chain)
    phases.go("norm_one")
    by_rows(rows, 16, norm_one)

    side_grad = side[0:16, :] + side[16:32, :] + side[32:48, :]
    row_of = lax.broadcasted_iota(jnp.int32, side_grad.shape, 0)
    gain_one_grad = jnp.sum(acc[1], axis=0, keepdims=True)
    gain_two_grad = jnp.sum(acc[0], axis=0, keepdims=True)
    small_rows = jnp.where(
        row_of == n_experts + 1,
        gain_one_grad,
        jnp.where(row_of == n_experts + 2, gain_two_grad, side_grad),
    )
    bias_sums = jnp.sum(d_qkv[...].astype(f32), axis=0, keepdims=True)
    bias_rows = [
        bias_sums[:, start : start + head_dim] for start in range(0, 3 * cols, head_dim)
    ]
    bias_rows += [jnp.zeros((8 - len(bias_rows), head_dim), f32)]
    bias_rows = jnp.concatenate(bias_rows, axis=0)
    for target in range(n_dp * n_ctx):
        stage[target, 0:16, :] = small_rows[:, target * share : (target + 1) * share]
        stage[target, 16:24, :] = bias_rows
    mine = z * n_ctx + c
    small_items = [inside.start(stage.at[mine], landed.at[mine])]
    for dz, dc in others:
        target = lax.bitwise_xor(z, jnp.int32(dz)) * n_ctx + lax.bitwise_xor(c, jnp.int32(dc))
        item = wire.copy(stage.at[target], landed.at[mine], moved(dz, dc, y))
        item.start()
        small_items.append(item)
    phases.go("chains")
    next(heads_chain)
    finish(out_chain)
    phases.go("heads_chain")
    finish(heads_chain)
    phases.go("last")

    out_block[...] = g_out[:, rows_of(z, by_share)]
    last = []
    for dc in range(n_ctx):
        to = lax.bitwise_xor(c, jnp.int32(dc))
        pairs = [
            (
                g_heads.at[pl.ds(pl.multiple_of(z * by_share + to * share, share), share), :],
                heads_grad.at[c],
            ),
            (out_block.at[:, rows_of(to, share)], out_weight_grad.at[c]),
        ]
        for src, dst in pairs:
            if dc:
                item = wire.copy(src, dst, moved(0, dc, y))
                item.start()
            else:
                item = inside.start(src, dst)
            last.append(item)

    phases.go("small")
    for item in small_items:
        item.wait_recv()
    total = landed[0, 0:16, :]
    for source in range(1, n_dp * n_ctx):
        total = total + landed[source, 0:16, :]
    over_y[0] = total
    swap = wire.copy(over_y.at[0], over_y.at[1], place.over_y)
    swap.start()
    for context in range(n_ctx):
        sums = landed[context, 16:24, :]
        for source in range(1, n_dp):
            sums = sums + landed[source * n_ctx + context, 16:24, :]
        bias_grad[context] = sums
    swap.wait_recv()
    small_grad[...] = over_y[0] + over_y[1]
    phases.go("wait_all")
    for item in last + shared_last + routed_over:
        item.wait_recv()
    wire.drain()
    phases.go(None)


def moe_forward(
    n_dp, dy_begun, moe_in, smalls, ids, s_gate_in, s_up_in, s_down_in, e_gate, e_up, e_down,
    cols, pick, s_slope, s_silu, s_hidden, e_slope, e_silu, e_hidden, rows_in, part, e_out, shared,
    dy_group,
    x, wg, wu, wd, v_slope, v_silu, v_hidden, r_slope, r_silu, r_hidden, rows, out, sh,
    s_gate, s_up, s_down, send, recv, local,
):
    place_here = Place(n_dp)
    wire = Wire(send, recv)
    z, c, y = place_here.z, place_here.c, place_here.y
    f32, low = jnp.float32, jnp.bfloat16
    inside = Local(local)
    n_experts = ids.shape[0]
    tok_rows = ids.shape[2]
    phases = Phases()
    phases.go("entry")
    mine = z * 2 + y

    def block_of(slot):
        return dy_group.at[rows_of(slot * 2 + y, tok_rows), :]

    y_recv = wire.take(n_dp)
    y_send = wire.take_send(n_dp)

    def over_y(slot):
        ref = block_of(slot)
        return wire.copy_to(ref, ref, place_here.over_y, y_recv + slot, y_send + slot)

    loads = [
        inside.start(src, dst)
        for src, dst in ((moe_in, x), (s_gate_in, s_gate), (s_up_in, s_up), (s_down_in, s_down))
    ]
    near = [(lax.bitwise_xor(z, jnp.int32(dz)), c, y) for dz in range(1, n_dp)]
    barrier(near + [place_here.over_y])
    dy_chain = chain_gather(
        wire,
        place_here,
        lambda slot: [block_of(slot)],
        arrived=lambda slot: over_y(slot).start(),
        begun=True,
    )
    next(dy_chain)
    loads += [inside.start(src, dst) for src, dst in ((e_gate, wg), (e_up, wu), (e_down, wd))]
    hit = jnp.concatenate(
        [jnp.any(ids[s] == mine, axis=0, keepdims=True).astype(f32) for s in range(n_experts)], axis=0
    )
    upto = (
        lax.broadcasted_iota(jnp.int32, (tok_rows, tok_rows), 0)
        <= lax.broadcasted_iota(jnp.int32, (tok_rows, tok_rows), 1)
    ).astype(low)
    place = dot_f32(hit.astype(low), upto, 1, 0) - 1.0
    slots = lax.broadcasted_iota(jnp.int32, (CAP, tok_rows), 0).astype(f32)
    for s in range(n_experts):
        chosen = (hit[s : s + 1] > 0.5) & (place[s : s + 1] == slots)
        pick[s] = jnp.where(chosen, 1.0, 0.0).astype(low)
    phases.go("x_wait")
    for item in loads[:4]:
        item.wait()

    def gated(g, u):
        sigma = 1.0 / (1.0 + jnp.exp(-g))
        silu = g * sigma
        return u * (sigma * (1.0 + g * (1.0 - sigma))), silu, silu * u

    def shared_tile(at):
        here = x[at, :]
        logits = dot_f32(here, smalls[...], 1, 1)
        lane = lax.broadcasted_iota(jnp.int32, logits.shape, 1)
        routed = lane < n_experts
        top = jnp.max(jnp.where(routed, logits, -jnp.inf), axis=1, keepdims=True)
        expo = jnp.where(routed, jnp.exp(jnp.where(routed, logits, top) - top), 0.0)
        probs = expo / jnp.sum(expo, axis=1, keepdims=True)
        mix = jnp.sum(jnp.where(lane == n_experts, logits, 0.0), axis=1, keepdims=True)
        mix = 1.0 / (1.0 + jnp.exp(-mix))
        gate = jnp.sum(jnp.where(lane == mine, probs, 0.0), axis=1, keepdims=True)
        cols[at, 0:16] = jnp.where(
            routed, probs, jnp.where(lane == n_experts, mix, jnp.where(lane == n_experts + 1, gate, 0.0))
        )
        slope, silu, hidden = gated(dot_f32(here, s_gate[...], 1, 0), dot_f32(here, s_up[...], 1, 0))
        v_slope[at, :] = slope.astype(low)
        v_silu[at, :] = silu.astype(low)
        v_hidden[at, :] = hidden.astype(low)
        sh[at, :] = dot_f32(v_hidden[at, :], s_down[...], 1, 0).astype(low)

    phases.go("shared")
    by_rows(x.shape[0], 512, shared_tile)
    phases.go("dy_two")
    next(dy_chain)
    stores = [
        inside.start(src, dst)
        for src, dst in ((v_slope, s_slope), (v_silu, s_silu), (v_hidden, s_hidden), (sh, shared))
    ]

    def gather(s, carry):
        block = x[rows_of(s, tok_rows), :]
        rows[rows_of(s, CAP), :] = dot_f32(pick[s], block, 1, 0).astype(low)
        return carry

    phases.go("gather")
    lax.fori_loop(0, n_experts, gather, 0)
    stores.append(inside.start(rows, rows_in))
    phases.go("w_wait")
    for item in loads[4:]:
        item.wait()

    def routed_tile(at):
        here = rows[at, :]
        slope, silu, hidden = gated(dot_f32(here, wg[...], 1, 0), dot_f32(here, wu[...], 1, 0))
        r_slope[at, :] = slope.astype(low)
        r_silu[at, :] = silu.astype(low)
        r_hidden[at, :] = hidden.astype(low)
        out[at, :] = dot_f32(r_hidden[at, :], wd[...], 1, 0).astype(low)

    phases.go("routed")
    routed_tile(pl.ds(0, 384))
    phases.go("dy_three")
    next(dy_chain)
    phases.go("routed_end")
    routed_tile(pl.ds(384, 384))
    stores.append(inside.start(out, e_out))
    stores += [
        inside.start(src, dst)
        for src, dst in ((r_slope, e_slope), (r_silu, e_silu), (r_hidden, e_hidden))
    ]

    def scatter(s, carry):
        at = rows_of(s, tok_rows)
        back = dot_f32(pick[s], out[rows_of(s, CAP), :], 0, 0)
        mix = cols[at, n_experts : n_experts + 1]
        gate = cols[at, n_experts + 1 : n_experts + 2]
        x[at, :] = (gate * back + mix * sh[at, :].astype(f32)).astype(low)
        return carry

    phases.go("scatter")
    lax.fori_loop(0, n_experts // 2, scatter, 0)
    first = pl.ds(0, n_experts // 2 * tok_rows)
    last = pl.ds(n_experts // 2 * tok_rows, n_experts // 2 * tok_rows)
    stores.append(inside.start(x.at[first, :], part.at[first, :]))
    lax.fori_loop(n_experts // 2, n_experts, scatter, 0)
    phases.go("stores")
    stores.append(inside.start(x.at[last, :], part.at[last, :]))
    for item in stores:
        item.wait()
    phases.go("over_y")
    finish(dy_chain)
    for slot in range(n_dp):

        @pl.when(z != slot)
        def _():
            over_y(slot).wait_recv()
            over_y(slot).wait_send()

    phases.go(None)


def shared_backward(
    n_dp, dy_group, cols, pick, s_gate_in, s_up_in, s_down_in, s_slope_in, s_silu_in,
    s_hidden, e_out, shared, moe_in,
    grads_in, part, scalars, keep_gate, keep_up, keep_down, give_gate, give_up, give_down,
    dy, out, sh, d_sh, rows, grads, total, x, hidden,
    g_gate, g_up, g_down, got_gate, got_up, got_down,
    s_gate, s_up, s_down, s_slope, s_silu, sums, picked, slot_sums, send, recv, local, slots,
):
    f32, low = jnp.float32, jnp.bfloat16
    inside = Local(local)
    wire = Wire(send, recv)
    place = Place(n_dp)
    n_experts = pick.shape[0]
    tok_rows = pick.shape[2]
    units = s_gate.shape[1]
    lanes = grads.shape[1] // 2
    share = g_gate.shape[1]
    n_ctx = 4
    core = lax.rem(place.c, 2)
    chip = lax.div(place.c, 2)
    phases = Phases()
    phases.go("entry")

    depth = dy.shape[0]

    def fetch(index):
        slot = index % depth
        at = pl.ds(index * tok_rows, tok_rows)
        items = [
            pltpu.make_async_copy(src, dst.at[slot], slots.at[3 * slot + k])
            for k, (src, dst) in enumerate(
                (
                    (dy_group.at[at, :], dy),
                    (e_out.at[pl.ds(index * CAP, CAP), :], out),
                    (shared.at[at, :], sh),
                )
            )
        ]
        for item in items:
            item.start()
        return items

    coming = [fetch(index) for index in range(depth - 1)]
    to_load = [
        (s_down_in, s_down), (s_slope_in, s_slope), (s_silu_in, s_silu),
        (s_gate_in, s_gate), (s_up_in, s_up), (moe_in, x), (s_hidden, hidden),
    ]
    loads = []
    barrier([place.core])
    grads[...] = jnp.zeros_like(grads)
    sums[...] = jnp.zeros_like(sums)
    for index in range(n_experts):
        slot = index % depth
        if index + depth - 1 < n_experts:
            coming.append(fetch(index + depth - 1))
        if index < len(to_load):
            loads.append(inside.start(*to_load[index]))
        for item in coming[index]:
            item.wait()
        here = pl.ds(index * tok_rows, tok_rows)
        chosen = pick[index].astype(f32)
        gate = jnp.transpose(cols[here, :])[n_experts + 1 : n_experts + 2, :]
        gate = jnp.sum(chosen * gate, axis=1, keepdims=True)
        picked[...] = dot_f32(pick[index], dy[slot], 1, 0)

        def slot_rows(at):
            grad = picked[at, :]
            this = out[slot, at, :].astype(f32)
            slot_sums[at, 0:1] = jnp.sum(this * grad, axis=1, keepdims=True)

        by_rows(CAP, 32, slot_rows)
        rows[pl.ds(index * CAP, CAP), :] = (gate * picked[...]).astype(low)
        d_gate = jnp.sum(chosen * slot_sums[:, 0:1], axis=0, keepdims=True)

        def chunk(at):
            there = pl.ds(pl.multiple_of(index * tok_rows + at.start, at.size), at.size)
            grad = dy[slot, at, :].astype(f32)
            mix = cols[there, n_experts : n_experts + 1]
            d_sh[there, :] = (mix * grad).astype(low)
            sums[at, 0:1] = jnp.sum(sh[slot, at, :].astype(f32) * grad, axis=1, keepdims=True)

        by_rows(tok_rows, 32, chunk)
        shared_dot = jnp.transpose(sums[...])[0:1, :]
        row_of = lax.broadcasted_iota(jnp.int32, (8, tok_rows), 0)
        scalars[index] = jnp.where(row_of == 0, d_gate, jnp.where(row_of == 1, shared_dot, 0.0))
    stores = [inside.start(rows, grads_in)]

    def shared_tile(at):
        d_hidden = dot_f32(d_sh[at, :], s_down[...], 1, 1)
        d_gate = (d_hidden * s_slope[at, :].astype(f32)).astype(low)
        d_up = (d_hidden * s_silu[at, :].astype(f32)).astype(low)
        grads[at, 0:units] = d_gate
        grads[at, lanes : lanes + units] = d_up
        total[at, :] = (dot_f32(d_gate, s_gate[...], 1, 1) + dot_f32(d_up, s_up[...], 1, 1)).astype(low)

    for item in loads[:5]:
        item.wait()
    phases.go("shared")
    by_rows(d_sh.shape[0], 512, shared_tile)
    stores.append(inside.start(total, part))
    for item in loads[5:]:
        item.wait()
    phases.go("in_grads")

    def block_index(dx, dz, sibling):
        side = lax.bitwise_xor(chip, jnp.int32(dx)) * 2
        return dz * n_ctx + side + (1 - core if sibling else core)

    sent = {}

    def to_sibling(dz, mats):
        for dx in (1, 0):
            for grad, got in mats:
                item = wire.copy(grad.at[block_index(dx, dz, True)], got.at[dx, dz], place.core)
                item.start()
                sent.setdefault(dz, []).append(item)

    step = n_ctx * share
    for dz in range(n_dp):
        product = dot_f32(x[:, dz * step : (dz + 1) * step], grads[...], 0, 0)
        for k in range(n_ctx):
            here = slice(k * share, (k + 1) * share)
            g_gate[dz * n_ctx + k] = product[here, 0:units].astype(low)
            g_up[dz * n_ctx + k] = product[here, lanes : lanes + units].astype(low)
        to_sibling(dz, ((g_gate, got_gate), (g_up, got_up)))
    phases.go("down_grads")
    down = {}
    for dz in range(n_dp):
        product = dot_f32(hidden[...], d_sh[:, dz * step : (dz + 1) * step], 0, 0)
        for k in range(n_ctx):
            g_down[dz * n_ctx + k] = product[:, k * share : (k + 1) * share].astype(low)
        for dx in (1, 0):
            item = wire.copy(g_down.at[block_index(dx, dz, True)], got_down.at[dx, dz], place.core)
            item.start()
            down.setdefault(dz, []).append(item)
    phases.go("sums")

    def collect(dx, dz, grad, got, out_ref):
        mine = block_index(dx, dz, False)
        add_block(grad.at[mine], got.at[dx, dz])
        size = grad.shape[1]
        stores.append(inside.start(grad.at[mine], out_ref.at[pl.ds(dz * size, size), :]))

    for dz in range(n_dp):
        for item in sent[dz]:
            item.wait_recv()
        for dx, outs in ((1, (give_gate, give_up)), (0, (keep_gate, keep_up))):
            for grad, got, out_ref in zip((g_gate, g_up), (got_gate, got_up), outs):
                collect(dx, dz, grad, got, out_ref)
    for dz in range(n_dp):
        for item in down[dz]:
            item.wait_recv()
        for dx, out_ref in ((1, give_down), (0, keep_down)):
            collect(dx, dz, g_down, got_down, out_ref)
    phases.go("stores")
    for item in stores:
        item.wait()
    wire.drain()
    phases.go(None)


def routed_backward(
    n_dp, grads_in, rows_in, e_gate, e_up, e_down, slope_in, silu_in, hidden_in, shared_part, scalars,
    keep_sgate, give_sgate, give_sup, give_sdown, pick,
    own_sum, got_scalars, t_sgate, x_sup, x_sdown,
    keep_gate, keep_up, keep_down, give_up, give_down, x_gate,
    wg, wu, wd, grads, rows, slope, silu, hidden, d_hid, d_in, total,
    got_gate, got_up, got_down, got_y, got_dp, x_sgate, sum_sgate, send, recv, local,
):
    f32, low = jnp.float32, jnp.bfloat16
    inside = Local(local)
    wire = Wire(send, recv)
    place = Place(n_dp)
    z, c, y = place.z, place.c, place.y
    n_experts = pick.shape[0]
    tok_rows = pick.shape[2]
    units = wg.shape[1]
    width = rows.shape[1]
    core = lax.rem(c, 2)
    chip = lax.div(c, 2)
    group = z * 2 + y
    phases = Phases()
    phases.go("entry")
    loads = [
        inside.start(src, dst)
        for src, dst in (
            (grads_in, grads), (e_down, wd), (slope_in, slope), (silu_in, silu),
            (e_gate, wg), (e_up, wu), (shared_part, total), (rows_in, rows), (hidden_in, hidden),
            (keep_sgate, sum_sgate),
        )
    ]

    def near(dz, y_to):
        return (lax.bitwise_xor(z, jnp.int32(dz)), c, y_to)

    members = [(dz, y_to) for dz in range(n_dp) for y_to in (y, place.yn) if dz or y_to is not y]
    barrier([place.core, place.over_x] + [near(dz, y_to) for dz, y_to in members])

    over_x = []

    def go_over_x(src, dst):
        item = wire.copy(src, dst, place.over_x)
        item.start()
        over_x.append(item)

    go_over_x(give_sgate, x_sgate)
    scalar_items = [inside.start(scalars.at[group], got_scalars.at[group])]
    for dz, y_to in members:
        target = lax.bitwise_xor(z, jnp.int32(dz)) * 2 + y_to
        item = wire.copy(scalars.at[target], got_scalars.at[group], near(dz, y_to))
        item.start()
        scalar_items.append(item)
    for item in loads[:4]:
        item.wait()
    phases.go("routed")
    half = grads.shape[0] // 2

    def routed_tile(at, wait):
        d_hidden = dot_f32(grads[at, :], wd[...], 1, 1)
        d_gate = (d_hidden * slope[at, :].astype(f32)).astype(low)
        d_up = (d_hidden * silu[at, :].astype(f32)).astype(low)
        d_hid[at, 0:units] = d_gate
        d_hid[at, units : 2 * units] = d_up
        for item in wait:
            item.wait()
        d_in[at, :] = (dot_f32(d_gate, wg[...], 1, 1) + dot_f32(d_up, wu[...], 1, 1)).astype(low)

    routed_tile(pl.ds(0, half), loads[4:6])
    go_over_x(give_sup, x_sup)
    go_over_x(give_sdown, x_sdown)
    routed_tile(pl.ds(half, half), [])
    for item in loads[6:]:
        item.wait()
    phases.go("to_tokens")

    def to_tokens(s, carry):
        at = rows_of(s, tok_rows)
        back = dot_f32(pick[s], d_in[rows_of(s, CAP), :], 0, 0)
        total[at, :] = (back + total[at, :].astype(f32)).astype(low)
        return carry

    lax.fori_loop(0, n_experts, to_tokens, 0)

    orders = ((3, 2, 1, 0), (3, 0, 2, 1), (0, 3, 1, 2), (0, 1, 2, 3))
    lower = 1 - lax.div(z, 2)
    order = (
        3 * lower,
        lower * (2 - 2 * z) + (1 - lower) * (7 - 2 * z),
        1 + lax.rem(z, 2),
        z,
    )
    y_swaps = []
    for step in range(n_dp):
        from_row = order[step] * 2 + place.yn
        item = wire.copy(total.at[rows_of(from_row, tok_rows), :], got_y.at[step], place.over_y)
        item.start()
        y_swaps.append(item)
    dp_recv = wire.take(2 * n_dp)
    dp_send = wire.take_send(2 * n_dp)

    def along(target, up):
        slot = target - 1 if up else n_dp - 1 + target
        return wire.copy_to(
            total.at[pl.ds(pl.multiple_of((target * 2 + y) * tok_rows, tok_rows), tok_rows), :],
            got_dp.at[slot],
            place.up if up else place.down,
            dp_recv + slot,
            dp_send + slot,
        )

    def add_from(target, up):
        along(target, up).wait_recv()
        slot = target - 1 if up else n_dp - 1 + target
        add_into(total, pl.ds(0, width), (target * 2 + y) * tok_rows, got_dp.at[slot])

    def over_dp(step):
        y_swaps[step].wait_recv()
        add_into(total, pl.ds(0, width), (order[step] * 2 + y) * tok_rows, got_y.at[step])
        for here in range(n_dp):
            target = orders[here][step]

            @pl.when(z == here)
            def _():
                if target == here:
                    if here > 0:
                        add_from(target, True)
                    if here < n_dp - 1:
                        add_from(target, False)
                else:
                    up = target > here
                    if 0 < here < n_dp - 1:
                        add_from(target, up)
                    along(target, up).start()

    phases.go("shared_gate")
    over_x[0].wait_recv()
    add_block(sum_sgate, x_sgate)
    size = t_sgate.shape[1]
    along_dp = []
    for dz in (2, 3, 1, 0):
        to = lax.bitwise_xor(z, jnp.int32(dz))
        src = sum_sgate.at[rows_of(to, size), :]
        if dz:
            item = wire.copy(src, t_sgate.at[z], near(dz, y))
            item.start()
        else:
            item = inside.start(src, t_sgate.at[z])
        along_dp.append(item)

    def piece(dx, sibling):
        return lax.bitwise_xor(chip, jnp.int32(dx)) * 2 + (1 - core if sibling else core)

    quarter = width // 4
    tile = quarter // 2

    def in_grads(index):
        def one(part, carry):
            at = pl.ds(pl.multiple_of(index * quarter + part * tile, tile), tile)
            value = dot_f32(rows[:, at], d_hid[...], 0, 0)
            wg[at, :] = value[:, 0:units].astype(low)
            wu[at, :] = value[:, units : 2 * units].astype(low)
            return carry

        lax.fori_loop(0, 2, one, 0)

    def down_grads(index):
        at = rows_of(index, quarter)
        wd[:, at] = dot_f32(hidden[...], grads[:, at], 0, 0).astype(low)

    phases.go("in_grads")
    sent = {}
    for dx in (1, 0):
        index = piece(dx, True)
        in_grads(index)
        at = rows_of(index, quarter)
        sent[dx] = [
            wire.copy(wg.at[at, :], got_gate.at[dx], place.core),
            wire.copy(wu.at[at, :], got_up.at[dx], place.core),
        ]
        for item in sent[dx]:
            item.start()
    for dx in (1, 0):
        in_grads(piece(dx, False))
    phases.go("gate_sums")

    def finish_piece(grad, dx, got, target):
        at = rows_of(piece(dx, False), quarter)
        add_block(grad.at[at, :], got.at[dx])
        if target is not None:
            stores.append(inside.start(grad.at[at, :], target))
        return grad.at[at, :]

    stores = []
    sent[1][0].wait_recv()
    gate_over = wire.copy(finish_piece(wg, 1, got_gate, None), x_gate, place.over_x)
    gate_over.start()
    phases.go("over_dp_one")
    over_dp(0)
    phases.go("down_grads")
    down = {}
    for dx in (1, 0):
        index = piece(dx, True)
        down_grads(index)
        down[dx] = wire.copy(wd.at[:, rows_of(index, quarter)], got_down.at[dx], place.core)
        down[dx].start()
    for dx in (1, 0):
        down_grads(piece(dx, False))
    phases.go("over_dp_two")
    over_dp(1)
    phases.go("sums")
    sent[1][1].wait_recv()
    finish_piece(wu, 1, got_up, give_up)
    for item in sent[0]:
        item.wait_recv()
    finish_piece(wg, 0, got_gate, keep_gate)
    finish_piece(wu, 0, got_up, keep_up)
    for dx, target in ((1, give_down), (0, keep_down)):
        down[dx].wait_recv()
        at = rows_of(piece(dx, False), quarter)
        add_into(wd, at, 0, got_down.at[dx])
        stores.append(inside.start(wd.at[:, at], target))
    phases.go("over_dp_three")
    over_dp(2)
    phases.go("over_dp_own")
    over_dp(3)
    for here in range(n_dp):

        @pl.when(z == here)
        def _():
            for target in range(n_dp):
                if target != here:
                    along(target, target > here).wait_send()


    def add_up(at):
        mine = pl.ds(pl.multiple_of(group * tok_rows + at.start, at.size), at.size)
        own_sum[at, :] = total[mine, :].astype(f32)

    by_rows(tok_rows, 16, add_up)
    phases.go("wait_all")
    for item in stores:
        item.wait()
    for item in over_x[1:] + scalar_items + along_dp + [gate_over]:
        item.wait_recv()
    wire.drain()
    phases.go(None)


def finish_grads(n_ctx, *refs):
    (
        t_gate, t_up, t_down, own_gate, own_up, own_down,
        far_gate, far_up, far_down, heads, out_weight, hidden, moe_sum,
        o_sgate, o_sup, o_sdown, o_egate, o_eup, o_edown, o_query, o_key, o_value, o_out, o_mixed,
    ) = refs
    f32 = jnp.float32
    n_dp, share, units = t_gate.shape
    for source, target in ((t_gate, o_sgate), (t_up, o_sup)):
        target[...] = jnp.concatenate([source[k].astype(f32) for k in range(n_dp)], axis=1)
    o_sdown[...] = t_down[0].astype(f32)
    for own, far, target in (
        (own_gate, far_gate, o_egate), (own_up, far_up, o_eup), (own_down, far_down, o_edown),
    ):

        def add(at):
            target[at, :] = own[at, :].astype(f32) + far[at, :].astype(f32)

        by_rows(target.shape[0], 32, add)

    o_mixed[...] = (hidden[...] + moe_sum[...].astype(f32)).astype(o_mixed.dtype)
    cols = heads.shape[2] // 3
    for k, target in enumerate((o_query, o_key, o_value)):
        for c in range(n_ctx):
            target[:, c * cols : (c + 1) * cols] = heads[c, :, k * cols : (k + 1) * cols].astype(f32)
    o_out[...] = out_weight[0].astype(f32)


def whole_tables(seq_len, head_dim):
    half = head_dim // 2
    freq = np.float32(THETA) ** (-(2.0 * np.arange(half, dtype=np.float32)) / np.float32(head_dim))
    angle = np.arange(seq_len, dtype=np.float32)[:, None] * freq.astype(np.float32)[None, :]
    cosine, sine = np.cos(angle), np.sin(angle)
    return (
        jnp.asarray(np.concatenate([cosine, cosine], axis=1), jnp.float32),
        jnp.asarray(np.concatenate([-sine, sine], axis=1), jnp.float32),
    )


def tokens_plan(
    tokens,
    out_grad,
    expert_ids,
    norm1_gain,
    w_query,
    w_key,
    w_value,
    query_bias_heads,
    bias_key,
    bias_value,
    w_out,
    norm2_gain,
    w_router,
    shared_mix,
    shared_in_gate,
    shared_in_up,
    shared_down,
    expert_gate,
    expert_up,
    expert_down,
):
    low = jnp.bfloat16
    f32 = jnp.float32
    tok_rows, width = tokens.shape
    n_dp, n_ctx, n_half = (lax.axis_size(name) for name in (DP, CONTEXT, EXPERT))
    dp, ctx, half = (lax.axis_index(name) for name in (DP, CONTEXT, EXPERT))
    half_heads, head_dim = query_bias_heads.shape
    heads = half_heads // n_ctx
    cols = heads * head_dim
    seq_len = tok_rows * n_ctx * n_half
    n_blocks = seq_len // BLOCK
    n_experts = w_router.shape[1]
    n_group = n_dp * n_half
    my_expert = dp * n_half + half

    def group_out(rows):
        return lax.psum_scatter(rows, (DP, EXPERT), scatter_dimension=0, tiled=True)

    small = jnp.concatenate(
        [w_router.T, shared_mix[None], norm1_gain[None], norm2_gain[None]], axis=0
    )
    small = jnp.pad(small, ((0, 16 - small.shape[0]), (0, 0)))
    ids = jnp.pad(expert_ids.T, ((0, 8 - expert_ids.shape[1]), (0, 0)), constant_values=-1)
    hidden_units = shared_in_gate.shape[1] // n_dp

    biases = jnp.stack([query_bias_heads, bias_key, bias_value]).astype(f32)
    biases = lax.dynamic_slice_in_dim(biases, ctx * heads, heads, 1).reshape(3, cols)
    cosine, sine = whole_tables(seq_len, head_dim)
    vmem = pl.BlockSpec(memory_space=pltpu.VMEM)
    anywhere = pl.BlockSpec(memory_space=pl.ANY)
    share = w_query.shape[0]
    half_width = width // 2
    (
        attn_in, query, keys, values, attn, lse, hidden_own, moe_in,
        heads_weight, wo, sg, su, sd, small, ids_group, dy_begun,
    ) = pl.pallas_call(
        lambda *refs: forward_kernel(n_blocks, n_dp, *refs),
        out_shape=[
            like((seq_len, width), low),
            like((seq_len, cols), low),
            like((seq_len, cols), low),
            like((seq_len, cols), low),
            like((seq_len, cols), low),
            like((seq_len, cols), f32),
            like((tok_rows, width), f32),
            like((n_group * tok_rows, width), low),
            like((width, 3 * cols), low),
            like((cols, width), low),
            like((n_dp, n_ctx, share, hidden_units), low),
            like((n_dp, n_ctx, share, hidden_units), low),
            like((hidden_units, width), low),
            like((16, width), low),
            like((n_group, 8, tok_rows), jnp.int32),
            like((n_group * tok_rows, width), low),
        ],
        in_specs=[anywhere] * 11 + [vmem] * 3,
        out_specs=[anywhere] * 13 + [vmem] + [anywhere] * 2,
        scratch_shapes=[
            pltpu.VMEM((seq_len, width), low),
            pltpu.VMEM((seq_len, width), low),
            pltpu.VMEM((4, tok_rows, width), low),
            pltpu.VMEM((4, tok_rows, half_width), low),
            pltpu.VMEM((2, tok_rows, half_width), low),
            pltpu.VMEM((seq_len, width), low),
            pltpu.VMEM((seq_len, cols), low),
            pltpu.VMEM((seq_len, cols), low),
            pltpu.VMEM((seq_len, cols), low),
            pltpu.VMEM((seq_len, cols), low),
            pltpu.VMEM((seq_len, cols), f32),
            pltpu.VMEM((tok_rows, width), f32),
            pltpu.VMEM((width, 3 * cols), low),
            pltpu.VMEM((cols, width), low),
            pltpu.VMEM((2, share, n_dp * hidden_units), low),
            pltpu.VMEM((2, n_dp, share, hidden_units), low),
            pltpu.SemaphoreType.DMA((160,)),
            pltpu.SemaphoreType.DMA((160,)),
            pltpu.SemaphoreType.DMA((32,)),
        ],
        name="forward",
        compiler_params=pltpu.CompilerParams(
            collective_id=1, has_side_effects=True, vmem_limit_bytes=60 * 2**20
        ),
    )(
        tokens, out_grad, small, ids, w_query, w_key, w_value, w_out,
        shared_in_gate, shared_in_up, shared_down, biases, cosine, sine,
    )
    sg, su = sg.reshape(width, hidden_units), su.reshape(width, hidden_units)
    units = expert_gate.shape[2]
    s_weights = [
        pltpu.VMEM((width, hidden_units), low),
        pltpu.VMEM((width, hidden_units), low),
        pltpu.VMEM((hidden_units, width), low),
    ]
    gate_weight, up_weight, down_weight = expert_gate[0], expert_up[0], expert_down[0]
    slots = n_group * CAP
    group_rows = n_group * tok_rows
    (
        token_cols, pick, s_slope, s_silu, s_hidden, e_slope, e_silu, e_hidden, rows_in,
        moe_part, e_out, shared, dy_group,
    ) = pl.pallas_call(
        lambda *refs: moe_forward(n_dp, *refs),
        out_shape=[
            like((group_rows, 128), f32),
            like((n_group, CAP, tok_rows), low),
        ]
        + [like((group_rows, hidden_units), low)] * 3
        + [like((slots, units), low)] * 3
        + [
            like((slots, width), low),
            like((group_rows, width), low),
            like((slots, width), low),
            like((group_rows, width), low),
            like((group_rows, width), low),
        ],
        in_specs=[anywhere] * 2 + [vmem] * 2 + [anywhere] * 6,
        out_specs=[vmem] * 2 + [anywhere] * 11,
        scratch_shapes=[
            pltpu.VMEM((group_rows, width), low),
            pltpu.VMEM((width, units), low),
            pltpu.VMEM((width, units), low),
            pltpu.VMEM((units, width), low),
        ]
        + [pltpu.VMEM((group_rows, hidden_units), low)] * 3
        + [pltpu.VMEM((slots, units), low)] * 3
        + [pltpu.VMEM((slots, width), low)] * 2
        + [pltpu.VMEM((group_rows, width), low)]
        + s_weights
        + [pltpu.SemaphoreType.DMA((16,))] * 2
        + [pltpu.SemaphoreType.DMA((24,))],
        name="moe_forward",
        compiler_params=pltpu.CompilerParams(
            collective_id=3, has_side_effects=True, vmem_limit_bytes=63 * 2**20
        ),
        cost_estimate=pl.CostEstimate(
            flops=6 * width * (group_rows * hidden_units + slots * units),
            bytes_accessed=2 * (9 * width * units + 4 * group_rows * width),
            transcendentals=0,
        ),
        input_output_aliases={0: 12},
    )(dy_begun, moe_in, small, ids_group, sg, su, sd, gate_weight, up_weight, down_weight)
    lanes = -(-hidden_units // 128) * 128
    block_kinds = [(n_dp, share, hidden_units)] * 2 + [(n_dp, hidden_units, share)]
    shared_all = [(n_dp * n_ctx, share, hidden_units)] * 2 + [(n_dp * n_ctx, hidden_units, share)]
    results = pl.pallas_call(
        lambda *refs: shared_backward(n_dp, *refs),
        out_shape=[
            like((slots, width), low),
            like((group_rows, width), low),
            like((n_group, 8, tok_rows), f32),
        ]
        + [like((kind[0] * kind[1], kind[2]), low) for kind in block_kinds] * 2,
        in_specs=[anywhere] + [vmem] * 2 + [anywhere] * 9,
        out_specs=[anywhere] * 2 + [vmem] + [anywhere] * 6,
        scratch_shapes=[
            pltpu.VMEM((4, tok_rows, width), low),
            pltpu.VMEM((4, CAP, width), low),
            pltpu.VMEM((4, tok_rows, width), low),
            pltpu.VMEM((group_rows, width), low),
            pltpu.VMEM((slots, width), low),
            pltpu.VMEM((group_rows, 2 * lanes), low),
            pltpu.VMEM((group_rows, width), low),
            pltpu.VMEM((group_rows, width), low),
            pltpu.VMEM((group_rows, hidden_units), low),
        ]
        + [pltpu.VMEM(kind, low) for kind in shared_all]
        + [pltpu.VMEM((2, *kind), low) for kind in block_kinds]
        + s_weights
        + [pltpu.VMEM((group_rows, hidden_units), low)] * 2
        + [
            pltpu.VMEM((tok_rows, 128), f32),
            pltpu.VMEM((CAP, width), f32),
            pltpu.VMEM((CAP, 128), f32),
        ]
        + [pltpu.SemaphoreType.DMA((32,))] * 2
        + [pltpu.SemaphoreType.DMA((48,)), pltpu.SemaphoreType.DMA((12,))],
        name="shared_backward",
        compiler_params=pltpu.CompilerParams(
            collective_id=4, has_side_effects=True, vmem_limit_bytes=63 * 2**20
        ),
        cost_estimate=pl.CostEstimate(
            flops=12 * width * group_rows * hidden_units,
            bytes_accessed=2 * (9 * width * hidden_units + 8 * group_rows * width),
            transcendentals=0,
        ),
    )(
        dy_group, token_cols, pick, sg, su, sd, s_slope, s_silu, s_hidden, e_out, shared, moe_in,
    )
    grads_in, shared_part, scalars = results[:3]
    keep = results[3:6]
    give = results[6:9]
    quarter = width // n_ctx
    e_wide, e_tall = (quarter, units), (units, quarter)
    flat_kinds = [(kind[0] * kind[1], kind[2]) for kind in block_kinds]
    (
        own_sum, got_scalars, t_sgate, x_sup, x_sdown,
        keep_gate, keep_up, keep_down, give_up, give_down, x_gate,
    ) = pl.pallas_call(
        lambda *refs: routed_backward(n_dp, *refs),
        out_shape=[like((tok_rows, width), f32), like((n_group, 8, tok_rows), f32)]
        + [like(block_kinds[0], low)]
        + [like(kind, low) for kind in flat_kinds[1:]]
        + [like(kind, low) for kind in (e_wide, e_wide, e_tall, e_wide, e_tall, e_wide)],
        in_specs=[anywhere] * 14 + [vmem],
        out_specs=[vmem] + [anywhere] * 10,
        scratch_shapes=[
            pltpu.VMEM((width, units), low),
            pltpu.VMEM((width, units), low),
            pltpu.VMEM((units, width), low),
            pltpu.VMEM((slots, width), low),
            pltpu.VMEM((slots, width), low),
            pltpu.VMEM((slots, units), low),
            pltpu.VMEM((slots, units), low),
            pltpu.VMEM((slots, units), low),
            pltpu.VMEM((slots, 2 * units), low),
            pltpu.VMEM((slots, width), low),
            pltpu.VMEM((group_rows, width), low),
            pltpu.VMEM((2, *e_wide), low),
            pltpu.VMEM((2, *e_wide), low),
            pltpu.VMEM((2, *e_tall), low),
            pltpu.VMEM((n_dp, tok_rows, width), low),
            pltpu.VMEM((2 * (n_dp - 1), tok_rows, width), low),
            pltpu.VMEM(flat_kinds[0], low),
            pltpu.VMEM(flat_kinds[0], low),
            pltpu.SemaphoreType.DMA((32,)),
            pltpu.SemaphoreType.DMA((32,)),
            pltpu.SemaphoreType.DMA((24,)),
        ],
        name="routed_backward",
        compiler_params=pltpu.CompilerParams(
            collective_id=5, has_side_effects=True, vmem_limit_bytes=63 * 2**20
        ),
        cost_estimate=pl.CostEstimate(
            flops=12 * width * slots * units,
            bytes_accessed=2 * (12 * width * units + 4 * group_rows * width),
            transcendentals=0,
        ),
    )(
        grads_in, rows_in, gate_weight, up_weight, down_weight, e_slope, e_silu, e_hidden,
        shared_part, scalars, keep[0], *give, pick,
    )
    moe_sum = group_out(moe_part)

    own_cols = lax.dynamic_slice_in_dim(token_cols, my_expert * tok_rows, tok_rows, 0)
    probs_own = own_cols[:, :n_experts].T
    mix_own = own_cols[:, n_experts][None]
    by_share = n_ctx * share
    s_wide = (share, hidden_units)
    s_tall = (hidden_units, share)
    s_kinds = (s_wide, s_wide, s_tall)
    e_kinds = (e_wide, e_wide, e_tall)
    results = pl.pallas_call(
        lambda *refs: backward_kernel(n_blocks, n_dp, *refs),
        out_shape=[
            like((tok_rows, width), low),
            like((n_ctx, share, 3 * cols), low),
            like((n_ctx, cols, share), low),
            like((16, share), f32),
            like((n_ctx, 8, head_dim), f32),
        ]
        + [like((n_dp, *kind), low) for kind in s_kinds[1:]]
        + [like(kind, low) for kind in e_kinds[1:]]
        + [like((n_dp, *kind), low) for kind in s_kinds[1:]],
        in_specs=[vmem] * 2 + [anywhere] * 9 + [vmem] * 3 + [anywhere] * 10,
        out_specs=[vmem] + [anywhere] * 2 + [vmem] * 2 + [anywhere] * 6,
        scratch_shapes=[
            pltpu.VMEM((seq_len, width), low),
            pltpu.VMEM((tok_rows, width), f32),
            pltpu.VMEM((tok_rows, width), f32),
            pltpu.VMEM((tok_rows, width), low),
            pltpu.VMEM((48, tok_rows), low),
            pltpu.VMEM((2, 16, width), f32),
            pltpu.VMEM((seq_len, width), low),
            pltpu.VMEM((seq_len, cols), low),
            pltpu.VMEM((seq_len, 3 * cols), low),
            pltpu.VMEM((seq_len, head_dim), f32),
            pltpu.VMEM((seq_len, head_dim), f32),
            pltpu.VMEM((4, tok_rows, width), low),
            pltpu.VMEM((4, tok_rows, half_width), low),
            pltpu.VMEM((2, tok_rows, half_width), low),
            pltpu.VMEM((width, 3 * cols), low),
            pltpu.VMEM((cols, width), low),
            pltpu.VMEM((n_dp, by_share, 3 * cols), low),
            pltpu.VMEM((n_dp, by_share, 3 * cols), low),
            pltpu.VMEM((n_dp, cols, by_share), low),
            pltpu.VMEM((n_dp, cols, by_share), low),
            pltpu.VMEM((cols, by_share), low),
            pltpu.VMEM((n_dp * n_ctx, 24, share), f32),
            pltpu.VMEM((n_dp * n_ctx, 24, share), f32),
            pltpu.VMEM((2, 16, share), f32),
            pltpu.VMEM((3, 2, *s_wide), low),
            pltpu.VMEM((3, 2, *s_tall), low),
            pltpu.VMEM((tok_rows, width), f32),
            pltpu.VMEM((tok_rows, width), low),
            pltpu.VMEM((tok_rows, width), low),
            pltpu.VMEM((width, 3 * cols), low),
            pltpu.VMEM((cols, width), low),
            pltpu.VMEM((seq_len, cols), low),
            pltpu.VMEM((seq_len, cols), low),
            pltpu.VMEM((seq_len, cols), low),
            pltpu.VMEM((seq_len, cols), low),
            pltpu.VMEM((seq_len, cols), f32),
            pltpu.VMEM((seq_len, width), low),
            pltpu.VMEM((seq_len, head_dim), f32),
            pltpu.VMEM((seq_len, head_dim), f32),
            pltpu.SemaphoreType.DMA((160,)),
            pltpu.SemaphoreType.DMA((160,)),
            pltpu.SemaphoreType.DMA((32,)),
            pltpu.SemaphoreType.DMA((6,)),
        ],
        name="backward",
        compiler_params=pltpu.CompilerParams(
            collective_id=2, has_side_effects=True, vmem_limit_bytes=63 * 2**20
        ),
    )(
        own_sum, got_scalars, *keep[1:], x_sup, x_sdown, give_up, give_down,
        hidden_own, out_grad, tokens, small, probs_own, mix_own,
        heads_weight, wo, query, keys, values, attn, lse, attn_in, cosine, sine,
    )
    input_grad, heads_grad, out_weight_grad, small_grad, bias_grad = results[:5]
    s_done = (t_sgate, *results[5:7])
    e_own, e_other = (keep_gate, keep_up, keep_down), (x_gate, *results[7:9])
    finished = pl.pallas_call(
        lambda *refs: finish_grads(n_ctx, *refs),
        out_shape=[
            like((share, n_dp * hidden_units), f32),
            like((share, n_dp * hidden_units), f32),
            like((n_dp * hidden_units, share), f32),
            like(e_wide, f32),
            like(e_wide, f32),
            like(e_tall, f32),
            like((share, n_ctx * cols), f32),
            like((share, n_ctx * cols), f32),
            like((share, n_ctx * cols), f32),
            like((n_ctx * cols, share), f32),
            like((tok_rows, width), low),
        ],
        grid=(4,),
        in_specs=[pl.BlockSpec((n_dp, share // 4, hidden_units), lambda i: (0, i, 0))] * 2
        + [pl.BlockSpec((1, hidden_units, share), lambda i: (i, 0, 0))]
        + [pl.BlockSpec((kind[0] // 4, kind[1]), lambda i: (i, 0)) for kind in e_kinds * 2]
        + [
            pl.BlockSpec((n_ctx, share // 4, 3 * cols), lambda i: (0, i, 0)),
            pl.BlockSpec((1, cols, share), lambda i: (i, 0, 0)),
            pl.BlockSpec((tok_rows // 4, width), lambda i: (i, 0)),
            pl.BlockSpec((tok_rows // 4, width), lambda i: (i, 0)),
        ],
        out_specs=[pl.BlockSpec((share // 4, n_dp * hidden_units), lambda i: (i, 0))] * 2
        + [pl.BlockSpec((hidden_units, share), lambda i: (i, 0))]
        + [pl.BlockSpec((kind[0] // 4, kind[1]), lambda i: (i, 0)) for kind in e_kinds]
        + [pl.BlockSpec((share // 4, n_ctx * cols), lambda i: (i, 0))] * 3
        + [
            pl.BlockSpec((cols, share), lambda i: (i, 0)),
            pl.BlockSpec((tok_rows // 4, width), lambda i: (i, 0)),
        ],
        name="finish_grads",
        compiler_params=pltpu.CompilerParams(vmem_limit_bytes=63 * 2**20),
    )(*s_done, *e_own, *e_other, heads_grad, out_weight_grad, hidden_own, moe_sum)
    grad_sgate, grad_sup, grad_sdown = finished[:3]
    routed = [item[None] for item in finished[3:6]]
    heads_grad = finished[6:9]
    grad_out, mixed = finished[9:11]
    bias_sum = bias_grad[:, : 3 * heads].reshape(n_ctx, 3, heads, head_dim)
    bias_sum = bias_sum.transpose(1, 0, 2, 3).reshape(3, half_heads, head_dim)
    bias_share = head_dim // (n_dp * n_ctx)
    bias_sum = lax.dynamic_slice_in_dim(bias_sum, (dp * n_ctx + ctx) * bias_share, bias_share, 2)
    return (
        mixed,
        input_grad,
        small_grad[n_experts + 1],
        heads_grad[0],
        heads_grad[1],
        heads_grad[2],
        bias_sum[0],
        bias_sum[1],
        bias_sum[2],
        grad_out,
        small_grad[n_experts + 2],
        small_grad[:n_experts].T,
        small_grad[n_experts],
        grad_sgate,
        grad_sup,
        grad_sdown,
        routed[0],
        routed[1],
        routed[2],
    )


def on_device(*arrays):
    sizes = [lax.axis_size(name) for name in (DP, CONTEXT, EXPERT)]
    if sizes == [4, 4, 2] and arrays[7].shape[0] % sizes[1] == 0:
        return tokens_plan(*arrays)
    return weights_plan(*arrays)


def solution(mesh):
    placed = (
        P((DP, CONTEXT, EXPERT), None),
        P((DP, CONTEXT, EXPERT), None),
        P((DP, CONTEXT, EXPERT), None),
        P((DP, CONTEXT)),
        P((DP, CONTEXT), EXPERT),
        P((DP, CONTEXT), EXPERT),
        P((DP, CONTEXT), EXPERT),
        P(EXPERT, None),
        P(EXPERT, None),
        P(EXPERT, None),
        P(EXPERT, (DP, CONTEXT)),
        P((DP, CONTEXT)),
        P((DP, CONTEXT), None),
        P((DP, CONTEXT)),
        P((DP, CONTEXT), EXPERT),
        P((DP, CONTEXT), EXPERT),
        P(EXPERT, (DP, CONTEXT)),
        P((DP, EXPERT), None, None),
        P((DP, EXPERT), None, None),
        P((DP, EXPERT), None, None),
    )
    return jax.shard_map(
        on_device,
        mesh=mesh,
        in_specs=placed,
        out_specs=(
            P((DP, CONTEXT, EXPERT), None),
            P((DP, CONTEXT, EXPERT), None),
            P((DP, CONTEXT)),
            P((DP, CONTEXT), EXPERT),
            P((DP, CONTEXT), EXPERT),
            P((DP, CONTEXT), EXPERT),
            P(EXPERT, (DP, CONTEXT)),
            P(EXPERT, (DP, CONTEXT)),
            P(EXPERT, (DP, CONTEXT)),
            P(EXPERT, (DP, CONTEXT)),
            P((DP, CONTEXT)),
            P((DP, CONTEXT), None),
            P((DP, CONTEXT)),
            P((DP, CONTEXT), EXPERT),
            P((DP, CONTEXT), EXPERT),
            P(EXPERT, (DP, CONTEXT)),
            P((DP, EXPERT), CONTEXT, None),
            P((DP, EXPERT), CONTEXT, None),
            P((DP, EXPERT), None, CONTEXT),
        ),
        check_vma=False,
    )
```

```python
import math

import jax
import jax.numpy as jnp
import numpy as np
from jax import lax
from jax.experimental import pallas as pl
from jax.experimental.pallas import tpu as pltpu
from jax.sharding import PartitionSpec as P

DP, CONTEXT, EXPERT = "dp", "context", "expert"
BLOCK = 256
CAP = 96


EPS = 1e-06
THETA = 1000000.0
HIGH = lax.Precision.HIGHEST


def rope_tables(positions, head_dim):
    half = head_dim // 2
    freq = THETA ** (-(2.0 * jnp.arange(half, dtype=jnp.float32)) / head_dim)
    angle = positions.astype(jnp.float32)[:, None] * freq[None, :]
    return (jnp.cos(angle)[:, None, :], jnp.sin(angle)[:, None, :])


def rotate(values, cosine, sine):
    half = values.shape[-1] // 2
    first = values[..., :half]
    second = values[..., half:]
    return jnp.concatenate(
        [first * cosine - second * sine, second * cosine + first * sine], axis=-1
    )


def rotate_back(values, cosine, sine):
    half = values.shape[-1] // 2
    first = values[..., :half]
    second = values[..., half:]
    return jnp.concatenate(
        [first * cosine + second * sine, second * cosine - first * sine], axis=-1
    )


def to_groups(matrix, groups, group_size, head_dim):
    return matrix.reshape(matrix.shape[0], groups, group_size, head_dim).transpose(1, 2, 0, 3)


def from_groups(stacked):
    return stacked.transpose(2, 0, 1, 3).reshape(stacked.shape[2], -1)


def silu_slope(values):
    sigma = jax.nn.sigmoid(values)
    return sigma * (1.0 + values * (1.0 - sigma))


def left_operand(left, right):
    return jnp.dot(left.T, right, preferred_element_type=jnp.float32)


def mat_right(left, right):
    return jnp.dot(left, right.T, preferred_element_type=jnp.float32)


def weights_plan(
    tokens,
    out_grad,
    expert_ids,
    norm1_gain,
    w_query,
    w_key,
    w_value,
    query_bias_heads,
    bias_key,
    bias_value,
    w_out,
    norm2_gain,
    w_router,
    shared_mix,
    shared_in_gate,
    shared_in_up,
    shared_down,
    expert_gate,
    expert_up,
    expert_down,
):
    tok_rows = tokens.shape[0]
    width = tokens.shape[1]
    my_half = lax.axis_index(EXPERT)
    my_piece = lax.axis_index(CONTEXT)
    n_pieces = lax.axis_size(CONTEXT)
    local_heads = query_bias_heads.shape[0]
    head_dim = query_bias_heads.shape[1]
    group_size = 2
    groups = local_heads // group_size
    score_scale = 1.0 / math.sqrt(head_dim)
    (
        full_query,
        full_key,
        full_value,
        full_out,
        full_sgate,
        full_sup,
        full_sdown,
        full_router,
        full_mix,
        full_gain_one,
        full_gain_two,
    ) = (
        lax.all_gather(w_query, (DP, CONTEXT), axis=0, tiled=True),
        lax.all_gather(w_key, (DP, CONTEXT), axis=0, tiled=True),
        lax.all_gather(w_value, (DP, CONTEXT), axis=0, tiled=True),
        lax.all_gather(w_out, (DP, CONTEXT), axis=1, tiled=True),
        lax.all_gather(shared_in_gate, (DP, CONTEXT), axis=0, tiled=True),
        lax.all_gather(shared_in_up, (DP, CONTEXT), axis=0, tiled=True),
        lax.all_gather(shared_down, (DP, CONTEXT), axis=1, tiled=True),
        lax.all_gather(w_router, (DP, CONTEXT), axis=0, tiled=True),
        lax.all_gather(shared_mix, (DP, CONTEXT), axis=0, tiled=True),
        lax.all_gather(norm1_gain, (DP, CONTEXT), axis=0, tiled=True),
        lax.all_gather(norm2_gain, (DP, CONTEXT), axis=0, tiled=True),
    )
    x_piece, dy_piece = (
        lax.all_gather(tokens, EXPERT, axis=0, tiled=True),
        lax.all_gather(out_grad, EXPERT, axis=0, tiled=True),
    )
    piece_rows = x_piece.shape[0]
    seq_len = piece_rows * n_pieces
    own_start = my_half * tok_rows
    positions = my_piece * piece_rows + jnp.arange(piece_rows)
    cosine, sine = rope_tables(positions, head_dim)
    query_blocks = positions // BLOCK
    key_blocks = jnp.arange(seq_len) // BLOCK
    visible = key_blocks[None, :] <= query_blocks[:, None]
    x_float = x_piece.astype(jnp.float32)
    rstd_one = lax.rsqrt(jnp.mean(x_float * x_float, axis=1, keepdims=True) + EPS)
    normed_one = x_float * rstd_one
    gain_one = full_gain_one.astype(jnp.float32)
    attn_in = (normed_one * gain_one).astype(jnp.bfloat16)
    q_pre = jnp.dot(
        attn_in, full_query, preferred_element_type=jnp.float32
    ) + query_bias_heads.astype(jnp.float32).reshape(-1)
    k_pre = jnp.dot(attn_in, full_key, preferred_element_type=jnp.float32) + bias_key.astype(
        jnp.float32
    ).reshape(-1)
    v_pre = jnp.dot(attn_in, full_value, preferred_element_type=jnp.float32) + bias_value.astype(
        jnp.float32
    ).reshape(-1)
    q_rot = (
        rotate(q_pre.reshape(piece_rows, local_heads, head_dim), cosine, sine)
        .reshape(piece_rows, -1)
        .astype(jnp.bfloat16)
    )
    k_rot = (
        rotate(k_pre.reshape(piece_rows, local_heads, head_dim), cosine, sine)
        .reshape(piece_rows, -1)
        .astype(jnp.bfloat16)
    )
    v_low = v_pre.astype(jnp.bfloat16)
    keys_all, values_all = (
        lax.all_gather(k_rot, CONTEXT, axis=0, tiled=True),
        lax.all_gather(v_low, CONTEXT, axis=0, tiled=True),
    )
    query_grp = to_groups(q_rot, groups, group_size, head_dim)
    keys_grp = to_groups(keys_all, groups, group_size, head_dim)
    values_grp = to_groups(values_all, groups, group_size, head_dim)

    def attend_group(args):
        group_query, group_keys, group_values = args
        scores = (
            jnp.einsum("hqd,hkd->hqk", group_query, group_keys, preferred_element_type=jnp.float32)
            * score_scale
        )
        scores = jnp.where(visible[None], scores, -jnp.inf)
        row_top = jnp.max(scores, axis=2, keepdims=True)
        expo = jnp.exp(scores - row_top)
        totals = jnp.sum(expo, axis=2, keepdims=True)
        probs = (expo / totals).astype(jnp.bfloat16)
        result = jnp.einsum("hqk,hkd->hqd", probs, group_values, preferred_element_type=jnp.float32)
        return (result, row_top[..., 0] + jnp.log(totals[..., 0]))

    attn_grp, lse_grp = lax.map(attend_group, (query_grp, keys_grp, values_grp))
    attn_low = from_groups(attn_grp).astype(jnp.bfloat16)
    out_partial = jnp.dot(attn_low, full_out, preferred_element_type=jnp.float32)
    out_full = lax.psum(out_partial, EXPERT)
    hidden_one = x_float + out_full
    rstd_two = lax.rsqrt(jnp.mean(hidden_one * hidden_one, axis=1, keepdims=True) + EPS)
    normed_two = hidden_one * rstd_two
    gain_two = full_gain_two.astype(jnp.float32)
    moe_in = (normed_two * gain_two).astype(jnp.bfloat16)
    mix = jax.nn.sigmoid(jnp.dot(moe_in, full_mix, preferred_element_type=jnp.float32))
    s_gate = jnp.dot(moe_in, full_sgate, preferred_element_type=jnp.float32)
    s_up = jnp.dot(moe_in, full_sup, preferred_element_type=jnp.float32)
    s_silu = jax.nn.silu(s_gate)
    s_hidden = (s_silu * s_up).astype(jnp.bfloat16)
    shared_own = lax.psum_scatter(
        jnp.dot(s_hidden, full_sdown, preferred_element_type=jnp.float32),
        EXPERT,
        scatter_dimension=0,
        tiled=True,
    )
    moe_own = lax.dynamic_slice_in_dim(moe_in, own_start, tok_rows, 0)
    hidden_own = lax.dynamic_slice_in_dim(hidden_one, own_start, tok_rows, 0)
    mix_own = lax.dynamic_slice_in_dim(mix, own_start, tok_rows, 0)
    dy_own = out_grad.astype(jnp.float32)
    n_experts = full_router.shape[1]
    router_probs = jax.nn.softmax(
        jnp.dot(moe_own, full_router, preferred_element_type=jnp.float32), axis=1
    )
    picked = (expert_ids[:, :, None] == jnp.arange(n_experts)[None, None, :]).astype(jnp.float32)
    gates = jnp.sum(picked * router_probs[:, None, :], axis=2)
    route_hot = (
        (expert_ids[:, :, None] == jnp.arange(n_experts)[None, None, :])
        .astype(jnp.int32)
        .reshape(-1, n_experts)
    )
    earlier = jnp.cumsum(route_hot, axis=0) - route_hot
    slots = jnp.sum(earlier * route_hot, axis=1)
    places = expert_ids.reshape(-1) * CAP + slots
    route_rows = jnp.repeat(moe_own, expert_ids.shape[1], axis=0)
    route_grads = (
        gates.reshape(-1)[:, None] * jnp.repeat(dy_own, expert_ids.shape[1], axis=0)
    ).astype(jnp.bfloat16)
    send_rows = (
        jnp.zeros((n_experts * CAP, width), jnp.bfloat16)
        .at[places]
        .set(route_rows)
        .reshape(n_experts, CAP, width)
    )
    send_grads = (
        jnp.zeros((n_experts * CAP, width), jnp.bfloat16)
        .at[places]
        .set(route_grads)
        .reshape(n_experts, CAP, width)
    )
    gate_weight = expert_gate[0]
    up_weight = expert_up[0]
    down_weight = expert_down[0]
    rows_in = lax.all_to_all(send_rows, (DP, EXPERT), split_axis=0, concat_axis=0, tiled=True)
    grads_in = lax.all_to_all(send_grads, (DP, EXPERT), split_axis=0, concat_axis=0, tiled=True)
    sources = rows_in.shape[0]
    items = rows_in.shape[1]
    flat_in = rows_in.reshape(-1, width)
    flat_grad = grads_in.reshape(-1, width)
    e_gate = jnp.dot(flat_in, gate_weight, preferred_element_type=jnp.float32)
    e_up = jnp.dot(flat_in, up_weight, preferred_element_type=jnp.float32)
    e_silu = jax.nn.silu(e_gate)
    e_hidden = (e_silu * e_up).astype(jnp.bfloat16)
    e_out = jnp.dot(e_hidden, down_weight, preferred_element_type=jnp.float32).astype(jnp.bfloat16)
    d_hidden = mat_right(flat_grad, down_weight)
    d_gate = (d_hidden * e_up * silu_slope(e_gate)).astype(jnp.bfloat16)
    d_up = (d_hidden * e_silu).astype(jnp.bfloat16)
    d_in = (mat_right(d_gate, gate_weight) + mat_right(d_up, up_weight)).astype(jnp.bfloat16)
    back_out = lax.all_to_all(
        e_out.reshape(sources, items, width),
        (DP, EXPERT),
        split_axis=0,
        concat_axis=0,
        tiled=True,
    )
    back_in = lax.all_to_all(
        d_in.reshape(sources, items, width),
        (DP, EXPERT),
        split_axis=0,
        concat_axis=0,
        tiled=True,
    )
    back_out, back_in, rows_seen, grads_seen, hidden_seen, dgate_seen, duplicate_visits = (
        back_out,
        back_in,
        rows_in,
        grads_in,
        e_hidden.reshape(sources, items, -1),
        d_gate.reshape(sources, items, -1),
        d_up.reshape(sources, items, -1),
    )
    flattened_rows = rows_seen.reshape(-1, width)
    routed_gate_gradient = left_operand(
        flattened_rows, dgate_seen.reshape(flattened_rows.shape[0], -1)
    )
    routed_up_gradient = left_operand(
        flattened_rows, duplicate_visits.reshape(flattened_rows.shape[0], -1)
    )
    routed_down_gradient = left_operand(
        hidden_seen.reshape(flattened_rows.shape[0], -1), grads_seen.reshape(-1, width)
    )
    routed_gate_gradient, routed_up_gradient, routed_down_gradient = (
        lax.psum_scatter(
            routed_gate_gradient[None].astype(jnp.bfloat16),
            CONTEXT,
            scatter_dimension=1,
            tiled=True,
        ).astype(jnp.float32),
        lax.psum_scatter(
            routed_up_gradient[None].astype(jnp.bfloat16),
            CONTEXT,
            scatter_dimension=1,
            tiled=True,
        ).astype(jnp.float32),
        lax.psum_scatter(
            routed_down_gradient[None].astype(jnp.bfloat16),
            CONTEXT,
            scatter_dimension=2,
            tiled=True,
        ).astype(jnp.float32),
    )
    route_out = back_out.reshape(-1, width)[places].astype(jnp.float32).reshape(tok_rows, -1, width)
    route_din = back_in.reshape(-1, width)[places].astype(jnp.float32).reshape(tok_rows, -1, width)
    moe_sum = jnp.sum(gates[:, :, None] * route_out, axis=1)
    mixed = (hidden_own + moe_sum + mix_own[:, None] * shared_own).astype(jnp.bfloat16)
    d_gates = jnp.sum(route_out * dy_own[:, None, :], axis=2)
    d_rprobs = jnp.sum(picked * d_gates[:, :, None], axis=1)
    d_logits = router_probs * (d_rprobs - jnp.sum(router_probs * d_rprobs, axis=1, keepdims=True))
    moe_own_float = moe_own.astype(jnp.float32)
    router_part = jnp.dot(moe_own_float.T, d_logits, precision=HIGH)
    d_mixlogit = jnp.sum(shared_own * dy_own, axis=1) * mix_own * (1.0 - mix_own)
    mix_part = jnp.dot(moe_own_float.T, d_mixlogit, precision=HIGH)
    d_in_own = (
        jnp.sum(route_din, axis=1)
        + jnp.dot(d_logits, full_router.astype(jnp.float32).T, precision=HIGH)
        + d_mixlogit[:, None] * full_mix.astype(jnp.float32)[None, :]
    )
    dy_float = dy_piece.astype(jnp.float32)
    d_shared = (mix[:, None] * dy_float).astype(jnp.bfloat16)
    grad_sdown = left_operand(s_hidden, d_shared)
    d_shidden = mat_right(d_shared, full_sdown)
    d_sgate = (d_shidden * s_up * silu_slope(s_gate)).astype(jnp.bfloat16)
    d_sup = (d_shidden * s_silu).astype(jnp.bfloat16)
    grad_sgate = left_operand(moe_in, d_sgate)
    grad_sup = left_operand(moe_in, d_sup)
    d_in_part = mat_right(d_sgate, full_sgate) + mat_right(d_sup, full_sup)
    d_in_part = lax.dynamic_update_slice_in_dim(
        d_in_part,
        lax.dynamic_slice_in_dim(d_in_part, own_start, tok_rows, 0) + d_in_own,
        own_start,
        0,
    )
    d_moe_in, router_grad, mix_grad = lax.psum((d_in_part, router_part, mix_part), EXPERT)
    d_norm_two = d_moe_in * gain_two
    gain_two_grad = jnp.sum(d_moe_in * normed_two, axis=0)
    d_hidden_one = dy_float + rstd_two * (
        d_norm_two - normed_two * jnp.mean(d_norm_two * normed_two, axis=1, keepdims=True)
    )
    d_proj = d_hidden_one.astype(jnp.bfloat16)
    grad_out = left_operand(attn_low, d_proj)
    d_attn = mat_right(d_proj, full_out).astype(jnp.bfloat16)
    dattn_grp = to_groups(d_attn, groups, group_size, head_dim)

    def query_side(args):
        group_query, group_keys, group_values, group_lse, group_attention_gradient = args
        scores = (
            jnp.einsum("hqd,hkd->hqk", group_query, group_keys, preferred_element_type=jnp.float32)
            * score_scale
        )
        probs = jnp.where(
            visible[None],
            jnp.exp(jnp.where(visible[None], scores, 0.0) - group_lse[..., None]),
            0.0,
        )
        d_probs = jnp.einsum(
            "hqd,hkd->hqk",
            group_attention_gradient,
            group_values,
            preferred_element_type=jnp.float32,
        )
        delta = jnp.sum(probs * d_probs, axis=2)
        d_scores = (probs * (d_probs - delta[..., None])).astype(jnp.bfloat16)
        d_query = (
            jnp.einsum("hqk,hkd->hqd", d_scores, group_keys, preferred_element_type=jnp.float32)
            * score_scale
        )
        return (probs, d_scores, d_query, delta)

    def both_sides(args):
        probs, d_scores, d_query, delta = query_side(args)
        d_key = (
            jnp.einsum("hqk,hqd->hkd", d_scores, args[0], preferred_element_type=jnp.float32)
            * score_scale
        )
        d_value = jnp.einsum(
            "hqk,hqd->hkd", probs.astype(jnp.bfloat16), args[4], preferred_element_type=jnp.float32
        )
        return (d_query, d_key, d_value)

    dq_grp, dk_grp, dv_grp = lax.map(
        both_sides, (query_grp, keys_grp, values_grp, lse_grp, dattn_grp)
    )
    d_query = from_groups(dq_grp)
    d_key_own, d_value_own = (
        lax.psum_scatter(from_groups(dk_grp), CONTEXT, scatter_dimension=0, tiled=True),
        lax.psum_scatter(from_groups(dv_grp), CONTEXT, scatter_dimension=0, tiled=True),
    )
    d_q_pre = (
        rotate_back(d_query.reshape(piece_rows, local_heads, head_dim), cosine, sine)
        .reshape(piece_rows, -1)
        .astype(jnp.bfloat16)
    )
    d_k_pre = (
        rotate_back(d_key_own.reshape(piece_rows, local_heads, head_dim), cosine, sine)
        .reshape(piece_rows, -1)
        .astype(jnp.bfloat16)
    )
    d_v_pre = d_value_own.astype(jnp.bfloat16)
    grad_bq = jnp.sum(d_q_pre.astype(jnp.float32), axis=0).reshape(local_heads, head_dim)
    grad_bk = jnp.sum(d_k_pre.astype(jnp.float32), axis=0).reshape(local_heads, head_dim)
    grad_bv = jnp.sum(d_v_pre.astype(jnp.float32), axis=0).reshape(local_heads, head_dim)
    grad_query = left_operand(attn_in, d_q_pre)
    grad_key = left_operand(attn_in, d_k_pre)
    grad_value = left_operand(attn_in, d_v_pre)
    d_attn_in = (
        mat_right(d_q_pre, full_query)
        + mat_right(d_k_pre, full_key)
        + mat_right(d_v_pre, full_value)
    )
    d_attn_in = lax.psum(d_attn_in.astype(jnp.bfloat16), EXPERT).astype(jnp.float32)
    d_norm_one = d_attn_in * gain_one
    gain_one_grad = jnp.sum(d_attn_in * normed_one, axis=0)
    d_x = d_hidden_one + rstd_one * (
        d_norm_one - normed_one * jnp.mean(d_norm_one * normed_one, axis=1, keepdims=True)
    )
    input_grad = lax.dynamic_slice_in_dim(d_x, own_start, tok_rows, 0).astype(jnp.bfloat16)
    (
        grad_query,
        grad_key,
        grad_value,
        grad_out,
        grad_sgate,
        grad_sup,
        grad_sdown,
        router_grad,
        mix_grad,
        gain_one_grad,
        gain_two_grad,
        grad_bq,
        grad_bk,
        grad_bv,
    ) = (
        lax.psum_scatter(grad_query, (DP, CONTEXT), scatter_dimension=0, tiled=True),
        lax.psum_scatter(grad_key, (DP, CONTEXT), scatter_dimension=0, tiled=True),
        lax.psum_scatter(grad_value, (DP, CONTEXT), scatter_dimension=0, tiled=True),
        lax.psum_scatter(grad_out, (DP, CONTEXT), scatter_dimension=1, tiled=True),
        lax.psum_scatter(grad_sgate, (DP, CONTEXT), scatter_dimension=0, tiled=True),
        lax.psum_scatter(grad_sup, (DP, CONTEXT), scatter_dimension=0, tiled=True),
        lax.psum_scatter(grad_sdown, (DP, CONTEXT), scatter_dimension=1, tiled=True),
        lax.psum_scatter(router_grad, (DP, CONTEXT), scatter_dimension=0, tiled=True),
        lax.psum_scatter(mix_grad, (DP, CONTEXT), scatter_dimension=0, tiled=True),
        lax.psum_scatter(gain_one_grad, (DP, CONTEXT), scatter_dimension=0, tiled=True),
        lax.psum_scatter(gain_two_grad, (DP, CONTEXT), scatter_dimension=0, tiled=True),
        lax.psum_scatter(grad_bq, (DP, CONTEXT), scatter_dimension=1, tiled=True),
        lax.psum_scatter(grad_bk, (DP, CONTEXT), scatter_dimension=1, tiled=True),
        lax.psum_scatter(grad_bv, (DP, CONTEXT), scatter_dimension=1, tiled=True),
    )
    return (
        mixed,
        input_grad,
        gain_one_grad,
        grad_query,
        grad_key,
        grad_value,
        grad_bq,
        grad_bk,
        grad_bv,
        grad_out,
        gain_two_grad,
        router_grad,
        mix_grad,
        grad_sgate,
        grad_sup,
        grad_sdown,
        routed_gate_gradient,
        routed_up_gradient,
        routed_down_gradient,
    )


def dot_f32(left, right, left_dim, right_dim):
    return lax.dot_general(
        left, right, (((left_dim,), (right_dim,)), ((), ())), preferred_element_type=jnp.float32
    )


def whole_vmem(count):
    return [pl.BlockSpec(memory_space=pltpu.VMEM)] * count


def like(shape, dtype):
    return jax.ShapeDtypeStruct(shape, dtype)


MESH_ID = pl.DeviceIdType.MESH


class Wire:
    def __init__(self, send, recv):
        self.send = send
        self.recv = recv
        self.sent = 0
        self.received = 0
        self.own = []

    def copy(self, src, dst, device):
        out = self.copy_to(src, dst, device, self.take(1), self.take_send(1))
        self.own.append(out)
        return out

    def take(self, count):
        self.received += count
        assert self.received <= self.recv.shape[0], self.received
        return self.received - count

    def take_send(self, count):
        self.sent += count
        assert self.sent <= self.send.shape[0], self.sent
        return self.sent - count

    def copy_to(self, src, dst, device, recv_slot, send_slot):
        return pltpu.make_async_remote_copy(
            src_ref=src,
            dst_ref=dst,
            send_sem=self.send.at[send_slot],
            recv_sem=self.recv.at[recv_slot],
            device_id=device,
            device_id_type=MESH_ID,
        )

    def drain(self, some=None):
        for item in self.own if some is None else some:
            item.wait_send()
        done = {id(item) for item in some} if some is not None else None
        self.own = [] if done is None else [item for item in self.own if id(item) not in done]


class Local:
    def __init__(self, sems):
        self.sems = sems
        self.count = 0

    def start(self, src, dst):
        assert self.count < self.sems.shape[0], self.count
        item = pltpu.make_async_copy(src, dst, self.sems.at[self.count])
        self.count += 1
        item.start()
        return item


class Phases:
    def __init__(self):
        self.scope = None

    def go(self, name):
        if self.scope is not None:
            self.scope.__exit__(None, None, None)
        self.scope = jax.named_scope(name) if name else None
        if name:
            self.scope.__enter__()


class Place:
    def __init__(self, n_dp):
        self.n_dp = n_dp
        self.z = lax.axis_index(DP)
        self.c = lax.axis_index(CONTEXT)
        self.y = lax.axis_index(EXPERT)
        self.cx = lax.bitwise_xor(self.c, jnp.int32(2))
        self.cs = lax.bitwise_xor(self.c, jnp.int32(1))
        self.cd = lax.bitwise_xor(self.c, jnp.int32(3))
        self.yn = lax.bitwise_xor(self.y, jnp.int32(1))
        self.core = (self.z, self.cs, self.y)
        self.over_x = (self.z, self.cx, self.y)
        self.over_y = (self.z, self.c, self.yn)
        self.up = (self.z + 1, self.c, self.y)
        self.down = (self.z - 1, self.c, self.y)

    def block(self, c, y):
        return c * 2 + y


def barrier(devices):
    sem = pltpu.get_barrier_semaphore()
    for device in devices:
        pl.semaphore_signal(sem, inc=1, device_id=device, device_id_type=MESH_ID)
    pl.semaphore_wait(sem, len(devices))


def rows_of(index, count):
    return pl.ds(pl.multiple_of(index * count, count), count)


def by_rows(total, step, body):
    def one(index, carry):
        body(rows_of(index, step))
        return carry

    lax.fori_loop(0, total // step, one, 0)


def chain_gather(wire, place, refs, arrived=None, begun=False):
    n = place.n_dp
    z = place.z
    width = len(refs(z))
    recv = wire.take(n * width)
    send = wire.take_send(2 * n * width)

    def copies(slot, up, dist):
        return [
            wire.copy_to(
                ref,
                ref,
                place.up if up else place.down,
                recv + slot * width + index,
                send + (2 * dist + (0 if up else 1)) * width + index,
            )
            for index, ref in enumerate(refs(slot))
        ]

    def start(slot, up, dist):
        for item in copies(slot, up, dist):
            item.start()

    def land(slot, up, dist):
        if dist > 1 or not begun:
            for item in copies(slot, up, dist):
                item.wait_recv()
        if arrived is not None:
            arrived(slot)

    def sent(slot, up, dist):
        for item in copies(slot, up, dist):
            item.wait_send()

    if not begun:
        pl.when(z < n - 1)(lambda: start(z, True, 0))
        pl.when(z > 0)(lambda: start(z, False, 0))
        yield
    for dist in range(1, n):
        below, above = z - dist, z + dist

        @pl.when(below >= 0)
        def _():
            land(below, True, dist)
            pl.when(z < n - 1)(lambda: start(below, True, dist))

        @pl.when(above < n)
        def _():
            land(above, False, dist)
            pl.when(z > 0)(lambda: start(above, False, dist))

        yield
    for dist in range(1 if begun else 0, n):
        below, above = z - dist, z + dist
        pl.when((below >= 0) & (z < n - 1))(lambda: sent(below, True, dist))
        pl.when((above < n) & (z > 0))(lambda: sent(above, False, dist))


def finish(*steps):
    for step in steps:
        for _ in step:
            pass


def plane_gather(wire, place, buf):
    rows = buf.shape[0] // 8
    half = buf.shape[1] // 2
    left, right = pl.ds(0, half), pl.ds(half, half)
    own = rows_of(place.block(place.c, place.y), rows)
    from_x = rows_of(place.block(place.cx, place.y), rows)
    from_y = rows_of(place.block(place.c, place.yn), rows)
    across = rows_of(place.block(place.cx, place.yn), rows)

    def go(where, lanes, device):
        ref = buf.at[where, lanes] if lanes is not None else buf.at[where, :]
        item = wire.copy(ref, ref, device)
        item.start()
        return item

    x_left = go(own, left, place.over_x)
    y_right = go(own, right, place.over_y)
    x_right = go(own, right, place.over_x)
    y_left = go(own, left, place.over_y)
    waits = [go(own, None, place.core)]
    yield
    x_left.wait_recv()
    far_left = go(from_x, left, place.over_y)
    y_right.wait_recv()
    far_right = go(from_y, right, place.over_x)
    yield
    x_right.wait_recv()
    waits.append(go(from_x, None, place.core))
    y_left.wait_recv()
    waits.append(go(from_y, None, place.core))
    yield
    far_left.wait_recv()
    far_right.wait_recv()
    waits.append(go(across, None, place.core))
    for item in waits:
        item.wait_recv()


def add_into(target, lanes, rows, extra):
    count = extra.shape[0]
    step = 16

    def one(index, carry):
        here = pl.ds(pl.multiple_of(rows + index * step, step), step)
        there = rows_of(index, step)
        total = target[here, lanes].astype(jnp.float32) + extra[there, :].astype(jnp.float32)
        target[here, lanes] = total.astype(target.dtype)
        return carry

    lax.fori_loop(0, count // step, one, 0)


def plane_reduce(wire, place, part, got_core, got_one, got_two):
    rows = part.shape[0] // 8
    half = part.shape[1] // 2
    left, right = pl.ds(0, half), pl.ds(half, half)
    chips = ((place.cx, place.yn), (place.cx, place.y), (place.c, place.yn), (place.c, place.y))
    starts = [place.block(c, y) * rows for c, y in chips]
    blocks = [pl.ds(pl.multiple_of(start, rows), rows) for start in starts]
    sibling = [
        rows_of(place.block(lax.bitwise_xor(c, jnp.int32(1)), y), rows) for c, y in chips
    ]
    swaps = []
    for index in range(4):
        item = wire.copy(part.at[sibling[index], :], got_core.at[index], place.core)
        item.start()
        swaps.append(item)
    whole = pl.ds(0, 2 * half)

    def one(index, lanes, slot, device):
        item = wire.copy(part.at[blocks[index], lanes], got_one.at[slot], device)
        item.start()
        return item

    swaps[0].wait_recv()
    add_into(part, whole, starts[0], got_core.at[0])
    far_x = one(0, left, 0, place.over_x)
    far_y = one(0, right, 2, place.over_y)
    swaps[1].wait_recv()
    add_into(part, whole, starts[1], got_core.at[1])
    near_x = one(1, left, 1, place.over_x)
    swaps[2].wait_recv()
    add_into(part, whole, starts[2], got_core.at[2])
    near_y = one(2, right, 3, place.over_y)
    yield
    swaps[3].wait_recv()
    add_into(part, whole, starts[3], got_core.at[3])
    far_x.wait_recv()
    add_into(part, left, starts[2], got_one.at[0])
    last_y = wire.copy(part.at[blocks[2], left], got_two.at[0], place.over_y)
    last_y.start()
    far_y.wait_recv()
    add_into(part, right, starts[1], got_one.at[2])
    last_x = wire.copy(part.at[blocks[1], right], got_two.at[1], place.over_x)
    last_x.start()
    yield
    near_x.wait_recv()
    near_y.wait_recv()
    last_x.wait_recv()
    last_y.wait_recv()


def plane_sum(place, part, got_one, got_two, here):
    rows = part.shape[0] // 8
    half = part.shape[1] // 2
    start = place.block(place.c, place.y) * rows + here.start
    at = pl.ds(pl.multiple_of(start, here.size), here.size)

    def value(ref):
        return ref.astype(jnp.float32)

    left = value(part[at, 0:half]) + value(got_one[1, here, :]) + value(got_two[0, here, :])
    right = value(part[at, half:]) + value(got_one[3, here, :]) + value(got_two[1, here, :])
    return jnp.concatenate([left, right], axis=1)


def forward_kernel(
    n_blocks, n_dp,
    tokens, out_grad, small, ids, w_query, w_key, w_value, w_out, s_gate, s_up, s_down,
    bias, cosine, sine,
    attn_in_to, query_to, keys_to, values_to, attn_to, lse_to, hidden_to, moe_in,
    heads_weight_to, out_weight_to, gate_weight, up_weight, down_weight, smalls, all_ids, dy_group,
    x_seq, partial, got_core, got_one, got_two,
    attn_in, query, keys, values, attn, lse, hidden, heads_weight, out_weight,
    shared_raw, shared_packed, send, recv, local,
):
    place = Place(n_dp)
    wire = Wire(send, recv)
    inside = Local(local)
    z, c, y = place.z, place.c, place.y
    rows, width = tokens.shape
    seq = x_seq.shape[0]
    cols = query.shape[1]
    head_dim = cosine.shape[1]
    block = seq // n_blocks
    scale = 1.0 / math.sqrt(head_dim)
    n_ctx = 4
    share = w_query.shape[0]
    f32, low = jnp.float32, jnp.bfloat16

    others = [(dz, dc) for dz in range(n_dp) for dc in range(n_ctx) if dz or dc]
    phases = Phases()
    phases.go("entry")
    raw_in = [inside.start(src, shared_raw.at[k]) for k, src in enumerate((s_gate, s_up))]

    def moved(dz, dc, y_to):
        return (lax.bitwise_xor(z, jnp.int32(dz)), lax.bitwise_xor(c, jnp.int32(dc)), y_to)

    barrier(
        [moved(dz, dc, y) for dz, dc in others] + [moved(dz, 0, place.yn) for dz in range(n_dp)]
    )

    mine = z * n_ctx + c
    my_rows = rows_of(mine, share)
    group = z * 2 + y
    shared_pieces = [[], [], []]

    units = gate_weight.shape[3]

    def pack(index):
        raw_in[index].wait()
        for part in range(n_dp):
            shared_packed[index, part] = shared_raw[index, :, part * units : (part + 1) * units]

    def shared_along_dp(index):
        if index < 2:
            pack(index)
        for dz in (2, 3, 1, 0):
            to = lax.bitwise_xor(z, jnp.int32(dz))
            if index == 2:
                src = s_down.at[rows_of(to, s_down.shape[0] // n_dp), :]
                dst = down_weight.at[:, my_rows]
            else:
                src = shared_packed.at[index, to]
                dst = (gate_weight, up_weight)[index].at[z, c]
            if dz == 0:
                item = inside.start(src, dst)
            else:
                item = wire.copy(src, dst, moved(dz, 0, y))
                item.start()
            shared_pieces[index].append(item)

    shared_along_dp(0)

    exchanges = []
    for dc in range(n_ctx):
        to = lax.bitwise_xor(c, jnp.int32(dc))
        lanes = pl.ds(pl.multiple_of(to * cols, cols), cols)
        pairs = [
            (weight.at[:, lanes], heads_weight.at[my_rows, pl.ds(index * cols, cols)])
            for index, weight in enumerate((w_query, w_key, w_value))
        ]
        pairs.append((w_out.at[rows_of(to, cols), :], out_weight.at[:, my_rows]))
        for src, dst in pairs:
            if dc == 0:
                exchanges.append(inside.start(src, dst))
            else:
                item = wire.copy(src, dst, moved(0, dc, y))
                item.start()
                exchanges.append(item)
    own_rows = rows_of(place.block(c, y), rows)
    here = inside.start(tokens, x_seq.at[own_rows, :])
    here.wait()
    small_copies = [inside.start(small, smalls.at[:, my_rows])]
    for dz, dc in others:
        item = wire.copy(small, smalls.at[:, my_rows], moved(dz, dc, y))
        item.start()
        small_copies.append(item)
    small_copies.append(inside.start(ids, all_ids.at[group]))
    for dz in range(n_dp):
        for y_to in (y, place.yn):
            if dz or y_to is not y:
                item = wire.copy(ids, all_ids.at[group], moved(dz, 0, y_to))
                item.start()
                small_copies.append(item)
    def dy_rows(slot, half):
        return dy_group.at[rows_of(slot * 2 + half, rows), :]

    stores = [inside.start(out_grad, dy_rows(z, y))]
    dy_over_y = wire.copy(out_grad, dy_rows(z, y), place.over_y)
    dy_over_y.start()
    phases.go("exchanges")
    for item in exchanges:
        item.wait_recv()

    def from_place(slot):
        return rows_of(slot, n_ctx * share)

    weights_in = chain_gather(wire, place, lambda slot: [heads_weight.at[from_place(slot), :]])
    next(weights_in)
    phases.go("tokens")
    tokens_in = plane_gather(wire, place, x_seq)
    finish(tokens_in)
    next(weights_in)
    for item in small_copies:
        item.wait_recv()

    gain_one = smalls[9:10, :].astype(f32)
    gain_two = smalls[10:11, :].astype(f32)

    def norm_one(at):
        x_float = x_seq[at, :].astype(f32)
        rstd = lax.rsqrt(jnp.mean(x_float * x_float, axis=1, keepdims=True) + EPS)
        attn_in[at, :] = (x_float * rstd * gain_one).astype(low)

    by_rows(seq, 64, norm_one)
    def shared_set(index, context):
        if index < 2:
            return [(gate_weight, up_weight)[index].at[:, context]]
        return [
            down_weight.at[:, rows_of(dz * n_ctx + context, share)] for dz in range(n_dp)
        ]

    over = [[], [], []]
    close = []

    def shared_over_x(index):
        for item in shared_pieces[index]:
            item.wait_recv()
        for ref in shared_set(index, c):
            item = wire.copy(ref, ref, place.over_x)
            item.start()
            over[index].append(item)
        for ref in shared_set(index, c):
            item = wire.copy(ref, ref, place.core)
            item.start()
            close.append(item)

    def shared_close(index):
        for item, ref in zip(over[index], shared_set(index, place.cx)):
            item.wait_recv()
            item = wire.copy(ref, ref, place.core)
            item.start()
            close.append(item)

    shared_over_x(0)
    phases.go("heads_weights")
    finish(weights_in)
    phases.go("attention")
    out_in = chain_gather(wire, place, lambda slot: [out_weight.at[:, from_place(slot)]])
    next(out_in)

    def project(at):
        pre = dot_f32(attn_in[at, :], heads_weight[...], 1, 0)
        cos = cosine[at, :]
        sin = sine[at, :]
        for index, kept in enumerate((query, keys, values)):
            for start in range(0, cols, head_dim):
                from_lane = index * cols + start
                part = pre[:, from_lane : from_lane + head_dim]
                part = part + bias[index : index + 1, start : start + head_dim]
                if index < 2:
                    part = part * cos + pltpu.roll(part, head_dim // 2, 1) * sin
                kept[at, start : start + head_dim] = part.astype(low)

    by_rows(seq, block, project)
    next(out_in)
    for start in range(0, cols, head_dim):
        lanes = slice(start, start + head_dim)
        for step in range(n_blocks):
            at = slice(step * block, (step + 1) * block)
            seen = slice(0, (step + 1) * block)
            scores = dot_f32(query[at, lanes], keys[seen, lanes], 1, 1) * scale
            top = jnp.max(scores, axis=1, keepdims=True)
            expo = jnp.exp(scores - top)
            total = jnp.sum(expo, axis=1, keepdims=True)
            probs = (expo / total).astype(low)
            attn[at, lanes] = dot_f32(probs, values[seen, lanes], 1, 0).astype(low)
            lse[at, lanes] = jnp.broadcast_to(top + jnp.log(total), (block, head_dim))
        if start == 0:
            next(out_in)
    phases.go("out_weights")
    finish(out_in)
    shared_along_dp(1)
    shared_along_dp(2)
    phases.go("attention_out")

    def output(at):
        partial[at, :] = dot_f32(attn[at, :], out_weight[...], 1, 0).astype(low)

    by_rows(seq, block, output)
    stores += [
        inside.start(src, dst)
        for src, dst in (
            (attn_in, attn_in_to), (query, query_to), (keys, keys_to), (values, values_to),
            (attn, attn_to), (lse, lse_to), (heads_weight, heads_weight_to),
            (out_weight, out_weight_to),
        )
    ]
    phases.go("sum_in_plane")
    reduce = plane_reduce(wire, place, partial, got_core, got_one, got_two)
    next(reduce)

    next(reduce)
    finish(reduce)
    phases.go("norm_two")

    def norm_two(at):
        start = place.block(c, y) * rows + at.start
        own = pl.ds(pl.multiple_of(start, at.size), at.size)
        total = x_seq[own, :].astype(f32) + plane_sum(place, partial, got_one, got_two, at)
        hidden[at, :] = total
        rstd = lax.rsqrt(jnp.mean(total * total, axis=1, keepdims=True) + EPS)
        got_core[0, at, :] = (total * rstd * gain_two).astype(low)

    by_rows(rows, 16, norm_two)
    stores.append(inside.start(hidden, hidden_to))
    at_group = rows_of(group, rows)
    here = inside.start(got_core.at[0], moe_in.at[at_group, :])
    here.wait()

    half_width = width // 2
    y_recv = wire.take(2 * n_dp)
    y_send = wire.take_send(2 * n_dp)

    def moe_block(slot, half, part):
        return moe_in.at[rows_of(slot * 2 + half, rows), pl.ds(part * half_width, half_width)]

    def to_y(slot, part, half=None):
        ref = moe_block(slot, y if half is None else half, part)
        sem = 2 * slot + part
        return wire.copy_to(ref, ref, place.over_y, y_recv + sem, y_send + sem)

    chains = [
        chain_gather(
            wire,
            place,
            lambda slot, part=part: [moe_block(slot, y, part)],
            arrived=lambda slot, part=part: to_y(slot, part).start(),
        )
        for part in range(2)
    ]
    for part in range(2):
        next(chains[part])
        to_y(z, part).start()
    phases.go("shared_one")
    shared_over_x(1)
    phases.go("rows_one")
    for chain in chains:
        next(chain)
    phases.go("shared_two")
    shared_over_x(2)
    phases.go("rows_two")
    for chain in chains:
        next(chain)
    phases.go("rows_three")
    for chain in chains:
        next(chain)
    dy_recv = wire.take(2)
    dy_send = wire.take_send(2)

    def dy_step(up):
        ref = dy_rows(z, y)
        to = place.up if up else place.down
        return wire.copy_to(out_grad, ref, to, dy_recv + (0 if up else 1), dy_send + (0 if up else 1))

    pl.when(z < n_dp - 1)(lambda: dy_step(True).start())
    pl.when(z > 0)(lambda: dy_step(False).start())
    finish(*chains)
    phases.go("shared_close")
    for index in range(3):
        shared_close(index)
    for item in close:
        item.wait_recv()
    phases.go("rows_over_y")
    for slot in range(n_dp):
        for part in range(2):
            to_y(slot, part, place.yn).wait_recv()
            to_y(slot, part).wait_send()
    phases.go("dy")
    dy_over_y.wait_recv()

    @pl.when(z > 0)
    def _():
        dy_step(True).wait_recv()
        dy_step(False).wait_send()

    @pl.when(z < n_dp - 1)
    def _():
        dy_step(False).wait_recv()
        dy_step(True).wait_send()

    for item in stores:
        item.wait()
    wire.drain()
    phases.go(None)


def chain_reduce(wire, place, parts):
    n = place.n_dp
    z = place.z
    count = len(parts)
    recv = wire.take(2 * n * count)
    send = wire.take_send(2 * n * count)

    def copies(target, up):
        out = []
        for index, (block, below, above) in enumerate(parts):
            slot = (2 * target + (0 if up else 1)) * count + index
            landing = below if up else above
            out.append(
                wire.copy_to(
                    block(target),
                    landing.at[target],
                    place.up if up else place.down,
                    recv + slot,
                    send + slot,
                )
            )
        return out

    def collect(target, up):
        for item, (block, below, above) in zip(copies(target, up), parts):
            item.wait_recv()
            add_block(block(target), (below if up else above).at[target])

    def pass_on(target, up):
        collect(target, up)
        for item in copies(target, up):
            item.start()

    def first(target, up):
        for item in copies(target, up):
            item.start()

    @pl.when(z == 0)
    def _():
        for target in range(n - 1, 0, -1):
            first(target, True)

    @pl.when(z == n - 1)
    def _():
        for target in range(n - 1):
            first(target, False)

    yield
    for step in range(n - 1):
        high, low = n - 1 - step, step

        @pl.when((z > 0) & (z < n // 2))
        def _():
            pl.when(z < high)(lambda: pass_on(high, True))
            pl.when(z > low)(lambda: pass_on(low, False))

        @pl.when((z >= n // 2) & (z < n - 1))
        def _():
            pl.when(z > low)(lambda: pass_on(low, False))
            pl.when(z < high)(lambda: pass_on(high, True))

        yield
    pl.when(z > 0)(lambda: collect(z, True))
    pl.when(z < n - 1)(lambda: collect(z, False))
    for target in range(n):

        @pl.when(z < target)
        def _():
            for item in copies(target, True):
                item.wait_send()

        @pl.when(z > target)
        def _():
            for item in copies(target, False):
                item.wait_send()


def add_block(target, extra):
    step = 16

    def one(index, carry):
        here = rows_of(index, step)
        total = target[here, :].astype(jnp.float32) + extra[here, :].astype(jnp.float32)
        target[here, :] = total.astype(target.dtype)
        return carry

    lax.fori_loop(0, extra.shape[0] // step, one, 0)


class Adder:
    def __init__(self, sems):
        self.sems = sems

    def run(self, buf, chunks):
        def load(index):
            first, second, _ = chunks[index]
            slot = index % 2
            items = [
                pltpu.make_async_copy(first, buf.at[0, slot], self.sems.at[3 * slot]),
                pltpu.make_async_copy(second, buf.at[1, slot], self.sems.at[3 * slot + 1]),
            ]
            for item in items:
                item.start()
            return items

        stores = [None, None]
        loads = load(0)
        for index, (_, _, target) in enumerate(chunks):
            slot = index % 2
            after = load(index + 1) if index + 1 < len(chunks) else None
            for item in loads:
                item.wait()
            loads = after
            if stores[slot] is not None:
                stores[slot].wait()
            total, first, second = buf.at[2, slot], buf.at[0, slot], buf.at[1, slot]

            def one(step, carry):
                here = rows_of(step, 16)
                value = first[here, :].astype(jnp.float32) + second[here, :].astype(jnp.float32)
                total[here, :] = value.astype(total.dtype)
                return carry

            lax.fori_loop(0, total.shape[0] // 16, one, 0)
            stores[slot] = pltpu.make_async_copy(total, target, self.sems.at[3 * slot + 2])
            stores[slot].start()
        for item in stores:
            if item is not None:
                item.wait()


def backward_kernel(
    n_blocks, n_dp,
    own_sum, got_scalars, k_sup, k_sdown, x_sup, x_sdown, r_eup, r_edown,
    hidden_in, out_grad_in, tokens_in, smalls, probs, mix,
    heads_weight_in, w_out_in, query_in, keys_in, values_in, attn_from, lse_in, attn_in_from,
    cosine_in, sine_in,
    input_grad, heads_grad, out_weight_grad, small_grad, bias_grad,
    t_sup, t_sdown, x_eup, x_edown, s_sup, s_sdown,
    partial, d_hidden, side, moe_own, terms, acc,
    proj, d_attn, d_qkv, d_keys, d_values, got_core, got_one, got_two,
    g_heads, g_out, heads_below, heads_above, out_below, out_above, out_block,
    stage, landed, over_y, gate_buf, down_buf,
    hidden, out_grad, tokens, heads_weight, w_out, query, keys, values, attn, lse, attn_in,
    cosine, sine, send, recv, local, adds,
):
    place = Place(n_dp)
    wire = Wire(send, recv)
    inside = Local(local)
    adder = Adder(adds)
    z, c, y = place.z, place.c, place.y
    rows, width = tokens.shape
    seq = proj.shape[0]
    cols = query.shape[1]
    head_dim = cosine.shape[1]
    block = seq // n_blocks
    scale = 1.0 / math.sqrt(head_dim)
    n_ctx = 4
    share = width // (n_dp * n_ctx)
    n_experts = probs.shape[0]
    f32, low = jnp.float32, jnp.bfloat16
    core = lax.rem(c, 2)
    others = [(dz, dc) for dz in range(n_dp) for dc in range(n_ctx) if dz or dc]

    def moved(dz, dc, y_to):
        return (lax.bitwise_xor(z, jnp.int32(dz)), lax.bitwise_xor(c, jnp.int32(dc)), y_to)

    phases = Phases()
    phases.go("entry")
    barrier(
        [moved(dz, dc, y) for dz, dc in others] + [moved(dz, 0, place.yn) for dz in range(n_dp)]
    )
    def go_over_x(index, part=0, parts=1):
        total = (r_eup, r_edown)[index]
        got = (x_eup, x_edown)[index]
        count = got.shape[0] // parts
        at = pl.ds(part * count, count)
        item = wire.copy(total.at[at, :], got.at[at, :], place.over_x)
        item.start()
        return item

    def part_of(ref, dz):
        size = ref.shape[0] // n_dp
        return ref.at[pl.ds(dz * size, size), :]

    def shared_ready(index):
        buf = (gate_buf, down_buf)[index]
        kept = (k_sup, k_sdown)[index]
        got = (x_sup, x_sdown)[index]
        ready = (s_sup, s_sdown)[index]
        adder.run(buf, [(part_of(kept, dz), part_of(got, dz), ready.at[dz]) for dz in range(n_dp)])

    shared_last = []

    def shared_along_dp(index):
        ready = (s_sup, s_sdown)[index]
        target = (t_sup, t_sdown)[index]
        for dz in (2, 3, 1, 0):
            to = lax.bitwise_xor(z, jnp.int32(dz))
            if dz:
                item = wire.copy(ready.at[to], target.at[z], moved(dz, 0, y))
                item.start()
            else:
                item = inside.start(ready.at[to], target.at[z])
            shared_last.append(item)

    loads = [
        inside.start(src, dst)
        for src, dst in (
            (hidden_in, hidden), (out_grad_in, out_grad), (tokens_in, tokens), (attn_from, attn),
            (w_out_in, w_out), (query_in, query), (keys_in, keys), (values_in, values),
            (lse_in, lse), (cosine_in, cosine), (sine_in, sine), (heads_weight_in, heads_weight),
            (attn_in_from, attn_in),
        )
    ]
    phases.go("router")
    d_rprobs = got_scalars[:, 0, :]
    probs_own = probs[...]
    d_logits = probs_own * (d_rprobs - jnp.sum(probs_own * d_rprobs, axis=0, keepdims=True))
    shared_dot = jnp.sum(got_scalars[:, 1, :], axis=0, keepdims=True)
    d_mix = shared_dot * mix[...] * (1.0 - mix[...])
    d_side = jnp.concatenate(
        [d_logits, jnp.broadcast_to(d_mix, (16 - n_experts, rows))], axis=0
    )
    row_of = lax.broadcasted_iota(jnp.int32, d_side.shape, 0)
    d_side = jnp.where(row_of <= n_experts, d_side, 0.0)
    first = d_side.astype(low)
    rest = d_side - first.astype(f32)
    second = rest.astype(low)
    third = (rest - second.astype(f32)).astype(low)
    terms[...] = jnp.concatenate([first, second, third], axis=0)
    side[...] = dot_f32(terms[...], jnp.concatenate([smalls[...]] * 3, axis=0), 0, 0)
    gain_one = smalls[n_experts + 1 : n_experts + 2, :].astype(f32)
    gain_two = smalls[n_experts + 2 : n_experts + 3, :].astype(f32)
    acc[...] = jnp.zeros_like(acc)
    own_plane = place.block(c, y) * rows

    def norm_two(at):
        d_moe = side[at, :] + own_sum[at, :]
        total = hidden[at, :]
        rstd = lax.rsqrt(jnp.mean(total * total, axis=1, keepdims=True) + EPS)
        normed = total * rstd
        acc[0] += d_moe * normed
        d_norm = d_moe * gain_two
        back = out_grad[at, :].astype(f32) + rstd * (
            d_norm - normed * jnp.mean(d_norm * normed, axis=1, keepdims=True)
        )
        d_hidden[at, :] = back
        moe_own[at, :] = (normed * gain_two).astype(low)
        proj[pl.ds(pl.multiple_of(own_plane + at.start, at.size), at.size), :] = back.astype(low)

    phases.go("norm_two")
    for item in loads[:3]:
        item.wait()
    by_rows(rows, 16, norm_two)
    phases.go("gather_in_plane")
    proj_in = plane_gather(wire, place, proj)
    next(proj_in)
    side[0:48, :] = dot_f32(terms[...], moe_own[...], 1, 0)

    phases.go("shared_up")
    shared_ready(0)
    shared_along_dp(0)
    phases.go("gather_relay")
    next(proj_in)
    phases.go("shared_down")
    shared_ready(1)
    shared_along_dp(1)
    phases.go("gather_close")
    next(proj_in)
    phases.go("gather_end")
    finish(proj_in)

    phases.go("attention")
    routed_over = [go_over_x(0, part, 4) for part in range(3)]
    for item in loads[3:]:
        item.wait()
    by_share = n_ctx * share

    def out_weight(target):
        at = rows_of(target, by_share)
        g_out[:, at] = dot_f32(attn[...], proj[:, at], 0, 0).astype(low)

    def each(count, body):
        def one(index, carry):
            body(index)
            return carry

        lax.fori_loop(0, count, one, 0)

    each(n_dp, out_weight)
    out_chain = chain_reduce(
        wire, place, [(lambda t: g_out.at[:, rows_of(t, by_share)], out_below, out_above)]
    )
    next(out_chain)

    def project(at):
        d_attn[at, :] = dot_f32(proj[at, :], w_out[...], 1, 1).astype(low)

    by_rows(seq, block, project)

    def turn(part, at):
        return part * cosine[at, :] - pltpu.roll(part, head_dim // 2, 1) * sine[at, :]

    every = slice(0, seq)
    for start in range(0, cols, head_dim):
        lanes = slice(start, start + head_dim)
        d_keys[...] = jnp.zeros_like(d_keys)
        d_values[...] = jnp.zeros_like(d_values)
        for step in range(n_blocks):
            at = slice(step * block, (step + 1) * block)
            seen = slice(0, (step + 1) * block)
            q_here = query[at, lanes]
            k_seen = keys[seen, lanes]
            grad = d_attn[at, lanes]
            scores = dot_f32(q_here, k_seen, 1, 1) * scale
            weights = jnp.exp(scores - lse[at, start : start + 1])
            d_probs = dot_f32(grad, values[seen, lanes], 1, 1)
            delta = jnp.sum(weights * d_probs, axis=1, keepdims=True)
            d_scores = (weights * (d_probs - delta)).astype(low)
            d_query = dot_f32(d_scores, k_seen, 1, 0) * scale
            d_qkv[at, lanes] = turn(d_query, at).astype(low)
            d_keys[seen, :] += dot_f32(d_scores, q_here, 0, 0) * scale
            d_values[seen, :] += dot_f32(weights.astype(low), grad, 0, 0)
        d_qkv[:, cols + start : cols + start + head_dim] = turn(d_keys[...], every).astype(low)
        d_qkv[:, 2 * cols + start : 2 * cols + start + head_dim] = d_values[...].astype(low)

    phases.go("heads_grad")

    def heads_weights(target):
        at = rows_of(target, by_share)
        g_heads[at, :] = dot_f32(attn_in[:, at], d_qkv[...], 0, 0).astype(low)

    each(n_dp, heads_weights)
    heads_chain = chain_reduce(
        wire,
        place,
        [(lambda t: g_heads.at[rows_of(t, by_share), :], heads_below, heads_above)],
    )
    next(heads_chain)
    phases.go("attention_in_grad")

    def output(at):
        partial[at, :] = dot_f32(d_qkv[at, :], heads_weight[...], 1, 1).astype(low)

    by_rows(seq, block, output)
    phases.go("sum_in_plane")
    reduce = plane_reduce(wire, place, partial, got_core, got_one, got_two)
    next(reduce)
    next(out_chain)
    next(reduce)
    next(out_chain)
    phases.go("sum_in_plane_end")
    finish(reduce)
    routed_over += [go_over_x(0, 3, 4), go_over_x(1)]

    def norm_one(at):
        d_attn_in = plane_sum(place, partial, got_one, got_two, at)
        x_float = tokens[at, :].astype(f32)
        rstd = lax.rsqrt(jnp.mean(x_float * x_float, axis=1, keepdims=True) + EPS)
        normed = x_float * rstd
        acc[1] += d_attn_in * normed
        d_norm = d_attn_in * gain_one
        input_grad[at, :] = (
            d_hidden[at, :]
            + rstd * (d_norm - normed * jnp.mean(d_norm * normed, axis=1, keepdims=True))
        ).astype(low)

    phases.go("heads_chain_one")
    next(heads_chain)
    phases.go("norm_one")
    by_rows(rows, 16, norm_one)

    side_grad = side[0:16, :] + side[16:32, :] + side[32:48, :]
    row_of = lax.broadcasted_iota(jnp.int32, side_grad.shape, 0)
    gain_one_grad = jnp.sum(acc[1], axis=0, keepdims=True)
    gain_two_grad = jnp.sum(acc[0], axis=0, keepdims=True)
    small_rows = jnp.where(
        row_of == n_experts + 1,
        gain_one_grad,
        jnp.where(row_of == n_experts + 2, gain_two_grad, side_grad),
    )
    bias_sums = jnp.sum(d_qkv[...].astype(f32), axis=0, keepdims=True)
    bias_rows = [
        bias_sums[:, start : start + head_dim] for start in range(0, 3 * cols, head_dim)
    ]
    bias_rows += [jnp.zeros((8 - len(bias_rows), head_dim), f32)]
    bias_rows = jnp.concatenate(bias_rows, axis=0)
    for target in range(n_dp * n_ctx):
        stage[target, 0:16, :] = small_rows[:, target * share : (target + 1) * share]
        stage[target, 16:24, :] = bias_rows
    mine = z * n_ctx + c
    small_items = [inside.start(stage.at[mine], landed.at[mine])]
    for dz, dc in others:
        target = lax.bitwise_xor(z, jnp.int32(dz)) * n_ctx + lax.bitwise_xor(c, jnp.int32(dc))
        item = wire.copy(stage.at[target], landed.at[mine], moved(dz, dc, y))
        item.start()
        small_items.append(item)
    phases.go("chains")
    next(heads_chain)
    finish(out_chain)

    out_block[...] = g_out[:, rows_of(z, by_share)]
    last = []

    def to_pieces(src_of, target):
        for dc in range(n_ctx):
            src = src_of(lax.bitwise_xor(c, jnp.int32(dc)))
            if dc:
                item = wire.copy(src, target.at[c], moved(0, dc, y))
                item.start()
            else:
                item = inside.start(src, target.at[c])
            last.append(item)

    to_pieces(lambda to: out_block.at[:, rows_of(to, share)], out_weight_grad)
    phases.go("heads_chain")
    finish(heads_chain)
    phases.go("last")

    to_pieces(
        lambda to: g_heads.at[pl.ds(pl.multiple_of(z * by_share + to * share, share), share), :],
        heads_grad,
    )
    phases.go("small")
    for item in small_items:
        item.wait_recv()
    total = landed[0, 0:16, :]
    for source in range(1, n_dp * n_ctx):
        total = total + landed[source, 0:16, :]
    over_y[0] = total
    swap = wire.copy(over_y.at[0], over_y.at[1], place.over_y)
    swap.start()
    for context in range(n_ctx):
        sums = landed[context, 16:24, :]
        for source in range(1, n_dp):
            sums = sums + landed[source * n_ctx + context, 16:24, :]
        bias_grad[context] = sums
    swap.wait_recv()
    small_grad[...] = over_y[0] + over_y[1]
    phases.go("wait_all")
    for item in last + shared_last + routed_over:
        item.wait_recv()
    wire.drain()
    phases.go(None)


def moe_forward(
    n_dp, dy_begun, moe_in, smalls, ids, s_gate_in, s_up_in, s_down_in, e_gate, e_up, e_down,
    cols, pick, s_slope, s_silu, s_hidden, e_slope, e_silu, e_hidden, rows_in, part, e_out, shared,
    dy_group,
    x, wg, wu, wd, v_slope, v_silu, v_hidden, r_slope, r_silu, r_hidden, rows, out, sh,
    s_gate, s_up, s_down, send, recv, local,
):
    place_here = Place(n_dp)
    wire = Wire(send, recv)
    z, c, y = place_here.z, place_here.c, place_here.y
    f32, low = jnp.float32, jnp.bfloat16
    inside = Local(local)
    n_experts = ids.shape[0]
    tok_rows = ids.shape[2]
    phases = Phases()
    phases.go("entry")
    mine = z * 2 + y

    def block_of(slot):
        return dy_group.at[rows_of(slot * 2 + y, tok_rows), :]

    y_recv = wire.take(n_dp)
    y_send = wire.take_send(n_dp)

    def over_y(slot):
        ref = block_of(slot)
        return wire.copy_to(ref, ref, place_here.over_y, y_recv + slot, y_send + slot)

    loads = [
        inside.start(src, dst)
        for src, dst in ((moe_in, x), (s_gate_in, s_gate), (s_up_in, s_up), (s_down_in, s_down))
    ]
    near = [(lax.bitwise_xor(z, jnp.int32(dz)), c, y) for dz in range(1, n_dp)]
    barrier(near + [place_here.over_y])
    dy_chain = chain_gather(
        wire,
        place_here,
        lambda slot: [block_of(slot)],
        arrived=lambda slot: over_y(slot).start(),
        begun=True,
    )
    next(dy_chain)
    loads += [inside.start(src, dst) for src, dst in ((e_gate, wg), (e_up, wu), (e_down, wd))]
    hit = jnp.concatenate(
        [jnp.any(ids[s] == mine, axis=0, keepdims=True).astype(f32) for s in range(n_experts)], axis=0
    )
    upto = (
        lax.broadcasted_iota(jnp.int32, (tok_rows, tok_rows), 0)
        <= lax.broadcasted_iota(jnp.int32, (tok_rows, tok_rows), 1)
    ).astype(low)
    place = dot_f32(hit.astype(low), upto, 1, 0) - 1.0
    slots = lax.broadcasted_iota(jnp.int32, (CAP, tok_rows), 0).astype(f32)
    for s in range(n_experts):
        chosen = (hit[s : s + 1] > 0.5) & (place[s : s + 1] == slots)
        pick[s] = jnp.where(chosen, 1.0, 0.0).astype(low)
    phases.go("x_wait")
    for item in loads[:4]:
        item.wait()

    def gated(g, u):
        sigma = 1.0 / (1.0 + jnp.exp(-g))
        silu = g * sigma
        return u * (sigma * (1.0 + g * (1.0 - sigma))), silu, silu * u

    def shared_tile(at):
        here = x[at, :]
        logits = dot_f32(here, smalls[...], 1, 1)
        lane = lax.broadcasted_iota(jnp.int32, logits.shape, 1)
        routed = lane < n_experts
        top = jnp.max(jnp.where(routed, logits, -jnp.inf), axis=1, keepdims=True)
        expo = jnp.where(routed, jnp.exp(jnp.where(routed, logits, top) - top), 0.0)
        probs = expo / jnp.sum(expo, axis=1, keepdims=True)
        mix = jnp.sum(jnp.where(lane == n_experts, logits, 0.0), axis=1, keepdims=True)
        mix = 1.0 / (1.0 + jnp.exp(-mix))
        gate = jnp.sum(jnp.where(lane == mine, probs, 0.0), axis=1, keepdims=True)
        cols[at, 0:16] = jnp.where(
            routed, probs, jnp.where(lane == n_experts, mix, jnp.where(lane == n_experts + 1, gate, 0.0))
        )
        slope, silu, hidden = gated(dot_f32(here, s_gate[...], 1, 0), dot_f32(here, s_up[...], 1, 0))
        v_slope[at, :] = slope.astype(low)
        v_silu[at, :] = silu.astype(low)
        v_hidden[at, :] = hidden.astype(low)
        sh[at, :] = dot_f32(v_hidden[at, :], s_down[...], 1, 0).astype(low)

    phases.go("shared")
    by_rows(x.shape[0], 512, shared_tile)
    phases.go("dy_two")
    next(dy_chain)
    stores = [
        inside.start(src, dst)
        for src, dst in ((v_slope, s_slope), (v_silu, s_silu), (v_hidden, s_hidden), (sh, shared))
    ]

    def gather(s, carry):
        block = x[rows_of(s, tok_rows), :]
        rows[rows_of(s, CAP), :] = dot_f32(pick[s], block, 1, 0).astype(low)
        return carry

    phases.go("gather")
    lax.fori_loop(0, n_experts, gather, 0)
    stores.append(inside.start(rows, rows_in))
    phases.go("w_wait")
    for item in loads[4:]:
        item.wait()

    def routed_tile(at):
        here = rows[at, :]
        slope, silu, hidden = gated(dot_f32(here, wg[...], 1, 0), dot_f32(here, wu[...], 1, 0))
        r_slope[at, :] = slope.astype(low)
        r_silu[at, :] = silu.astype(low)
        r_hidden[at, :] = hidden.astype(low)
        out[at, :] = dot_f32(r_hidden[at, :], wd[...], 1, 0).astype(low)

    phases.go("routed")
    routed_tile(pl.ds(0, 384))
    phases.go("dy_three")
    next(dy_chain)
    phases.go("routed_end")
    routed_tile(pl.ds(384, 384))
    stores.append(inside.start(out, e_out))
    stores += [
        inside.start(src, dst)
        for src, dst in ((r_slope, e_slope), (r_silu, e_silu), (r_hidden, e_hidden))
    ]

    def scatter(s, carry):
        at = rows_of(s, tok_rows)
        back = dot_f32(pick[s], out[rows_of(s, CAP), :], 0, 0)
        mix = cols[at, n_experts : n_experts + 1]
        gate = cols[at, n_experts + 1 : n_experts + 2]
        x[at, :] = (gate * back + mix * sh[at, :].astype(f32)).astype(low)
        return carry

    phases.go("scatter")
    lax.fori_loop(0, n_experts // 2, scatter, 0)
    first = pl.ds(0, n_experts // 2 * tok_rows)
    last = pl.ds(n_experts // 2 * tok_rows, n_experts // 2 * tok_rows)
    stores.append(inside.start(x.at[first, :], part.at[first, :]))
    lax.fori_loop(n_experts // 2, n_experts, scatter, 0)
    phases.go("stores")
    stores.append(inside.start(x.at[last, :], part.at[last, :]))
    for item in stores:
        item.wait()
    phases.go("over_y")
    finish(dy_chain)
    for slot in range(n_dp):

        @pl.when(z != slot)
        def _():
            over_y(slot).wait_recv()
            over_y(slot).wait_send()

    phases.go(None)


def shared_backward(
    n_dp, dy_group, cols, pick, s_gate_in, s_up_in, s_down_in, s_slope_in, s_silu_in,
    s_hidden, e_out, shared, moe_in,
    grads_in, part, scalars, keep_gate, keep_up, keep_down, give_gate, give_up, give_down,
    dy, out, sh, d_sh, rows, grads, total, x, hidden,
    g_gate, g_up, g_down, got_gate, got_up, got_down,
    s_gate, s_up, s_down, s_slope, s_silu, sums, picked, slot_sums, send, recv, local, slots,
):
    f32, low = jnp.float32, jnp.bfloat16
    inside = Local(local)
    wire = Wire(send, recv)
    place = Place(n_dp)
    n_experts = pick.shape[0]
    tok_rows = pick.shape[2]
    units = s_gate.shape[1]
    lanes = grads.shape[1] // 2
    share = g_gate.shape[1]
    n_ctx = 4
    core = lax.rem(place.c, 2)
    chip = lax.div(place.c, 2)
    phases = Phases()
    phases.go("entry")

    depth = dy.shape[0]

    def fetch(index):
        slot = index % depth
        at = pl.ds(index * tok_rows, tok_rows)
        items = [
            pltpu.make_async_copy(src, dst.at[slot], slots.at[3 * slot + k])
            for k, (src, dst) in enumerate(
                (
                    (dy_group.at[at, :], dy),
                    (e_out.at[pl.ds(index * CAP, CAP), :], out),
                    (shared.at[at, :], sh),
                )
            )
        ]
        for item in items:
            item.start()
        return items

    coming = [fetch(index) for index in range(depth - 1)]
    to_load = [
        (s_down_in, s_down), (s_slope_in, s_slope), (s_silu_in, s_silu),
        (s_gate_in, s_gate), (s_up_in, s_up), (moe_in, x), (s_hidden, hidden),
    ]
    loads = []
    barrier([place.core])
    grads[...] = jnp.zeros_like(grads)
    sums[...] = jnp.zeros_like(sums)
    for index in range(n_experts):
        slot = index % depth
        if index + depth - 1 < n_experts:
            coming.append(fetch(index + depth - 1))
        if index < len(to_load):
            loads.append(inside.start(*to_load[index]))
        for item in coming[index]:
            item.wait()
        here = pl.ds(index * tok_rows, tok_rows)
        chosen = pick[index].astype(f32)
        gate = jnp.transpose(cols[here, :])[n_experts + 1 : n_experts + 2, :]
        gate = jnp.sum(chosen * gate, axis=1, keepdims=True)
        picked[...] = dot_f32(pick[index], dy[slot], 1, 0)

        def slot_rows(at):
            grad = picked[at, :]
            this = out[slot, at, :].astype(f32)
            slot_sums[at, 0:1] = jnp.sum(this * grad, axis=1, keepdims=True)

        by_rows(CAP, 32, slot_rows)
        rows[pl.ds(index * CAP, CAP), :] = (gate * picked[...]).astype(low)
        d_gate = jnp.sum(chosen * slot_sums[:, 0:1], axis=0, keepdims=True)

        def chunk(at):
            there = pl.ds(pl.multiple_of(index * tok_rows + at.start, at.size), at.size)
            grad = dy[slot, at, :].astype(f32)
            mix = cols[there, n_experts : n_experts + 1]
            d_sh[there, :] = (mix * grad).astype(low)
            sums[at, 0:1] = jnp.sum(sh[slot, at, :].astype(f32) * grad, axis=1, keepdims=True)

        by_rows(tok_rows, 32, chunk)
        shared_dot = jnp.transpose(sums[...])[0:1, :]
        row_of = lax.broadcasted_iota(jnp.int32, (8, tok_rows), 0)
        scalars[index] = jnp.where(row_of == 0, d_gate, jnp.where(row_of == 1, shared_dot, 0.0))
    stores = [inside.start(rows, grads_in)]

    def shared_tile(at):
        d_hidden = dot_f32(d_sh[at, :], s_down[...], 1, 1)
        d_gate = (d_hidden * s_slope[at, :].astype(f32)).astype(low)
        d_up = (d_hidden * s_silu[at, :].astype(f32)).astype(low)
        grads[at, 0:units] = d_gate
        grads[at, lanes : lanes + units] = d_up
        total[at, :] = (dot_f32(d_gate, s_gate[...], 1, 1) + dot_f32(d_up, s_up[...], 1, 1)).astype(low)

    for item in loads[:5]:
        item.wait()
    phases.go("shared")
    by_rows(d_sh.shape[0], 512, shared_tile)
    stores.append(inside.start(total, part))
    for item in loads[5:]:
        item.wait()
    phases.go("in_grads")

    def block_index(dx, dz, sibling):
        side = lax.bitwise_xor(chip, jnp.int32(dx)) * 2
        return dz * n_ctx + side + (1 - core if sibling else core)

    sent = {}

    def to_sibling(dz, mats):
        for dx in (1, 0):
            for grad, got in mats:
                item = wire.copy(grad.at[block_index(dx, dz, True)], got.at[dx, dz], place.core)
                item.start()
                sent.setdefault(dz, []).append(item)

    step = n_ctx * share
    for dz in range(n_dp):
        product = dot_f32(x[:, dz * step : (dz + 1) * step], grads[...], 0, 0)
        for k in range(n_ctx):
            here = slice(k * share, (k + 1) * share)
            g_gate[dz * n_ctx + k] = product[here, 0:units].astype(low)
            g_up[dz * n_ctx + k] = product[here, lanes : lanes + units].astype(low)
        to_sibling(dz, ((g_gate, got_gate), (g_up, got_up)))
    phases.go("down_grads")
    down = {}
    for dz in range(n_dp):
        product = dot_f32(hidden[...], d_sh[:, dz * step : (dz + 1) * step], 0, 0)
        for k in range(n_ctx):
            g_down[dz * n_ctx + k] = product[:, k * share : (k + 1) * share].astype(low)
        for dx in (1, 0):
            item = wire.copy(g_down.at[block_index(dx, dz, True)], got_down.at[dx, dz], place.core)
            item.start()
            down.setdefault(dz, []).append(item)
    phases.go("sums")

    def collect(dx, dz, grad, got, out_ref):
        mine = block_index(dx, dz, False)
        add_block(grad.at[mine], got.at[dx, dz])
        size = grad.shape[1]
        stores.append(inside.start(grad.at[mine], out_ref.at[pl.ds(dz * size, size), :]))

    for dz in range(n_dp):
        for item in sent[dz]:
            item.wait_recv()
        for dx, outs in ((1, (give_gate, give_up)), (0, (keep_gate, keep_up))):
            for grad, got, out_ref in zip((g_gate, g_up), (got_gate, got_up), outs):
                collect(dx, dz, grad, got, out_ref)
    for dz in range(n_dp):
        for item in down[dz]:
            item.wait_recv()
        for dx, out_ref in ((1, give_down), (0, keep_down)):
            collect(dx, dz, g_down, got_down, out_ref)
    phases.go("stores")
    for item in stores:
        item.wait()
    wire.drain()
    phases.go(None)


def routed_backward(
    n_dp, grads_in, rows_in, e_gate, e_up, e_down, slope_in, silu_in, hidden_in, shared_part, scalars,
    keep_sgate, give_sgate, give_sup, give_sdown, pick,
    own_sum, got_scalars, t_sgate, x_sup, x_sdown,
    keep_gate, keep_up, keep_down, give_up, give_down, x_gate,
    wg, wu, wd, grads, rows, slope, silu, hidden, d_hid, d_in, total,
    got_gate, got_up, got_down, got_y, got_dp, x_sgate, sum_sgate, send, recv, local,
):
    f32, low = jnp.float32, jnp.bfloat16
    inside = Local(local)
    wire = Wire(send, recv)
    place = Place(n_dp)
    z, c, y = place.z, place.c, place.y
    n_experts = pick.shape[0]
    tok_rows = pick.shape[2]
    units = wg.shape[1]
    width = rows.shape[1]
    core = lax.rem(c, 2)
    chip = lax.div(c, 2)
    group = z * 2 + y
    phases = Phases()
    phases.go("entry")
    loads = [
        inside.start(src, dst)
        for src, dst in (
            (grads_in, grads), (e_down, wd), (slope_in, slope), (silu_in, silu),
            (e_gate, wg), (e_up, wu), (shared_part, total), (rows_in, rows), (hidden_in, hidden),
            (keep_sgate, sum_sgate),
        )
    ]

    def near(dz, y_to):
        return (lax.bitwise_xor(z, jnp.int32(dz)), c, y_to)

    members = [(dz, y_to) for dz in range(n_dp) for y_to in (y, place.yn) if dz or y_to is not y]
    barrier([place.core, place.over_x] + [near(dz, y_to) for dz, y_to in members])

    over_x = []

    def go_over_x(src, dst):
        item = wire.copy(src, dst, place.over_x)
        item.start()
        over_x.append(item)

    go_over_x(give_sgate, x_sgate)
    scalar_items = [inside.start(scalars.at[group], got_scalars.at[group])]
    for dz, y_to in members:
        target = lax.bitwise_xor(z, jnp.int32(dz)) * 2 + y_to
        item = wire.copy(scalars.at[target], got_scalars.at[group], near(dz, y_to))
        item.start()
        scalar_items.append(item)
    for item in loads[:4]:
        item.wait()
    phases.go("routed")
    half = grads.shape[0] // 2

    def routed_tile(at, wait):
        d_hidden = dot_f32(grads[at, :], wd[...], 1, 1)
        d_gate = (d_hidden * slope[at, :].astype(f32)).astype(low)
        d_up = (d_hidden * silu[at, :].astype(f32)).astype(low)
        d_hid[at, 0:units] = d_gate
        d_hid[at, units : 2 * units] = d_up
        for item in wait:
            item.wait()
        d_in[at, :] = (dot_f32(d_gate, wg[...], 1, 1) + dot_f32(d_up, wu[...], 1, 1)).astype(low)

    routed_tile(pl.ds(0, half), loads[4:6])
    go_over_x(give_sup, x_sup)
    go_over_x(give_sdown, x_sdown)
    routed_tile(pl.ds(half, half), [])
    for item in loads[6:]:
        item.wait()
    phases.go("to_tokens")

    def to_tokens(s, carry):
        at = rows_of(s, tok_rows)
        back = dot_f32(pick[s], d_in[rows_of(s, CAP), :], 0, 0)
        total[at, :] = (back + total[at, :].astype(f32)).astype(low)
        return carry

    lax.fori_loop(0, n_experts, to_tokens, 0)

    orders = ((3, 2, 1, 0), (3, 0, 2, 1), (0, 3, 1, 2), (0, 1, 2, 3))
    lower = 1 - lax.div(z, 2)
    order = (
        3 * lower,
        lower * (2 - 2 * z) + (1 - lower) * (7 - 2 * z),
        1 + lax.rem(z, 2),
        z,
    )
    y_swaps = []
    for step in range(n_dp):
        from_row = order[step] * 2 + place.yn
        item = wire.copy(total.at[rows_of(from_row, tok_rows), :], got_y.at[step], place.over_y)
        item.start()
        y_swaps.append(item)
    dp_recv = wire.take(2 * n_dp)
    dp_send = wire.take_send(2 * n_dp)

    def along(target, up):
        slot = target - 1 if up else n_dp - 1 + target
        return wire.copy_to(
            total.at[pl.ds(pl.multiple_of((target * 2 + y) * tok_rows, tok_rows), tok_rows), :],
            got_dp.at[slot],
            place.up if up else place.down,
            dp_recv + slot,
            dp_send + slot,
        )

    def add_from(target, up):
        along(target, up).wait_recv()
        slot = target - 1 if up else n_dp - 1 + target
        add_into(total, pl.ds(0, width), (target * 2 + y) * tok_rows, got_dp.at[slot])

    def over_dp(step):
        y_swaps[step].wait_recv()
        add_into(total, pl.ds(0, width), (order[step] * 2 + y) * tok_rows, got_y.at[step])
        for here in range(n_dp):
            target = orders[here][step]

            @pl.when(z == here)
            def _():
                if target == here:
                    if here > 0:
                        add_from(target, True)
                    if here < n_dp - 1:
                        add_from(target, False)
                else:
                    up = target > here
                    if 0 < here < n_dp - 1:
                        add_from(target, up)
                    along(target, up).start()

    phases.go("shared_gate")
    over_x[0].wait_recv()
    add_block(sum_sgate, x_sgate)
    size = t_sgate.shape[1]
    along_dp = []
    for dz in (2, 3, 1, 0):
        to = lax.bitwise_xor(z, jnp.int32(dz))
        src = sum_sgate.at[rows_of(to, size), :]
        if dz:
            item = wire.copy(src, t_sgate.at[z], near(dz, y))
            item.start()
        else:
            item = inside.start(src, t_sgate.at[z])
        along_dp.append(item)

    def piece(dx, sibling):
        return lax.bitwise_xor(chip, jnp.int32(dx)) * 2 + (1 - core if sibling else core)

    quarter = width // 4
    tile = quarter // 2

    def in_grads(index):
        def one(part, carry):
            at = pl.ds(pl.multiple_of(index * quarter + part * tile, tile), tile)
            value = dot_f32(rows[:, at], d_hid[...], 0, 0)
            wg[at, :] = value[:, 0:units].astype(low)
            wu[at, :] = value[:, units : 2 * units].astype(low)
            return carry

        lax.fori_loop(0, 2, one, 0)

    def down_grads(index):
        at = rows_of(index, quarter)
        wd[:, at] = dot_f32(hidden[...], grads[:, at], 0, 0).astype(low)

    phases.go("in_grads")
    sent = {}
    for dx in (1, 0):
        index = piece(dx, True)
        in_grads(index)
        at = rows_of(index, quarter)
        sent[dx] = [
            wire.copy(wg.at[at, :], got_gate.at[dx], place.core),
            wire.copy(wu.at[at, :], got_up.at[dx], place.core),
        ]
        for item in sent[dx]:
            item.start()
    for dx in (1, 0):
        in_grads(piece(dx, False))
    phases.go("gate_sums")

    def finish_piece(grad, dx, got, target):
        at = rows_of(piece(dx, False), quarter)
        add_block(grad.at[at, :], got.at[dx])
        if target is not None:
            stores.append(inside.start(grad.at[at, :], target))
        return grad.at[at, :]

    stores = []
    sent[1][0].wait_recv()
    gate_over = wire.copy(finish_piece(wg, 1, got_gate, None), x_gate, place.over_x)
    gate_over.start()
    phases.go("over_dp_one")
    over_dp(0)
    phases.go("down_grads")
    down = {}
    for dx in (1, 0):
        index = piece(dx, True)
        down_grads(index)
        down[dx] = wire.copy(wd.at[:, rows_of(index, quarter)], got_down.at[dx], place.core)
        down[dx].start()
    for dx in (1, 0):
        down_grads(piece(dx, False))
    phases.go("over_dp_two")
    over_dp(1)
    phases.go("sums")
    sent[1][1].wait_recv()
    finish_piece(wu, 1, got_up, give_up)
    for item in sent[0]:
        item.wait_recv()
    finish_piece(wg, 0, got_gate, keep_gate)
    finish_piece(wu, 0, got_up, keep_up)
    for dx, target in ((1, give_down), (0, keep_down)):
        down[dx].wait_recv()
        at = rows_of(piece(dx, False), quarter)
        add_into(wd, at, 0, got_down.at[dx])
        stores.append(inside.start(wd.at[:, at], target))
    phases.go("over_dp_three")
    over_dp(2)
    phases.go("over_dp_own")
    over_dp(3)
    for here in range(n_dp):

        @pl.when(z == here)
        def _():
            for target in range(n_dp):
                if target != here:
                    along(target, target > here).wait_send()


    def add_up(at):
        mine = pl.ds(pl.multiple_of(group * tok_rows + at.start, at.size), at.size)
        own_sum[at, :] = total[mine, :].astype(f32)

    by_rows(tok_rows, 16, add_up)
    phases.go("wait_all")
    for item in stores:
        item.wait()
    for item in over_x[1:] + scalar_items + along_dp + [gate_over]:
        item.wait_recv()
    wire.drain()
    phases.go(None)


def finish_grads(n_ctx, *refs):
    (
        t_gate, t_up, t_down, own_gate, own_up, own_down,
        far_gate, far_up, far_down, heads, out_weight, hidden, moe_sum,
        o_sgate, o_sup, o_sdown, o_egate, o_eup, o_edown, o_query, o_key, o_value, o_out, o_mixed,
    ) = refs
    f32 = jnp.float32
    n_dp, share, units = t_gate.shape
    for source, target in ((t_gate, o_sgate), (t_up, o_sup)):
        target[...] = jnp.concatenate([source[k].astype(f32) for k in range(n_dp)], axis=1)
    o_sdown[...] = t_down[0].astype(f32)
    for own, far, target in (
        (own_gate, far_gate, o_egate), (own_up, far_up, o_eup), (own_down, far_down, o_edown),
    ):

        def add(at):
            target[at, :] = own[at, :].astype(f32) + far[at, :].astype(f32)

        by_rows(target.shape[0], 32, add)

    o_mixed[...] = (hidden[...] + moe_sum[...].astype(f32)).astype(o_mixed.dtype)
    cols = heads.shape[2] // 3
    for k, target in enumerate((o_query, o_key, o_value)):
        for c in range(n_ctx):
            target[:, c * cols : (c + 1) * cols] = heads[c, :, k * cols : (k + 1) * cols].astype(f32)
    o_out[...] = out_weight[0].astype(f32)


def whole_tables(seq_len, head_dim):
    half = head_dim // 2
    freq = np.float32(THETA) ** (-(2.0 * np.arange(half, dtype=np.float32)) / np.float32(head_dim))
    angle = np.arange(seq_len, dtype=np.float32)[:, None] * freq.astype(np.float32)[None, :]
    cosine, sine = np.cos(angle), np.sin(angle)
    return (
        jnp.asarray(np.concatenate([cosine, cosine], axis=1), jnp.float32),
        jnp.asarray(np.concatenate([-sine, sine], axis=1), jnp.float32),
    )


def tokens_plan(
    tokens,
    out_grad,
    expert_ids,
    norm1_gain,
    w_query,
    w_key,
    w_value,
    query_bias_heads,
    bias_key,
    bias_value,
    w_out,
    norm2_gain,
    w_router,
    shared_mix,
    shared_in_gate,
    shared_in_up,
    shared_down,
    expert_gate,
    expert_up,
    expert_down,
):
    low = jnp.bfloat16
    f32 = jnp.float32
    tok_rows, width = tokens.shape
    n_dp, n_ctx, n_half = (lax.axis_size(name) for name in (DP, CONTEXT, EXPERT))
    dp, ctx, half = (lax.axis_index(name) for name in (DP, CONTEXT, EXPERT))
    half_heads, head_dim = query_bias_heads.shape
    heads = half_heads // n_ctx
    cols = heads * head_dim
    seq_len = tok_rows * n_ctx * n_half
    n_blocks = seq_len // BLOCK
    n_experts = w_router.shape[1]
    n_group = n_dp * n_half
    my_expert = dp * n_half + half

    def group_out(rows):
        return lax.psum_scatter(rows, (DP, EXPERT), scatter_dimension=0, tiled=True)

    small = jnp.concatenate(
        [w_router.T, shared_mix[None], norm1_gain[None], norm2_gain[None]], axis=0
    )
    small = jnp.pad(small, ((0, 16 - small.shape[0]), (0, 0)))
    ids = jnp.pad(expert_ids.T, ((0, 8 - expert_ids.shape[1]), (0, 0)), constant_values=-1)
    hidden_units = shared_in_gate.shape[1] // n_dp

    biases = jnp.stack([query_bias_heads, bias_key, bias_value]).astype(f32)
    biases = lax.dynamic_slice_in_dim(biases, ctx * heads, heads, 1).reshape(3, cols)
    cosine, sine = whole_tables(seq_len, head_dim)
    vmem = pl.BlockSpec(memory_space=pltpu.VMEM)
    anywhere = pl.BlockSpec(memory_space=pl.ANY)
    share = w_query.shape[0]
    half_width = width // 2
    (
        attn_in, query, keys, values, attn, lse, hidden_own, moe_in,
        heads_weight, wo, sg, su, sd, small, ids_group, dy_begun,
    ) = pl.pallas_call(
        lambda *refs: forward_kernel(n_blocks, n_dp, *refs),
        out_shape=[
            like((seq_len, width), low),
            like((seq_len, cols), low),
            like((seq_len, cols), low),
            like((seq_len, cols), low),
            like((seq_len, cols), low),
            like((seq_len, cols), f32),
            like((tok_rows, width), f32),
            like((n_group * tok_rows, width), low),
            like((width, 3 * cols), low),
            like((cols, width), low),
            like((n_dp, n_ctx, share, hidden_units), low),
            like((n_dp, n_ctx, share, hidden_units), low),
            like((hidden_units, width), low),
            like((16, width), low),
            like((n_group, 8, tok_rows), jnp.int32),
            like((n_group * tok_rows, width), low),
        ],
        in_specs=[anywhere] * 11 + [vmem] * 3,
        out_specs=[anywhere] * 13 + [vmem] + [anywhere] * 2,
        scratch_shapes=[
            pltpu.VMEM((seq_len, width), low),
            pltpu.VMEM((seq_len, width), low),
            pltpu.VMEM((4, tok_rows, width), low),
            pltpu.VMEM((4, tok_rows, half_width), low),
            pltpu.VMEM((2, tok_rows, half_width), low),
            pltpu.VMEM((seq_len, width), low),
            pltpu.VMEM((seq_len, cols), low),
            pltpu.VMEM((seq_len, cols), low),
            pltpu.VMEM((seq_len, cols), low),
            pltpu.VMEM((seq_len, cols), low),
            pltpu.VMEM((seq_len, cols), f32),
            pltpu.VMEM((tok_rows, width), f32),
            pltpu.VMEM((width, 3 * cols), low),
            pltpu.VMEM((cols, width), low),
            pltpu.VMEM((2, share, n_dp * hidden_units), low),
            pltpu.VMEM((2, n_dp, share, hidden_units), low),
            pltpu.SemaphoreType.DMA((160,)),
            pltpu.SemaphoreType.DMA((160,)),
            pltpu.SemaphoreType.DMA((32,)),
        ],
        name="forward",
        compiler_params=pltpu.CompilerParams(
            collective_id=1, has_side_effects=True, vmem_limit_bytes=60 * 2**20
        ),
    )(
        tokens, out_grad, small, ids, w_query, w_key, w_value, w_out,
        shared_in_gate, shared_in_up, shared_down, biases, cosine, sine,
    )
    sg, su = sg.reshape(width, hidden_units), su.reshape(width, hidden_units)
    units = expert_gate.shape[2]
    s_weights = [
        pltpu.VMEM((width, hidden_units), low),
        pltpu.VMEM((width, hidden_units), low),
        pltpu.VMEM((hidden_units, width), low),
    ]
    gate_weight, up_weight, down_weight = expert_gate[0], expert_up[0], expert_down[0]
    slots = n_group * CAP
    group_rows = n_group * tok_rows
    (
        token_cols, pick, s_slope, s_silu, s_hidden, e_slope, e_silu, e_hidden, rows_in,
        moe_part, e_out, shared, dy_group,
    ) = pl.pallas_call(
        lambda *refs: moe_forward(n_dp, *refs),
        out_shape=[
            like((group_rows, 128), f32),
            like((n_group, CAP, tok_rows), low),
        ]
        + [like((group_rows, hidden_units), low)] * 3
        + [like((slots, units), low)] * 3
        + [
            like((slots, width), low),
            like((group_rows, width), low),
            like((slots, width), low),
            like((group_rows, width), low),
            like((group_rows, width), low),
        ],
        in_specs=[anywhere] * 2 + [vmem] * 2 + [anywhere] * 6,
        out_specs=[vmem] * 2 + [anywhere] * 11,
        scratch_shapes=[
            pltpu.VMEM((group_rows, width), low),
            pltpu.VMEM((width, units), low),
            pltpu.VMEM((width, units), low),
            pltpu.VMEM((units, width), low),
        ]
        + [pltpu.VMEM((group_rows, hidden_units), low)] * 3
        + [pltpu.VMEM((slots, units), low)] * 3
        + [pltpu.VMEM((slots, width), low)] * 2
        + [pltpu.VMEM((group_rows, width), low)]
        + s_weights
        + [pltpu.SemaphoreType.DMA((16,))] * 2
        + [pltpu.SemaphoreType.DMA((24,))],
        name="moe_forward",
        compiler_params=pltpu.CompilerParams(
            collective_id=3, has_side_effects=True, vmem_limit_bytes=63 * 2**20
        ),
        cost_estimate=pl.CostEstimate(
            flops=6 * width * (group_rows * hidden_units + slots * units),
            bytes_accessed=2 * (9 * width * units + 4 * group_rows * width),
            transcendentals=0,
        ),
        input_output_aliases={0: 12},
    )(dy_begun, moe_in, small, ids_group, sg, su, sd, gate_weight, up_weight, down_weight)
    lanes = -(-hidden_units // 128) * 128
    block_kinds = [(n_dp, share, hidden_units)] * 2 + [(n_dp, hidden_units, share)]
    shared_all = [(n_dp * n_ctx, share, hidden_units)] * 2 + [(n_dp * n_ctx, hidden_units, share)]
    results = pl.pallas_call(
        lambda *refs: shared_backward(n_dp, *refs),
        out_shape=[
            like((slots, width), low),
            like((group_rows, width), low),
            like((n_group, 8, tok_rows), f32),
        ]
        + [like((kind[0] * kind[1], kind[2]), low) for kind in block_kinds] * 2,
        in_specs=[anywhere] + [vmem] * 2 + [anywhere] * 9,
        out_specs=[anywhere] * 2 + [vmem] + [anywhere] * 6,
        scratch_shapes=[
            pltpu.VMEM((4, tok_rows, width), low),
            pltpu.VMEM((4, CAP, width), low),
            pltpu.VMEM((4, tok_rows, width), low),
            pltpu.VMEM((group_rows, width), low),
            pltpu.VMEM((slots, width), low),
            pltpu.VMEM((group_rows, 2 * lanes), low),
            pltpu.VMEM((group_rows, width), low),
            pltpu.VMEM((group_rows, width), low),
            pltpu.VMEM((group_rows, hidden_units), low),
        ]
        + [pltpu.VMEM(kind, low) for kind in shared_all]
        + [pltpu.VMEM((2, *kind), low) for kind in block_kinds]
        + s_weights
        + [pltpu.VMEM((group_rows, hidden_units), low)] * 2
        + [
            pltpu.VMEM((tok_rows, 128), f32),
            pltpu.VMEM((CAP, width), f32),
            pltpu.VMEM((CAP, 128), f32),
        ]
        + [pltpu.SemaphoreType.DMA((32,))] * 2
        + [pltpu.SemaphoreType.DMA((48,)), pltpu.SemaphoreType.DMA((12,))],
        name="shared_backward",
        compiler_params=pltpu.CompilerParams(
            collective_id=4, has_side_effects=True, vmem_limit_bytes=63 * 2**20
        ),
        cost_estimate=pl.CostEstimate(
            flops=12 * width * group_rows * hidden_units,
            bytes_accessed=2 * (9 * width * hidden_units + 8 * group_rows * width),
            transcendentals=0,
        ),
    )(
        dy_group, token_cols, pick, sg, su, sd, s_slope, s_silu, s_hidden, e_out, shared, moe_in,
    )
    grads_in, shared_part, scalars = results[:3]
    keep = results[3:6]
    give = results[6:9]
    quarter = width // n_ctx
    e_wide, e_tall = (quarter, units), (units, quarter)
    flat_kinds = [(kind[0] * kind[1], kind[2]) for kind in block_kinds]
    (
        own_sum, got_scalars, t_sgate, x_sup, x_sdown,
        keep_gate, keep_up, keep_down, give_up, give_down, x_gate,
    ) = pl.pallas_call(
        lambda *refs: routed_backward(n_dp, *refs),
        out_shape=[like((tok_rows, width), f32), like((n_group, 8, tok_rows), f32)]
        + [like(block_kinds[0], low)]
        + [like(kind, low) for kind in flat_kinds[1:]]
        + [like(kind, low) for kind in (e_wide, e_wide, e_tall, e_wide, e_tall, e_wide)],
        in_specs=[anywhere] * 14 + [vmem],
        out_specs=[vmem] + [anywhere] * 10,
        scratch_shapes=[
            pltpu.VMEM((width, units), low),
            pltpu.VMEM((width, units), low),
            pltpu.VMEM((units, width), low),
            pltpu.VMEM((slots, width), low),
            pltpu.VMEM((slots, width), low),
            pltpu.VMEM((slots, units), low),
            pltpu.VMEM((slots, units), low),
            pltpu.VMEM((slots, units), low),
            pltpu.VMEM((slots, 2 * units), low),
            pltpu.VMEM((slots, width), low),
            pltpu.VMEM((group_rows, width), low),
            pltpu.VMEM((2, *e_wide), low),
            pltpu.VMEM((2, *e_wide), low),
            pltpu.VMEM((2, *e_tall), low),
            pltpu.VMEM((n_dp, tok_rows, width), low),
            pltpu.VMEM((2 * (n_dp - 1), tok_rows, width), low),
            pltpu.VMEM(flat_kinds[0], low),
            pltpu.VMEM(flat_kinds[0], low),
            pltpu.SemaphoreType.DMA((32,)),
            pltpu.SemaphoreType.DMA((32,)),
            pltpu.SemaphoreType.DMA((24,)),
        ],
        name="routed_backward",
        compiler_params=pltpu.CompilerParams(
            collective_id=5, has_side_effects=True, vmem_limit_bytes=63 * 2**20
        ),
        cost_estimate=pl.CostEstimate(
            flops=12 * width * slots * units,
            bytes_accessed=2 * (12 * width * units + 4 * group_rows * width),
            transcendentals=0,
        ),
    )(
        grads_in, rows_in, gate_weight, up_weight, down_weight, e_slope, e_silu, e_hidden,
        shared_part, scalars, keep[0], *give, pick,
    )
    moe_sum = group_out(moe_part)

    own_cols = lax.dynamic_slice_in_dim(token_cols, my_expert * tok_rows, tok_rows, 0)
    probs_own = own_cols[:, :n_experts].T
    mix_own = own_cols[:, n_experts][None]
    by_share = n_ctx * share
    s_wide = (share, hidden_units)
    s_tall = (hidden_units, share)
    s_kinds = (s_wide, s_wide, s_tall)
    e_kinds = (e_wide, e_wide, e_tall)
    results = pl.pallas_call(
        lambda *refs: backward_kernel(n_blocks, n_dp, *refs),
        out_shape=[
            like((tok_rows, width), low),
            like((n_ctx, share, 3 * cols), low),
            like((n_ctx, cols, share), low),
            like((16, share), f32),
            like((n_ctx, 8, head_dim), f32),
        ]
        + [like((n_dp, *kind), low) for kind in s_kinds[1:]]
        + [like(kind, low) for kind in e_kinds[1:]]
        + [like((n_dp, *kind), low) for kind in s_kinds[1:]],
        in_specs=[vmem] * 2 + [anywhere] * 9 + [vmem] * 3 + [anywhere] * 10,
        out_specs=[vmem] + [anywhere] * 2 + [vmem] * 2 + [anywhere] * 6,
        scratch_shapes=[
            pltpu.VMEM((seq_len, width), low),
            pltpu.VMEM((tok_rows, width), f32),
            pltpu.VMEM((tok_rows, width), f32),
            pltpu.VMEM((tok_rows, width), low),
            pltpu.VMEM((48, tok_rows), low),
            pltpu.VMEM((2, 16, width), f32),
            pltpu.VMEM((seq_len, width), low),
            pltpu.VMEM((seq_len, cols), low),
            pltpu.VMEM((seq_len, 3 * cols), low),
            pltpu.VMEM((seq_len, head_dim), f32),
            pltpu.VMEM((seq_len, head_dim), f32),
            pltpu.VMEM((4, tok_rows, width), low),
            pltpu.VMEM((4, tok_rows, half_width), low),
            pltpu.VMEM((2, tok_rows, half_width), low),
            pltpu.VMEM((width, 3 * cols), low),
            pltpu.VMEM((cols, width), low),
            pltpu.VMEM((n_dp, by_share, 3 * cols), low),
            pltpu.VMEM((n_dp, by_share, 3 * cols), low),
            pltpu.VMEM((n_dp, cols, by_share), low),
            pltpu.VMEM((n_dp, cols, by_share), low),
            pltpu.VMEM((cols, by_share), low),
            pltpu.VMEM((n_dp * n_ctx, 24, share), f32),
            pltpu.VMEM((n_dp * n_ctx, 24, share), f32),
            pltpu.VMEM((2, 16, share), f32),
            pltpu.VMEM((3, 2, *s_wide), low),
            pltpu.VMEM((3, 2, *s_tall), low),
            pltpu.VMEM((tok_rows, width), f32),
            pltpu.VMEM((tok_rows, width), low),
            pltpu.VMEM((tok_rows, width), low),
            pltpu.VMEM((width, 3 * cols), low),
            pltpu.VMEM((cols, width), low),
            pltpu.VMEM((seq_len, cols), low),
            pltpu.VMEM((seq_len, cols), low),
            pltpu.VMEM((seq_len, cols), low),
            pltpu.VMEM((seq_len, cols), low),
            pltpu.VMEM((seq_len, cols), f32),
            pltpu.VMEM((seq_len, width), low),
            pltpu.VMEM((seq_len, head_dim), f32),
            pltpu.VMEM((seq_len, head_dim), f32),
            pltpu.SemaphoreType.DMA((160,)),
            pltpu.SemaphoreType.DMA((160,)),
            pltpu.SemaphoreType.DMA((32,)),
            pltpu.SemaphoreType.DMA((6,)),
        ],
        name="backward",
        compiler_params=pltpu.CompilerParams(
            collective_id=2, has_side_effects=True, vmem_limit_bytes=63 * 2**20
        ),
    )(
        own_sum, got_scalars, *keep[1:], x_sup, x_sdown, give_up, give_down,
        hidden_own, out_grad, tokens, small, probs_own, mix_own,
        heads_weight, wo, query, keys, values, attn, lse, attn_in, cosine, sine,
    )
    input_grad, heads_grad, out_weight_grad, small_grad, bias_grad = results[:5]
    s_done = (t_sgate, *results[5:7])
    e_own, e_other = (keep_gate, keep_up, keep_down), (x_gate, *results[7:9])
    finished = pl.pallas_call(
        lambda *refs: finish_grads(n_ctx, *refs),
        out_shape=[
            like((share, n_dp * hidden_units), f32),
            like((share, n_dp * hidden_units), f32),
            like((n_dp * hidden_units, share), f32),
            like(e_wide, f32),
            like(e_wide, f32),
            like(e_tall, f32),
            like((share, n_ctx * cols), f32),
            like((share, n_ctx * cols), f32),
            like((share, n_ctx * cols), f32),
            like((n_ctx * cols, share), f32),
            like((tok_rows, width), low),
        ],
        grid=(4,),
        in_specs=[pl.BlockSpec((n_dp, share // 4, hidden_units), lambda i: (0, i, 0))] * 2
        + [pl.BlockSpec((1, hidden_units, share), lambda i: (i, 0, 0))]
        + [pl.BlockSpec((kind[0] // 4, kind[1]), lambda i: (i, 0)) for kind in e_kinds * 2]
        + [
            pl.BlockSpec((n_ctx, share // 4, 3 * cols), lambda i: (0, i, 0)),
            pl.BlockSpec((1, cols, share), lambda i: (i, 0, 0)),
            pl.BlockSpec((tok_rows // 4, width), lambda i: (i, 0)),
            pl.BlockSpec((tok_rows // 4, width), lambda i: (i, 0)),
        ],
        out_specs=[pl.BlockSpec((share // 4, n_dp * hidden_units), lambda i: (i, 0))] * 2
        + [pl.BlockSpec((hidden_units, share), lambda i: (i, 0))]
        + [pl.BlockSpec((kind[0] // 4, kind[1]), lambda i: (i, 0)) for kind in e_kinds]
        + [pl.BlockSpec((share // 4, n_ctx * cols), lambda i: (i, 0))] * 3
        + [
            pl.BlockSpec((cols, share), lambda i: (i, 0)),
            pl.BlockSpec((tok_rows // 4, width), lambda i: (i, 0)),
        ],
        name="finish_grads",
        compiler_params=pltpu.CompilerParams(vmem_limit_bytes=63 * 2**20),
    )(*s_done, *e_own, *e_other, heads_grad, out_weight_grad, hidden_own, moe_sum)
    grad_sgate, grad_sup, grad_sdown = finished[:3]
    routed = [item[None] for item in finished[3:6]]
    heads_grad = finished[6:9]
    grad_out, mixed = finished[9:11]
    bias_sum = bias_grad[:, : 3 * heads].reshape(n_ctx, 3, heads, head_dim)
    bias_sum = bias_sum.transpose(1, 0, 2, 3).reshape(3, half_heads, head_dim)
    bias_share = head_dim // (n_dp * n_ctx)
    bias_sum = lax.dynamic_slice_in_dim(bias_sum, (dp * n_ctx + ctx) * bias_share, bias_share, 2)
    return (
        mixed,
        input_grad,
        small_grad[n_experts + 1],
        heads_grad[0],
        heads_grad[1],
        heads_grad[2],
        bias_sum[0],
        bias_sum[1],
        bias_sum[2],
        grad_out,
        small_grad[n_experts + 2],
        small_grad[:n_experts].T,
        small_grad[n_experts],
        grad_sgate,
        grad_sup,
        grad_sdown,
        routed[0],
        routed[1],
        routed[2],
    )


def on_device(*arrays):
    sizes = [lax.axis_size(name) for name in (DP, CONTEXT, EXPERT)]
    if sizes == [4, 4, 2] and arrays[7].shape[0] % sizes[1] == 0:
        return tokens_plan(*arrays)
    return weights_plan(*arrays)


def solution(mesh):
    placed = (
        P((DP, CONTEXT, EXPERT), None),
        P((DP, CONTEXT, EXPERT), None),
        P((DP, CONTEXT, EXPERT), None),
        P((DP, CONTEXT)),
        P((DP, CONTEXT), EXPERT),
        P((DP, CONTEXT), EXPERT),
        P((DP, CONTEXT), EXPERT),
        P(EXPERT, None),
        P(EXPERT, None),
        P(EXPERT, None),
        P(EXPERT, (DP, CONTEXT)),
        P((DP, CONTEXT)),
        P((DP, CONTEXT), None),
        P((DP, CONTEXT)),
        P((DP, CONTEXT), EXPERT),
        P((DP, CONTEXT), EXPERT),
        P(EXPERT, (DP, CONTEXT)),
        P((DP, EXPERT), None, None),
        P((DP, EXPERT), None, None),
        P((DP, EXPERT), None, None),
    )
    return jax.shard_map(
        on_device,
        mesh=mesh,
        in_specs=placed,
        out_specs=(
            P((DP, CONTEXT, EXPERT), None),
            P((DP, CONTEXT, EXPERT), None),
            P((DP, CONTEXT)),
            P((DP, CONTEXT), EXPERT),
            P((DP, CONTEXT), EXPERT),
            P((DP, CONTEXT), EXPERT),
            P(EXPERT, (DP, CONTEXT)),
            P(EXPERT, (DP, CONTEXT)),
            P(EXPERT, (DP, CONTEXT)),
            P(EXPERT, (DP, CONTEXT)),
            P((DP, CONTEXT)),
            P((DP, CONTEXT), None),
            P((DP, CONTEXT)),
            P((DP, CONTEXT), EXPERT),
            P((DP, CONTEXT), EXPERT),
            P(EXPERT, (DP, CONTEXT)),
            P((DP, EXPERT), CONTEXT, None),
            P((DP, EXPERT), CONTEXT, None),
            P((DP, EXPERT), None, CONTEXT),
        ),
        check_vma=False,
    )
```
